32 devices in a mesh: wide: 8 (over y, x, core), narrow: 4 (over z).
Axes of the slice: x: 2, y: 2, z: 4, core: 2. Of those that a mesh axis runs over, the one named last changes fastest.
Arguments:
- tokens: bfloat16 [8192, 768], P(('wide', 'narrow')), may hold values from -6 to 6
- norm_gain: bfloat16 [768], P(('wide', 'narrow')), may hold values from 0.25 to 1.75
- w_in: bfloat16 [768, 3, 3072], P(('wide', 'narrow')), may hold values from -0.21875 to 0.21875
- conv_w: bfloat16 [4, 1536], P(None, ('wide', 'narrow')), may hold values from -0.5 to 0.5
- conv_b: bfloat16 [1536], P(('wide', 'narrow')), may hold values from -0.5 to 0.5
- w_x: bfloat16 [1536, 3, 80], P(('wide', 'narrow')), may hold values from -0.15625 to 0.15625
- w_dt: bfloat16 [48, 3, 1536], P(None, None, ('wide', 'narrow')), may hold values from -0.875 to 0.875
- dt_bias: bfloat16 [3, 1536], P(None, ('wide', 'narrow')), may hold values from -6.875 to -2.25
- a_log: bfloat16 [1536, 16], P(('wide', 'narrow')), may hold values from 0 to 2.765625
- d_skip: bfloat16 [1536], P(('wide', 'narrow')), may hold values from 0.5 to 1.5
- w_out: bfloat16 [1536, 3, 768], P(('wide', 'narrow')), may hold values from -0.4375 to 0.4375
- mod_ids: int32 [8192], P(('wide', 'narrow')), may hold values from 0 to 2, as said below
- split_at: int32 [8], P('wide'), may hold values from 128 to 896, as said below
- cotangent: bfloat16 [8192, 768], P(('wide', 'narrow')), may hold values from -6 to 6
Outputs:
- mixed: bfloat16 [8192, 768], P(('wide', 'narrow'))
- grad_tokens: bfloat16 [8192, 768], P(('wide', 'narrow'))
- grad_norm_gain: float32 [768], P(('wide', 'narrow'))
- grad_w_in: float32 [768, 3, 3072], P(('wide', 'narrow'))
- grad_conv_w: float32 [4, 1536], P(None, ('wide', 'narrow'))
- grad_conv_b: float32 [1536], P(('wide', 'narrow'))
- grad_w_x: float32 [1536, 3, 80], P(('wide', 'narrow'))
- grad_w_dt: float32 [48, 3, 1536], P(None, None, ('wide', 'narrow'))
- grad_dt_bias: float32 [3, 1536], P(None, ('wide', 'narrow'))
- grad_a_log: float32 [1536, 16], P(('wide', 'narrow'))
- grad_d_skip: float32 [1536], P(('wide', 'narrow'))
- grad_w_out: float32 [1536, 3, 768], P(('wide', 'narrow'))
The draws below stay inside these ranges and needn't reach their ends.
Inputs may be any that keep to these rules, and one draw needn't show every extreme that they name: `mod_ids`: each aligned run of 128 tokens holds one modality. Tokens [0, split_at[g]) of group g form one sequence and [split_at[g], 1024) another; the shorter one has fewer than 256 tokens.
All inputs are finite; a program needn't handle non-finite values.
Results may differ from the reference program's by a relative error of at most 0.014.
Values may be sent and summed in bfloat16 or wider, within the bound.
No kernel may reach another device: no remote copies, remote signals or barrier semaphores. Data moves between devices by JAX's collectives and lax.ppermute only.
A program may use at most 384 MiB of HBM per device.

```python
import jax
import jax.numpy as jnp
from jax import lax

D = 768
E = 1536
N = 16
R = 48
K = 4
MODS = 3
XW = 80
TOK_DEV = 256
RUN = 128
SCAN_BLOCK = 64
GROUP = 1024
GROUPS = 8
TOKENS = 8192


def draw_mod_ids(key, part):
    key = jax.random.fold_in(key, 11)
    run_kinds = jax.random.randint(key, (TOKENS // RUN,), 0, MODS)
    return jnp.repeat(run_kinds, RUN).astype(jnp.int32)


def draw_split_at(key, part):
    key = jax.random.fold_in(key, 23)
    side_key, size_key = jax.random.split(key)
    side_pick = jax.random.randint(side_key, (GROUPS,), 0, 2)
    shorter = jax.random.randint(size_key, (GROUPS,), TOK_DEV // 2, TOK_DEV)
    places = jnp.arange(GROUPS)
    side_pick = jnp.where(places == 0, 0, jnp.where(places == GROUPS - 1, 1, side_pick))
    shorter = jnp.where((places == 0) | (places == GROUPS - 1), TOK_DEV // 2, shorter)
    return jnp.where(side_pick == 0, shorter, GROUP - shorter).astype(jnp.int32)


def block_levels(stream_key, shape, pieces, least, largest):
    factor_of, own = 1.0, jax.random.fold_in(stream_key, 6)
    for axis_at, blocks in pieces:
        draws = jnp.exp(jax.random.uniform(jax.random.fold_in(own, axis_at), (blocks,), jnp.float32, least / len(pieces), largest / len(pieces)))
        factor_of = factor_of * jnp.repeat(draws, shape[axis_at] // blocks).reshape([-1 if axis == axis_at else 1 for axis in range(len(shape))])
    return factor_of


def normal_values(key, extent, width, limit, pieces=(), kind=jnp.bfloat16):
    entries = jax.random.normal(key, extent, jnp.float32) * width
    if len(pieces) > 0:
        entries = block_levels(key, extent, pieces, -0.22, 0.18) * entries
    return jnp.clip(entries, min=-limit, max=limit).astype(kind)


def setup_inputs(seed: int = 0) -> dict:
    keys = jax.random.split(jax.random.key(seed), 15)
    tokens = normal_values(keys[0], (TOKENS, D), 1.0, 6.0, ((0, 32),))
    norm_gain = jnp.clip(1.0 + 0.15 * jax.random.normal(keys[1], (D,), jnp.float32), 0.25, 1.75).astype(jnp.bfloat16)
    w_in = normal_values(keys[2], (D, MODS, 2 * E), D ** -0.5, 0.21875, ((0, 32),))
    conv_w = jnp.clip(jax.random.uniform(keys[3], (K, E), jnp.float32, -0.5, 0.5) * block_levels(keys[3], (K, E), ((1, 32),), -0.4, 0.0), -0.5, 0.5).astype(jnp.bfloat16)
    conv_b = jnp.clip(jax.random.uniform(keys[4], (E,), jnp.float32, -0.5, 0.5) * block_levels(keys[4], (E,), ((0, 32),), -0.4, 0.0), -0.5, 0.5).astype(jnp.bfloat16)
    w_x = normal_values(keys[5], (E, MODS, XW), E ** -0.5, 0.15625, ((0, 32),))
    w_dt = normal_values(keys[6], (R, MODS, E), R ** -0.5, 0.875, ((2, 32),))
    dt_bias = jnp.clip(-6.875 + 4.625 * jax.random.uniform(keys[7], (MODS, E), jnp.float32) ** block_levels(keys[7], (MODS, E), ((1, 32),), -0.2, 0.2), -6.875, -2.25).astype(jnp.bfloat16)
    a_log = jnp.clip(2.765625 * jax.random.uniform(keys[8], (E, N), jnp.float32) ** block_levels(keys[8], (E, N), ((0, 32),), -0.2, 0.2), 0.0, 2.765625).astype(jnp.bfloat16)
    d_skip = jnp.clip(0.5 + 1.0 * jax.random.uniform(keys[9], (E,), jnp.float32) ** block_levels(keys[9], (E,), ((0, 32),), -0.2, 0.2), 0.5, 1.5).astype(jnp.bfloat16)
    w_out = normal_values(keys[10], (E, MODS, D), (E // 8) ** -0.5, 0.4375, ((0, 32),))
    mod_ids = draw_mod_ids(jax.random.fold_in(keys[14], 71), 0)
    split_at = draw_split_at(jax.random.fold_in(keys[14], 71), 0)
    cotangent = normal_values(keys[13], (TOKENS, D), 1.0, 6.0, ((0, 32),))
    return dict(tokens=tokens, norm_gain=norm_gain, w_in=w_in, conv_w=conv_w, conv_b=conv_b, w_x=w_x, w_dt=w_dt, dt_bias=dt_bias, a_log=a_log, d_skip=d_skip, w_out=w_out, mod_ids=mod_ids, split_at=split_at, cotangent=cotangent)


@jax.custom_vjp
def low(v):
    return lax.optimization_barrier(v.astype(jnp.bfloat16)).astype(jnp.float32)

@jax.custom_vjp
def low_back(v):
    return v

def low_keep(v):
    return (low(v), None)

def low_pass(kept, grad):
    return (grad,)

def back_keep(v):
    return (v, None)

def back_low(kept, grad):
    return (low(grad),)
low.defvjp(low_keep, low_pass)
low_back.defvjp(back_keep, back_low)
highest = lax.Precision.HIGHEST
epsilon = 1e-05

def matmul(left_rows, weights):
    return jnp.dot(left_rows, weights, precision=highest, preferred_element_type=jnp.float32)

def select_rows(chosen, left_rows, weights):
    running = jnp.zeros((left_rows.shape[0], weights.shape[2]), jnp.float32)
    for modality in range(MODS):
        running = running + chosen[:, modality:modality + 1] * matmul(left_rows, weights[:, modality, :])
    return running

def modality_layer(tokens, norm_gain, w_in, conv_w, conv_b, w_x, w_dt, dt_bias, a_log, d_skip, w_out, mod_ids, split_at):
    decay_rates = -jnp.exp(a_log)

    def advance(carried, token_in):
        step_dt, step_b, step_c, step_u, step_keep = token_in
        decay_now = jnp.exp(step_dt[:, None] * decay_rates) * step_keep
        carried = decay_now * carried + (step_dt * step_u)[:, None] * step_b[None, :]
        return (carried, lax.optimization_barrier(jnp.sum(carried * step_c[None, :], axis=1)))

    def scan_piece(carried, block_in):
        return lax.scan(advance, carried, block_in)

    def one_group(inputs):
        rows_in, group_mods, split_point = inputs
        places = jnp.arange(GROUP, dtype=jnp.int32)
        offsets = places - jnp.where(places >= split_point, split_point, 0)
        keeps = jnp.where((places == 0) | (places == split_point), 0.0, 1.0).astype(jnp.float32)
        chosen = (group_mods[:, None] == jnp.arange(MODS, dtype=jnp.int32)[None, :]).astype(jnp.float32)
        row_scale = lax.rsqrt(lax.optimization_barrier(jnp.mean(rows_in * rows_in, axis=1, keepdims=True)) + epsilon)
        normed = low(rows_in * row_scale * norm_gain)
        projected_in = low_back(select_rows(chosen, normed, w_in))
        front_half = projected_in[:, :E]
        gate_half = projected_in[:, E:]
        summed = jnp.zeros_like(front_half) + conv_b
        for shift_by in range(K):
            lagged = jnp.pad(front_half, ((shift_by, 0), (0, 0)))[:GROUP]
            summed = summed + conv_w[K - 1 - shift_by] * lagged * (offsets >= shift_by).astype(jnp.float32)[:, None]
        mixed_in = low(jax.nn.silu(summed))
        projected_x = low_back(select_rows(chosen, mixed_in, w_x))
        dt_low = low(projected_x[:, :R])
        b_rows = projected_x[:, R:R + N]
        c_rows = projected_x[:, R + N:]
        bias_rows = jnp.dot(chosen, dt_bias, precision=highest, preferred_element_type=jnp.float32)
        dt_pre = low_back(select_rows(chosen, dt_low, w_dt) + bias_rows)
        steps_dt = jax.nn.softplus(dt_pre)
        block_count = GROUP // SCAN_BLOCK
        shaped = tuple((member.reshape((block_count, SCAN_BLOCK) + member.shape[1:]) for member in (steps_dt, b_rows, c_rows, mixed_in, keeps)))
        zero_state = jnp.zeros((E, N), jnp.float32)
        outputs = lax.scan(jax.checkpoint(scan_piece), zero_state, shaped)[1]
        ssm_out = outputs.reshape(GROUP, E) + d_skip * mixed_in
        gated_out = low(ssm_out * jax.nn.silu(gate_half))
        return rows_in + select_rows(chosen, gated_out, w_out)
    groups_in = tokens.reshape(GROUPS, GROUP, D)
    groups_mod = mod_ids.reshape(GROUPS, GROUP)
    result = lax.map(jax.checkpoint(one_group), (groups_in, groups_mod, split_at))
    return result.reshape(TOKENS, D)

def reference(tokens, norm_gain, w_in, conv_w, conv_b, w_x, w_dt, dt_bias, a_log, d_skip, w_out, mod_ids, split_at, cotangent):
    floats = tuple((member.astype(jnp.float32) for member in (tokens, norm_gain, w_in, conv_w, conv_b, w_x, w_dt, dt_bias, a_log, d_skip, w_out)))

    def forward(*params):
        return modality_layer(*params, mod_ids, split_at)
    output, pullback = jax.vjp(forward, *floats)
    gradients = pullback(cotangent.astype(jnp.float32))
    return (output.astype(jnp.bfloat16), gradients[0].astype(jnp.bfloat16), gradients[1], gradients[2], gradients[3], gradients[4], gradients[5], gradients[6], gradients[7], gradients[8], gradients[9], gradients[10])
```

```python
import functools

import jax
import jax.numpy as jnp
from jax import lax
from jax.experimental import pallas as pl
from jax.experimental.pallas import tpu as pltpu
from jax.sharding import PartitionSpec as P

MODS = 3
RUN = 128
LANES = 128
EPSILON = 1e-05
LOG2E = 1.4426950408889634
FAR = 1e30
VMEM_LIMIT = 60 * 1024 * 1024

f32 = jnp.float32
bf16 = jnp.bfloat16


def swap(block, axis, flip):
    count = lax.axis_size(axis)
    return lax.ppermute(block, axis, [(i, i ^ flip) for i in range(count)])


def gather_narrow(block):
    return [block] + [swap(block, "narrow", s) for s in range(1, lax.axis_size("narrow"))]


def gather_wide(block):
    chips = lax.axis_size("wide") // 2
    near = [block] + [swap(block, "wide", 2 * s) for s in range(1, chips)]
    far = [swap(piece, "wide", 1) for piece in near]
    return [piece for pair in zip(near, far) for piece in pair]


def dot(a, b, ca, cb):
    return lax.dot_general(a, b, (((ca,), (cb,)), ((), ())), preferred_element_type=f32)


def call(kernel, outs, ins, scratch=(), cost=None):
    spaces = {"v": pltpu.VMEM, "s": pltpu.SMEM, "a": pl.ANY}
    return pl.pallas_call(
        kernel,
        out_shape=[jax.ShapeDtypeStruct(shape, dtype) for shape, dtype, _ in outs],
        in_specs=[pl.BlockSpec(memory_space=spaces[space]) for _, space in ins],
        out_specs=[pl.BlockSpec(memory_space=spaces[space]) for _, _, space in outs],
        scratch_shapes=list(scratch),
        compiler_params=pltpu.CompilerParams(vmem_limit_bytes=VMEM_LIMIT),
        cost_estimate=cost,
    )(*[array for array, _ in ins])


def place_pieces(pieces, target, sem, me, rows):
    copies = []
    for s, piece in enumerate(pieces):
        at = pl.multiple_of((me ^ s) * rows, 16)
        copy = pltpu.make_async_copy(piece, target.at[pl.ds(at, rows), :], sem.at[s])
        copy.start()
        copies.append(copy)
    return copies


def run_kind(kinds, n, run, per):
    return kinds[((run // per) ^ n) * per + run % per]


def spread_kernel(wid, ep, out_cols, x_cols, meta, *refs):
    pieces = refs[:wid]
    w_out, w_x, w_dt, table = refs[wid : wid + 4]
    rest, sems = refs[wid + 4 :]
    w = meta[1]
    copies = []
    for s, piece in enumerate(pieces):
        at = pl.multiple_of((w ^ s) * ep, 16)
        rows = pl.ds(at, ep)
        for k, (target, first, width) in enumerate(
            ((rest, out_cols + x_cols, rest.shape[1]), (w_x, out_cols, x_cols), (w_out, 0, out_cols))
        ):
            copy = pltpu.make_async_copy(
                piece.at[:, pl.ds(first, width)], target.at[rows, :], sems.at[k, s]
            )
            copy.start()
            copies.append(copy)
    for copy in copies:
        copy.wait()
    turned = rest[...].astype(f32).T
    dt_rows = w_dt.shape[0]
    w_dt[...] = turned[:dt_rows].astype(bf16)
    table[...] = turned[dt_rows:]


T_BIAS, T_CONV_B, T_CONV, T_SKIP, T_LOG = 0, 3, 4, 8, 16


def in_kernel(nar, wid, rpd, taps, meta, kinds, *refs):
    toks, w_pieces = refs[:nar], refs[nar : nar + wid]
    table, w_x = refs[nar + wid : nar + wid + 2]
    normed_o, front_o, gate_o, csum_o, mixed_o, px_o = refs[nar + wid + 2 : nar + wid + 8]
    xs, wf, tok_sem, w_sem = refs[nar + wid + 8 :]
    n, w, split = meta[0], meta[1], meta[2]
    es = gate_o.shape[1]
    tok_copies = place_pieces(toks, xs, tok_sem, n, toks[0].shape[0])
    w_copies = place_pieces(w_pieces, wf, w_sem, w, w_pieces[0].shape[0])
    for copy in tok_copies + w_copies:
        copy.wait()
    gain_at = MODS * 2 * es
    gain = wf[:, gain_at : gain_at + LANES].astype(f32).T[0:1, :]
    front_o[0:8, :] = jnp.zeros((8, es), f32)

    def one_run(r, carry):
        rows = pl.ds(pl.multiple_of(r * RUN, RUN), RUN)
        kind = run_kind(kinds, n, r, rpd)
        x = xs[rows, :].astype(f32)
        scale = lax.rsqrt(jnp.mean(x * x, axis=1, keepdims=True) + EPSILON)
        normed = (x * scale * gain).astype(bf16)
        normed_o[rows, :] = normed
        both = dot(normed, wf[:, pl.ds(pl.multiple_of(kind * (2 * es), LANES), 2 * es)], 1, 0)
        front_o[pl.ds(pl.multiple_of(r * RUN + 8, 8), RUN), :] = both[:, :es]
        gate_o[rows, :] = both[:, es:]
        ext = front_o[pl.ds(pl.multiple_of(r * RUN, 8), RUN + 8), :]
        place = r * RUN + lax.broadcasted_iota(jnp.int32, (RUN, 1), 0)
        offset = place - jnp.where(place >= split, split, 0)
        csum = jnp.broadcast_to(table[T_CONV_B : T_CONV_B + 1, :], (RUN, es))
        for lag in range(taps):
            tap = table[T_CONV + taps - 1 - lag : T_CONV + taps - lag, :]
            valid = (offset >= lag).astype(f32)
            csum = csum + tap * ext[8 - lag : 8 - lag + RUN, :] * valid
        csum_o[rows, :] = csum
        mixed = (csum * jax.nn.sigmoid(csum)).astype(bf16)
        mixed_o[rows, :] = mixed
        px = dot(mixed, w_x[:, pl.ds(pl.multiple_of(kind * LANES, LANES), LANES)], 1, 0)
        px_o[:, pl.ds(pl.multiple_of(r * RUN, LANES), RUN)] = px.T[: px_o.shape[0]].astype(bf16)
        return carry

    lax.fori_loop(0, xs.shape[0] // RUN, one_run, 0)


def cot_kernel(nar, rpd, meta, kinds, *refs):
    pieces = refs[:nar]
    w_out, gate_r = refs[nar : nar + 2]
    cot_o, dssm_o, dgate_o, act_o = refs[nar + 2 : nar + 6]
    (sem,) = refs[nar + 6 :]
    n = meta[0]
    d = cot_o.shape[1]
    for copy in place_pieces(pieces, cot_o, sem, n, pieces[0].shape[0]):
        copy.wait()

    def one_run(r, carry):
        rows = pl.ds(pl.multiple_of(r * RUN, RUN), RUN)
        kind = run_kind(kinds, n, r, rpd)
        d_gated = dot(cot_o[rows, :], w_out[:, pl.ds(pl.multiple_of(kind * d, LANES), d)], 1, 1)
        gate = gate_r[rows, :]
        sig = jax.nn.sigmoid(gate)
        act = gate * sig
        act_o[rows, :] = act
        dssm_o[rows, :] = d_gated * act
        dgate_o[rows, :] = d_gated * sig * (1.0 + gate * (1.0 - sig))
        return carry

    lax.fori_loop(0, cot_o.shape[0] // RUN, one_run, 0)


def softplus(v):
    return jnp.maximum(v, 0.0) + jnp.log1p(jnp.exp(-jnp.abs(v)))


def scan_kernel(nar, rpd, rank, meta, kinds, *refs):
    px_pieces = refs[:nar]
    w_dt, table, mixed_r, dssm_r = refs[nar : nar + 4]
    ssm_o, dpx_o, gmix_o, dpre_o, dlow_o, glog_o, gskip_o = refs[nar + 4 : nar + 11]
    pxs, pre_s, step_s, states, bb, cb, ps, qs, gb, gc, dtk, dtu = refs[nar + 11 :]
    n, split = meta[0], meta[2]
    total, es = mixed_r.shape
    ns = states.shape[1]
    groups = es // LANES
    runs = total // RUN
    lane = [slice(g * LANES, (g + 1) * LANES) for g in range(groups)]
    rates = -jnp.exp(table[T_LOG : T_LOG + ns, :])
    rates2 = rates * LOG2E
    half = ns // 2
    pxs[...] = sum(piece[...].astype(f32) for piece in px_pieces)
    skip = table[T_SKIP : T_SKIP + 1, :]

    def rows_of(r):
        return pl.ds(pl.multiple_of(r * RUN, RUN), RUN)

    def spread(r, at, target):
        block = pxs[at : at + ns, pl.ds(pl.multiple_of(r * RUN, LANES), RUN)]
        for t in range(RUN):
            target[t] = jnp.broadcast_to(block[:, t : t + 1], (ns, LANES))

    def prepare(r):
        rows = rows_of(r)
        steps = step_s[rows, :]
        place = r * RUN + lax.broadcasted_iota(jnp.int32, (RUN, 1), 0)
        reset = (place == 0) | (place == split)
        dtk[...] = jnp.where(reset, FAR, steps)
        dtu[...] = steps * mixed_r[rows, :].astype(f32)
        spread(r, rank, bb)
        spread(r, rank + ns, cb)

    def row(tile, j, g):
        return jnp.broadcast_to(tile[j : j + 1, lane[g]], (ns, LANES))

    def folded(ref):
        outs = []
        for g in range(groups):
            out = ref[g, pl.ds(0, RUN, stride=half), :]
            for s in range(1, half):
                out = out + ref[g, pl.ds(s, RUN, stride=half), :]
            outs.append(out)
        return jnp.concatenate(outs, axis=1)

    states[0] = jnp.zeros((ns, es), f32)

    def forward(r, hs):
        rows = rows_of(r)
        kind = run_kind(kinds, n, r, rpd)
        low = pxs[:rank, pl.ds(pl.multiple_of(r * RUN, LANES), RUN)].astype(bf16)
        dlow_o[:, pl.ds(pl.multiple_of(r * RUN, LANES), RUN)] = low
        weights = w_dt[pl.ds(pl.multiple_of(kind * rank, 16), rank), :]
        pre = dot(low, weights, 0, 0) + table[pl.ds(T_BIAS + kind, 1), :]
        pre_s[rows, :] = pre
        step_s[rows, :] = softplus(pre)
        prepare(r)

        def eight(i, hs):
            hs = list(hs)
            at = pl.ds(pl.multiple_of(i * 8, 8), 8)
            k8, u8 = dtk[at, :], dtu[at, :]
            for j in range(8):
                t = i * 8 + j
                bt, ct = bb[t], cb[t]
                for g in range(groups):
                    decay = jnp.exp2(row(k8, j, g) * rates2[:, lane[g]])
                    hs[g] = decay * hs[g] + row(u8, j, g) * bt
                    states[r * RUN + t + 1, :, lane[g]] = hs[g]
                    part = hs[g] * ct
                    ps[g, pl.ds(pl.multiple_of(t * half, half), half), :] = part[:half] + part[half:]
            return tuple(hs)

        hs = lax.fori_loop(0, RUN // 8, eight, hs)
        ssm_o[rows, :] = folded(ps) + skip * mixed_r[rows, :].astype(f32)
        return hs

    zero = jnp.zeros((ns, LANES), f32)
    lax.fori_loop(0, runs, forward, (zero,) * groups)
    gskip_o[...] = jnp.zeros_like(gskip_o)
    picks = lax.broadcasted_iota(jnp.int32, (2 * ns, LANES), 0)

    def backward(back, carry):
        r = runs - 1 - back
        rows = rows_of(r)
        kind = run_kind(kinds, n, r, rpd)
        prepare(r)

        def eight(back_i, carry):
            ms, hs, gr = [list(part) for part in carry]
            i = RUN // 8 - 1 - back_i
            at = pl.ds(pl.multiple_of(i * 8, 8), 8)
            k8, u8 = dtk[at, :], dtu[at, :]
            y8 = dssm_r[pl.ds(pl.multiple_of(r * RUN + i * 8, 8), 8), :]
            for j in reversed(range(8)):
                t = i * 8 + j
                bt, ct = bb[t], cb[t]
                gb_sum, gc_sum = None, None
                for g in range(groups):
                    dt = row(k8, j, g)
                    dy = row(y8, j, g)
                    adjoint = dy * ct + ms[g]
                    before = states[r * RUN + t, :, lane[g]]
                    c_part = dy * hs[g]
                    b_part = adjoint * row(u8, j, g)
                    gb_sum = b_part if gb_sum is None else gb_sum + b_part
                    gc_sum = c_part if gc_sum is None else gc_sum + c_part
                    lb = adjoint * bt
                    fold_at = pl.ds(pl.multiple_of(t * half, half), half)
                    ps[g, fold_at, :] = lb[:half] + lb[half:]
                    ms[g] = jnp.exp2(dt * rates2[:, lane[g]]) * adjoint
                    weighted = ms[g] * before
                    by_rate = weighted * rates[:, lane[g]]
                    qs[g, fold_at, :] = by_rate[:half] + by_rate[half:]
                    gr[g] = gr[g] + weighted * dt
                    hs[g] = before
                gb[pl.ds(pl.multiple_of(t * ns, ns), ns), :] = gb_sum
                gc[pl.ds(pl.multiple_of(t * ns, ns), ns), :] = gc_sum
            return tuple(ms), tuple(hs), tuple(gr)

        carry = lax.fori_loop(0, RUN // 8, eight, carry)
        mixed = mixed_r[rows, :].astype(f32)
        lb, by_rate = folded(ps), folded(qs)
        dssm = dssm_r[rows, :]
        grad_steps = by_rate + lb * mixed
        gmix_o[rows, :] = dssm * skip + lb * step_s[rows, :]
        gskip_o[...] += jnp.sum(dssm * mixed, axis=0, keepdims=True)
        dpre = (grad_steps * jax.nn.sigmoid(pre_s[rows, :])).astype(bf16)
        dpre_o[rows, :] = dpre
        weights = w_dt[pl.ds(pl.multiple_of(kind * rank, 16), rank), :]
        dlow = dot(weights, dpre, 1, 1)
        dbc = jnp.zeros((2 * ns, RUN), f32)
        for k in range(ns):
            for shift, ref in ((0, gb), (ns, gc)):
                pick = (picks == k + shift).astype(bf16)
                dbc = dbc + dot(pick, ref[pl.ds(k, RUN, stride=ns), :].astype(bf16), 1, 1)
        at = pl.ds(pl.multiple_of(r * RUN, LANES), RUN)
        dpx_o[:rank, at] = dlow.astype(bf16)
        dpx_o[rank:, at] = dbc.astype(bf16)
        return carry

    last = tuple(states[total, :, lane[g]] for g in range(groups))
    done = lax.fori_loop(0, runs, backward, ((zero,) * groups, last, (zero,) * groups))
    for g in range(groups):
        glog_o[:, lane[g]] = done[2][g] * rates[:, lane[g]]


def out_kernel(nar, wid, rpd, ep, rank, meta, kinds, *refs):
    ssm_r, act_r, dgate_r, w_out, cot_r, normed_r, dpre_r, dlow_r, glog_r, gskip_r = refs[:10]
    mixed_os = refs[10 : 10 + nar]
    dgate_o, table_o, same_o, peer_o = refs[10 + nar : 14 + nar]
    acc_out, acc_in, branch = refs[14 + nar :]
    n, w = meta[0], meta[1]
    total, es = ssm_r.shape
    d = cot_r.shape[1]
    acc_out[...] = jnp.zeros_like(acc_out)
    acc_in[...] = jnp.zeros_like(acc_in)
    table_o[...] = jnp.zeros_like(table_o)

    def one_run(r, carry):
        rows = pl.ds(pl.multiple_of(r * RUN, RUN), RUN)
        kind = run_kind(kinds, n, r, rpd)
        ssm = ssm_r[rows, :]
        gated = (ssm * act_r[rows, :]).astype(bf16)
        wide_at = pl.ds(pl.multiple_of(kind * d, LANES), d)
        es_at = pl.ds(pl.multiple_of(kind * es, LANES), es)
        branch[rows, :] = dot(gated, w_out[:, wide_at], 1, 0).astype(bf16)
        acc_out[:, wide_at] += dot(gated, cot_r[rows, :], 0, 0)
        dgate = (dgate_r[rows, :] * ssm).astype(bf16)
        dgate_o[rows, :] = dgate
        acc_in[:, es_at] += dot(normed_r[rows, :], dgate, 0, 0)
        dpre = dpre_r[rows, :]
        low = dlow_r[:, pl.ds(pl.multiple_of(r * RUN, LANES), RUN)]
        table_o[pl.ds(pl.multiple_of(kind * rank, 8), rank), :] += dot(low, dpre, 1, 0)
        table_o[pl.ds(MODS * rank + T_BIAS + kind, 1), :] += jnp.sum(
            dpre.astype(f32), axis=0, keepdims=True
        )
        return carry

    lax.fori_loop(0, total // RUN, one_run, 0)
    base = MODS * rank
    table_o[base + T_SKIP : base + T_SKIP + 1, :] = gskip_r[...]
    table_o[base + T_LOG : base + T_LOG + glog_r.shape[0], :] = glog_r[...]
    size = mixed_os[0].shape[0]
    for s in range(nar):
        mixed_os[s][...] = branch[pl.ds(pl.multiple_of((n ^ s) * size, RUN), size), :]
    core = w & 1
    in_rows = acc_in.shape[0] // wid
    width = acc_in.shape[1]
    for ref, parity in ((same_o, core), (peer_o, 1 - core)):
        for c in range(wid // 2):
            place = 2 * c + parity
            ref[c, :in_rows, :] = acc_in[
                pl.ds(pl.multiple_of(place * in_rows, 16), in_rows), :
            ].astype(bf16)
            block = acc_out[pl.ds(pl.multiple_of(place * ep, 16), ep), :].astype(bf16)
            for k in range(block.shape[1] // width):
                first = in_rows + k * ep
                ref[c, first : first + ep, :] = block[:, k * width : (k + 1) * width]


def pair_kernel(chips, meta, same, peer, *outs):
    chip = meta[1] // 2
    for s in range(chips):
        outs[s][...] = (same[chip ^ s].astype(f32) + peer[chip ^ s].astype(f32)).astype(bf16)


def total_kernel(count, *refs):
    refs[count][...] = sum(piece[...].astype(f32) for piece in refs[:count])


def back_kernel(nar, wid, rpd, taps, ep, meta, kinds, *refs):
    dpx_pieces = refs[:nar]
    w_pieces = refs[nar : nar + wid]
    toks = refs[nar + wid : nar + wid + nar]
    at = 2 * nar + wid
    table, w_x, gmix_r, csum_r, front_r, mixed_r, normed_r, dgate_r, table_r = refs[at : at + 9]
    dn_os = refs[at + 9 : at + 9 + nar]
    same_o, peer_o = refs[at + 9 + nar : at + 11 + nar]
    wf, xs, dconv, dn_s, acc_in, acc_x, small, gain_s, w_sem, tok_sem = refs[at + 11 + nar :]
    n, w, split = meta[0], meta[1], meta[2]
    total, es = gmix_r.shape
    d = normed_r.shape[1]
    runs = total // RUN
    w_copies = place_pieces(w_pieces, wf, w_sem, w, w_pieces[0].shape[0])
    tok_copies = place_pieces(toks, xs, tok_sem, n, toks[0].shape[0])
    acc_in[...] = jnp.zeros_like(acc_in)
    acc_x[...] = jnp.zeros_like(acc_x)
    small[...] = jnp.zeros_like(small)
    gain_s[...] = jnp.zeros_like(gain_s)
    dconv[total : total + 8, :] = jnp.zeros((8, es), f32)
    for copy in w_copies + tok_copies:
        copy.wait()
    xw = dpx_pieces[0].shape[0]

    def one_run(back, carry):
        r = runs - 1 - back
        rows = pl.ds(pl.multiple_of(r * RUN, RUN), RUN)
        kind = run_kind(kinds, n, r, rpd)
        lanes_at = pl.ds(pl.multiple_of(r * RUN, LANES), RUN)
        dpx = sum(piece[:, lanes_at].astype(f32) for piece in dpx_pieces)
        dpx = jnp.concatenate([dpx, jnp.zeros((LANES - xw, RUN), f32)], axis=0).T.astype(bf16)
        x_at = pl.ds(pl.multiple_of(kind * LANES, LANES), LANES)
        acc_x[:, x_at] += dot(mixed_r[rows, :], dpx, 0, 0)
        gmix = gmix_r[rows, :] + dot(dpx, w_x[:, x_at], 1, 1)
        csum = csum_r[rows, :]
        sig = jax.nn.sigmoid(csum)
        dc = gmix * sig * (1.0 + csum * (1.0 - sig))
        dconv[rows, :] = dc
        place = r * RUN + lax.broadcasted_iota(jnp.int32, (RUN + 8, 1), 0)
        offset = place - jnp.where(place >= split, split, 0)
        ext = dconv[pl.ds(pl.multiple_of(r * RUN, 8), RUN + 8), :]
        lagged = front_r[pl.ds(pl.multiple_of(r * RUN, 8), RUN + 8), :]
        d_front = jnp.zeros((RUN, es), f32)
        for lag in range(taps):
            tap = taps - 1 - lag
            valid = (offset >= lag).astype(f32)
            masked = ext * valid
            d_front = d_front + table[T_CONV + tap : T_CONV + tap + 1, :] * masked[lag : lag + RUN, :]
            small[T_CONV + tap : T_CONV + tap + 1, :] += jnp.sum(
                masked[:RUN] * lagged[8 - lag : 8 - lag + RUN, :], axis=0, keepdims=True
            )
        small[T_CONV_B : T_CONV_B + 1, :] += jnp.sum(dc, axis=0, keepdims=True)
        d_both = jnp.concatenate([d_front.astype(bf16), dgate_r[rows, :]], axis=1)
        acc_in[:, pl.ds(pl.multiple_of(kind * es, LANES), es)] += dot(
            normed_r[rows, :], d_both[:, :es], 0, 0
        )
        weights = wf[:, pl.ds(pl.multiple_of(kind * (2 * es), LANES), 2 * es)]
        dn = dot(d_both, weights, 1, 1)
        dn_s[rows, :] = dn.astype(bf16)
        x = xs[rows, :].astype(f32)
        scale = lax.rsqrt(jnp.mean(x * x, axis=1, keepdims=True) + EPSILON)
        gain_s[...] += jnp.sum(dn * (x * scale), axis=0, keepdims=True)
        return carry

    lax.fori_loop(0, runs, one_run, 0)
    size = dn_os[0].shape[0]
    for s in range(nar):
        dn_os[s][...] = dn_s[pl.ds(pl.multiple_of((n ^ s) * size, RUN), size), :]
    width = acc_in.shape[1]
    acc_in_rows = acc_in.shape[0] // wid
    gain = jnp.broadcast_to(gain_s[...], (LANES, d)).T
    xs_gain = dconv
    xs_gain[0:d, 0:LANES] = gain
    base = table_r.shape[0] - 2 * 16 if False else table_r.shape[0] - small.shape[0]
    rest = jnp.concatenate([table_r[:base, :], table_r[base:, :] + small[...]], axis=0)
    pad = 256 - rest.shape[0]
    rest = jnp.concatenate([rest, jnp.zeros((pad, es), f32)], axis=0).T
    xcols = acc_x.shape[1]
    acc_x_all = jnp.concatenate([acc_x[...], rest], axis=1)
    fill = width + LANES - acc_x_all.shape[1]
    if fill:
        acc_x_all = jnp.concatenate([acc_x_all, jnp.zeros((es, fill), f32)], axis=1)
    wf_rows = acc_x_all.astype(bf16)
    wf[0:es, 0 : width + LANES] = wf_rows
    core = w & 1
    for ref, parity in ((same_o, core), (peer_o, 1 - core)):
        for c in range(wid // 2):
            place = 2 * c + parity
            in_at = pl.ds(pl.multiple_of(place * acc_in_rows, 16), acc_in_rows)
            ref[c, :acc_in_rows, :width] = acc_in[in_at, :].astype(bf16)
            ref[c, :acc_in_rows, width:] = xs_gain[in_at, 0:LANES].astype(bf16)
            ref[c, acc_in_rows:, :] = wf[pl.ds(pl.multiple_of(place * ep, 16), ep), 0 : width + LANES]


def tokens_kernel(nar, x_r, cot_r, gain_r, *refs):
    dn = sum(piece[...].astype(f32) for piece in refs[:nar])
    out = refs[nar]
    x = x_r[...].astype(f32)
    scale = lax.rsqrt(jnp.mean(x * x, axis=1, keepdims=True) + EPSILON)
    q = dn * gain_r[...]
    dotted = jnp.mean(q * x, axis=1, keepdims=True)
    out[...] = (cot_r[...].astype(f32) + scale * q - x * (scale * scale * scale) * dotted).astype(bf16)


def body(
    tokens,
    norm_gain,
    w_in,
    conv_w,
    conv_b,
    w_x,
    w_dt,
    dt_bias,
    a_log,
    d_skip,
    w_out,
    mod_ids,
    split_at,
    cotangent,
):
    nar, wid = lax.axis_size("narrow"), lax.axis_size("wide")
    chips = wid // 2
    n, w = lax.axis_index("narrow"), lax.axis_index("wide")
    own, d = tokens.shape
    total = nar * own
    rpd = own // RUN
    rank, xw, ns, taps = w_dt.shape[0], w_x.shape[2], a_log.shape[1], conv_w.shape[0]
    er = w_out.shape[0]
    inner = er * nar * wid
    ep = -(-er // 16) * 16
    es = ep * wid
    dr = w_in.shape[0]
    width = MODS * es
    meta = jnp.stack([n, w, split_at[0]]).astype(jnp.int32)

    kinds = mod_ids.reshape(rpd, RUN)[:, 0]
    kinds = jnp.concatenate(gather_narrow(kinds))
    out_cols, x_cols = MODS * d, MODS * LANES
    lane_rows = jnp.concatenate(
        [
            w_dt.reshape(rank * MODS, er).reshape(rank, MODS, er).transpose(1, 0, 2).reshape(-1, er),
            dt_bias,
            conv_b[None],
            conv_w,
            d_skip[None],
            jnp.zeros((T_LOG - T_SKIP - 1, er), bf16),
            a_log.T,
        ],
        axis=0,
    )
    table_rows = T_LOG + ns
    lane_rows = jnp.pad(lane_rows, ((0, 256 - lane_rows.shape[0]), (0, 0)))
    pack = jnp.concatenate(
        [
            w_out.reshape(er, out_cols),
            jnp.pad(w_x, ((0, 0), (0, 0), (0, LANES - xw))).reshape(er, x_cols),
            lane_rows.T,
        ],
        axis=1,
    )
    pack = jnp.pad(pack, ((0, ep - er), (0, 0)))
    pack_pieces = gather_wide(pack)
    wi = w_in.reshape(dr, MODS, 2, wid, nar, er)
    wi = jnp.pad(wi, ((0, 0),) * 5 + ((0, ep - er),))
    wi = wi.transpose(4, 0, 1, 2, 3, 5).reshape(nar, dr, 2 * width)
    wi = jnp.concatenate(
        [wi, jnp.broadcast_to(norm_gain[None, :, None], (nar, dr, LANES))], axis=2
    )
    wi = lax.all_to_all(wi, "narrow", 0, 0)
    wi = wi.reshape(nar * dr, 2 * width + LANES)
    wi_pieces = gather_wide(wi)
    tok_pieces = gather_narrow(tokens)
    cot_pieces = gather_narrow(cotangent)

    w_out_l, w_x_l, w_dt_l, table = call(
        functools.partial(spread_kernel, wid, ep, out_cols, x_cols),
        [
            ((es, out_cols), bf16, "v"),
            ((es, x_cols), bf16, "v"),
            ((MODS * rank, es), bf16, "v"),
            ((256 - MODS * rank, es), f32, "v"),
        ],
        [(meta, "s")] + [(p, "a") for p in pack_pieces],
        [pltpu.VMEM((es, 256), bf16), pltpu.SemaphoreType.DMA((3, wid))],
    )
    wf_shape = (nar * dr * wid, 2 * width + LANES)
    normed, front, gate, csum, mixed, px = call(
        functools.partial(in_kernel, nar, wid, rpd, taps),
        [
            ((total, d), bf16, "v"),
            ((total + 8, es), f32, "v"),
            ((total, es), f32, "v"),
            ((total, es), f32, "v"),
            ((total, es), bf16, "v"),
            ((xw, total), bf16, "v"),
        ],
        [(meta, "s"), (kinds, "s")]
        + [(p, "a") for p in tok_pieces]
        + [(p, "a") for p in wi_pieces]
        + [(table, "v"), (w_x_l, "v")],
        [
            pltpu.VMEM((total, d), bf16),
            pltpu.VMEM(wf_shape, bf16),
            pltpu.SemaphoreType.DMA((nar,)),
            pltpu.SemaphoreType.DMA((wid,)),
        ],
    )
    px_pieces = gather_narrow(px)
    cot, dssm, dgate_f, act = call(
        functools.partial(cot_kernel, nar, rpd),
        [((total, d), bf16, "v")] + [((total, es), f32, "v")] * 3,
        [(meta, "s"), (kinds, "s")]
        + [(p, "a") for p in cot_pieces]
        + [(w_out_l, "v"), (gate, "v")],
        [pltpu.SemaphoreType.DMA((nar,))],
    )
    ssm, dpx, gmix, dpre, dlow, glog, gskip = call(
        functools.partial(scan_kernel, nar, rpd, rank),
        [
            ((total, es), f32, "v"),
            ((xw, total), bf16, "v"),
            ((total, es), f32, "v"),
            ((total, es), bf16, "v"),
            ((rank, total), bf16, "v"),
            ((ns, es), f32, "v"),
            ((1, es), f32, "v"),
        ],
        [(meta, "s"), (kinds, "s")]
        + [(p, "v") for p in px_pieces]
        + [(w_dt_l, "v"), (table, "v"), (mixed, "v"), (dssm, "v")],
        [
            pltpu.VMEM((xw, total), f32),
            pltpu.VMEM((total, es), f32),
            pltpu.VMEM((total, es), f32),
            pltpu.VMEM((total + 1, ns, es), f32),
            pltpu.VMEM((RUN, ns, LANES), f32),
            pltpu.VMEM((RUN, ns, LANES), f32),
            pltpu.VMEM((es // LANES, RUN * ns // 2, LANES), f32),
            pltpu.VMEM((es // LANES, RUN * ns // 2, LANES), f32),
            pltpu.VMEM((RUN * ns, LANES), f32),
            pltpu.VMEM((RUN * ns, LANES), f32),
            pltpu.VMEM((RUN, es), f32),
            pltpu.VMEM((RUN, es), f32),
        ],
    )
    dpx_pieces = gather_narrow(dpx)
    in_rows = d // wid
    rows_a = in_rows + ep * (out_cols // width)
    res = call(
        functools.partial(out_kernel, nar, wid, rpd, ep, rank),
        [((own, d), bf16, "v")] * nar
        + [((total, es), bf16, "v"), ((MODS * rank + table_rows, es), f32, "v")]
        + [((chips, rows_a, width), bf16, "v")] * 2,
        [(meta, "s"), (kinds, "s")]
        + [(a, "v") for a in (ssm, act, dgate_f, w_out_l, cot, normed, dpre, dlow, glog, gskip)],
        [
            pltpu.VMEM((es, out_cols), f32),
            pltpu.VMEM((d, width), f32),
            pltpu.VMEM((total, d), bf16),
        ],
    )
    branch_parts, (dgate, table_g, same_a, peer_a) = res[:nar], res[nar:]
    branch_pieces = [branch_parts[0]] + [
        swap(branch_parts[s], "narrow", s) for s in range(1, nar)
    ]

    def over_wide(same, peer):
        peer = swap(peer, "wide", 1)
        shape = same.shape[1:]
        parts = call(
            functools.partial(pair_kernel, chips),
            [(shape, bf16, "v")] * chips,
            [(meta, "s"), (same, "v"), (peer, "v")],
        )
        parts = [parts[0]] + [swap(parts[s], "wide", 2 * s) for s in range(1, chips)]
        return call(
            functools.partial(total_kernel, chips), [(shape, f32, "v")], [(p, "v") for p in parts]
        )[0]

    sum_a = over_wide(same_a, peer_a)
    rows_b = in_rows + ep
    res = call(
        functools.partial(back_kernel, nar, wid, rpd, taps, ep),
        [((own, d), bf16, "v")] * nar + [((chips, rows_b, width + LANES), bf16, "v")] * 2,
        [(meta, "s"), (kinds, "s")]
        + [(p, "v") for p in dpx_pieces]
        + [(p, "a") for p in wi_pieces]
        + [(p, "a") for p in tok_pieces]
        + [(a, "v") for a in (table, w_x_l, gmix, csum, front, mixed, normed, dgate, table_g)],
        [
            pltpu.VMEM(wf_shape, bf16),
            pltpu.VMEM((total, d), bf16),
            pltpu.VMEM((total + 8, es), f32),
            pltpu.VMEM((total, d), bf16),
            pltpu.VMEM((d, width), f32),
            pltpu.VMEM((es, x_cols), f32),
            pltpu.VMEM((table_rows, es), f32),
            pltpu.VMEM((1, d), f32),
            pltpu.SemaphoreType.DMA((wid,)),
            pltpu.SemaphoreType.DMA((nar,)),
        ],
    )
    dn_parts, (same_b, peer_b) = res[:nar], res[nar:]
    dn_pieces = [dn_parts[0]] + [swap(dn_parts[s], "narrow", s) for s in range(1, nar)]
    sum_b = over_wide(same_b, peer_b)

    mixed_out = (
        tokens.astype(f32) + sum(p.astype(f32) for p in branch_pieces)
    ).astype(bf16)
    gain_row = jnp.concatenate(
        [wi_pieces[0][:, 2 * width]], axis=0
    )
    gain_full = jnp.zeros((wid, nar * dr), bf16)
    for s in range(wid):
        gain_full = lax.dynamic_update_slice(
            gain_full, wi_pieces[s][:, 2 * width][None], (w ^ s, 0)
        )
    del gain_row
    grad_tokens = call(
        functools.partial(tokens_kernel, nar),
        [((own, d), bf16, "v")],
        [(tokens, "v"), (cotangent, "v"), (gain_full.reshape(1, d).astype(f32), "v")]
        + [(p, "v") for p in dn_pieces],
    )[0]

    back = jnp.concatenate(
        [sum_a[:in_rows].astype(bf16), sum_b[:in_rows].astype(bf16)], axis=1
    ).reshape(nar, dr, -1)
    back = lax.all_to_all(back, "narrow", 0, 0).astype(f32)

    def channels(part):
        part = part.reshape(nar, dr, MODS, wid, ep)[..., :er]
        return part.transpose(1, 2, 3, 0, 4).reshape(dr, MODS, inner)

    grad_w_in = jnp.concatenate(
        [channels(back[:, :, width : 2 * width]), channels(back[:, :, :width])], axis=2
    )
    grad_gain = jnp.sum(back[:, :, 2 * width], axis=0)
    grad_w_out = sum_a[in_rows:].reshape(out_cols // width, ep, width)
    grad_w_out = grad_w_out.transpose(1, 0, 2).reshape(ep, MODS, d)[:er]
    small = sum_b[in_rows:][:er]
    grad_w_x = small[:, :x_cols].reshape(er, MODS, LANES)[:, :, :xw]
    lane_g = small[:, x_cols : x_cols + 256].T
    base = MODS * rank
    grad_w_dt = lane_g[:base].reshape(MODS, rank, er).transpose(1, 0, 2)
    grad_dt_bias = lane_g[base + T_BIAS : base + T_BIAS + MODS]
    grad_conv_w = lane_g[base + T_CONV : base + T_CONV + taps]
    grad_conv_b = lane_g[base + T_CONV_B]
    grad_skip = lane_g[base + T_SKIP]
    grad_log = lane_g[base + T_LOG : base + T_LOG + ns].T
    return (
        mixed_out,
        grad_tokens,
        grad_gain,
        grad_w_in,
        grad_conv_w,
        grad_conv_b,
        grad_w_x,
        grad_w_dt,
        grad_dt_bias,
        grad_log,
        grad_skip,
        grad_w_out,
    )


def solution(mesh):
    both = ("wide", "narrow")
    return jax.shard_map(
        body,
        mesh=mesh,
        in_specs=(
            P(both, None),
            P(both),
            P(both, None, None),
            P(None, both),
            P(both),
            P(both, None, None),
            P(None, None, both),
            P(None, both),
            P(both, None),
            P(both),
            P(both, None, None),
            P(both),
            P("wide"),
            P(both, None),
        ),
        out_specs=(
            P(both, None),
            P(both, None),
            P(both),
            P(both, None, None),
            P(None, both),
            P(both),
            P(both, None, None),
            P(None, None, both),
            P(None, both),
            P(both, None),
            P(both),
            P(both, None, None),
        ),
        check_vma=False,
    )
```

```python
import functools
import math

import jax
import jax.numpy as jnp
from jax import lax
from jax.experimental import pallas as pl
from jax.experimental.pallas import tpu as pltpu
from jax.sharding import PartitionSpec as P

MODS = 3
RUN = 128
LANES = 128
EPSILON = 1e-05
LOG2E = 1.4426950408889634
FAR = 1e30
VMEM_LIMIT = 60 * 1024 * 1024
VMEM_SPARE = 6 * 1024 * 1024

f32 = jnp.float32
bf16 = jnp.bfloat16


def swap(block, axis, flip):
    count = lax.axis_size(axis)
    return lax.ppermute(block, axis, [(i, i ^ flip) for i in range(count)])


def gather_narrow(block):
    return [block] + [swap(block, "narrow", s) for s in range(1, lax.axis_size("narrow"))]


def relay_narrow(block, *earlier):
    count = lax.axis_size("narrow")
    pieces = {0: block}
    for s in sorted(range(1, count), key=lambda s: (s.bit_count(), -s)):
        low_bit = s & -s
        if s == low_bit:
            pieces[s] = swap(block, "narrow", s)
        else:
            pieces[s] = swap(after(pieces[s ^ low_bit], *earlier), "narrow", low_bit)
    return [pieces[s] for s in range(count)]


def add_narrow(block, *beside):
    flip = lax.axis_size("narrow") // 2
    while flip:
        got = swap(block, "narrow", flip)
        block = (after(block, *beside).astype(f32) + got.astype(f32)).astype(bf16)
        flip //= 2
        beside = ()
    return block


def scatter_narrow(parts):
    return [parts[0]] + [swap(parts[s], "narrow", s) for s in range(1, len(parts))]


def sum_narrow(parts, *earlier):
    parts = list(parts)
    arrived = [parts[0]]
    for s in range(len(parts) - 1, 0, -1):
        low_bit = s & -s
        got = swap(parts[s], "narrow", low_bit)
        if s == low_bit:
            arrived.append(got)
        else:
            rest = s ^ low_bit
            parts[rest] = (after(parts[rest], *earlier).astype(f32) + got.astype(f32)).astype(bf16)
    return arrived, parts[-2]


def near_wide(block):
    return [block] + [swap(block, "wide", 2 * s) for s in range(1, lax.axis_size("wide") // 2)]


def far_wide(near):
    return [piece for block in near for piece in (block, swap(block, "wide", 1))]


def after(value, *earlier):
    return lax.optimization_barrier((value,) + earlier)[0] if earlier else value


def dot(a, b, ca, cb):
    return lax.dot_general(a, b, (((ca,), (cb,)), ((), ())), preferred_element_type=f32)


def call(kernel, outs, ins, scratch=(), us=1.0):
    spaces = {"v": pltpu.VMEM, "s": pltpu.SMEM, "a": pl.ANY}
    held = [(array.shape, array.dtype) for array, space in ins if space == "v"]
    held += [(shape, dtype) for shape, dtype, space in outs if space == "v"]
    held += [(part.shape, part.dtype) for part in scratch if part.memory_space == pltpu.VMEM]
    need = sum(math.prod(shape) * jnp.dtype(dtype).itemsize for shape, dtype in held)
    need = VMEM_LIMIT
    return pl.pallas_call(
        kernel,
        out_shape=[jax.ShapeDtypeStruct(shape, dtype) for shape, dtype, _ in outs],
        in_specs=[pl.BlockSpec(memory_space=spaces[space]) for _, space in ins],
        out_specs=[pl.BlockSpec(memory_space=spaces[space]) for _, _, space in outs],
        scratch_shapes=list(scratch),
        compiler_params=pltpu.CompilerParams(vmem_limit_bytes=need),
        cost_estimate=pl.CostEstimate(flops=int(us * 1.1e9), bytes_accessed=1, transcendentals=0),
    )(*[array for array, _ in ins])


def place_pieces(pieces, target, sem, me, rows):
    copies = []
    for s, piece in enumerate(pieces):
        at = pl.multiple_of((me ^ s) * rows, 16)
        copy = pltpu.make_async_copy(piece, target.at[pl.ds(at, rows), :], sem.at[s])
        copy.start()
        copies.append(copy)
    return copies


def split_kernel(
    er, ep, wid, below, meta, w_r, gain_r, out_r, x_r, dt_r, bias_r, conv_r, conv_b_r, skip_r, log_r, *refs
):
    nar = len(refs) - 4
    outs, (small_o, out_o, rows_s, lanes) = refs[:nar], refs[nar:]
    inner = wid * nar * er
    es = wid * ep
    dr = w_r.shape[1]
    gain = jnp.broadcast_to(gain_r[...], (dr, LANES)).astype(bf16)
    for half in range(2):
        first = half * (MODS * es + LANES)
        for m in range(MODS):
            row = w_r[m, :, half * inner : (half + 1) * inner].astype(f32)
            for k in range(nar):
                parts = []
                for v in range(wid):
                    parts.append(row[:, (v * nar + k) * er : (v * nar + k + 1) * er])
                    if ep > er:
                        parts.append(jnp.zeros((dr, ep - er), f32))
                rows_s[k, :, first + m * es : first + (m + 1) * es] = jnp.concatenate(parts, axis=1).astype(bf16)
    for s in range(nar):
        rows_s[s, :, MODS * es : MODS * es + LANES] = gain
    for s in range(nar):
        outs[s][...] = rows_s[meta[0] ^ s]
    out_whole = jnp.concatenate([out_r[m].astype(f32) for m in range(MODS)], axis=1)
    if ep > er:
        out_whole = jnp.concatenate([out_whole, jnp.zeros((ep - er, out_whole.shape[1]), f32)], axis=0)
    out_w = out_o.shape[1]
    for k in range(out_whole.shape[1] // out_w):
        out_o[k * ep : (k + 1) * ep, :] = out_whole[:, k * out_w : (k + 1) * out_w].astype(bf16)
    rank = dt_r.shape[1]
    lanes[...] = jnp.zeros_like(lanes)
    for m in range(MODS):
        lanes[m * rank : (m + 1) * rank, :er] = dt_r[m].astype(f32)
    base = MODS * rank
    for at, ref in ((T_BIAS, bias_r), (T_CONV_B, conv_b_r), (T_CONV, conv_r), (T_SKIP, skip_r), (T_LOG, log_r)):
        lanes[base + at : base + at + ref.shape[0], :er] = ref[...].astype(f32)
    turned = lanes[...].T[:ep]
    xw = x_r.shape[2]
    columns = []
    for m in range(MODS):
        part = x_r[m].astype(f32)
        if ep > er:
            part = jnp.concatenate([part, jnp.zeros((ep - er, xw), f32)], axis=0)
        columns += [part, jnp.zeros((ep, LANES - xw), f32)]
    small = jnp.concatenate(columns + [turned], axis=1)
    cols = small.shape[1]
    small_o[...] = jnp.zeros_like(small_o)
    for c in range(-(-ep // below)):
        part = small[c * below : min(ep, (c + 1) * below)]
        small_o[: part.shape[0], c * cols : (c + 1) * cols] = part.astype(bf16)


def join_kernel(meta, *refs):
    pieces, (small, out_rows, front_o, gate_o) = refs[:-4], refs[-4:]
    nar, dr = len(pieces), pieces[0].shape[0]
    row = lax.broadcasted_iota(jnp.int32, (nar * dr, dr), 0)
    col = lax.broadcasted_iota(jnp.int32, (nar * dr, dr), 1)
    joined = sum(
        dot((row == (meta[0] ^ s) * dr + col).astype(bf16), piece[...], 1, 0)
        for s, piece in enumerate(pieces)
    ).astype(bf16)
    front_o[: nar * dr, :] = joined[:, : front_o.shape[1]]
    front_o[nar * dr :, :] = small[...]
    gate_o[: nar * dr, :] = joined[:, front_o.shape[1] :]
    gate_o[nar * dr :, :] = out_rows[...]


T_BIAS, T_CONV_B, T_CONV, T_SKIP, T_LOG = 0, 3, 4, 8, 16


def in_kernel(nar, wid, rpd, taps, ep, rank, meta, *refs):
    toks, w_pieces = refs[:nar], refs[nar : nar + wid]
    normed_o, front_o, csum_o, mixed_o, px_o, kinds_o, w_x, w_dt_o, table_o, gain_o = refs[nar + wid : nar + wid + 10]
    xs, wf, rest, tok_sem, w_sem, rest_sem = refs[nar + wid + 10 :]
    n, w, split = meta[0], meta[1], meta[2]
    total, es = csum_o.shape
    width = MODS * es
    rows_w = wf.shape[0] // wid
    piece_rows = toks[0].shape[0]
    copies = []
    cols = rest.shape[1]
    below = w_pieces[0].shape[0] - rows_w
    x_cols = w_x.shape[1]
    for s, piece in enumerate(w_pieces):
        for c in range(-(-ep // below)):
            count = min(below, ep - c * below)
            at = pl.multiple_of((w ^ s) * ep + c * below, 16)
            copies.append(
                pltpu.make_async_copy(
                    piece.at[pl.ds(rows_w, count), pl.ds(c * cols, cols)],
                    rest.at[pl.ds(at, count), :],
                    rest_sem.at[c, s],
                )
            )
    tok_copies, w_copies = [], []
    for s, piece in enumerate(toks):
        at = pl.multiple_of((n ^ s) * piece_rows, 16)
        tok_copies.append(
            pltpu.make_async_copy(piece, xs.at[pl.ds(at, piece_rows), :], tok_sem.at[s])
        )
    for s, piece in enumerate(w_pieces):
        at = pl.multiple_of((w ^ s) * rows_w, 16)
        w_copies.append(
            pltpu.make_async_copy(
                piece.at[pl.ds(0, rows_w), pl.ds(0, wf.shape[1])], wf.at[pl.ds(at, rows_w), :], w_sem.at[s]
            )
        )
    for copy in copies + tok_copies + w_copies:
        copy.start()
    for copy in copies:
        copy.wait()
    w_x[...] = rest[:, :x_cols]
    turned = rest[:, x_cols:].astype(f32).T
    w_dt_o[...] = turned[: MODS * rank].astype(bf16)
    table_o[...] = turned[MODS * rank :]
    for copy in tok_copies:
        copy.wait()
    for p in range(nar):
        tail = xs[(p + 1) * piece_rows - 16 : (p + 1) * piece_rows, :LANES].astype(f32)
        row = lax.broadcasted_iota(jnp.int32, tail.shape, 0)
        for j in range(rpd):
            kinds_o[p * rpd + j] = jnp.max(jnp.where(row == j, tail, 0.0)).astype(jnp.int32)
    for copy in w_copies:
        copy.wait()
    gain = wf[:, width : width + LANES].astype(f32).T[0:1, :]
    gain_o[...] = gain
    front_o[0:8, :] = jnp.zeros((8, es), f32)

    def one_run(r, before):
        rows = pl.ds(pl.multiple_of(r * RUN, RUN), RUN)
        kind = kinds_o[r]
        x_at = pl.multiple_of((r // rpd) * piece_rows + (r % rpd) * RUN, 16)
        x = xs[pl.ds(x_at, RUN), :].astype(f32)
        scale = lax.rsqrt(jnp.mean(x * x, axis=1, keepdims=True) + EPSILON)
        normed = (x * scale * gain).astype(bf16)
        normed_o[rows, :] = normed
        front = dot(normed, wf[:, pl.ds(pl.multiple_of(kind * es, LANES), es)], 1, 0)
        front_o[pl.ds(pl.multiple_of(r * RUN + 8, 8), RUN), :] = front
        ext = jnp.concatenate([before, front], axis=0)
        place = r * RUN + lax.broadcasted_iota(jnp.int32, (RUN, 1), 0)
        offset = place - jnp.where(place >= split, split, 0)
        csum = jnp.broadcast_to(table_o[T_CONV_B : T_CONV_B + 1, :], (RUN, es))
        for lag in range(taps):
            tap = table_o[T_CONV + taps - 1 - lag : T_CONV + taps - lag, :]
            valid = (offset >= lag).astype(f32)
            csum = csum + tap * ext[8 - lag : 8 - lag + RUN, :] * valid
        csum_o[rows, :] = csum
        mixed = (csum * jax.nn.sigmoid(csum)).astype(bf16)
        mixed_o[rows, :] = mixed
        px = dot(mixed, w_x[:, pl.ds(pl.multiple_of(kind * LANES, LANES), LANES)], 1, 0)
        px_o[:, pl.ds(pl.multiple_of(r * RUN, LANES), RUN)] = px.T[: px_o.shape[0]].astype(bf16)
        return front[RUN - 8 :]

    lax.fori_loop(0, total // RUN, one_run, jnp.zeros((8, es), f32))


def gate_kernel(wid, meta, kinds, *refs):
    pieces, (normed_r, act_o, slope_o, wg, w_sem) = refs[:wid], refs[wid:]
    es = act_o.shape[1]
    width = wg.shape[1]
    rows_w = wg.shape[0] // wid
    copies = []
    for s, piece in enumerate(pieces):
        at = pl.multiple_of((meta[1] ^ s) * rows_w, 16)
        source = piece.at[pl.ds(0, rows_w), :]
        copies.append(pltpu.make_async_copy(source, wg.at[pl.ds(at, rows_w), :], w_sem.at[s]))
        copies[-1].start()
    for copy in copies:
        copy.wait()

    def one_run(r, carry):
        rows = pl.ds(pl.multiple_of(r * RUN, RUN), RUN)
        gate = dot(normed_r[rows, :], wg[:, pl.ds(pl.multiple_of(kinds[r] * es, LANES), es)], 1, 0)
        sig = jax.nn.sigmoid(gate)
        act_o[rows, :] = gate * sig
        slope_o[rows, :] = sig * (1.0 + gate * (1.0 - sig))
        return carry

    lax.fori_loop(0, normed_r.shape[0] // RUN, one_run, 0)


def cot_kernel(nar, wid, meta, kinds, *refs):
    cots, pieces = refs[:nar], refs[nar : nar + wid]
    act_r, slope_r, cot_o, w_out_o, dssm_o, dgate_o, cot_sem, out_sem = refs[nar + wid :]
    total, d = cot_o.shape
    copies = place_pieces(cots, cot_o, cot_sem, meta[0], cots[0].shape[0])
    width = pieces[0].shape[1]
    ep = w_out_o.shape[0] // wid
    blocks = w_out_o.shape[1] // width
    first = pieces[0].shape[0] - blocks * ep
    for s, piece in enumerate(pieces):
        at = pl.multiple_of((meta[1] ^ s) * ep, 16)
        for k in range(blocks):
            copies.append(
                pltpu.make_async_copy(
                    piece.at[pl.ds(first + k * ep, ep), :],
                    w_out_o.at[pl.ds(at, ep), pl.ds(k * width, width)],
                    out_sem.at[k, s],
                )
            )
            copies[-1].start()
    for copy in copies:
        copy.wait()

    def one_run(r, carry):
        rows = pl.ds(pl.multiple_of(r * RUN, RUN), RUN)
        d_gated = dot(cot_o[rows, :], w_out_o[:, pl.ds(pl.multiple_of(kinds[r] * d, LANES), d)], 1, 1)
        dssm_o[rows, :] = d_gated * act_r[rows, :]
        dgate_o[rows, :] = d_gated * slope_r[rows, :]
        return carry

    lax.fori_loop(0, total // RUN, one_run, 0)


def softplus(v):
    return jnp.maximum(v, 0.0) + jnp.log1p(jnp.exp(-jnp.abs(v)))


def scan_kernel(rank, meta, kinds, *refs):
    px_r, w_dt, table, mixed_r, dssm_r = refs[:5]
    ssm_o, dpx_o, gmix_o, dpre_o, dlow_o, glog_o, gskip_o = refs[5:12]
    pxs, pre_s, step_s, states, bc, ps, qs, gs, fs, dtk, dtu, r1s, r2s = refs[12:]
    split = meta[2]
    total, es = mixed_r.shape
    ns = states.shape[1]
    groups = es // LANES
    runs = total // RUN
    lane = [slice(g * LANES, (g + 1) * LANES) for g in range(groups)]
    rates = -jnp.exp(table[T_LOG : T_LOG + ns, :])
    r1s[...] = rates
    r2s[...] = rates * LOG2E
    half = ns // 2
    pxs[...] = px_r[...].astype(f32)
    skip = table[T_SKIP : T_SKIP + 1, :]

    def rows_of(r):
        return pl.ds(pl.multiple_of(r * RUN, RUN), RUN)

    k_row = lax.broadcasted_iota(jnp.int32, (ns, LANES), 1)
    own_row = (k_row % ns == lax.broadcasted_iota(jnp.int32, (ns, LANES), 0)) & (k_row < 4 * ns)
    own_row = own_row.astype(f32)
    k_col = lax.broadcasted_iota(jnp.int32, (LANES, 2 * LANES), 0)
    b_or_c = lax.broadcasted_iota(jnp.int32, (LANES, 2 * LANES), 1) // LANES
    ones = ((k_col % (2 * ns)) // ns == b_or_c).astype(bf16)

    def spread(r):
        block = pxs[rank : rank + 2 * ns, pl.ds(pl.multiple_of(r * RUN, LANES), RUN)]
        high = block.astype(bf16).astype(f32)
        parts = jnp.concatenate([high, block - high, jnp.zeros((LANES - 4 * ns, RUN), f32)], axis=0)
        picked = parts.T[:, None, :] * own_row[None]
        bc[bc_rows(r), :] = dot(picked.reshape(RUN * ns, LANES).astype(bf16), ones, 1, 0)

    def bc_rows(r):
        if bc.shape[0] == RUN * ns:
            return pl.ds(0, RUN * ns)
        return pl.ds(pl.multiple_of(r * (RUN * ns), RUN * ns), RUN * ns)

    def prepare(r, again):
        rows = rows_of(r)
        steps = step_s[rows, :]
        place = r * RUN + lax.broadcasted_iota(jnp.int32, (RUN, 1), 0)
        reset = (place == 0) | (place == split)
        dtk[...] = jnp.where(reset, FAR, steps)
        dtu[...] = steps * mixed_r[rows, :].astype(f32)
        if not again or bc.shape[0] == RUN * ns:
            spread(r)

    def row(tile, j, g):
        return jnp.broadcast_to(tile[j : j + 1, lane[g]], (ns, LANES))

    def folded(ref):
        outs = []
        for g in range(groups):
            out = ref[g, pl.ds(0, RUN, stride=half), :]
            for s in range(1, half):
                out = out + ref[g, pl.ds(s, RUN, stride=half), :]
            outs.append(out)
        return jnp.concatenate(outs, axis=1)

    states[0] = jnp.zeros((ns, es), bf16)

    def forward(r, hs):
        rows = rows_of(r)
        kind = kinds[r]
        low = pxs[:rank, pl.ds(pl.multiple_of(r * RUN, LANES), RUN)].astype(bf16)
        dlow_o[:, pl.ds(pl.multiple_of(r * RUN, LANES), RUN)] = low
        weights = w_dt[pl.ds(pl.multiple_of(kind * rank, 16), rank), :]
        pre = dot(low, weights, 0, 0) + table[pl.ds(T_BIAS + kind, 1), :]
        pre_s[rows, :] = pre
        step_s[rows, :] = softplus(pre)
        prepare(r, False)

        def eight(i, hs):
            hs = list(hs)
            at = pl.ds(pl.multiple_of(i * 16, 16), 16)
            k8, u8 = dtk[at, :], dtu[at, :]
            bcv = bc.at[bc_rows(r), :].at[pl.ds(pl.multiple_of(i * (16 * ns), 16 * ns), 16 * ns), :]
            psv = ps.at[:, pl.ds(pl.multiple_of(i * (16 * half), 16 * half), 16 * half), :]
            stv = states.at[pl.ds(r * RUN + i * 16 + 1, 16)]
            for j in range(16):
                bt = bcv[j * ns : (j + 1) * ns, :LANES]
                ct = bcv[j * ns : (j + 1) * ns, LANES:]
                for g in range(groups):
                    decay = jnp.exp2(row(k8, j, g) * r2s[:, lane[g]])
                    hs[g] = decay * hs[g] + row(u8, j, g) * bt
                    stv[j, :, lane[g]] = hs[g].astype(bf16)
                    part = hs[g] * ct
                    psv[g, j * half : (j + 1) * half, :] = part[:half] + part[half:]
            return tuple(hs)

        hs = lax.fori_loop(0, RUN // 16, eight, hs)
        ssm_o[rows, :] = folded(ps) + skip * mixed_r[rows, :].astype(f32)
        return hs

    zero = jnp.zeros((ns, LANES), f32)
    lax.fori_loop(0, runs, forward, (zero,) * groups)
    gskip_o[...] = jnp.zeros_like(gskip_o)
    gather_k = lax.broadcasted_iota(jnp.int32, (2 * LANES, LANES), 0) // LANES
    gather_l = lax.broadcasted_iota(jnp.int32, (2 * LANES, LANES), 1) // ns
    gather = (gather_k == gather_l).astype(bf16)
    keep_n = lax.broadcasted_iota(jnp.int32, (ns, LANES), 0)
    keep = (lax.broadcasted_iota(jnp.int32, (ns, LANES), 1) % ns == keep_n).astype(f32)

    def backward(back, carry):
        r = runs - 1 - back
        rows = rows_of(r)
        kind = kinds[r]
        prepare(r, True)

        def eight(back_i, carry):
            ms, hs, gr = [list(part) for part in carry]
            i = RUN // 16 - 1 - back_i
            at = pl.ds(pl.multiple_of(i * 16, 16), 16)
            k8, u8 = dtk[at, :], dtu[at, :]
            y8 = dssm_r[pl.ds(pl.multiple_of(r * RUN + i * 16, 16), 16), :]
            bcv = bc.at[bc_rows(r), :].at[pl.ds(pl.multiple_of(i * (16 * ns), 16 * ns), 16 * ns), :]
            psv = ps.at[:, pl.ds(pl.multiple_of(i * (16 * half), 16 * half), 16 * half), :]
            qsv = qs.at[:, pl.ds(pl.multiple_of(i * (16 * half), 16 * half), 16 * half), :]
            stv = states.at[pl.ds(r * RUN + i * 16, 16)]
            gsv = gs.at[pl.ds(pl.multiple_of(i * (16 * ns), 16 * ns), 16 * ns), :]
            for j in reversed(range(16)):
                bt = bcv[j * ns : (j + 1) * ns, :LANES]
                ct = bcv[j * ns : (j + 1) * ns, LANES:]
                gb_sum, gc_sum = None, None
                for g in range(groups):
                    dt = row(k8, j, g)
                    dy = row(y8, j, g)
                    adjoint = dy * ct + ms[g]
                    before = stv[j, :, lane[g]].astype(f32)
                    c_part = dy * hs[g]
                    b_part = adjoint * row(u8, j, g)
                    gb_sum = b_part if gb_sum is None else gb_sum + b_part
                    gc_sum = c_part if gc_sum is None else gc_sum + c_part
                    lb = adjoint * bt
                    fold_at = slice(j * half, (j + 1) * half)
                    psv[g, fold_at, :] = lb[:half] + lb[half:]
                    ms[g] = jnp.exp2(dt * r2s[:, lane[g]]) * adjoint
                    weighted = ms[g] * before
                    by_rate = weighted * r1s[:, lane[g]]
                    qsv[g, fold_at, :] = by_rate[:half] + by_rate[half:]
                    gr[g] = gr[g] + weighted * dt
                    hs[g] = before
                gsv[j * ns : (j + 1) * ns, :LANES] = gb_sum.astype(bf16)
                gsv[j * ns : (j + 1) * ns, LANES:] = gc_sum.astype(bf16)
            return tuple(ms), tuple(hs), tuple(gr)

        carry = lax.fori_loop(0, RUN // 16, eight, carry)
        mixed = mixed_r[rows, :].astype(f32)
        lb, by_rate = folded(ps), folded(qs)
        dssm = dssm_r[rows, :]
        grad_steps = by_rate + lb * mixed
        gmix_o[rows, :] = dssm * skip + lb * step_s[rows, :]
        gskip_o[...] += jnp.sum(dssm * mixed, axis=0, keepdims=True)
        dpre = (grad_steps * jax.nn.sigmoid(pre_s[rows, :])).astype(bf16)
        dpre_o[rows, :] = dpre
        weights = w_dt[pl.ds(pl.multiple_of(kind * rank, 16), rank), :]
        dlow = dot(weights, dpre, 1, 1)
        sums = dot(gs[...], gather, 1, 0).reshape(RUN, ns, LANES) * keep[None]
        fs[...] = (sums[:, :half] + sums[:, half:]).reshape(RUN * half, LANES)
        dbc = fs[pl.ds(0, RUN, stride=half), :]
        for s in range(1, half):
            dbc = dbc + fs[pl.ds(s, RUN, stride=half), :]
        dbc = dbc.T[: 2 * ns]
        at = pl.ds(pl.multiple_of(r * RUN, LANES), RUN)
        dpx_o[:rank, at] = dlow.astype(bf16)
        dpx_o[rank:, at] = dbc.astype(bf16)
        return carry

    last = tuple(states[total, :, lane[g]].astype(f32) for g in range(groups))
    done = lax.fori_loop(0, runs, backward, ((zero,) * groups, last, (zero,) * groups))
    for g in range(groups):
        glog_o[:, lane[g]] = done[2][g] * rates[:, lane[g]]


def scan_call(rank, xw, ns, meta, kinds, px, w_dt_l, table, mixed, dssm):
    total, es = mixed.shape
    bc_runs = total // RUN if total * ns * 2 * LANES * 4 <= 20 * 1024 * 1024 else 1
    return call(
        functools.partial(scan_kernel, rank),
        [
            ((total, es), f32, "v"),
            ((xw, total), bf16, "v"),
            ((total, es), f32, "v"),
            ((total, es), bf16, "v"),
            ((rank, total), bf16, "v"),
            ((ns, es), f32, "v"),
            ((1, es), f32, "v"),
        ],
        [(meta, "s"), (kinds, "s")]
        + [(px, "v"), (w_dt_l, "v"), (table, "v"), (mixed, "v"), (dssm, "v")],
        [
            pltpu.VMEM((xw, total), f32),
            pltpu.VMEM((total, es), f32),
            pltpu.VMEM((total, es), f32),
            pltpu.VMEM((total + 1, ns, es), bf16),
            pltpu.VMEM((bc_runs * RUN * ns, 2 * LANES), f32),
            pltpu.VMEM((es // LANES, RUN * ns // 2, LANES), f32),
            pltpu.VMEM((es // LANES, RUN * ns // 2, LANES), f32),
            pltpu.VMEM((RUN * ns, 2 * LANES), bf16),
            pltpu.VMEM((RUN * ns // 2, LANES), f32),
            pltpu.VMEM((RUN, es), f32),
            pltpu.VMEM((RUN, es), f32),
            pltpu.VMEM((ns, es), f32),
            pltpu.VMEM((ns, es), f32),
        ],
        us=40.0,
    )


def split_rows(acc, place, rows):
    return acc[pl.ds(pl.multiple_of(place * rows, 16), rows), :]


def grads_kernel(wid, ep, rank, meta, kinds, *refs):
    ssm_r, gated_r, dgate_r, cot_r, normed_r, dpre_r, dlow_r, glog_r, gskip_r = refs[:9]
    dgate_o, table_o, blocks_o, acc_out, acc_in = refs[9:]
    total, es = ssm_r.shape
    d = cot_r.shape[1]
    acc_out[...] = jnp.zeros_like(acc_out)
    acc_in[...] = jnp.zeros_like(acc_in)
    table_o[...] = jnp.zeros_like(table_o)
    base = MODS * rank

    def one_run(r, carry):
        rows = pl.ds(pl.multiple_of(r * RUN, RUN), RUN)
        kind = kinds[r]
        ssm = ssm_r[rows, :]
        gated = gated_r[rows, :]
        wide_at = pl.ds(pl.multiple_of(kind * d, LANES), d)
        es_at = pl.ds(pl.multiple_of(kind * es, LANES), es)
        acc_out[:, wide_at] += dot(gated, cot_r[rows, :], 0, 0)
        dgate = (dgate_r[rows, :] * ssm).astype(bf16)
        dgate_o[rows, :] = dgate
        acc_in[:, es_at] += dot(normed_r[rows, :], dgate, 0, 0)
        dpre = dpre_r[rows, :]
        low = dlow_r[:, pl.ds(pl.multiple_of(r * RUN, LANES), RUN)]
        table_o[pl.ds(pl.multiple_of(kind * rank, 8), rank), :] += dot(low, dpre, 1, 0)
        table_o[pl.ds(base + T_BIAS + kind, 1), :] += jnp.sum(dpre.astype(f32), axis=0, keepdims=True)
        return carry

    lax.fori_loop(0, total // RUN, one_run, 0)
    table_o[base + T_SKIP : base + T_SKIP + 1, :] = gskip_r[...]
    table_o[base + T_LOG : base + T_LOG + glog_r.shape[0], :] = glog_r[...]
    in_rows, width = acc_in.shape[0] // wid, acc_in.shape[1]
    for v in range(wid):
        blocks_o[v, :in_rows, :] = acc_in[v * in_rows : (v + 1) * in_rows, :].astype(bf16)
        block = acc_out[v * ep : (v + 1) * ep, :].astype(bf16)
        for k in range(block.shape[1] // width):
            first = in_rows + k * ep
            blocks_o[v, first : first + ep, :] = block[:, k * width : (k + 1) * width]


def branch_kernel(nar, meta, kinds, ssm_r, act_r, w_out, *refs):
    outs, gated_o, branch = refs[:nar], refs[nar], refs[nar + 1]
    d = branch.shape[1]

    def one_run(r, carry):
        rows = pl.ds(pl.multiple_of(r * RUN, RUN), RUN)
        wide_at = pl.ds(pl.multiple_of(kinds[r] * d, LANES), d)
        gated = (ssm_r[rows, :] * act_r[rows, :]).astype(bf16)
        gated_o[rows, :] = gated
        branch[rows, :] = dot(gated, w_out[:, wide_at], 1, 0).astype(bf16)
        return carry

    lax.fori_loop(0, branch.shape[0] // RUN, one_run, 0)
    size = outs[0].shape[0]
    for s in range(nar):
        outs[s][...] = branch[pl.ds(pl.multiple_of((meta[0] ^ s) * size, RUN), size), :]


def pair_kernel(chips, meta, same, peer, *outs):
    chip = meta[1] // 2
    for s in range(chips):
        outs[s][...] = (same[chip ^ s].astype(f32) + peer[chip ^ s].astype(f32)).astype(bf16)


def conv_kernel(nar, wid, taps, ep, meta, kinds, *refs):
    dpx_pieces = refs[:nar]
    table, w_x, gmix_r, csum_r, front_r, mixed_r, normed_r, table_r = refs[nar : nar + 8]
    dfront_o, same_o, peer_o, acc_in, acc_x, small, turned = refs[nar + 8 :]
    split = meta[2]
    total, es = gmix_r.shape
    runs = total // RUN
    acc_in[...] = jnp.zeros_like(acc_in)
    acc_x[...] = jnp.zeros_like(acc_x)
    small[...] = jnp.zeros_like(small)
    xw = dpx_pieces[0].shape[0]

    def one_run(back, later):
        r = runs - 1 - back
        rows = pl.ds(pl.multiple_of(r * RUN, RUN), RUN)
        kind = kinds[r]
        lanes_at = pl.ds(pl.multiple_of(r * RUN, LANES), RUN)
        dpx = sum(piece[:, lanes_at].astype(f32) for piece in dpx_pieces)
        dpx = jnp.concatenate([dpx, jnp.zeros((LANES - xw, RUN), f32)], axis=0).T.astype(bf16)
        x_at = pl.ds(pl.multiple_of(kind * LANES, LANES), LANES)
        acc_x[:, x_at] += dot(mixed_r[rows, :], dpx, 0, 0)
        gmix = gmix_r[rows, :] + dot(dpx, w_x[:, x_at], 1, 1)
        csum = csum_r[rows, :]
        sig = jax.nn.sigmoid(csum)
        dc = gmix * sig * (1.0 + csum * (1.0 - sig))
        place = r * RUN + lax.broadcasted_iota(jnp.int32, (RUN + 8, 1), 0)
        offset = place - jnp.where(place >= split, split, 0)
        ext = jnp.concatenate([dc, later], axis=0)
        lagged = front_r[pl.ds(pl.multiple_of(r * RUN, 8), RUN + 8), :]
        d_front = jnp.zeros((RUN, es), f32)
        for lag in range(taps):
            tap = taps - 1 - lag
            masked = ext * (offset >= lag).astype(f32)
            d_front = d_front + table[T_CONV + tap : T_CONV + tap + 1, :] * masked[lag : lag + RUN, :]
            small[T_CONV + tap : T_CONV + tap + 1, :] += jnp.sum(
                masked[:RUN] * lagged[8 - lag : 8 - lag + RUN, :], axis=0, keepdims=True
            )
        small[T_CONV_B : T_CONV_B + 1, :] += jnp.sum(dc, axis=0, keepdims=True)
        d_front = d_front.astype(bf16)
        dfront_o[rows, :] = d_front
        acc_in[:, pl.ds(pl.multiple_of(kind * es, LANES), es)] += dot(normed_r[rows, :], d_front, 0, 0)
        return dc[:8]

    lax.fori_loop(0, runs, one_run, jnp.zeros((8, es), f32))
    in_rows, width = acc_in.shape[0] // wid, acc_in.shape[1]
    base = table_r.shape[0] - small.shape[0]
    rest = jnp.concatenate([table_r[:base, :], table_r[base:, :] + small[...]], axis=0)
    rest = jnp.concatenate([rest, jnp.zeros((256 - rest.shape[0], es), f32)], axis=0).T
    x_cols = acc_x.shape[1]
    turned[:, :x_cols] = acc_x[...].astype(bf16)
    turned[:, x_cols : x_cols + 256] = rest.astype(bf16)
    turned[:, x_cols + 256 :] = jnp.zeros((es, width - x_cols - 256), bf16)
    core = meta[1] & 1
    for ref, parity in ((same_o, core), (peer_o, 1 - core)):
        for c in range(wid // 2):
            place = 2 * c + parity
            ref[c, :in_rows, :] = split_rows(acc_in, place, in_rows).astype(bf16)
            ref[c, in_rows:, :] = split_rows(turned, place, ep)


def normed_kernel(nar, wid, meta, kinds, *refs):
    fronts, gates = refs[:wid], refs[wid : 2 * wid]
    dfront_r, dgate_r = refs[2 * wid : 2 * wid + 2]
    outs = refs[2 * wid + 2 : 2 * wid + 2 + nar]
    wf, wg, dn, f_sem, g_sem = refs[2 * wid + 2 + nar :]
    w = meta[1]
    total, es = dfront_r.shape
    rows_w = wf.shape[0] // wid
    copies = []
    width = MODS * es
    for pieces, target, sem in ((fronts, wf, f_sem), (gates, wg, g_sem)):
        for s, piece in enumerate(pieces):
            at = pl.multiple_of((w ^ s) * rows_w, 16)
            copies.append(
                pltpu.make_async_copy(
                    piece.at[pl.ds(0, rows_w), pl.ds(0, width)], target.at[pl.ds(at, rows_w), :], sem.at[s]
                )
            )
            copies[-1].start()
    for copy in copies:
        copy.wait()

    def one_run(r, carry):
        rows = pl.ds(pl.multiple_of(r * RUN, RUN), RUN)
        at = pl.ds(pl.multiple_of(kinds[r] * es, LANES), es)
        dn[rows, :] = (dot(dfront_r[rows, :], wf[:, at], 1, 1) + dot(dgate_r[rows, :], wg[:, at], 1, 1)).astype(bf16)
        return carry

    lax.fori_loop(0, total // RUN, one_run, 0)
    size = outs[0].shape[0]
    for s in range(nar):
        outs[s][...] = dn[pl.ds(pl.multiple_of((meta[0] ^ s) * size, RUN), size), :]


def total_a_kernel(er, ep, blocks, in_o, out_o):
    d = out_o.shape[2]
    in_rows = in_o.shape[0]
    summed = sum(blocks[v].astype(f32) for v in range(blocks.shape[0]))
    in_o[...] = summed[:in_rows].astype(bf16)
    wide = jnp.concatenate([summed[at : at + ep] for at in range(in_rows, summed.shape[0], ep)], axis=1)
    for m in range(MODS):
        out_o[m] = wide[:er, m * d : (m + 1) * d]


def total_b_kernel(nar, chips, er, rank, taps, ns, meta, *refs):
    pieces, gate_r, outs = refs[:chips], refs[chips], refs[chips + 1 : chips + 1 + nar]
    x_o, dt_o, bias_o, conv_o, conv_b_o, log_o, skip_o, rows_s = refs[chips + 1 + nar :]
    in_rows, width = gate_r.shape
    dr = outs[0].shape[0]
    summed = sum(piece[...].astype(f32) for piece in pieces)
    gate = gate_r[...].astype(f32)
    for k in range(nar):
        rows_s[k, :, :width] = summed[k * dr : (k + 1) * dr].astype(bf16)
        rows_s[k, :, width:] = gate[k * dr : (k + 1) * dr].astype(bf16)
    for s in range(nar):
        outs[s][...] = rows_s[meta[0] ^ s]
    rest = summed[in_rows:]
    x_cols = MODS * LANES
    for m in range(MODS):
        x_o[m] = rest[:er, m * LANES : m * LANES + x_o.shape[2]]
    lanes = rest[:, x_cols : x_cols + 256]
    pad = LANES - lanes.shape[0]
    turned = jnp.concatenate([lanes, jnp.zeros((pad, 256), f32)], axis=0).T[:, :er]
    base = MODS * rank
    for m in range(MODS):
        dt_o[m] = turned[m * rank : (m + 1) * rank]
    bias_o[...] = turned[base + T_BIAS : base + T_BIAS + MODS]
    conv_o[...] = turned[base + T_CONV : base + T_CONV + taps]
    conv_b_o[...] = turned[base + T_CONV_B : base + T_CONV_B + 1]
    skip_o[...] = turned[base + T_SKIP : base + T_SKIP + 1]
    log_o[...] = turned[base + T_LOG : base + T_LOG + ns]


def tokens_kernel(x_r, cot_r, gain_r, *refs):
    pieces, out = refs[:-1], refs[-1]
    x = x_r[...].astype(f32)
    scale = lax.rsqrt(jnp.mean(x * x, axis=1, keepdims=True) + EPSILON)
    q = sum(piece[...].astype(f32) for piece in pieces) * gain_r[...]
    dotted = jnp.mean(q * x, axis=1, keepdims=True)
    out[...] = (cot_r[...].astype(f32) + scale * q - x * (scale * scale * scale) * dotted).astype(bf16)


def mixed_kernel(x_r, *refs):
    pieces, out = refs[:-1], refs[-1]
    out[...] = (x_r[...].astype(f32) + sum(piece[...].astype(f32) for piece in pieces)).astype(bf16)


def w_in_kernel(nar, wid, er, ep, meta, *refs):
    pieces, (w_r, gain_r, grad_o, gain_o, rows_s) = refs[:nar], refs[nar:]
    es = wid * ep
    inner = wid * nar * er
    for s in range(nar):
        rows_s[meta[0] ^ s] = pieces[s][...].astype(f32)
    sums = 0.0
    for half in range(2):
        for m in range(MODS):
            first = (half * MODS + m) * es
            parts = [rows_s[k, :, first : first + es] for k in range(nar)]
            row = jnp.concatenate(
                [parts[k][:, v * ep : v * ep + er] for v in range(wid) for k in range(nar)], axis=1
            )
            at = slice(half * inner, (half + 1) * inner)
            grad_o[m, :, at] = row
            sums = sums + jnp.sum(row * w_r[m, :, at].astype(f32), axis=1, keepdims=True)
    gain_o[...] = sums / gain_r[...]


def body(
    tokens,
    norm_gain,
    w_in,
    conv_w,
    conv_b,
    w_x,
    w_dt,
    dt_bias,
    a_log,
    d_skip,
    w_out,
    mod_ids,
    split_at,
    cotangent,
):
    nar, wid = lax.axis_size("narrow"), lax.axis_size("wide")
    chips = wid // 2
    n, w = lax.axis_index("narrow"), lax.axis_index("wide")
    own, d = tokens.shape
    total = nar * own
    rpd = own // RUN
    rank, xw, ns, taps = w_dt.shape[0], w_x.shape[2], a_log.shape[1], conv_w.shape[0]
    er = w_out.shape[0]
    inner = er * nar * wid
    ep = -(-er // 16) * 16
    es = ep * wid
    dr = w_in.shape[0]
    width = MODS * es
    meta = jnp.stack([n, w, split_at[0]]).astype(jnp.int32)

    front_w = width + LANES
    gain_col = norm_gain.astype(f32)[:, None]
    w_in_m = w_in.transpose(1, 0, 2)
    out_cols, x_cols = MODS * d, MODS * LANES
    table_rows = T_LOG + ns
    small_cols = x_cols + 256
    blocks = front_w // small_cols
    below = -(-(-(-ep // blocks)) // 16) * 16
    res = call(
        functools.partial(split_kernel, er, ep, wid, below),
        [((dr, front_w + width), bf16, "v")] * nar
        + [((below, front_w), bf16, "v"), ((ep * (out_cols // width), width), bf16, "v")],
        [(meta, "s")]
        + [
            (a, "v")
            for a in (
                w_in_m,
                gain_col,
                w_out.transpose(1, 0, 2),
                w_x.transpose(1, 0, 2),
                w_dt.transpose(1, 0, 2),
                dt_bias,
                conv_w,
                conv_b[None],
                d_skip[None],
                a_log.T,
            )
        ],
        [
            pltpu.VMEM((nar, dr, front_w + width), bf16),
            pltpu.VMEM((256, LANES), f32),
        ],
        us=3.0,
    )
    parts, (small, out_rows) = res[:nar], res[nar:]

    parts = scatter_narrow(parts)
    front_rows, gate_rows = call(
        join_kernel,
        [
            ((nar * dr + below, front_w), bf16, "v"),
            ((nar * dr + out_rows.shape[0], width), bf16, "v"),
        ],
        [(meta, "s")] + [(p, "v") for p in parts] + [(small, "v"), (out_rows, "v")],
        us=2.0,
    )
    front_near = near_wide(front_rows)
    front_pieces = far_wide(front_near)
    run_kinds = mod_ids.reshape(rpd, RUN)[:, :1].astype(bf16)
    tail = jnp.pad(jnp.broadcast_to(run_kinds, (rpd, d)), ((0, 16 - rpd), (0, 0)))
    tok_pieces = relay_narrow(jnp.concatenate([tokens, tail], axis=0))
    gate_near = near_wide(after(gate_rows, *front_near[1:]))
    normed, front, csum, mixed, px, kinds, w_x_l, w_dt_l, table, gain_full = call(
        functools.partial(in_kernel, nar, wid, rpd, taps, ep, rank),
        [
            ((total, d), bf16, "v"),
            ((total + 8, es), f32, "v"),
            ((total, es), f32, "v"),
            ((total, es), bf16, "v"),
            ((xw, total), bf16, "v"),
            ((nar * rpd,), jnp.int32, "s"),
            ((es, x_cols), bf16, "v"),
            ((MODS * rank, es), bf16, "v"),
            ((256 - MODS * rank, es), f32, "v"),
            ((1, d), f32, "v"),
        ],
        [(meta, "s")] + [(p, "a") for p in tok_pieces] + [(p, "a") for p in front_pieces],
        [
            pltpu.VMEM((nar * (own + 16), d), bf16),
            pltpu.VMEM((d, front_w), bf16),
            pltpu.VMEM((es, small_cols), bf16),
            pltpu.SemaphoreType.DMA((nar,)),
            pltpu.SemaphoreType.DMA((wid,)),
            pltpu.SemaphoreType.DMA((-(-ep // below), wid)),
        ],
        us=9.0,
    )
    cot_pieces = relay_narrow(after(cotangent, *tok_pieces[1:]), px)
    gate_pieces = far_wide([after(piece, px) for piece in gate_near])
    act, slope = call(
        functools.partial(gate_kernel, wid),
        [((total, es), f32, "v")] * 2,
        [(meta, "s"), (kinds, "s")] + [(p, "a") for p in gate_pieces] + [(after(normed, *cot_pieces[1:3]), "v")],
        [pltpu.VMEM((d, width), bf16), pltpu.SemaphoreType.DMA((wid,))],
        us=0.1,
    )
    px_total = add_narrow(px, act)
    cot, w_out_l, dssm, dgate_f = call(
        functools.partial(cot_kernel, nar, wid),
        [((total, d), bf16, "v"), ((es, out_cols), bf16, "v")] + [((total, es), f32, "v")] * 2,
        [(meta, "s"), (kinds, "s")]
        + [(p, "a") for p in cot_pieces]
        + [(p, "a") for p in gate_pieces]
        + [(act, "v"), (slope, "v")],
        [pltpu.SemaphoreType.DMA((nar,)), pltpu.SemaphoreType.DMA((out_cols // width, wid))],
        us=7.0,
    )
    ssm, dpx, gmix, dpre, dlow, glog, gskip = scan_call(
        rank, xw, ns, meta, kinds, px_total, w_dt_l, table, mixed, dssm
    )
    dpx_pieces = gather_narrow(dpx)
    res = call(
        functools.partial(branch_kernel, nar),
        [((own, d), bf16, "v")] * nar + [((total, es), bf16, "v")],
        [(meta, "s"), (kinds, "s"), (ssm, "v"), (act, "v"), (w_out_l, "v")],
        [pltpu.VMEM((total, d), bf16)],
        us=5.0,
    )

    branch_parts, gated = res[:nar], res[nar]
    branch_pieces, branch_kept = sum_narrow(branch_parts)
    branch_d1 = branch_pieces[-1]
    in_rows = d // wid
    rows_a = in_rows + ep * (out_cols // width)
    dgate, table_g, blocks_a = call(
        functools.partial(grads_kernel, wid, ep, rank),
        [((total, es), bf16, "v")]
        + [((MODS * rank + table_rows, es), f32, "v")]
        + [((wid, rows_a, width), bf16, "v")],
        [(meta, "s"), (kinds, "s")]
        + [(a, "v") for a in (ssm, gated, dgate_f, cot, normed, dpre, dlow, glog, gskip)],
        [pltpu.VMEM((es, out_cols), f32), pltpu.VMEM((d, width), f32)],
        us=9.0,
    )
    def over_wide(same, peer, *earlier):
        peer = swap(peer, "wide", 1)
        same = after(same, *earlier) if earlier else same
        parts = call(
            functools.partial(pair_kernel, chips),
            [(same.shape[1:], bf16, "v")] * chips,
            [(meta, "s"), (same, "v"), (peer, "v")],
            us=3.0,
        )
        return [parts[0]] + [swap(parts[s], "wide", 2 * s) for s in range(1, chips)]

    blocks_a = lax.all_to_all(blocks_a, "wide", 0, 0)
    rows_b = in_rows + ep
    dpx_pieces = after(tuple(dpx_pieces), branch_kept, branch_d1)
    dfront, same_b, peer_b = call(
        functools.partial(conv_kernel, nar, wid, taps, ep),
        [((total, es), bf16, "v")] + [((chips, rows_b, width), bf16, "v")] * 2,
        [(meta, "s"), (kinds, "s")]
        + [(p, "v") for p in dpx_pieces]
        + [(a, "v") for a in (table, w_x_l, gmix, csum, front, mixed, normed, table_g)],
        [
            pltpu.VMEM((d, width), f32),
            pltpu.VMEM((es, x_cols), f32),
            pltpu.VMEM((table_rows, es), f32),
            pltpu.VMEM((es, width), bf16),
        ],
        us=12.0,
    )
    dn_parts = call(
        functools.partial(normed_kernel, nar, wid),
        [((own, d), bf16, "v")] * nar,
        [(meta, "s"), (kinds, "s")]
        + [(p, "a") for p in front_pieces]
        + [(p, "a") for p in gate_pieces]
        + [(after(dfront, *branch_pieces[1:]), "v"), (dgate, "v")],
        [
            pltpu.VMEM((d, width), bf16),
            pltpu.VMEM((d, width), bf16),
            pltpu.VMEM((total, d), bf16),
            pltpu.SemaphoreType.DMA((wid,)),
            pltpu.SemaphoreType.DMA((wid,)),
        ],
        us=30.0,
    )
    pieces_b = over_wide(same_b, peer_b, dn_parts[0])
    dn_pieces, _ = sum_narrow(dn_parts, pieces_b[0])

    mixed_out = call(
        mixed_kernel,
        [((own, d), bf16, "v")],
        [(tokens, "v")] + [(p, "v") for p in after(tuple(branch_pieces), pieces_b[0])],
        us=2.0,
    )[0]
    gate_sum, grad_w_out = call(
        functools.partial(total_a_kernel, er, ep),
        [((in_rows, width), bf16, "v"), ((MODS, er, d), f32, "v")],
        [(after(blocks_a, mixed_out), "v")],
        us=3.0,
    )
    res = call(
        functools.partial(total_b_kernel, nar, chips, er, rank, taps, ns),
        [((dr, 2 * width), bf16, "v")] * nar
        + [
            ((MODS, er, xw), f32, "v"),
            ((MODS, rank, er), f32, "v"),
            ((MODS, er), f32, "v"),
            ((taps, er), f32, "v"),
            ((1, er), f32, "v"),
            ((ns, er), f32, "v"),
            ((1, er), f32, "v"),
        ],
        [(meta, "s")] + [(p, "v") for p in pieces_b] + [(gate_sum, "v")],
        [pltpu.VMEM((nar, dr, 2 * width), bf16)],
        us=3.0,
    )
    back_parts = res[:nar]
    grad_w_x, grad_w_dt, grad_dt_bias, grad_conv_w, grad_conv_b, grad_log, grad_skip = res[nar:]
    back_pieces = scatter_narrow(back_parts)
    grad_tokens = call(
        tokens_kernel,
        [((own, d), bf16, "v")],
        [(tokens, "v"), (cotangent, "v"), (gain_full, "v")]
        + [(p, "v") for p in after(tuple(dn_pieces), back_parts[0])],
        us=3.0,
    )[0]
    grad_w_in, grad_gain = call(
        functools.partial(w_in_kernel, nar, wid, er, ep),
        [((MODS, dr, 2 * inner), f32, "v"), ((dr, 1), f32, "v")],
        [(meta, "s")]
        + [(p, "v") for p in back_pieces]
        + [(w_in_m, "v"), (gain_col, "v")],
        [pltpu.VMEM((nar, dr, 2 * width), f32)],
        us=4.0,
    )
    grad_w_in, grad_w_out = grad_w_in.transpose(1, 0, 2), grad_w_out.transpose(1, 0, 2)
    grad_w_x, grad_w_dt = grad_w_x.transpose(1, 0, 2), grad_w_dt.transpose(1, 0, 2)
    grad_log = grad_log.T
    return (
        mixed_out,
        grad_tokens,
        grad_gain[:, 0],
        grad_w_in,
        grad_conv_w,
        grad_conv_b[0],
        grad_w_x,
        grad_w_dt,
        grad_dt_bias,
        grad_log,
        grad_skip[0],
        grad_w_out,
    )


def solution(mesh):
    both = ("wide", "narrow")
    return jax.shard_map(
        body,
        mesh=mesh,
        in_specs=(
            P(both, None),
            P(both),
            P(both, None, None),
            P(None, both),
            P(both),
            P(both, None, None),
            P(None, None, both),
            P(None, both),
            P(both, None),
            P(both),
            P(both, None, None),
            P(both),
            P("wide"),
            P(both, None),
        ),
        out_specs=(
            P(both, None),
            P(both, None),
            P(both),
            P(both, None, None),
            P(None, both),
            P(both),
            P(both, None, None),
            P(None, None, both),
            P(None, both),
            P(both, None),
            P(both),
            P(both, None, None),
        ),
        check_vma=False,
    )
```

```python
import functools
import math

import jax
import jax.numpy as jnp
from jax import lax
from jax.experimental import pallas as pl
from jax.experimental.pallas import tpu as pltpu
from jax.sharding import PartitionSpec as P

MODS = 3
RUN = 128
CHUNKS = 4
LANES = 128
EPSILON = 1e-05
LOG2E = 1.4426950408889634
FAR = 1e30
VMEM_LIMIT = 60 * 1024 * 1024
VMEM_SPARE = 6 * 1024 * 1024

f32 = jnp.float32
bf16 = jnp.bfloat16


def swap(block, axis, flip):
    count = lax.axis_size(axis)
    return lax.ppermute(block, axis, [(i, i ^ flip) for i in range(count)])


def gather_narrow(block):
    return [block] + [swap(block, "narrow", s) for s in range(1, lax.axis_size("narrow"))]


def relay_narrow(block, *earlier):
    count = lax.axis_size("narrow")
    pieces = {0: block}
    for s in sorted(range(1, count), key=lambda s: (s.bit_count(), -s)):
        low_bit = s & -s
        if s == low_bit:
            pieces[s] = swap(block, "narrow", s)
        else:
            pieces[s] = swap(after(pieces[s ^ low_bit], *earlier), "narrow", low_bit)
    return [pieces[s] for s in range(count)]


def add_narrow(block, *beside):
    flip = lax.axis_size("narrow") // 2
    while flip:
        got = swap(block, "narrow", flip)
        block = (after(block, *beside).astype(f32) + got.astype(f32)).astype(bf16)
        flip //= 2
        beside = ()
    return block


def scatter_narrow(parts):
    return [parts[0]] + [swap(parts[s], "narrow", s) for s in range(1, len(parts))]


def sum_narrow(parts, *earlier):
    parts = list(parts)
    arrived = [parts[0]]
    for s in range(len(parts) - 1, 0, -1):
        low_bit = s & -s
        got = swap(parts[s], "narrow", low_bit)
        if s == low_bit:
            arrived.append(got)
        else:
            rest = s ^ low_bit
            parts[rest] = (after(parts[rest], *earlier).astype(f32) + got.astype(f32)).astype(bf16)
    return arrived, parts[-2]


def near_wide(block):
    return [block] + [swap(block, "wide", 2 * s) for s in range(1, lax.axis_size("wide") // 2)]


def far_wide(near):
    return [piece for block in near for piece in (block, swap(block, "wide", 1))]


def after(value, *earlier):
    return lax.optimization_barrier((value,) + earlier)[0] if earlier else value


def dot(a, b, ca, cb):
    return lax.dot_general(a, b, (((ca,), (cb,)), ((), ())), preferred_element_type=f32)


def call(kernel, outs, ins, scratch=(), us=1.0, aliases=None):
    spaces = {"v": pltpu.VMEM, "s": pltpu.SMEM, "a": pl.ANY}
    held = [(array.shape, array.dtype) for array, space in ins if space == "v"]
    held += [(shape, dtype) for shape, dtype, space in outs if space == "v"]
    held += [(part.shape, part.dtype) for part in scratch if part.memory_space == pltpu.VMEM]
    need = sum(math.prod(shape) * jnp.dtype(dtype).itemsize for shape, dtype in held)
    need = VMEM_LIMIT
    return pl.pallas_call(
        kernel,
        out_shape=[jax.ShapeDtypeStruct(shape, dtype) for shape, dtype, _ in outs],
        in_specs=[pl.BlockSpec(memory_space=spaces[space]) for _, space in ins],
        out_specs=[pl.BlockSpec(memory_space=spaces[space]) for _, _, space in outs],
        scratch_shapes=list(scratch),
        input_output_aliases=aliases or {},
        compiler_params=pltpu.CompilerParams(vmem_limit_bytes=need),
        cost_estimate=pl.CostEstimate(flops=int(us * 1.1e9), bytes_accessed=1, transcendentals=0),
    )(*[array for array, _ in ins])


def place_pieces(pieces, target, sem, me, rows):
    return [
        pltpu.make_async_copy(
            piece.at[pl.ds(0, rows), pl.ds(0, target.shape[1])],
            target.at[pl.ds(pl.multiple_of((me ^ s) * rows, 16), rows), :],
            sem.at[s],
        )
        for s, piece in enumerate(pieces)
    ]


def place_w_out(pieces, target, sem, me):
    wid, width = len(pieces), pieces[0].shape[1]
    ep, blocks = target.shape[0] // len(pieces), target.shape[1] // pieces[0].shape[1]
    first = pieces[0].shape[0] - blocks * ep
    return [
        pltpu.make_async_copy(
            pieces[s].at[pl.ds(first + k * ep, ep), :],
            target.at[pl.ds(pl.multiple_of((me ^ s) * ep, 16), ep), pl.ds(k * width, width)],
            sem.at[k, s],
        )
        for s in range(wid)
        for k in range(blocks)
    ]


def move_rows(pairs, sem, slot, first, rows):
    at = pl.multiple_of(first, 16)
    return [
        pltpu.make_async_copy(
            pair[0].at[pl.ds(at, rows), :],
            pair[1].at[pl.ds(pl.multiple_of(first + (pair[2] if len(pair) > 2 else 0), 16), rows), :],
            sem.at[k, slot],
        )
        for k, pair in enumerate(pairs)
    ]


def each(first, count, step, carry=0):
    for k in range(count):
        carry = step(first + k, carry)
    return carry


def begin(copies):
    for copy in copies:
        copy.start()


def finish(copies):
    for copy in copies:
        copy.wait()


def split_kernel(
    er, ep, wid, below, meta, w_r, gain_r, out_r, x_r, dt_r, bias_r, conv_r, conv_b_r, skip_r, log_r, *refs
):
    nar = len(refs) - 4
    outs, (small_o, out_o, rows_s, lanes) = refs[:nar], refs[nar:]
    inner = wid * nar * er
    es = wid * ep
    dr = w_r.shape[1]
    gain = gain_r[...].astype(f32)
    gain = jnp.concatenate([gain, jnp.zeros((1, LANES - dr), f32)], axis=1)
    gain = jnp.broadcast_to(gain, (LANES, LANES)).T[:dr].astype(bf16)
    for half in range(2):
        first = half * (MODS * es + LANES)
        for m in range(MODS):
            row = w_r[m, :, half * inner : (half + 1) * inner].astype(f32)
            for k in range(nar):
                parts = []
                for v in range(wid):
                    parts.append(row[:, (v * nar + k) * er : (v * nar + k + 1) * er])
                    if ep > er:
                        parts.append(jnp.zeros((dr, ep - er), f32))
                rows_s[k, :, first + m * es : first + (m + 1) * es] = jnp.concatenate(parts, axis=1).astype(bf16)
    for s in range(nar):
        rows_s[s, :, MODS * es : MODS * es + LANES] = gain
    for s in range(nar):
        outs[s][...] = rows_s[meta[0] ^ s]
    out_whole = jnp.concatenate([out_r[m].astype(f32) for m in range(MODS)], axis=1)
    if ep > er:
        out_whole = jnp.concatenate([out_whole, jnp.zeros((ep - er, out_whole.shape[1]), f32)], axis=0)
    out_w = out_o.shape[1]
    for k in range(out_whole.shape[1] // out_w):
        out_o[k * ep : (k + 1) * ep, :] = out_whole[:, k * out_w : (k + 1) * out_w].astype(bf16)
    rank = dt_r.shape[1]
    lanes[...] = jnp.zeros_like(lanes)
    for m in range(MODS):
        lanes[m * rank : (m + 1) * rank, :er] = dt_r[m].astype(f32)
    base = MODS * rank
    for at, ref in ((T_BIAS, bias_r), (T_CONV_B, conv_b_r), (T_CONV, conv_r), (T_SKIP, skip_r), (T_LOG, log_r)):
        lanes[base + at : base + at + ref.shape[0], :er] = ref[...].astype(f32)
    turned = lanes[...].T[:ep]
    xw = x_r.shape[2]
    columns = []
    for m in range(MODS):
        part = x_r[m].astype(f32)
        if ep > er:
            part = jnp.concatenate([part, jnp.zeros((ep - er, xw), f32)], axis=0)
        columns += [part, jnp.zeros((ep, LANES - xw), f32)]
    small = jnp.concatenate(columns + [turned], axis=1)
    cols = small.shape[1]
    small_o[...] = jnp.zeros_like(small_o)
    for c in range(-(-ep // below)):
        part = small[c * below : min(ep, (c + 1) * below)]
        small_o[: part.shape[0], c * cols : (c + 1) * cols] = part.astype(bf16)


def join_kernel(meta, *refs):
    pieces, (small, out_rows, front_o, gate_o) = refs[:-4], refs[-4:]
    nar, dr = len(pieces), pieces[0].shape[0]
    row = lax.broadcasted_iota(jnp.int32, (nar * dr, dr), 0)
    col = lax.broadcasted_iota(jnp.int32, (nar * dr, dr), 1)
    joined = sum(
        dot((row == (meta[0] ^ s) * dr + col).astype(bf16), piece[...], 1, 0)
        for s, piece in enumerate(pieces)
    ).astype(bf16)
    front_o[: nar * dr, :] = joined[:, : front_o.shape[1]]
    front_o[nar * dr :, :] = small[...]
    gate_o[: nar * dr, :] = joined[:, front_o.shape[1] :]
    gate_o[nar * dr :, :] = out_rows[...]


T_BIAS, T_CONV_B, T_CONV, T_SKIP, T_LOG = 0, 3, 4, 8, 16


def in_kernel(nar, wid, rpd, taps, ep, rank, meta, *refs):
    toks, w_pieces = refs[:nar], refs[nar : nar + wid]
    hbm_os = refs[nar + wid : nar + wid + 4]
    px_o, kinds_o, w_x, w_dt_o, table_o, gain_o = refs[nar + wid + 4 : nar + wid + 10]
    normed_o, front_o, csum_o, mixed_o, xs, wf, rest, tok_sem, w_sem, rest_sem, out_sem = refs[nar + wid + 10 :]
    outs = list(zip((normed_o, front_o, csum_o, mixed_o), hbm_os))
    n, w, split = meta[0], meta[1], meta[2]
    total, es = csum_o.shape
    width = MODS * es
    rows_w = wf.shape[0] // wid
    piece_rows = toks[0].shape[0]
    copies = []
    cols = rest.shape[1]
    below = w_pieces[0].shape[0] - rows_w
    x_cols = w_x.shape[1]
    for s, piece in enumerate(w_pieces):
        for c in range(-(-ep // below)):
            count = min(below, ep - c * below)
            at = pl.multiple_of((w ^ s) * ep + c * below, 16)
            copies.append(
                pltpu.make_async_copy(
                    piece.at[pl.ds(rows_w, count), pl.ds(c * cols, cols)],
                    rest.at[pl.ds(at, count), :],
                    rest_sem.at[c, s],
                )
            )
    tok_copies, w_copies = [], []
    for s, piece in enumerate(toks):
        at = pl.multiple_of((n ^ s) * piece_rows, 16)
        tok_copies.append(
            pltpu.make_async_copy(piece, xs.at[pl.ds(at, piece_rows), :], tok_sem.at[s])
        )
    for s, piece in enumerate(w_pieces):
        at = pl.multiple_of((w ^ s) * rows_w, 16)
        w_copies.append(
            pltpu.make_async_copy(
                piece.at[pl.ds(0, rows_w), pl.ds(0, wf.shape[1])], wf.at[pl.ds(at, rows_w), :], w_sem.at[s]
            )
        )
    for copy in copies + tok_copies + w_copies:
        copy.start()
    for copy in copies:
        copy.wait()
    w_x[...] = rest[:, :x_cols]
    turned = rest[:, x_cols:].astype(f32).T
    w_dt_o[...] = turned[: MODS * rank].astype(bf16)
    table_o[...] = turned[MODS * rank :]
    for copy in tok_copies:
        copy.wait()
    for p in range(nar):
        tail = xs[(p + 1) * piece_rows - 16 : (p + 1) * piece_rows, :LANES].astype(f32)
        row = lax.broadcasted_iota(jnp.int32, tail.shape, 0)
        for j in range(rpd):
            kinds_o[p * rpd + j] = jnp.max(jnp.where(row == j, tail, 0.0)).astype(jnp.int32)
    for copy in w_copies:
        copy.wait()
    gain = wf[:, width : width + LANES].astype(f32).T[0:1, :]
    gain_o[...] = gain

    def one_run(r, before):
        rows = pl.ds(pl.multiple_of(r * RUN, RUN), RUN)
        kind = kinds_o[r]
        x_at = pl.multiple_of((r // rpd) * piece_rows + (r % rpd) * RUN, 16)
        x = xs[pl.ds(x_at, RUN), :].astype(f32)
        scale = lax.rsqrt(jnp.mean(x * x, axis=1, keepdims=True) + EPSILON)
        normed = (x * scale * gain).astype(bf16)
        normed_o[rows, :] = normed
        front = dot(normed, wf[:, pl.ds(pl.multiple_of(kind * es, LANES), es)], 1, 0)
        front_o[rows, :] = front
        ext = jnp.concatenate([before, front], axis=0)
        place = r * RUN + lax.broadcasted_iota(jnp.int32, (RUN, 1), 0)
        offset = place - jnp.where(place >= split, split, 0)
        csum = jnp.broadcast_to(table_o[T_CONV_B : T_CONV_B + 1, :], (RUN, es))
        for lag in range(taps):
            tap = table_o[T_CONV + taps - 1 - lag : T_CONV + taps - lag, :]
            valid = (offset >= lag).astype(f32)
            csum = csum + tap * ext[8 - lag : 8 - lag + RUN, :] * valid
        csum_o[rows, :] = csum
        mixed = (csum * jax.nn.sigmoid(csum)).astype(bf16)
        mixed_o[rows, :] = mixed
        px = dot(mixed, w_x[:, pl.ds(pl.multiple_of(kind * LANES, LANES), LANES)], 1, 0)
        px_o[:, pl.ds(pl.multiple_of(r * RUN, LANES), RUN)] = px.T[: px_o.shape[0]].astype(bf16)
        return front[RUN - 8 :]

    before = jnp.zeros((8, es), f32)
    size = total // CHUNKS
    for c in range(CHUNKS):
        before = each(c * size // RUN, size // RUN, one_run, before)
        begin(move_rows(outs, out_sem, c, c * size, size))
    for c in range(CHUNKS):
        finish(move_rows(outs, out_sem, c, c * size, size))


def gate_kernel(wid, meta, kinds, *refs):
    pieces, (normed_h, act_h, slope_h, normed_r, act_o, slope_o, wg, w_sem, in_sem, out_sem) = refs[:wid], refs[wid:]
    total, es = act_o.shape
    size = total // CHUNKS
    weights = place_pieces(pieces, wg, w_sem, meta[1], wg.shape[0] // wid)
    arriving = [move_rows([(normed_h, normed_r)], in_sem, c, c * size, size) for c in range(CHUNKS)]
    leaving = [
        move_rows([(act_o, act_h), (slope_o, slope_h)], out_sem, c, c * size, size) for c in range(CHUNKS)
    ]
    begin(weights)
    for copies in arriving:
        begin(copies)
    finish(weights)

    def one_run(r, carry):
        rows = pl.ds(pl.multiple_of(r * RUN, RUN), RUN)
        gate = dot(normed_r[rows, :], wg[:, pl.ds(pl.multiple_of(kinds[r] * es, LANES), es)], 1, 0)
        sig = jax.nn.sigmoid(gate)
        act_o[rows, :] = gate * sig
        slope_o[rows, :] = sig * (1.0 + gate * (1.0 - sig))
        return carry

    for c in range(CHUNKS):
        finish(arriving[c])
        each(c * size // RUN, size // RUN, one_run)
        begin(leaving[c])
    for copies in leaving:
        finish(copies)


def cot_kernel(nar, wid, meta, kinds, *refs):
    cots, pieces = refs[:nar], refs[nar : nar + wid]
    act_h, slope_h, cot_h, w_out_h, dssm_h, dgate_h = refs[nar + wid : nar + wid + 6]
    act_r, slope_r, cot_r, w_out, dssm_o, dgate_o = refs[nar + wid + 6 : nar + wid + 12]
    cot_sem, w_sem, in_sem, out_sem, w_out_sem = refs[nar + wid + 12 :]
    total, d = cot_r.shape
    size = total // nar
    weights = place_w_out(pieces, w_out, w_sem, meta[1])
    cot_copies = place_pieces(cots, cot_r, cot_sem, meta[0], size)
    firsts = [(meta[0] ^ s) * size for s in range(nar)]
    arriving = [move_rows([(act_h, act_r), (slope_h, slope_r)], in_sem, s, firsts[s], size) for s in range(nar)]
    leaving = [
        move_rows([(dssm_o, dssm_h), (dgate_o, dgate_h), (cot_r, cot_h)], out_sem, s, firsts[s], size)
        for s in range(nar)
    ]
    w_out_leaving = pltpu.make_async_copy(w_out, w_out_h, w_out_sem)
    begin(weights)
    for s in range(nar):
        begin([cot_copies[s]] + arriving[s])
    finish(weights)
    w_out_leaving.start()

    def one_run(r, carry):
        rows = pl.ds(pl.multiple_of(r * RUN, RUN), RUN)
        d_gated = dot(cot_r[rows, :], w_out[:, pl.ds(pl.multiple_of(kinds[r] * d, LANES), d)], 1, 1)
        dssm_o[rows, :] = d_gated * act_r[rows, :]
        dgate_o[rows, :] = d_gated * slope_r[rows, :]
        return carry

    for s in range(nar):
        finish([cot_copies[s]] + arriving[s])
        first = (meta[0] ^ s) * (size // RUN)
        each(first, size // RUN, one_run)
        begin(leaving[s])
    for copies in leaving:
        finish(copies)
    w_out_leaving.wait()


def softplus(v):
    return jnp.maximum(v, 0.0) + jnp.log1p(jnp.exp(-jnp.abs(v)))


def scan_kernel(rank, meta, kinds, *refs):
    px_r, w_dt, table, mixed_h, dssm_h = refs[:5]
    ssm_h, gmix_h, dpre_h, dpx_o, dlow_o, glog_o, gskip_o = refs[5:12]
    mixed_r, dssm_r, ssm_o, gmix_o, dpre_o, in_sem, ssm_sem, out_sem = refs[12:20]
    pxs, pre_s, step_s, states, bc, qs, gs, fs, dtk, dtu, r1s, r2s, cblk, bblk, adjs = refs[20:]
    split = meta[2]
    total, es = mixed_r.shape
    ns = states.shape[1]
    groups = es // LANES
    runs = total // RUN
    arriving = [
        pltpu.make_async_copy(mixed_h, mixed_r, in_sem.at[0]),
        pltpu.make_async_copy(dssm_h, dssm_r, in_sem.at[1]),
    ]
    begin(arriving)
    lane = [slice(g * LANES, (g + 1) * LANES) for g in range(groups)]
    rates = -jnp.exp(table[T_LOG : T_LOG + ns, :])
    r1s[...] = rates
    r2s[...] = rates * LOG2E
    half = ns // 2
    pxs[...] = px_r[...].astype(f32)
    skip = table[T_SKIP : T_SKIP + 1, :]

    def rows_of(r):
        return pl.ds(pl.multiple_of(r * RUN, RUN), RUN)

    k_row = lax.broadcasted_iota(jnp.int32, (ns, LANES), 1)
    own_row = (k_row % ns == lax.broadcasted_iota(jnp.int32, (ns, LANES), 0)) & (k_row < 2 * ns)
    own_row = own_row.astype(f32)
    k_col = lax.broadcasted_iota(jnp.int32, (LANES, 2 * LANES), 0)
    b_or_c = lax.broadcasted_iota(jnp.int32, (LANES, 2 * LANES), 1) // LANES
    ones = (k_col // ns == b_or_c).astype(bf16)

    tile_k = lax.broadcasted_iota(jnp.int32, (LANES, 16 * ns), 0)
    tile_l = lax.broadcasted_iota(jnp.int32, (LANES, 16 * ns), 1)
    tile_b = (tile_k == tile_l % ns).astype(bf16)
    tile_c = (tile_k == tile_l % ns + ns).astype(bf16)
    tile_t = lax.broadcasted_iota(jnp.int32, (RUN, 16 * ns), 0) % 16
    own_t = (tile_t == lax.broadcasted_iota(jnp.int32, (RUN, 16 * ns), 1) // ns).astype(f32)

    def spread(r):
        block = pxs[rank : rank + 2 * ns, pl.ds(pl.multiple_of(r * RUN, LANES), RUN)]
        parts = jnp.concatenate([block, jnp.zeros((LANES - 2 * ns, RUN), f32)], axis=0)
        picked = parts.T[:, None, :] * own_row[None]
        bc[bc_rows(r), :] = dot(picked.reshape(RUN * ns, LANES).astype(bf16), ones, 1, 0)
        cblk[rows_of(r), :] = (dot(parts.T.astype(bf16), tile_c, 1, 0) * own_t).astype(bf16)
        bblk[rows_of(r), :] = (dot(parts.T.astype(bf16), tile_b, 1, 0) * own_t).astype(bf16)

    def bc_rows(r):
        if bc.shape[0] == RUN * ns:
            return pl.ds(0, RUN * ns)
        return pl.ds(pl.multiple_of(r * (RUN * ns), RUN * ns), RUN * ns)

    arriving[0].wait()
    for r in range(runs):
        rows, lanes_at = slice(r * RUN, (r + 1) * RUN), slice(r * RUN, (r + 1) * RUN)
        low = px_r[:rank, lanes_at]
        dlow_o[:, lanes_at] = low
        weights = w_dt[pl.ds(pl.multiple_of(kinds[r] * rank, 16), rank), :]
        pre = dot(low, weights, 0, 0) + table[pl.ds(T_BIAS + kinds[r], 1), :]
        pre_s[rows, :] = pre
        steps = softplus(pre)
        step_s[rows, :] = steps
        place = r * RUN + lax.broadcasted_iota(jnp.int32, (RUN, 1), 0)
        dtk[rows, :] = jnp.where((place == 0) | (place == split), FAR, steps)
        dtu[rows, :] = steps * mixed_r[rows, :].astype(f32)
        if bc.shape[0] > RUN * ns:
            spread(r)

    def row(tile, j, g):
        return jnp.broadcast_to(tile[j : j + 1, lane[g]], (ns, LANES))

    def folded(ref):
        outs = []
        for g in range(groups):
            out = ref[g, pl.ds(0, RUN, stride=half), :]
            for s in range(1, half):
                out = out + ref[g, pl.ds(s, RUN, stride=half), :]
            outs.append(out)
        return jnp.concatenate(outs, axis=1)

    states[0] = jnp.zeros((ns, es), bf16)

    def forward(r, hs):
        rows = rows_of(r)
        if bc.shape[0] == RUN * ns:
            spread(r)

        def eight(i, hs):
            hs = list(hs)
            at = pl.ds(pl.multiple_of(r * RUN + i * 32, 32), 32)
            k8, u8 = dtk[at, :], dtu[at, :]
            bcv = bc.at[bc_rows(r), :].at[pl.ds(pl.multiple_of(i * (32 * ns), 32 * ns), 32 * ns), :]
            stv = states.at[pl.ds(r * RUN + i * 32 + 1, 32)]
            for j in range(32):
                bt = bcv[j * ns : (j + 1) * ns, :LANES]
                for g in range(groups):
                    decay = jnp.exp2(row(k8, j, g) * r2s[:, lane[g]])
                    hs[g] = decay * hs[g] + row(u8, j, g) * bt
                    stv[j, :, lane[g]] = hs[g].astype(bf16)
            return tuple(hs)

        hs = lax.fori_loop(0, RUN // 32, eight, hs)
        for q in range(RUN // 16):
            at = pl.ds(pl.multiple_of(r * RUN + q * 16, 16), 16)
            block = states[pl.ds(r * RUN + q * 16 + 1, 16)].reshape(16 * ns, es)
            ssm_o[at, :] = dot(cblk[at, :], block, 1, 0) + skip * mixed_r[at, :].astype(f32)
        begin(move_rows([(ssm_o, ssm_h)], ssm_sem, r, r * RUN, RUN))
        return hs

    zero = jnp.zeros((ns, LANES), f32)
    lax.fori_loop(0, runs, forward, (zero,) * groups)
    gskip_o[...] = jnp.zeros_like(gskip_o)
    arriving[1].wait()
    gather_k = lax.broadcasted_iota(jnp.int32, (2 * LANES, LANES), 0) // LANES
    gather_l = lax.broadcasted_iota(jnp.int32, (2 * LANES, LANES), 1) // ns
    gather = (gather_k == gather_l).astype(bf16)
    keep_n = lax.broadcasted_iota(jnp.int32, (ns, LANES), 0)
    keep = (lax.broadcasted_iota(jnp.int32, (ns, LANES), 1) % ns == keep_n).astype(f32)

    def backward(back, carry):
        r = runs - 1 - back
        rows = rows_of(r)
        kind = kinds[r]
        if bc.shape[0] == RUN * ns:
            spread(r)

        def eight(back_i, carry):
            ms, hs, gr = [list(part) for part in carry]
            i = RUN // 32 - 1 - back_i
            at = pl.ds(pl.multiple_of(r * RUN + i * 32, 32), 32)
            k8, u8 = dtk[at, :], dtu[at, :]
            y8 = dssm_r[pl.ds(pl.multiple_of(r * RUN + i * 32, 32), 32), :]
            bcv = bc.at[bc_rows(r), :].at[pl.ds(pl.multiple_of(i * (32 * ns), 32 * ns), 32 * ns), :]
            adv = adjs.at[pl.ds(i * 32, 32)]
            qsv = qs.at[:, pl.ds(pl.multiple_of(i * (32 * half), 32 * half), 32 * half), :]
            stv = states.at[pl.ds(r * RUN + i * 32, 32)]
            gsv = gs.at[pl.ds(pl.multiple_of(i * (32 * ns), 32 * ns), 32 * ns), :]
            for j in reversed(range(32)):
                ct = bcv[j * ns : (j + 1) * ns, LANES:]
                gb_sum, gc_sum = None, None
                for g in range(groups):
                    dt = row(k8, j, g)
                    dy = row(y8, j, g)
                    adjoint = dy * ct + ms[g]
                    before = stv[j, :, lane[g]].astype(f32)
                    c_part = dy * hs[g]
                    b_part = adjoint * row(u8, j, g)
                    gb_sum = b_part if gb_sum is None else gb_sum + b_part
                    gc_sum = c_part if gc_sum is None else gc_sum + c_part
                    fold_at = slice(j * half, (j + 1) * half)
                    adv[j, :, lane[g]] = adjoint.astype(bf16)
                    ms[g] = jnp.exp2(dt * r2s[:, lane[g]]) * adjoint
                    weighted = ms[g] * before
                    by_rate = weighted * r1s[:, lane[g]]
                    qsv[g, fold_at, :] = by_rate[:half] + by_rate[half:]
                    gr[g] = gr[g] + weighted * dt
                    hs[g] = before
                gsv[j * ns : (j + 1) * ns, :LANES] = gb_sum.astype(bf16)
                gsv[j * ns : (j + 1) * ns, LANES:] = gc_sum.astype(bf16)
            return tuple(ms), tuple(hs), tuple(gr)

        carry = lax.fori_loop(0, RUN // 32, eight, carry)
        mixed = mixed_r[rows, :].astype(f32)
        by_rate = folded(qs)
        lb = jnp.concatenate(
            [
                dot(
                    bblk[pl.ds(pl.multiple_of(r * RUN + q * 16, 16), 16), :],
                    adjs[q * 16 : (q + 1) * 16].reshape(16 * ns, es),
                    1,
                    0,
                )
                for q in range(RUN // 16)
            ],
            axis=0,
        )
        dssm = dssm_r[rows, :]
        grad_steps = by_rate + lb * mixed
        gmix_o[rows, :] = dssm * skip + lb * step_s[rows, :]
        gskip_o[...] += jnp.sum(dssm * mixed, axis=0, keepdims=True)
        dpre = (grad_steps * jax.nn.sigmoid(pre_s[rows, :])).astype(bf16)
        dpre_o[rows, :] = dpre
        weights = w_dt[pl.ds(pl.multiple_of(kind * rank, 16), rank), :]
        dlow = dot(weights, dpre, 1, 1)
        sums = dot(gs[...], gather, 1, 0).reshape(RUN, ns, LANES) * keep[None]
        fs[...] = (sums[:, :half] + sums[:, half:]).reshape(RUN * half, LANES)
        dbc = fs[pl.ds(0, RUN, stride=half), :]
        for s in range(1, half):
            dbc = dbc + fs[pl.ds(s, RUN, stride=half), :]
        dbc = dbc.T[: 2 * ns]
        at = pl.ds(pl.multiple_of(r * RUN, LANES), RUN)
        dpx_o[:rank, at] = dlow.astype(bf16)
        dpx_o[rank:, at] = dbc.astype(bf16)
        begin(move_rows([(gmix_o, gmix_h), (dpre_o, dpre_h)], out_sem, r, r * RUN, RUN))
        return carry

    last = tuple(states[total, :, lane[g]].astype(f32) for g in range(groups))
    done = lax.fori_loop(0, runs, backward, ((zero,) * groups, last, (zero,) * groups))
    for g in range(groups):
        glog_o[:, lane[g]] = done[2][g] * rates[:, lane[g]]

    def settle(r, carry):
        finish(move_rows([(ssm_o, ssm_h)], ssm_sem, r, r * RUN, RUN))
        finish(move_rows([(gmix_o, gmix_h), (dpre_o, dpre_h)], out_sem, r, r * RUN, RUN))
        return carry

    lax.fori_loop(0, runs, settle, 0)


def scan_call(rank, xw, ns, meta, kinds, px, w_dt_l, table, mixed, dssm):
    total, es = mixed.shape
    bc_runs = total // RUN if total * ns * 2 * LANES * 4 <= 20 * 1024 * 1024 else 1
    return call(
        functools.partial(scan_kernel, rank),
        [
            ((total, es), f32, "a"),
            ((total, es), f32, "a"),
            ((total, es), bf16, "a"),
            ((xw, total), bf16, "v"),
            ((rank, total), bf16, "v"),
            ((ns, es), f32, "v"),
            ((1, es), f32, "v"),
        ],
        [(meta, "s"), (kinds, "s")]
        + [(px, "v"), (w_dt_l, "v"), (table, "v"), (mixed, "a"), (dssm, "a")],
        [
            pltpu.VMEM((total, es), bf16),
            pltpu.VMEM((total, es), f32),
            pltpu.VMEM((total, es), f32),
            pltpu.VMEM((total, es), f32),
            pltpu.VMEM((total, es), bf16),
            pltpu.SemaphoreType.DMA((2,)),
            pltpu.SemaphoreType.DMA((1, total // RUN)),
            pltpu.SemaphoreType.DMA((2, total // RUN)),
            pltpu.VMEM((xw, total), f32),
            pltpu.VMEM((total, es), f32),
            pltpu.VMEM((total, es), f32),
            pltpu.VMEM((total + 1, ns, es), bf16),
            pltpu.VMEM((bc_runs * RUN * ns, 2 * LANES), f32),
            pltpu.VMEM((es // LANES, RUN * ns // 2, LANES), f32),
            pltpu.VMEM((RUN * ns, 2 * LANES), bf16),
            pltpu.VMEM((RUN * ns // 2, LANES), f32),
            pltpu.VMEM((total, es), f32),
            pltpu.VMEM((total, es), f32),
            pltpu.VMEM((ns, es), f32),
            pltpu.VMEM((ns, es), f32),
            pltpu.VMEM((total, 16 * ns), bf16),
            pltpu.VMEM((total, 16 * ns), bf16),
            pltpu.VMEM((RUN, ns, es), bf16),
        ],
        us=40.0,
    )


def split_rows(acc, place, rows):
    return acc[pl.ds(pl.multiple_of(place * rows, 16), rows), :]


def grads_kernel(wid, ep, rank, meta, kinds, *refs):
    hbm, (dlow_r, glog_r, gskip_r) = refs[:6], refs[6:9]
    dgate_h, blocks_h, table_o = refs[9:12]
    rows_in, (dgate_o, blocks_o, acc_out, acc_in, in_sem, out_sem, block_sem) = refs[12:18], refs[18:]
    ssm_r, gated_r, dgate_r, cot_r, normed_r, dpre_r = rows_in
    total, es = ssm_r.shape
    d = cot_r.shape[1]
    size = total // CHUNKS
    arriving = [move_rows(list(zip(hbm, rows_in)), in_sem, c, c * size, size) for c in range(CHUNKS)]
    leaving = [move_rows([(dgate_o, dgate_h)], out_sem, c, c * size, size) for c in range(CHUNKS)]
    for copies in arriving:
        begin(copies)
    acc_out[...] = jnp.zeros_like(acc_out)
    acc_in[...] = jnp.zeros_like(acc_in)
    table_o[...] = jnp.zeros_like(table_o)
    base = MODS * rank

    def one_run(r, carry):
        rows = pl.ds(pl.multiple_of(r * RUN, RUN), RUN)
        kind = kinds[r]
        wide_at = pl.ds(pl.multiple_of(kind * d, LANES), d)
        es_at = pl.ds(pl.multiple_of(kind * es, LANES), es)
        acc_out[:, wide_at] += dot(gated_r[rows, :], cot_r[rows, :], 0, 0)
        dgate = (dgate_r[rows, :] * ssm_r[rows, :]).astype(bf16)
        dgate_o[rows, :] = dgate
        acc_in[:, es_at] += dot(normed_r[rows, :], dgate, 0, 0)
        dpre = dpre_r[rows, :]
        low = dlow_r[:, pl.ds(pl.multiple_of(r * RUN, LANES), RUN)]
        table_o[pl.ds(pl.multiple_of(kind * rank, 8), rank), :] += dot(low, dpre, 1, 0)
        table_o[pl.ds(base + T_BIAS + kind, 1), :] += jnp.sum(dpre.astype(f32), axis=0, keepdims=True)
        return carry

    for c in range(CHUNKS):
        finish(arriving[c])
        each(c * size // RUN, size // RUN, one_run)
        begin(leaving[c])
    in_rows, width = acc_in.shape[0] // wid, acc_in.shape[1]
    block_copies = [
        pltpu.make_async_copy(blocks_o.at[v], blocks_h.at[v], block_sem.at[v]) for v in range(wid)
    ]
    for v in range(wid):
        blocks_o[v, :in_rows, :] = acc_in[v * in_rows : (v + 1) * in_rows, :].astype(bf16)
        block = acc_out[v * ep : (v + 1) * ep, :].astype(bf16)
        for k in range(block.shape[1] // width):
            first = in_rows + k * ep
            blocks_o[v, first : first + ep, :] = block[:, k * width : (k + 1) * width]
        block_copies[v].start()
    table_o[base + T_SKIP : base + T_SKIP + 1, :] = gskip_r[...]
    table_o[base + T_LOG : base + T_LOG + glog_r.shape[0], :] = glog_r[...]
    for copies in leaving + [block_copies]:
        finish(copies)


def branch_kernel(nar, meta, kinds, ssm_h, act_h, w_out_h, *refs):
    outs, gated_h = refs[:nar], refs[nar]
    ssm_r, act_r, w_out, gated_o, branch, w_sem, in_sem, out_sem, part_sem = refs[nar + 1 :]
    total, d = branch.shape
    size = total // nar
    weights = pltpu.make_async_copy(w_out_h, w_out, w_sem)
    firsts = [(meta[0] ^ s) * size for s in range(nar)]
    arriving = [move_rows([(ssm_h, ssm_r), (act_h, act_r)], in_sem, s, firsts[s], size) for s in range(nar)]
    leaving = [move_rows([(gated_o, gated_h)], out_sem, s, firsts[s], size) for s in range(nar)]
    part_copies = [
        pltpu.make_async_copy(
            branch.at[pl.ds(pl.multiple_of(firsts[s], RUN), size), :], outs[s], part_sem.at[s]
        )
        for s in range(nar)
    ]
    weights.start()
    for s in reversed(range(nar)):
        begin(arriving[s])
    weights.wait()

    def one_run(r, carry):
        rows = pl.ds(pl.multiple_of(r * RUN, RUN), RUN)
        wide_at = pl.ds(pl.multiple_of(kinds[r] * d, LANES), d)
        gated = (ssm_r[rows, :] * act_r[rows, :]).astype(bf16)
        gated_o[rows, :] = gated
        branch[rows, :] = dot(gated, w_out[:, wide_at], 1, 0).astype(bf16)
        return carry

    for s in reversed(range(nar)):
        finish(arriving[s])
        first = (meta[0] ^ s) * (size // RUN)
        each(first, size // RUN, one_run)
        begin(leaving[s] + [part_copies[s]])
    for copies in leaving + [part_copies]:
        finish(copies)


def pair_kernel(chips, meta, same, peer, *outs):
    chip = meta[1] // 2
    for s in range(chips):
        outs[s][...] = (same[chip ^ s].astype(f32) + peer[chip ^ s].astype(f32)).astype(bf16)


def conv_kernel(nar, wid, taps, ep, meta, kinds, *refs):
    dpx_pieces = refs[:nar]
    table, w_x, table_r = refs[nar : nar + 3]
    hbm = refs[nar + 3 : nar + 8]
    dfront_h, same_h, peer_h = refs[nar + 8 : nar + 11]
    rows_in = refs[nar + 11 : nar + 16]
    dfront_o, same_o, peer_o, acc_in, acc_x, small, turned, in_sem, out_sem, block_sem = refs[nar + 16 :]
    gmix_r, csum_r, front_r, mixed_r, normed_r = rows_in
    split = meta[2]
    total, es = gmix_r.shape
    runs = total // RUN
    size = total // CHUNKS
    moves = [(a, b, 16) if b is front_r else (a, b) for a, b in zip(hbm, rows_in)]
    arriving = [move_rows(moves, in_sem, c, c * size, size) for c in range(CHUNKS)]
    leaving = [move_rows([(dfront_o, dfront_h)], out_sem, c, c * size, size) for c in range(CHUNKS)]
    for c in reversed(range(CHUNKS)):
        begin(arriving[c])
    front_r[0:16, :] = jnp.zeros((16, es), f32)
    acc_in[...] = jnp.zeros_like(acc_in)
    acc_x[...] = jnp.zeros_like(acc_x)
    small[...] = jnp.zeros_like(small)
    xw = dpx_pieces[0].shape[0]

    def one_run(back, later):
        r = runs - 1 - back
        rows = pl.ds(pl.multiple_of(r * RUN, RUN), RUN)
        kind = kinds[r]
        lanes_at = pl.ds(pl.multiple_of(r * RUN, LANES), RUN)
        dpx = sum(piece[:, lanes_at].astype(f32) for piece in dpx_pieces)
        dpx = jnp.concatenate([dpx, jnp.zeros((LANES - xw, RUN), f32)], axis=0).T.astype(bf16)
        x_at = pl.ds(pl.multiple_of(kind * LANES, LANES), LANES)
        acc_x[:, x_at] += dot(mixed_r[rows, :], dpx, 0, 0)
        gmix = gmix_r[rows, :] + dot(dpx, w_x[:, x_at], 1, 1)
        csum = csum_r[rows, :]
        sig = jax.nn.sigmoid(csum)
        dc = gmix * sig * (1.0 + csum * (1.0 - sig))
        place = r * RUN + lax.broadcasted_iota(jnp.int32, (RUN + 8, 1), 0)
        offset = place - jnp.where(place >= split, split, 0)
        ext = jnp.concatenate([dc, later], axis=0)
        lagged = front_r[pl.ds(pl.multiple_of(r * RUN + 8, 8), RUN + 8), :]
        d_front = jnp.zeros((RUN, es), f32)
        for lag in range(taps):
            tap = taps - 1 - lag
            masked = ext * (offset >= lag).astype(f32)
            d_front = d_front + table[T_CONV + tap : T_CONV + tap + 1, :] * masked[lag : lag + RUN, :]
            small[T_CONV + tap : T_CONV + tap + 1, :] += jnp.sum(
                masked[:RUN] * lagged[8 - lag : 8 - lag + RUN, :], axis=0, keepdims=True
            )
        small[T_CONV_B : T_CONV_B + 1, :] += jnp.sum(dc, axis=0, keepdims=True)
        d_front = d_front.astype(bf16)
        dfront_o[rows, :] = d_front
        acc_in[:, pl.ds(pl.multiple_of(kind * es, LANES), es)] += dot(normed_r[rows, :], d_front, 0, 0)
        return dc[:8]

    later = jnp.zeros((8, es), f32)
    for c in reversed(range(CHUNKS)):
        if c == CHUNKS - 1:
            finish(arriving[c])
        if c:
            finish(arriving[c - 1])
        back = (CHUNKS - 1 - c) * size // RUN
        later = each(back, size // RUN, one_run, later)
        begin(leaving[c])
    in_rows, width = acc_in.shape[0] // wid, acc_in.shape[1]
    base = table_r.shape[0] - small.shape[0]
    rest = jnp.concatenate([table_r[:base, :], table_r[base:, :] + small[...]], axis=0)
    rest = jnp.concatenate([rest, jnp.zeros((256 - rest.shape[0], es), f32)], axis=0).T
    x_cols = acc_x.shape[1]
    turned[:, :x_cols] = acc_x[...].astype(bf16)
    turned[:, x_cols : x_cols + 256] = rest.astype(bf16)
    turned[:, x_cols + 256 :] = jnp.zeros((es, width - x_cols - 256), bf16)
    core = meta[1] & 1
    block_copies = []
    for k, (ref, out, parity) in enumerate(((peer_o, peer_h, 1 - core), (same_o, same_h, core))):
        for c in range(wid // 2):
            place = 2 * c + parity
            ref[c, :in_rows, :] = split_rows(acc_in, place, in_rows).astype(bf16)
            ref[c, in_rows:, :] = split_rows(turned, place, ep)
            block_copies.append(pltpu.make_async_copy(ref.at[c], out.at[c], block_sem.at[k, c]))
            block_copies[-1].start()
    for copies in leaving + [block_copies]:
        finish(copies)


def normed_kernel(nar, wid, meta, kinds, *refs):
    fronts, gates = refs[:wid], refs[wid : 2 * wid]
    dfront_h, dgate_h = refs[2 * wid : 2 * wid + 2]
    outs = refs[2 * wid + 2 : 2 * wid + 2 + nar]
    dfront_r, dgate_r, wf, wg, dn, f_sem, g_sem, in_sem, part_sem = refs[2 * wid + 2 + nar :]
    total, es = dfront_r.shape
    size = total // nar
    weights = place_pieces(fronts, wf, f_sem, meta[1], wf.shape[0] // wid)
    weights += place_pieces(gates, wg, g_sem, meta[1], wg.shape[0] // wid)
    firsts = [(meta[0] ^ s) * size for s in range(nar)]
    arriving = [
        move_rows([(dfront_h, dfront_r), (dgate_h, dgate_r)], in_sem, s, firsts[s], size) for s in range(nar)
    ]
    part_copies = [
        pltpu.make_async_copy(dn.at[pl.ds(pl.multiple_of(firsts[s], RUN), size), :], outs[s], part_sem.at[s])
        for s in range(nar)
    ]
    begin(weights)
    for s in reversed(range(nar)):
        begin(arriving[s])
    finish(weights)

    def one_run(r, carry):
        rows = pl.ds(pl.multiple_of(r * RUN, RUN), RUN)
        at = pl.ds(pl.multiple_of(kinds[r] * es, LANES), es)
        dn[rows, :] = (dot(dfront_r[rows, :], wf[:, at], 1, 1) + dot(dgate_r[rows, :], wg[:, at], 1, 1)).astype(bf16)
        return carry

    for s in reversed(range(nar)):
        finish(arriving[s])
        first = (meta[0] ^ s) * (size // RUN)
        each(first, size // RUN, one_run)
        part_copies[s].start()
    finish(part_copies)


def total_a_kernel(er, ep, blocks, in_o, out_o):
    d = out_o.shape[2]
    in_rows = in_o.shape[0]
    summed = sum(blocks[v].astype(f32) for v in range(blocks.shape[0]))
    in_o[...] = summed[:in_rows].astype(bf16)
    wide = jnp.concatenate([summed[at : at + ep] for at in range(in_rows, summed.shape[0], ep)], axis=1)
    for m in range(MODS):
        out_o[m] = wide[:er, m * d : (m + 1) * d]


def total_b_kernel(nar, chips, er, rank, taps, ns, meta, *refs):
    pieces, outs = refs[:chips], refs[chips : chips + nar]
    x_o, dt_o, bias_o, conv_o, conv_b_o, log_o, skip_o, rows_s = refs[chips + nar :]
    dr = outs[0].shape[0]
    in_rows = nar * dr
    summed = sum(piece[...].astype(f32) for piece in pieces)
    for k in range(nar):
        rows_s[k] = summed[k * dr : (k + 1) * dr].astype(bf16)
    for s in range(nar):
        outs[s][...] = rows_s[meta[0] ^ s]
    rest = summed[in_rows:]
    x_cols = MODS * LANES
    for m in range(MODS):
        x_o[m] = rest[:er, m * LANES : m * LANES + x_o.shape[2]]
    lanes = rest[:, x_cols : x_cols + 256]
    pad = LANES - lanes.shape[0]
    turned = jnp.concatenate([lanes, jnp.zeros((pad, 256), f32)], axis=0).T[:, :er]
    base = MODS * rank
    for m in range(MODS):
        dt_o[m] = turned[m * rank : (m + 1) * rank]
    bias_o[...] = turned[base + T_BIAS : base + T_BIAS + MODS]
    conv_o[...] = turned[base + T_CONV : base + T_CONV + taps]
    conv_b_o[...] = turned[base + T_CONV_B : base + T_CONV_B + 1]
    skip_o[...] = turned[base + T_SKIP : base + T_SKIP + 1]
    log_o[...] = turned[base + T_LOG : base + T_LOG + ns]


def tokens_kernel(x_r, cot_r, gain_r, *refs):
    pieces, out = refs[:-1], refs[-1]
    x = x_r[...].astype(f32)
    scale = lax.rsqrt(jnp.mean(x * x, axis=1, keepdims=True) + EPSILON)
    q = sum(piece[...].astype(f32) for piece in pieces) * gain_r[...]
    dotted = jnp.mean(q * x, axis=1, keepdims=True)
    out[...] = (cot_r[...].astype(f32) + scale * q - x * (scale * scale * scale) * dotted).astype(bf16)


def mixed_kernel(x_r, *refs):
    pieces, out = refs[:-1], refs[-1]
    out[...] = (x_r[...].astype(f32) + sum(piece[...].astype(f32) for piece in pieces)).astype(bf16)


def in_order(parts, er, ep, wid):
    return jnp.concatenate([part[:, v * ep : v * ep + er] for v in range(wid) for part in parts], axis=1)


def gate_rows_kernel(wid, er, ep, rows_r, w_h, grad_h, sums_o, w_r, grad_s, w_sem, out_sem):
    nar, dr, _ = rows_r.shape
    es, inner = wid * ep, wid * nar * er
    loading = pltpu.make_async_copy(w_h.at[:, :, pl.ds(inner, inner)], w_r, w_sem)
    loading.start()
    sums = 0.0
    for m in range(MODS):
        row = in_order([rows_r[k, :, m * es : (m + 1) * es].astype(f32) for k in range(nar)], er, ep, wid)
        grad_s[m] = row
        if m == 0:
            loading.wait()
        sums = sums + jnp.sum(row * w_r[m].astype(f32), axis=1, keepdims=True)
    storing = pltpu.make_async_copy(grad_s, grad_h.at[:, :, pl.ds(inner, inner)], out_sem)
    storing.start()
    sums_o[...] = jnp.broadcast_to(sums, (dr, LANES))
    storing.wait()


def front_rows_kernel(nar, wid, er, ep, meta, *refs):
    pieces, (w_h, gain_r, sums_r, _, grad_h, gain_o, rows_s, w_r, grad_s, w_sem, out_sem) = refs[:nar], refs[nar:]
    dr = pieces[0].shape[0]
    es, inner = wid * ep, wid * nar * er
    loading = pltpu.make_async_copy(w_h.at[:, :, pl.ds(0, inner)], w_r, w_sem)
    loading.start()
    for s in range(nar):
        rows_s[meta[0] ^ s] = pieces[s][...].astype(f32)
    sums = sums_r[...]
    storing = []
    for m in range(MODS):
        row = in_order([rows_s[k, :, m * es : (m + 1) * es] for k in range(nar)], er, ep, wid)
        grad_s[m] = row
        storing.append(
            pltpu.make_async_copy(grad_s.at[m], grad_h.at[m, :, pl.ds(0, inner)], out_sem.at[m])
        )
        storing[m].start()
        if m == 0:
            loading.wait()
        sums = sums + jnp.sum(row * w_r[m].astype(f32), axis=1, keepdims=True)
    sums = jnp.concatenate([sums, jnp.zeros((LANES - dr, LANES), f32)], axis=0).T[0:1, :dr]
    gain_o[...] = sums / gain_r[...].astype(f32)
    finish(storing)


def body(
    tokens,
    norm_gain,
    w_in,
    conv_w,
    conv_b,
    w_x,
    w_dt,
    dt_bias,
    a_log,
    d_skip,
    w_out,
    mod_ids,
    split_at,
    cotangent,
):
    nar, wid = lax.axis_size("narrow"), lax.axis_size("wide")
    chips = wid // 2
    n, w = lax.axis_index("narrow"), lax.axis_index("wide")
    own, d = tokens.shape
    total = nar * own
    rpd = own // RUN
    rank, xw, ns, taps = w_dt.shape[0], w_x.shape[2], a_log.shape[1], conv_w.shape[0]
    er = w_out.shape[0]
    inner = er * nar * wid
    ep = -(-er // 16) * 16
    es = ep * wid
    dr = w_in.shape[0]
    width = MODS * es
    meta = jnp.stack([n, w, split_at[0]]).astype(jnp.int32)

    front_w = width + LANES
    gain_row = norm_gain[None]
    w_in_m = w_in.transpose(1, 0, 2)
    out_cols, x_cols = MODS * d, MODS * LANES
    table_rows = T_LOG + ns
    small_cols = x_cols + 256
    blocks = front_w // small_cols
    below = -(-(-(-ep // blocks)) // 16) * 16
    res = call(
        functools.partial(split_kernel, er, ep, wid, below),
        [((dr, front_w + width), bf16, "v")] * nar
        + [((below, front_w), bf16, "v"), ((ep * (out_cols // width), width), bf16, "v")],
        [(meta, "s")]
        + [
            (a, "v")
            for a in (
                w_in_m,
                gain_row,
                w_out.transpose(1, 0, 2),
                w_x.transpose(1, 0, 2),
                w_dt.transpose(1, 0, 2),
                dt_bias,
                conv_w,
                conv_b[None],
                d_skip[None],
                a_log.T,
            )
        ],
        [
            pltpu.VMEM((nar, dr, front_w + width), bf16),
            pltpu.VMEM((256, LANES), f32),
        ],
        us=3.0,
    )
    parts, (small, out_rows) = res[:nar], res[nar:]

    parts = scatter_narrow(parts)
    front_rows, gate_rows = call(
        join_kernel,
        [
            ((nar * dr + below, front_w), bf16, "v"),
            ((nar * dr + out_rows.shape[0], width), bf16, "v"),
        ],
        [(meta, "s")] + [(p, "v") for p in parts] + [(small, "v"), (out_rows, "v")],
        us=2.0,
    )
    front_near = near_wide(front_rows)
    front_pieces = far_wide(front_near)
    run_kinds = mod_ids.reshape(rpd, RUN)[:, :1].astype(bf16)
    tail = jnp.pad(jnp.broadcast_to(run_kinds, (rpd, d)), ((0, 16 - rpd), (0, 0)))
    tok_pieces = relay_narrow(jnp.concatenate([tokens, tail], axis=0))
    gate_near = near_wide(after(gate_rows, *front_near[1:]))
    normed, front, csum, mixed, px, kinds, w_x_l, w_dt_l, table, gain_full = call(
        functools.partial(in_kernel, nar, wid, rpd, taps, ep, rank),
        [
            ((total, d), bf16, "a"),
            ((total, es), f32, "a"),
            ((total, es), f32, "a"),
            ((total, es), bf16, "a"),
            ((xw, total), bf16, "v"),
            ((nar * rpd,), jnp.int32, "s"),
            ((es, x_cols), bf16, "v"),
            ((MODS * rank, es), bf16, "v"),
            ((256 - MODS * rank, es), f32, "v"),
            ((1, d), f32, "v"),
        ],
        [(meta, "s")] + [(p, "a") for p in tok_pieces] + [(p, "a") for p in front_pieces],
        [
            pltpu.VMEM((total, d), bf16),
            pltpu.VMEM((total, es), f32),
            pltpu.VMEM((total, es), f32),
            pltpu.VMEM((total, es), bf16),
            pltpu.VMEM((nar * (own + 16), d), bf16),
            pltpu.VMEM((d, front_w), bf16),
            pltpu.VMEM((es, small_cols), bf16),
            pltpu.SemaphoreType.DMA((nar,)),
            pltpu.SemaphoreType.DMA((wid,)),
            pltpu.SemaphoreType.DMA((-(-ep // below), wid)),
            pltpu.SemaphoreType.DMA((4, CHUNKS)),
        ],
        us=9.0,
    )
    cot_pieces = relay_narrow(after(cotangent, *tok_pieces[1:]), px)
    gate_pieces = far_wide([after(piece, px) for piece in gate_near])
    act, slope = call(
        functools.partial(gate_kernel, wid),
        [((total, es), f32, "a")] * 2,
        [(meta, "s"), (kinds, "s")]
        + [(p, "a") for p in gate_pieces]
        + [(after(normed, *cot_pieces[1:3]), "a")],
        [
            pltpu.VMEM((total, d), bf16),
            pltpu.VMEM((total, es), f32),
            pltpu.VMEM((total, es), f32),
            pltpu.VMEM((d, width), bf16),
            pltpu.SemaphoreType.DMA((wid,)),
            pltpu.SemaphoreType.DMA((1, CHUNKS)),
            pltpu.SemaphoreType.DMA((2, CHUNKS)),
        ],
        us=0.1,
    )
    px_total = add_narrow(px, act, cot_pieces[-1])
    cot, w_out_l, dssm, dgate_f = call(
        functools.partial(cot_kernel, nar, wid),
        [((total, d), bf16, "a"), ((es, out_cols), bf16, "a")] + [((total, es), f32, "a")] * 2,
        [(meta, "s"), (kinds, "s")]
        + [(p, "a") for p in cot_pieces]
        + [(p, "a") for p in gate_pieces]
        + [(act, "a"), (slope, "a")],
        [
            pltpu.VMEM((total, es), f32),
            pltpu.VMEM((total, es), f32),
            pltpu.VMEM((total, d), bf16),
            pltpu.VMEM((es, out_cols), bf16),
            pltpu.VMEM((total, es), f32),
            pltpu.VMEM((total, es), f32),
            pltpu.SemaphoreType.DMA((nar,)),
            pltpu.SemaphoreType.DMA((out_cols // width, wid)),
            pltpu.SemaphoreType.DMA((2, nar)),
            pltpu.SemaphoreType.DMA((3, nar)),
            pltpu.SemaphoreType.DMA(()),
        ],
        us=7.0,
    )
    ssm, gmix, dpre, dpx, dlow, glog, gskip = scan_call(
        rank, xw, ns, meta, kinds, px_total, w_dt_l, table, mixed, dssm
    )
    dpx_pieces = gather_narrow(dpx)
    res = call(
        functools.partial(branch_kernel, nar),
        [((own, d), bf16, "a")] * nar + [((total, es), bf16, "a")],
        [(meta, "s"), (kinds, "s"), (ssm, "a"), (act, "a"), (w_out_l, "a")],
        [
            pltpu.VMEM((total, es), f32),
            pltpu.VMEM((total, es), f32),
            pltpu.VMEM((es, out_cols), bf16),
            pltpu.VMEM((total, es), bf16),
            pltpu.VMEM((total, d), bf16),
            pltpu.SemaphoreType.DMA(()),
            pltpu.SemaphoreType.DMA((2, nar)),
            pltpu.SemaphoreType.DMA((1, nar)),
            pltpu.SemaphoreType.DMA((nar,)),
        ],
        us=5.0,
    )
    branch_parts, gated = res[:nar], res[nar]
    branch_pieces = scatter_narrow(branch_parts)
    in_rows = d // wid
    rows_a = in_rows + ep * (out_cols // width)
    dgate, blocks_a, table_g = call(
        functools.partial(grads_kernel, wid, ep, rank),
        [
            ((total, es), bf16, "a"),
            ((wid, rows_a, width), bf16, "a"),
            ((MODS * rank + table_rows, es), f32, "v"),
        ],
        [(meta, "s"), (kinds, "s")]
        + [(a, "a") for a in (ssm, gated, dgate_f, cot, normed, dpre)]
        + [(a, "v") for a in (dlow, glog, gskip)],
        [
            pltpu.VMEM((total, es), f32),
            pltpu.VMEM((total, es), bf16),
            pltpu.VMEM((total, es), f32),
            pltpu.VMEM((total, d), bf16),
            pltpu.VMEM((total, d), bf16),
            pltpu.VMEM((total, es), bf16),
            pltpu.VMEM((total, es), bf16),
            pltpu.VMEM((wid, rows_a, width), bf16),
            pltpu.VMEM((es, out_cols), f32),
            pltpu.VMEM((d, width), f32),
            pltpu.SemaphoreType.DMA((6, CHUNKS)),
            pltpu.SemaphoreType.DMA((1, CHUNKS)),
            pltpu.SemaphoreType.DMA((wid,)),
        ],
        us=9.0,
    )

    def over_wide(same, peer, *earlier):
        peer = swap(peer, "wide", 1)
        same = after(same, *earlier) if earlier else same
        parts = call(
            functools.partial(pair_kernel, chips),
            [(same.shape[1:], bf16, "v")] * chips,
            [(meta, "s"), (same, "v"), (peer, "v")],
            us=3.0,
        )
        return [parts[0]] + [swap(parts[s], "wide", 2 * s) for s in range(1, chips)]

    blocks_a = lax.all_to_all(blocks_a, "wide", 0, 0)
    rows_b = in_rows + ep
    dfront, same_b, peer_b = call(
        functools.partial(conv_kernel, nar, wid, taps, ep),
        [((total, es), bf16, "a")] + [((chips, rows_b, width), bf16, "a")] * 2,
        [(meta, "s"), (kinds, "s")]
        + [(p, "v") for p in dpx_pieces]
        + [(a, "v") for a in (table, w_x_l, table_g)]
        + [(a, "a") for a in (gmix, csum, front, mixed, normed)],
        [
            pltpu.VMEM((total, es), f32),
            pltpu.VMEM((total, es), f32),
            pltpu.VMEM((total + 16, es), f32),
            pltpu.VMEM((total, es), bf16),
            pltpu.VMEM((total, d), bf16),
            pltpu.VMEM((total, es), bf16),
            pltpu.VMEM((chips, rows_b, width), bf16),
            pltpu.VMEM((chips, rows_b, width), bf16),
            pltpu.VMEM((d, width), f32),
            pltpu.VMEM((es, x_cols), f32),
            pltpu.VMEM((table_rows, es), f32),
            pltpu.VMEM((es, width), bf16),
            pltpu.SemaphoreType.DMA((5, CHUNKS)),
            pltpu.SemaphoreType.DMA((1, CHUNKS)),
            pltpu.SemaphoreType.DMA((2, chips)),
        ],
        us=12.0,
    )
    dn_parts = call(
        functools.partial(normed_kernel, nar, wid),
        [((own, d), bf16, "a")] * nar,
        [(meta, "s"), (kinds, "s")]
        + [(p, "a") for p in front_pieces]
        + [(p, "a") for p in gate_pieces]
        + [(dfront, "a"), (dgate, "a")],
        [
            pltpu.VMEM((total, es), bf16),
            pltpu.VMEM((total, es), bf16),
            pltpu.VMEM((d, width), bf16),
            pltpu.VMEM((d, width), bf16),
            pltpu.VMEM((total, d), bf16),
            pltpu.SemaphoreType.DMA((wid,)),
            pltpu.SemaphoreType.DMA((wid,)),
            pltpu.SemaphoreType.DMA((2, nar)),
            pltpu.SemaphoreType.DMA((nar,)),
        ],
        us=30.0,
    )
    pieces_b = over_wide(same_b, peer_b, dn_parts[0])
    dn_pieces, _ = sum_narrow(dn_parts, pieces_b[0])

    mixed_out = call(
        mixed_kernel,
        [((own, d), bf16, "v")],
        [(tokens, "v")] + [(p, "v") for p in after(tuple(branch_pieces), pieces_b[0])],
        us=2.0,
    )[0]
    gate_sum, grad_w_out = call(
        functools.partial(total_a_kernel, er, ep),
        [((in_rows, width), bf16, "v"), ((MODS, er, d), f32, "v")],
        [(after(blocks_a, mixed_out), "v")],
        us=3.0,
    )
    gate_back = lax.all_to_all(gate_sum.reshape(nar, dr, width), "narrow", 0, 0)
    res = call(
        functools.partial(total_b_kernel, nar, chips, er, rank, taps, ns),
        [((dr, width), bf16, "v")] * nar
        + [
            ((MODS, er, xw), f32, "v"),
            ((MODS, rank, er), f32, "v"),
            ((MODS, er), f32, "v"),
            ((taps, er), f32, "v"),
            ((1, er), f32, "v"),
            ((ns, er), f32, "v"),
            ((1, er), f32, "v"),
        ],
        [(meta, "s")] + [(p, "v") for p in after(tuple(pieces_b), gate_sum)],
        [pltpu.VMEM((nar, dr, width), bf16)],
        us=3.0,
    )
    back_parts = res[:nar]
    grad_w_x, grad_w_dt, grad_dt_bias, grad_conv_w, grad_conv_b, grad_log, grad_skip = res[nar:]
    back_pieces = scatter_narrow(back_parts)
    grad_tokens = call(
        tokens_kernel,
        [((own, d), bf16, "v")],
        [(tokens, "v"), (cotangent, "v"), (gain_full, "v")]
        + [(p, "v") for p in after(tuple(dn_pieces), back_parts[0])],
        us=3.0,
    )[0]
    half_scratch = [
        pltpu.VMEM((MODS, dr, inner), bf16),
        pltpu.VMEM((MODS, dr, inner), f32),
        pltpu.SemaphoreType.DMA(()),
    ]
    grad_w_in, gate_sums = call(
        functools.partial(gate_rows_kernel, wid, er, ep),
        [((MODS, dr, 2 * inner), f32, "a"), ((dr, LANES), f32, "v")],
        [(after(gate_back, grad_tokens), "v"), (w_in_m, "a")],
        half_scratch + [pltpu.SemaphoreType.DMA(())],
        us=3.0,
    )
    grad_w_in, grad_gain = call(
        functools.partial(front_rows_kernel, nar, wid, er, ep),
        [((MODS, dr, 2 * inner), f32, "a"), ((1, dr), f32, "v")],
        [(meta, "s")]
        + [(p, "v") for p in back_pieces]
        + [(w_in_m, "a"), (gain_row, "v"), (gate_sums, "v"), (grad_w_in, "a")],
        [pltpu.VMEM((nar, dr, width), f32)] + half_scratch + [pltpu.SemaphoreType.DMA((MODS,))],
        us=3.0,
        aliases={nar + 4: 0},
    )
    grad_w_in, grad_w_out = grad_w_in.transpose(1, 0, 2), grad_w_out.transpose(1, 0, 2)
    grad_w_x, grad_w_dt = grad_w_x.transpose(1, 0, 2), grad_w_dt.transpose(1, 0, 2)
    grad_log = grad_log.T
    return (
        mixed_out,
        grad_tokens,
        grad_gain[0],
        grad_w_in,
        grad_conv_w,
        grad_conv_b[0],
        grad_w_x,
        grad_w_dt,
        grad_dt_bias,
        grad_log,
        grad_skip[0],
        grad_w_out,
    )


def solution(mesh):
    both = ("wide", "narrow")
    return jax.shard_map(
        body,
        mesh=mesh,
        in_specs=(
            P(both, None),
            P(both),
            P(both, None, None),
            P(None, both),
            P(both),
            P(both, None, None),
            P(None, None, both),
            P(None, both),
            P(both, None),
            P(both),
            P(both, None, None),
            P(both),
            P("wide"),
            P(both, None),
        ),
        out_specs=(
            P(both, None),
            P(both, None),
            P(both),
            P(both, None, None),
            P(None, both),
            P(both),
            P(both, None, None),
            P(None, None, both),
            P(None, both),
            P(both, None),
            P(both),
            P(both, None, None),
        ),
        check_vma=False,
    )
```

```python
import functools
import math

import jax
import jax.numpy as jnp
from jax import lax
from jax.experimental import pallas as pl
from jax.experimental.pallas import tpu as pltpu
from jax.sharding import PartitionSpec as P

MODS = 3
RUN = 128
CHUNKS = 4
LANES = 128
EPSILON = 1e-05
LOG2E = 1.4426950408889634
FAR = 1e30
VMEM_LIMIT = 60 * 1024 * 1024
VMEM_SPARE = 6 * 1024 * 1024

f32 = jnp.float32
bf16 = jnp.bfloat16


def swap(block, axis, flip):
    count = lax.axis_size(axis)
    return lax.ppermute(block, axis, [(i, i ^ flip) for i in range(count)])


def gather_narrow(block):
    return [block] + [swap(block, "narrow", s) for s in range(1, lax.axis_size("narrow"))]


def relay_narrow(block, *earlier):
    count = lax.axis_size("narrow")
    pieces = {0: block}
    for s in sorted(range(1, count), key=lambda s: (s.bit_count(), -s)):
        low_bit = s & -s
        if s == low_bit:
            pieces[s] = swap(block, "narrow", s)
        else:
            pieces[s] = swap(after(pieces[s ^ low_bit], *earlier), "narrow", low_bit)
    return [pieces[s] for s in range(count)]


def add_narrow(block, *beside):
    flip = lax.axis_size("narrow") // 2
    while flip:
        got = swap(block, "narrow", flip)
        block = (after(block, *beside).astype(f32) + got.astype(f32)).astype(bf16)
        flip //= 2
        beside = ()
    return block


def scatter_narrow(parts):
    return [parts[0]] + [swap(parts[s], "narrow", s) for s in range(1, len(parts))]


def sum_narrow(parts, *earlier):
    parts = list(parts)
    arrived = [parts[0]]
    for s in range(len(parts) - 1, 0, -1):
        low_bit = s & -s
        got = swap(parts[s], "narrow", low_bit)
        if s == low_bit:
            arrived.append(got)
        else:
            rest = s ^ low_bit
            parts[rest] = (after(parts[rest], *earlier).astype(f32) + got.astype(f32)).astype(bf16)
    return arrived, parts[-2]


def near_wide(block):
    return [block] + [swap(block, "wide", 2 * s) for s in range(1, lax.axis_size("wide") // 2)]


def far_wide(near):
    return [piece for block in near for piece in (block, swap(block, "wide", 1))]


def after(value, *earlier):
    return lax.optimization_barrier((value,) + earlier)[0] if earlier else value


def dot(a, b, ca, cb):
    return lax.dot_general(a, b, (((ca,), (cb,)), ((), ())), preferred_element_type=f32)


def call(kernel, outs, ins, scratch=(), us=1.0):
    spaces = {"v": pltpu.VMEM, "s": pltpu.SMEM, "a": pl.ANY}
    held = [(array.shape, array.dtype) for array, space in ins if space == "v"]
    held += [(shape, dtype) for shape, dtype, space in outs if space == "v"]
    held += [(part.shape, part.dtype) for part in scratch if part.memory_space == pltpu.VMEM]
    need = sum(math.prod(shape) * jnp.dtype(dtype).itemsize for shape, dtype in held)
    need = VMEM_LIMIT
    return pl.pallas_call(
        kernel,
        out_shape=[jax.ShapeDtypeStruct(shape, dtype) for shape, dtype, _ in outs],
        in_specs=[pl.BlockSpec(memory_space=spaces[space]) for _, space in ins],
        out_specs=[pl.BlockSpec(memory_space=spaces[space]) for _, _, space in outs],
        scratch_shapes=list(scratch),
        compiler_params=pltpu.CompilerParams(vmem_limit_bytes=need),
        cost_estimate=pl.CostEstimate(flops=int(us * 1.1e9), bytes_accessed=1, transcendentals=0),
    )(*[array for array, _ in ins])


def place_pieces(pieces, target, sem, me, rows):
    return [
        pltpu.make_async_copy(
            piece.at[pl.ds(0, rows), pl.ds(0, target.shape[1])],
            target.at[pl.ds(pl.multiple_of((me ^ s) * rows, 16), rows), :],
            sem.at[s],
        )
        for s, piece in enumerate(pieces)
    ]


def place_w_out(pieces, target, sem, me):
    wid, width = len(pieces), pieces[0].shape[1]
    ep, blocks = target.shape[0] // len(pieces), target.shape[1] // pieces[0].shape[1]
    first = pieces[0].shape[0] - blocks * ep
    return [
        pltpu.make_async_copy(
            pieces[s].at[pl.ds(first + k * ep, ep), :],
            target.at[pl.ds(pl.multiple_of((me ^ s) * ep, 16), ep), pl.ds(k * width, width)],
            sem.at[k, s],
        )
        for s in range(wid)
        for k in range(blocks)
    ]


def move_rows(pairs, sem, slot, first, rows):
    at = pl.multiple_of(first, 16)
    return [
        pltpu.make_async_copy(
            pair[0].at[pl.ds(at, rows), :],
            pair[1].at[pl.ds(pl.multiple_of(first + (pair[2] if len(pair) > 2 else 0), 16), rows), :],
            sem.at[k, slot],
        )
        for k, pair in enumerate(pairs)
    ]


def each(first, count, step, carry=0):
    for k in range(count):
        carry = step(first + k, carry)
    return carry


def begin(copies):
    for copy in copies:
        copy.start()


def finish(copies):
    for copy in copies:
        copy.wait()


def split_kernel(
    er, ep, wid, below, meta, w_r, gain_r, out_r, x_r, dt_r, bias_r, conv_r, conv_b_r, skip_r, log_r, *refs
):
    nar = len(refs) - 4
    outs, (small_o, out_o, rows_s, lanes) = refs[:nar], refs[nar:]
    inner = wid * nar * er
    es = wid * ep
    dr = w_r.shape[1]
    gain = gain_r[...].astype(f32)
    gain = jnp.concatenate([gain, jnp.zeros((1, LANES - dr), f32)], axis=1)
    gain = jnp.broadcast_to(gain, (LANES, LANES)).T[:dr].astype(bf16)
    for half in range(2):
        first = half * (MODS * es + LANES)
        for m in range(MODS):
            row = w_r[m, :, half * inner : (half + 1) * inner].astype(f32)
            for k in range(nar):
                parts = []
                for v in range(wid):
                    parts.append(row[:, (v * nar + k) * er : (v * nar + k + 1) * er])
                    if ep > er:
                        parts.append(jnp.zeros((dr, ep - er), f32))
                rows_s[k, :, first + m * es : first + (m + 1) * es] = jnp.concatenate(parts, axis=1).astype(bf16)
    for s in range(nar):
        rows_s[s, :, MODS * es : MODS * es + LANES] = gain
    for s in range(nar):
        outs[s][...] = rows_s[meta[0] ^ s]
    out_whole = jnp.concatenate([out_r[m].astype(f32) for m in range(MODS)], axis=1)
    if ep > er:
        out_whole = jnp.concatenate([out_whole, jnp.zeros((ep - er, out_whole.shape[1]), f32)], axis=0)
    out_w = out_o.shape[1]
    for k in range(out_whole.shape[1] // out_w):
        out_o[k * ep : (k + 1) * ep, :] = out_whole[:, k * out_w : (k + 1) * out_w].astype(bf16)
    rank = dt_r.shape[1]
    lanes[...] = jnp.zeros_like(lanes)
    for m in range(MODS):
        lanes[m * rank : (m + 1) * rank, :er] = dt_r[m].astype(f32)
    base = MODS * rank
    for at, ref in ((T_BIAS, bias_r), (T_CONV_B, conv_b_r), (T_CONV, conv_r), (T_SKIP, skip_r), (T_LOG, log_r)):
        lanes[base + at : base + at + ref.shape[0], :er] = ref[...].astype(f32)
    turned = lanes[...].T[:ep]
    xw = x_r.shape[2]
    columns = []
    for m in range(MODS):
        part = x_r[m].astype(f32)
        if ep > er:
            part = jnp.concatenate([part, jnp.zeros((ep - er, xw), f32)], axis=0)
        columns += [part, jnp.zeros((ep, LANES - xw), f32)]
    small = jnp.concatenate(columns + [turned], axis=1)
    cols = small.shape[1]
    small_o[...] = jnp.zeros_like(small_o)
    for c in range(-(-ep // below)):
        part = small[c * below : min(ep, (c + 1) * below)]
        small_o[: part.shape[0], c * cols : (c + 1) * cols] = part.astype(bf16)


def join_kernel(meta, *refs):
    pieces, (small, out_rows, front_o, gate_o) = refs[:-4], refs[-4:]
    nar, dr = len(pieces), pieces[0].shape[0]
    row = lax.broadcasted_iota(jnp.int32, (nar * dr, dr), 0)
    col = lax.broadcasted_iota(jnp.int32, (nar * dr, dr), 1)
    joined = sum(
        dot((row == (meta[0] ^ s) * dr + col).astype(bf16), piece[...], 1, 0)
        for s, piece in enumerate(pieces)
    ).astype(bf16)
    front_o[: nar * dr, :] = joined[:, : front_o.shape[1]]
    front_o[nar * dr :, :] = small[...]
    gate_o[: nar * dr, :] = joined[:, front_o.shape[1] :]
    gate_o[nar * dr :, :] = out_rows[...]


T_BIAS, T_CONV_B, T_CONV, T_SKIP, T_LOG = 0, 3, 4, 8, 16


def in_kernel(nar, wid, rpd, taps, ep, rank, meta, *refs):
    toks, w_pieces = refs[:nar], refs[nar : nar + wid]
    hbm_os = refs[nar + wid : nar + wid + 4]
    px_o, kinds_o, w_x, w_dt_o, table_o, gain_o = refs[nar + wid + 4 : nar + wid + 10]
    normed_o, front_o, csum_o, mixed_o, xs, wf, rest, tok_sem, w_sem, rest_sem, out_sem = refs[nar + wid + 10 :]
    outs = list(zip((normed_o, front_o, csum_o, mixed_o), hbm_os))
    n, w, split = meta[0], meta[1], meta[2]
    total, es = csum_o.shape
    width = MODS * es
    rows_w = wf.shape[0] // wid
    piece_rows = toks[0].shape[0]
    copies = []
    cols = rest.shape[1]
    below = w_pieces[0].shape[0] - rows_w
    x_cols = w_x.shape[1]
    for s, piece in enumerate(w_pieces):
        for c in range(-(-ep // below)):
            count = min(below, ep - c * below)
            at = pl.multiple_of((w ^ s) * ep + c * below, 16)
            copies.append(
                pltpu.make_async_copy(
                    piece.at[pl.ds(rows_w, count), pl.ds(c * cols, cols)],
                    rest.at[pl.ds(at, count), :],
                    rest_sem.at[c, s],
                )
            )
    tok_copies, w_copies = [], []
    for s, piece in enumerate(toks):
        at = pl.multiple_of((n ^ s) * piece_rows, 16)
        tok_copies.append(
            pltpu.make_async_copy(piece, xs.at[pl.ds(at, piece_rows), :], tok_sem.at[s])
        )
    for s, piece in enumerate(w_pieces):
        at = pl.multiple_of((w ^ s) * rows_w, 16)
        w_copies.append(
            pltpu.make_async_copy(
                piece.at[pl.ds(0, rows_w), pl.ds(0, wf.shape[1])], wf.at[pl.ds(at, rows_w), :], w_sem.at[s]
            )
        )
    for copy in copies + tok_copies + w_copies:
        copy.start()
    for copy in copies:
        copy.wait()
    w_x[...] = rest[:, :x_cols]
    turned = rest[:, x_cols:].astype(f32).T
    w_dt_o[...] = turned[: MODS * rank].astype(bf16)
    table_o[...] = turned[MODS * rank :]
    for copy in tok_copies:
        copy.wait()
    for p in range(nar):
        tail = xs[(p + 1) * piece_rows - 16 : (p + 1) * piece_rows, :LANES].astype(f32)
        row = lax.broadcasted_iota(jnp.int32, tail.shape, 0)
        for j in range(rpd):
            kinds_o[p * rpd + j] = jnp.max(jnp.where(row == j, tail, 0.0)).astype(jnp.int32)
    for copy in w_copies:
        copy.wait()
    gain = wf[:, width : width + LANES].astype(f32).T[0:1, :]
    gain_o[...] = gain

    def one_run(r, before):
        rows = pl.ds(pl.multiple_of(r * RUN, RUN), RUN)
        kind = kinds_o[r]
        x_at = pl.multiple_of((r // rpd) * piece_rows + (r % rpd) * RUN, 16)
        x = xs[pl.ds(x_at, RUN), :].astype(f32)
        scale = lax.rsqrt(jnp.mean(x * x, axis=1, keepdims=True) + EPSILON)
        normed = (x * scale * gain).astype(bf16)
        normed_o[rows, :] = normed
        front = dot(normed, wf[:, pl.ds(pl.multiple_of(kind * es, LANES), es)], 1, 0)
        front_o[rows, :] = front
        ext = jnp.concatenate([before, front], axis=0)
        place = r * RUN + lax.broadcasted_iota(jnp.int32, (RUN, 1), 0)
        offset = place - jnp.where(place >= split, split, 0)
        csum = jnp.broadcast_to(table_o[T_CONV_B : T_CONV_B + 1, :], (RUN, es))
        for lag in range(taps):
            tap = table_o[T_CONV + taps - 1 - lag : T_CONV + taps - lag, :]
            valid = (offset >= lag).astype(f32)
            csum = csum + tap * ext[8 - lag : 8 - lag + RUN, :] * valid
        csum_o[rows, :] = csum
        mixed = (csum * jax.nn.sigmoid(csum)).astype(bf16)
        mixed_o[rows, :] = mixed
        px = dot(mixed, w_x[:, pl.ds(pl.multiple_of(kind * LANES, LANES), LANES)], 1, 0)
        px_o[:, pl.ds(pl.multiple_of(r * RUN, LANES), RUN)] = px.T[: px_o.shape[0]].astype(bf16)
        return front[RUN - 8 :]

    before = jnp.zeros((8, es), f32)
    size = total // CHUNKS
    for c in range(CHUNKS):
        before = each(c * size // RUN, size // RUN, one_run, before)
        begin(move_rows(outs, out_sem, c, c * size, size))
    for c in range(CHUNKS):
        finish(move_rows(outs, out_sem, c, c * size, size))


def gate_kernel(wid, meta, kinds, *refs):
    pieces, (normed_h, act_h, slope_h, normed_r, act_o, slope_o, wg, w_sem, in_sem, out_sem) = refs[:wid], refs[wid:]
    total, es = act_o.shape
    size = total // CHUNKS
    weights = place_pieces(pieces, wg, w_sem, meta[1], wg.shape[0] // wid)
    arriving = [move_rows([(normed_h, normed_r)], in_sem, c, c * size, size) for c in range(CHUNKS)]
    leaving = [
        move_rows([(act_o, act_h), (slope_o, slope_h)], out_sem, c, c * size, size) for c in range(CHUNKS)
    ]
    begin(weights)
    for copies in arriving:
        begin(copies)
    finish(weights)

    def one_run(r, carry):
        rows = pl.ds(pl.multiple_of(r * RUN, RUN), RUN)
        gate = dot(normed_r[rows, :], wg[:, pl.ds(pl.multiple_of(kinds[r] * es, LANES), es)], 1, 0)
        sig = jax.nn.sigmoid(gate)
        act_o[rows, :] = gate * sig
        slope_o[rows, :] = sig * (1.0 + gate * (1.0 - sig))
        return carry

    for c in range(CHUNKS):
        finish(arriving[c])
        each(c * size // RUN, size // RUN, one_run)
        begin(leaving[c])
    for copies in leaving:
        finish(copies)


def softplus(v):
    return jnp.maximum(v, 0.0) + jnp.log1p(jnp.exp(-jnp.abs(v)))


def scan_kernel(nar, wid, rank, meta, kinds, *refs):
    cots, pieces, refs = refs[:nar], refs[nar : nar + wid], refs[nar + wid :]
    px_r, w_dt, table, mixed_h, act_h = refs[:5]
    parts_h, refs = refs[5 : 5 + nar], refs[5 + nar :]
    gated_h, dgs_h, cot_h, gmix_h, dpre_h, dpx_o, dlow_o, glog_o, gskip_o = refs[:9]
    mixed_r, act_r, cot_r, w_out, dssm_r, ssm_o, gated_o, dgs_o, branch, gmix_o, dpre_o = refs[9:20]
    in_sem, cot_sem, w_sem, mid_sem, part_sem, out_sem = refs[20:26]
    pxs, pre_s, step_s, states, bc, qs, gs, fs, dtk, dtu, r1s, r2s, cblk, bblk, adjs = refs[26:]
    split = meta[2]
    total, es = mixed_r.shape
    ns = states.shape[1]
    groups = es // LANES
    runs = total // RUN
    d, size = cot_r.shape[1], total // nar
    mixed_in = pltpu.make_async_copy(mixed_h, mixed_r, in_sem.at[0])
    arriving = place_w_out(pieces, w_out, w_sem, meta[1]) + place_pieces(cots, cot_r, cot_sem, meta[0], size)
    arriving.append(pltpu.make_async_copy(act_h, act_r, in_sem.at[1]))
    begin([mixed_in] + arriving)
    lane = [slice(g * LANES, (g + 1) * LANES) for g in range(groups)]
    rates = -jnp.exp(table[T_LOG : T_LOG + ns, :])
    r1s[...] = rates
    r2s[...] = rates * LOG2E
    half = ns // 2
    pxs[...] = px_r[...].astype(f32)
    skip = table[T_SKIP : T_SKIP + 1, :]

    def rows_of(r):
        return pl.ds(pl.multiple_of(r * RUN, RUN), RUN)

    k_row = lax.broadcasted_iota(jnp.int32, (ns, LANES), 1)
    own_row = (k_row % ns == lax.broadcasted_iota(jnp.int32, (ns, LANES), 0)) & (k_row < 2 * ns)
    own_row = own_row.astype(f32)
    k_col = lax.broadcasted_iota(jnp.int32, (LANES, 2 * LANES), 0)
    b_or_c = lax.broadcasted_iota(jnp.int32, (LANES, 2 * LANES), 1) // LANES
    ones = (k_col // ns == b_or_c).astype(bf16)

    tile_k = lax.broadcasted_iota(jnp.int32, (LANES, 16 * ns), 0)
    tile_l = lax.broadcasted_iota(jnp.int32, (LANES, 16 * ns), 1)
    tile_b = (tile_k == tile_l % ns).astype(bf16)
    tile_c = (tile_k == tile_l % ns + ns).astype(bf16)
    tile_t = lax.broadcasted_iota(jnp.int32, (RUN, 16 * ns), 0) % 16
    own_t = (tile_t == lax.broadcasted_iota(jnp.int32, (RUN, 16 * ns), 1) // ns).astype(f32)

    def spread(r):
        block = pxs[rank : rank + 2 * ns, pl.ds(pl.multiple_of(r * RUN, LANES), RUN)]
        parts = jnp.concatenate([block, jnp.zeros((LANES - 2 * ns, RUN), f32)], axis=0)
        picked = parts.T[:, None, :] * own_row[None]
        bc[bc_rows(r), :] = dot(picked.reshape(RUN * ns, LANES).astype(bf16), ones, 1, 0)
        cblk[rows_of(r), :] = (dot(parts.T.astype(bf16), tile_c, 1, 0) * own_t).astype(bf16)
        bblk[rows_of(r), :] = (dot(parts.T.astype(bf16), tile_b, 1, 0) * own_t).astype(bf16)

    def bc_rows(r):
        if bc.shape[0] == RUN * ns:
            return pl.ds(0, RUN * ns)
        return pl.ds(pl.multiple_of(r * (RUN * ns), RUN * ns), RUN * ns)

    mixed_in.wait()
    for r in range(runs):
        rows, lanes_at = slice(r * RUN, (r + 1) * RUN), slice(r * RUN, (r + 1) * RUN)
        low = px_r[:rank, lanes_at]
        dlow_o[:, lanes_at] = low
        weights = w_dt[pl.ds(pl.multiple_of(kinds[r] * rank, 16), rank), :]
        pre = dot(low, weights, 0, 0) + table[pl.ds(T_BIAS + kinds[r], 1), :]
        pre_s[rows, :] = pre
        steps = softplus(pre)
        step_s[rows, :] = steps
        place = r * RUN + lax.broadcasted_iota(jnp.int32, (RUN, 1), 0)
        dtk[rows, :] = jnp.where((place == 0) | (place == split), FAR, steps)
        dtu[rows, :] = steps * mixed_r[rows, :].astype(f32)
        if bc.shape[0] > RUN * ns:
            spread(r)

    def row(tile, j, g):
        return jnp.broadcast_to(tile[j : j + 1, lane[g]], (ns, LANES))

    def folded(ref):
        outs = []
        for g in range(groups):
            out = ref[g, pl.ds(0, RUN, stride=half), :]
            for s in range(1, half):
                out = out + ref[g, pl.ds(s, RUN, stride=half), :]
            outs.append(out)
        return jnp.concatenate(outs, axis=1)

    states[0] = jnp.zeros((ns, es), bf16)

    def forward(r, hs):
        rows = rows_of(r)
        if bc.shape[0] == RUN * ns:
            spread(r)

        def eight(i, hs):
            hs = list(hs)
            at = pl.ds(pl.multiple_of(r * RUN + i * 32, 32), 32)
            k8, u8 = dtk[at, :], dtu[at, :]
            bcv = bc.at[bc_rows(r), :].at[pl.ds(pl.multiple_of(i * (32 * ns), 32 * ns), 32 * ns), :]
            stv = states.at[pl.ds(r * RUN + i * 32 + 1, 32)]
            for j in range(32):
                bt = bcv[j * ns : (j + 1) * ns, :LANES]
                for g in range(groups):
                    decay = jnp.exp2(row(k8, j, g) * r2s[:, lane[g]])
                    hs[g] = decay * hs[g] + row(u8, j, g) * bt
                    stv[j, :, lane[g]] = hs[g].astype(bf16)
            return tuple(hs)

        hs = lax.fori_loop(0, RUN // 32, eight, hs)
        for q in range(RUN // 16):
            at = pl.ds(pl.multiple_of(r * RUN + q * 16, 16), 16)
            block = states[pl.ds(r * RUN + q * 16 + 1, 16)].reshape(16 * ns, es)
            ssm_o[at, :] = dot(cblk[at, :], block, 1, 0) + skip * mixed_r[at, :].astype(f32)
        return hs

    zero = jnp.zeros((ns, LANES), f32)
    lax.fori_loop(0, runs, forward, (zero,) * groups)
    gskip_o[...] = jnp.zeros_like(gskip_o)
    finish(arriving)
    leaving = []
    for r in range(runs):
        rows = slice(r * RUN, (r + 1) * RUN)
        wide_at = pl.ds(pl.multiple_of(kinds[r] * d, LANES), d)
        ssm, act = ssm_o[rows, :], act_r[rows, :]
        d_gated = dot(cot_r[rows, :], w_out[:, wide_at], 1, 1)
        dssm_r[rows, :] = d_gated * act
        dgs_o[rows, :] = d_gated * ssm
        gated = (ssm * act).astype(bf16)
        gated_o[rows, :] = gated
        branch[rows, :] = dot(gated, w_out[:, wide_at], 1, 0).astype(bf16)
    for k, (source, target) in enumerate(((gated_o, gated_h), (dgs_o, dgs_h), (cot_r, cot_h))):
        leaving.append(pltpu.make_async_copy(source, target, mid_sem.at[k]))
    for s, part in enumerate(parts_h):
        first = pl.multiple_of((meta[0] ^ s) * size, RUN)
        leaving.append(pltpu.make_async_copy(branch.at[pl.ds(first, size), :], part, part_sem.at[s]))
    begin(leaving)
    gather_k = lax.broadcasted_iota(jnp.int32, (2 * LANES, LANES), 0) // LANES
    gather_l = lax.broadcasted_iota(jnp.int32, (2 * LANES, LANES), 1) // ns
    gather = (gather_k == gather_l).astype(bf16)
    keep_n = lax.broadcasted_iota(jnp.int32, (ns, LANES), 0)
    keep = (lax.broadcasted_iota(jnp.int32, (ns, LANES), 1) % ns == keep_n).astype(f32)

    def backward(back, carry):
        r = runs - 1 - back
        rows = rows_of(r)
        kind = kinds[r]
        if bc.shape[0] == RUN * ns:
            spread(r)

        def eight(back_i, carry):
            ms, hs, gr = [list(part) for part in carry]
            i = RUN // 32 - 1 - back_i
            at = pl.ds(pl.multiple_of(r * RUN + i * 32, 32), 32)
            k8, u8 = dtk[at, :], dtu[at, :]
            y8 = dssm_r[pl.ds(pl.multiple_of(r * RUN + i * 32, 32), 32), :]
            bcv = bc.at[bc_rows(r), :].at[pl.ds(pl.multiple_of(i * (32 * ns), 32 * ns), 32 * ns), :]
            adv = adjs.at[pl.ds(i * 32, 32)]
            qsv = qs.at[:, pl.ds(pl.multiple_of(i * (32 * half), 32 * half), 32 * half), :]
            stv = states.at[pl.ds(r * RUN + i * 32, 32)]
            gsv = gs.at[pl.ds(pl.multiple_of(i * (32 * ns), 32 * ns), 32 * ns), :]
            for j in reversed(range(32)):
                ct = bcv[j * ns : (j + 1) * ns, LANES:]
                gb_sum, gc_sum = None, None
                for g in range(groups):
                    dt = row(k8, j, g)
                    dy = row(y8, j, g)
                    adjoint = dy * ct + ms[g]
                    before = stv[j, :, lane[g]].astype(f32)
                    c_part = dy * hs[g]
                    b_part = adjoint * row(u8, j, g)
                    gb_sum = b_part if gb_sum is None else gb_sum + b_part
                    gc_sum = c_part if gc_sum is None else gc_sum + c_part
                    fold_at = slice(j * half, (j + 1) * half)
                    adv[j, :, lane[g]] = adjoint.astype(bf16)
                    ms[g] = jnp.exp2(dt * r2s[:, lane[g]]) * adjoint
                    weighted = ms[g] * before
                    by_rate = weighted * r1s[:, lane[g]]
                    qsv[g, fold_at, :] = by_rate[:half] + by_rate[half:]
                    gr[g] = gr[g] + weighted * dt
                    hs[g] = before
                gsv[j * ns : (j + 1) * ns, :LANES] = gb_sum.astype(bf16)
                gsv[j * ns : (j + 1) * ns, LANES:] = gc_sum.astype(bf16)
            return tuple(ms), tuple(hs), tuple(gr)

        carry = lax.fori_loop(0, RUN // 32, eight, carry)
        mixed = mixed_r[rows, :].astype(f32)
        by_rate = folded(qs)
        lb = jnp.concatenate(
            [
                dot(
                    bblk[pl.ds(pl.multiple_of(r * RUN + q * 16, 16), 16), :],
                    adjs[q * 16 : (q + 1) * 16].reshape(16 * ns, es),
                    1,
                    0,
                )
                for q in range(RUN // 16)
            ],
            axis=0,
        )
        dssm = dssm_r[rows, :]
        grad_steps = by_rate + lb * mixed
        gmix_o[rows, :] = dssm * skip + lb * step_s[rows, :]
        gskip_o[...] += jnp.sum(dssm * mixed, axis=0, keepdims=True)
        dpre = (grad_steps * jax.nn.sigmoid(pre_s[rows, :])).astype(bf16)
        dpre_o[rows, :] = dpre
        weights = w_dt[pl.ds(pl.multiple_of(kind * rank, 16), rank), :]
        dlow = dot(weights, dpre, 1, 1)
        sums = dot(gs[...], gather, 1, 0).reshape(RUN, ns, LANES) * keep[None]
        fs[...] = (sums[:, :half] + sums[:, half:]).reshape(RUN * half, LANES)
        dbc = fs[pl.ds(0, RUN, stride=half), :]
        for s in range(1, half):
            dbc = dbc + fs[pl.ds(s, RUN, stride=half), :]
        dbc = dbc.T[: 2 * ns]
        at = pl.ds(pl.multiple_of(r * RUN, LANES), RUN)
        dpx_o[:rank, at] = dlow.astype(bf16)
        dpx_o[rank:, at] = dbc.astype(bf16)
        begin(move_rows([(gmix_o, gmix_h), (dpre_o, dpre_h)], out_sem, r, r * RUN, RUN))
        return carry

    last = tuple(states[total, :, lane[g]].astype(f32) for g in range(groups))
    done = lax.fori_loop(0, runs, backward, ((zero,) * groups, last, (zero,) * groups))
    for g in range(groups):
        glog_o[:, lane[g]] = done[2][g] * rates[:, lane[g]]

    def settle(r, carry):
        finish(move_rows([(gmix_o, gmix_h), (dpre_o, dpre_h)], out_sem, r, r * RUN, RUN))
        return carry

    lax.fori_loop(0, runs, settle, 0)
    finish(leaving)


def scan_call(rank, xw, ns, meta, kinds, cots, pieces, px, w_dt_l, table, mixed, act):
    (total, es), (own, d) = mixed.shape, cots[0].shape
    nar, wid = len(cots), len(pieces)
    out_cols = MODS * d
    bc_runs = total // RUN if total * ns * 2 * LANES * 4 <= 20 * 1024 * 1024 else 1
    return call(
        functools.partial(scan_kernel, nar, wid, rank),
        [((own, d), bf16, "a")] * nar
        + [
            ((total, es), bf16, "a"),
            ((total, es), f32, "a"),
            ((total, d), bf16, "a"),
            ((total, es), f32, "a"),
            ((total, es), bf16, "a"),
            ((xw, total), bf16, "v"),
            ((rank, total), bf16, "v"),
            ((ns, es), f32, "v"),
            ((1, es), f32, "v"),
        ],
        [(meta, "s"), (kinds, "s")]
        + [(p, "a") for p in cots]
        + [(p, "a") for p in pieces]
        + [(px, "v"), (w_dt_l, "v"), (table, "v"), (mixed, "a"), (act, "a")],
        [
            pltpu.VMEM((total, es), bf16),
            pltpu.VMEM((total, es), f32),
            pltpu.VMEM((total, d), bf16),
            pltpu.VMEM((es, out_cols), bf16),
            pltpu.VMEM((total, es), f32),
            pltpu.VMEM((total, es), f32),
            pltpu.VMEM((total, es), bf16),
            pltpu.VMEM((total, es), f32),
            pltpu.VMEM((total, d), bf16),
            pltpu.VMEM((total, es), f32),
            pltpu.VMEM((total, es), bf16),
            pltpu.SemaphoreType.DMA((2,)),
            pltpu.SemaphoreType.DMA((nar,)),
            pltpu.SemaphoreType.DMA((out_cols // pieces[0].shape[1], wid)),
            pltpu.SemaphoreType.DMA((3,)),
            pltpu.SemaphoreType.DMA((nar,)),
            pltpu.SemaphoreType.DMA((2, total // RUN)),
            pltpu.VMEM((xw, total), f32),
            pltpu.VMEM((total, es), f32),
            pltpu.VMEM((total, es), f32),
            pltpu.VMEM((total + 1, ns, es), bf16),
            pltpu.VMEM((bc_runs * RUN * ns, 2 * LANES), f32),
            pltpu.VMEM((es // LANES, RUN * ns // 2, LANES), f32),
            pltpu.VMEM((RUN * ns, 2 * LANES), bf16),
            pltpu.VMEM((RUN * ns // 2, LANES), f32),
            pltpu.VMEM((total, es), f32),
            pltpu.VMEM((total, es), f32),
            pltpu.VMEM((ns, es), f32),
            pltpu.VMEM((ns, es), f32),
            pltpu.VMEM((total, 16 * ns), bf16),
            pltpu.VMEM((total, 16 * ns), bf16),
            pltpu.VMEM((RUN, ns, es), bf16),
        ],
        us=40.0,
    )


def split_rows(acc, place, rows):
    return acc[pl.ds(pl.multiple_of(place * rows, 16), rows), :]


def grads_kernel(wid, ep, rank, meta, kinds, *refs):
    hbm, (dlow_r, glog_r, gskip_r) = refs[:6], refs[6:9]
    dgate_h, gate_h, w_out_h, table_o = refs[9:13]
    rows_in, (dgate_o, gate_o, w_out_o, acc_out, acc_in, in_sem, out_sem, block_sem) = refs[13:19], refs[19:]
    gated_r, dgs_r, slope_r, cot_r, normed_r, dpre_r = rows_in
    total, es = gated_r.shape
    d = cot_r.shape[1]
    size = total // CHUNKS
    arriving = [move_rows(list(zip(hbm, rows_in)), in_sem, c, c * size, size) for c in range(CHUNKS)]
    leaving = [move_rows([(dgate_o, dgate_h)], out_sem, c, c * size, size) for c in range(CHUNKS)]
    for copies in arriving:
        begin(copies)
    acc_out[...] = jnp.zeros_like(acc_out)
    acc_in[...] = jnp.zeros_like(acc_in)
    table_o[...] = jnp.zeros_like(table_o)
    base = MODS * rank

    def one_run(r, carry):
        rows = pl.ds(pl.multiple_of(r * RUN, RUN), RUN)
        kind = kinds[r]
        wide_at = pl.ds(pl.multiple_of(kind * d, LANES), d)
        es_at = pl.ds(pl.multiple_of(kind * es, LANES), es)
        acc_out[:, wide_at] += dot(gated_r[rows, :], cot_r[rows, :], 0, 0)
        dgate = (dgs_r[rows, :] * slope_r[rows, :]).astype(bf16)
        dgate_o[rows, :] = dgate
        acc_in[:, es_at] += dot(normed_r[rows, :], dgate, 0, 0)
        dpre = dpre_r[rows, :]
        low = dlow_r[:, pl.ds(pl.multiple_of(r * RUN, LANES), RUN)]
        table_o[pl.ds(pl.multiple_of(kind * rank, 8), rank), :] += dot(low, dpre, 1, 0)
        table_o[pl.ds(base + T_BIAS + kind, 1), :] += jnp.sum(dpre.astype(f32), axis=0, keepdims=True)
        return carry

    for c in range(CHUNKS):
        finish(arriving[c])
        each(c * size // RUN, size // RUN, one_run)
        begin(leaving[c])
    in_rows = acc_in.shape[0] // wid
    block_copies = []
    for k, (source, target) in enumerate(((gate_o, gate_h), (w_out_o, w_out_h))):
        for v in range(wid):
            if k == 0:
                gate_o[v] = acc_in[v * in_rows : (v + 1) * in_rows, :].astype(bf16)
            else:
                w_out_o[v] = acc_out[v * ep : (v + 1) * ep, :].astype(bf16)
            block_copies.append(pltpu.make_async_copy(source.at[v], target.at[v], block_sem.at[k, v]))
            block_copies[-1].start()
    table_o[base + T_SKIP : base + T_SKIP + 1, :] = gskip_r[...]
    table_o[base + T_LOG : base + T_LOG + glog_r.shape[0], :] = glog_r[...]
    for copies in leaving + [block_copies]:
        finish(copies)


def pair_kernel(chips, meta, same, peer, *outs):
    chip = meta[1] // 2
    for s in range(chips):
        outs[s][...] = (same[chip ^ s].astype(f32) + peer[chip ^ s].astype(f32)).astype(bf16)


def conv_kernel(nar, wid, taps, ep, meta, kinds, *refs):
    dpx_pieces = refs[:nar]
    table, w_x, table_r = refs[nar : nar + 3]
    hbm = refs[nar + 3 : nar + 8]
    dfront_h, same_h, peer_h = refs[nar + 8 : nar + 11]
    rows_in = refs[nar + 11 : nar + 16]
    dfront_o, same_o, peer_o, acc_in, acc_x, small, turned, in_sem, out_sem, block_sem = refs[nar + 16 :]
    gmix_r, csum_r, front_r, mixed_r, normed_r = rows_in
    split = meta[2]
    total, es = gmix_r.shape
    runs = total // RUN
    size = total // CHUNKS
    moves = [(a, b, 16) if b is front_r else (a, b) for a, b in zip(hbm, rows_in)]
    arriving = [move_rows(moves, in_sem, c, c * size, size) for c in range(CHUNKS)]
    leaving = [move_rows([(dfront_o, dfront_h)], out_sem, c, c * size, size) for c in range(CHUNKS)]
    for c in reversed(range(CHUNKS)):
        begin(arriving[c])
    front_r[0:16, :] = jnp.zeros((16, es), f32)
    acc_in[...] = jnp.zeros_like(acc_in)
    acc_x[...] = jnp.zeros_like(acc_x)
    small[...] = jnp.zeros_like(small)
    xw = dpx_pieces[0].shape[0]

    def one_run(back, later):
        r = runs - 1 - back
        rows = pl.ds(pl.multiple_of(r * RUN, RUN), RUN)
        kind = kinds[r]
        lanes_at = pl.ds(pl.multiple_of(r * RUN, LANES), RUN)
        dpx = sum(piece[:, lanes_at].astype(f32) for piece in dpx_pieces)
        dpx = jnp.concatenate([dpx, jnp.zeros((LANES - xw, RUN), f32)], axis=0).T.astype(bf16)
        x_at = pl.ds(pl.multiple_of(kind * LANES, LANES), LANES)
        acc_x[:, x_at] += dot(mixed_r[rows, :], dpx, 0, 0)
        gmix = gmix_r[rows, :] + dot(dpx, w_x[:, x_at], 1, 1)
        csum = csum_r[rows, :]
        sig = jax.nn.sigmoid(csum)
        dc = gmix * sig * (1.0 + csum * (1.0 - sig))
        place = r * RUN + lax.broadcasted_iota(jnp.int32, (RUN + 8, 1), 0)
        offset = place - jnp.where(place >= split, split, 0)
        ext = jnp.concatenate([dc, later], axis=0)
        lagged = front_r[pl.ds(pl.multiple_of(r * RUN + 8, 8), RUN + 8), :]
        d_front = jnp.zeros((RUN, es), f32)
        for lag in range(taps):
            tap = taps - 1 - lag
            masked = ext * (offset >= lag).astype(f32)
            d_front = d_front + table[T_CONV + tap : T_CONV + tap + 1, :] * masked[lag : lag + RUN, :]
            small[T_CONV + tap : T_CONV + tap + 1, :] += jnp.sum(
                masked[:RUN] * lagged[8 - lag : 8 - lag + RUN, :], axis=0, keepdims=True
            )
        small[T_CONV_B : T_CONV_B + 1, :] += jnp.sum(dc, axis=0, keepdims=True)
        d_front = d_front.astype(bf16)
        dfront_o[rows, :] = d_front
        acc_in[:, pl.ds(pl.multiple_of(kind * es, LANES), es)] += dot(normed_r[rows, :], d_front, 0, 0)
        return dc[:8]

    later = jnp.zeros((8, es), f32)
    for c in reversed(range(CHUNKS)):
        if c == CHUNKS - 1:
            finish(arriving[c])
        if c:
            finish(arriving[c - 1])
        back = (CHUNKS - 1 - c) * size // RUN
        later = each(back, size // RUN, one_run, later)
        begin(leaving[c])
    in_rows, width = acc_in.shape[0] // wid, acc_in.shape[1]
    base = table_r.shape[0] - small.shape[0]
    rest = jnp.concatenate([table_r[:base, :], table_r[base:, :] + small[...]], axis=0)
    rest = jnp.concatenate([rest, jnp.zeros((256 - rest.shape[0], es), f32)], axis=0).T
    x_cols = acc_x.shape[1]
    turned[:, :x_cols] = acc_x[...].astype(bf16)
    turned[:, x_cols : x_cols + 256] = rest.astype(bf16)
    turned[:, x_cols + 256 :] = jnp.zeros((es, width - x_cols - 256), bf16)
    core = meta[1] & 1
    block_copies = []
    for k, (ref, out, parity) in enumerate(((peer_o, peer_h, 1 - core), (same_o, same_h, core))):
        for c in range(wid // 2):
            place = 2 * c + parity
            ref[c, :in_rows, :] = split_rows(acc_in, place, in_rows).astype(bf16)
            ref[c, in_rows:, :] = split_rows(turned, place, ep)
            block_copies.append(pltpu.make_async_copy(ref.at[c], out.at[c], block_sem.at[k, c]))
            block_copies[-1].start()
    for copies in leaving + [block_copies]:
        finish(copies)


def normed_kernel(nar, wid, meta, kinds, *refs):
    fronts, gates = refs[:wid], refs[wid : 2 * wid]
    dfront_h, dgate_h = refs[2 * wid : 2 * wid + 2]
    outs = refs[2 * wid + 2 : 2 * wid + 2 + nar]
    dfront_r, dgate_r, wf, wg, dn, f_sem, g_sem, in_sem, part_sem = refs[2 * wid + 2 + nar :]
    total, es = dfront_r.shape
    size = total // nar
    weights = place_pieces(fronts, wf, f_sem, meta[1], wf.shape[0] // wid)
    weights += place_pieces(gates, wg, g_sem, meta[1], wg.shape[0] // wid)
    firsts = [(meta[0] ^ s) * size for s in range(nar)]
    arriving = [
        move_rows([(dfront_h, dfront_r), (dgate_h, dgate_r)], in_sem, s, firsts[s], size) for s in range(nar)
    ]
    part_copies = [
        pltpu.make_async_copy(dn.at[pl.ds(pl.multiple_of(firsts[s], RUN), size), :], outs[s], part_sem.at[s])
        for s in range(nar)
    ]
    begin(weights)
    for s in reversed(range(nar)):
        begin(arriving[s])
    finish(weights)

    def one_run(r, carry):
        rows = pl.ds(pl.multiple_of(r * RUN, RUN), RUN)
        at = pl.ds(pl.multiple_of(kinds[r] * es, LANES), es)
        dn[rows, :] = (dot(dfront_r[rows, :], wf[:, at], 1, 1) + dot(dgate_r[rows, :], wg[:, at], 1, 1)).astype(bf16)
        return carry

    for s in reversed(range(nar)):
        finish(arriving[s])
        first = (meta[0] ^ s) * (size // RUN)
        each(first, size // RUN, one_run)
        part_copies[s].start()
    finish(part_copies)


def total_gate_kernel(blocks, out):
    out[...] = sum(blocks[v].astype(f32) for v in range(blocks.shape[0])).astype(bf16)


def total_out_kernel(er, blocks, out):
    d = out.shape[2]
    summed = sum(blocks[v, :er, :].astype(f32) for v in range(blocks.shape[0]))
    for m in range(MODS):
        out[m] = summed[:, m * d : (m + 1) * d]


def total_b_kernel(nar, chips, er, rank, taps, ns, meta, *refs):
    pieces, gate_r, outs = refs[:chips], refs[chips], refs[chips + 1 : chips + 1 + nar]
    x_o, dt_o, bias_o, conv_o, conv_b_o, log_o, skip_o, rows_s = refs[chips + 1 + nar :]
    dr, width = outs[0].shape[0], gate_r.shape[1]
    in_rows = nar * dr
    summed = sum(piece[...].astype(f32) for piece in pieces)
    gate = gate_r[...].astype(f32)
    for k in range(nar):
        rows_s[k, :, :width] = summed[k * dr : (k + 1) * dr].astype(bf16)
        rows_s[k, :, width:] = gate[k * dr : (k + 1) * dr].astype(bf16)
    for s in range(nar):
        outs[s][...] = rows_s[meta[0] ^ s]
    rest = summed[in_rows:]
    x_cols = MODS * LANES
    for m in range(MODS):
        x_o[m] = rest[:er, m * LANES : m * LANES + x_o.shape[2]]
    lanes = rest[:, x_cols : x_cols + 256]
    pad = LANES - lanes.shape[0]
    turned = jnp.concatenate([lanes, jnp.zeros((pad, 256), f32)], axis=0).T[:, :er]
    base = MODS * rank
    for m in range(MODS):
        dt_o[m] = turned[m * rank : (m + 1) * rank]
    bias_o[...] = turned[base + T_BIAS : base + T_BIAS + MODS]
    conv_o[...] = turned[base + T_CONV : base + T_CONV + taps]
    conv_b_o[...] = turned[base + T_CONV_B : base + T_CONV_B + 1]
    skip_o[...] = turned[base + T_SKIP : base + T_SKIP + 1]
    log_o[...] = turned[base + T_LOG : base + T_LOG + ns]


def tokens_kernel(x_r, cot_r, gain_r, *refs):
    pieces, out = refs[:-1], refs[-1]
    x = x_r[...].astype(f32)
    scale = lax.rsqrt(jnp.mean(x * x, axis=1, keepdims=True) + EPSILON)
    q = sum(piece[...].astype(f32) for piece in pieces) * gain_r[...]
    dotted = jnp.mean(q * x, axis=1, keepdims=True)
    out[...] = (cot_r[...].astype(f32) + scale * q - x * (scale * scale * scale) * dotted).astype(bf16)


def mixed_kernel(x_r, *refs):
    pieces, out = refs[:-1], refs[-1]
    out[...] = (x_r[...].astype(f32) + sum(piece[...].astype(f32) for piece in pieces)).astype(bf16)


def in_order(parts, er, ep, wid):
    return jnp.concatenate([part[:, v * ep : v * ep + er] for v in range(wid) for part in parts], axis=1)


def w_in_kernel(nar, wid, er, ep, meta, *refs):
    pieces, (w_h, gain_r, grad_h, gain_o, rows_s, w_r, grad_s, w_sem, out_sem) = refs[:nar], refs[nar:]
    dr = pieces[0].shape[0]
    es, inner = wid * ep, wid * nar * er
    loading = pltpu.make_async_copy(w_h, w_r, w_sem)
    loading.start()
    for s in range(nar):
        rows_s[meta[0] ^ s] = pieces[s][...].astype(f32)
    sums, storing = 0.0, []
    for m in range(MODS):
        for half in range(2):
            first = (half * MODS + m) * es
            row = in_order([rows_s[k, :, first : first + es] for k in range(nar)], er, ep, wid)
            at = slice(half * inner, (half + 1) * inner)
            grad_s[m, :, at] = row
            if m + half == 0:
                loading.wait()
            sums = sums + jnp.sum(row * w_r[m, :, at].astype(f32), axis=1, keepdims=True)
        storing.append(pltpu.make_async_copy(grad_s.at[m], grad_h.at[m], out_sem.at[m]))
        storing[m].start()
    sums = jnp.broadcast_to(sums, (dr, LANES))
    sums = jnp.concatenate([sums, jnp.zeros((LANES - dr, LANES), f32)], axis=0).T[0:1, :dr]
    gain_o[...] = sums / gain_r[...].astype(f32)
    finish(storing)


def body(
    tokens,
    norm_gain,
    w_in,
    conv_w,
    conv_b,
    w_x,
    w_dt,
    dt_bias,
    a_log,
    d_skip,
    w_out,
    mod_ids,
    split_at,
    cotangent,
):
    nar, wid = lax.axis_size("narrow"), lax.axis_size("wide")
    chips = wid // 2
    n, w = lax.axis_index("narrow"), lax.axis_index("wide")
    own, d = tokens.shape
    total = nar * own
    rpd = own // RUN
    rank, xw, ns, taps = w_dt.shape[0], w_x.shape[2], a_log.shape[1], conv_w.shape[0]
    er = w_out.shape[0]
    inner = er * nar * wid
    ep = -(-er // 16) * 16
    es = ep * wid
    dr = w_in.shape[0]
    width = MODS * es
    meta = jnp.stack([n, w, split_at[0]]).astype(jnp.int32)

    front_w = width + LANES
    gain_row = norm_gain[None]
    w_in_m = w_in.transpose(1, 0, 2)
    out_cols, x_cols = MODS * d, MODS * LANES
    table_rows = T_LOG + ns
    small_cols = x_cols + 256
    blocks = front_w // small_cols
    below = -(-(-(-ep // blocks)) // 16) * 16
    res = call(
        functools.partial(split_kernel, er, ep, wid, below),
        [((dr, front_w + width), bf16, "v")] * nar
        + [((below, front_w), bf16, "v"), ((ep * (out_cols // width), width), bf16, "v")],
        [(meta, "s")]
        + [
            (a, "v")
            for a in (
                w_in_m,
                gain_row,
                w_out.transpose(1, 0, 2),
                w_x.transpose(1, 0, 2),
                w_dt.transpose(1, 0, 2),
                dt_bias,
                conv_w,
                conv_b[None],
                d_skip[None],
                a_log.T,
            )
        ],
        [
            pltpu.VMEM((nar, dr, front_w + width), bf16),
            pltpu.VMEM((256, LANES), f32),
        ],
        us=3.0,
    )
    parts, (small, out_rows) = res[:nar], res[nar:]

    parts = scatter_narrow(parts)
    front_rows, gate_rows = call(
        join_kernel,
        [
            ((nar * dr + below, front_w), bf16, "v"),
            ((nar * dr + out_rows.shape[0], width), bf16, "v"),
        ],
        [(meta, "s")] + [(p, "v") for p in parts] + [(small, "v"), (out_rows, "v")],
        us=2.0,
    )
    front_near = near_wide(front_rows)
    front_pieces = far_wide(front_near)
    run_kinds = mod_ids.reshape(rpd, RUN)[:, :1].astype(bf16)
    tail = jnp.pad(jnp.broadcast_to(run_kinds, (rpd, d)), ((0, 16 - rpd), (0, 0)))
    tok_pieces = relay_narrow(jnp.concatenate([tokens, tail], axis=0))
    gate_near = near_wide(after(gate_rows, *front_near[1:]))
    normed, front, csum, mixed, px, kinds, w_x_l, w_dt_l, table, gain_full = call(
        functools.partial(in_kernel, nar, wid, rpd, taps, ep, rank),
        [
            ((total, d), bf16, "a"),
            ((total, es), f32, "a"),
            ((total, es), f32, "a"),
            ((total, es), bf16, "a"),
            ((xw, total), bf16, "v"),
            ((nar * rpd,), jnp.int32, "s"),
            ((es, x_cols), bf16, "v"),
            ((MODS * rank, es), bf16, "v"),
            ((256 - MODS * rank, es), f32, "v"),
            ((1, d), f32, "v"),
        ],
        [(meta, "s")] + [(p, "a") for p in tok_pieces] + [(p, "a") for p in front_pieces],
        [
            pltpu.VMEM((total, d), bf16),
            pltpu.VMEM((total, es), f32),
            pltpu.VMEM((total, es), f32),
            pltpu.VMEM((total, es), bf16),
            pltpu.VMEM((nar * (own + 16), d), bf16),
            pltpu.VMEM((d, front_w), bf16),
            pltpu.VMEM((es, small_cols), bf16),
            pltpu.SemaphoreType.DMA((nar,)),
            pltpu.SemaphoreType.DMA((wid,)),
            pltpu.SemaphoreType.DMA((-(-ep // below), wid)),
            pltpu.SemaphoreType.DMA((4, CHUNKS)),
        ],
        us=9.0,
    )
    cot_pieces = relay_narrow(after(cotangent, *tok_pieces[1:]), px)
    gate_pieces = far_wide([after(piece, px) for piece in gate_near])
    act, slope = call(
        functools.partial(gate_kernel, wid),
        [((total, es), f32, "a")] * 2,
        [(meta, "s"), (kinds, "s")]
        + [(p, "a") for p in gate_pieces]
        + [(after(normed, *cot_pieces[1:3]), "a")],
        [
            pltpu.VMEM((total, d), bf16),
            pltpu.VMEM((total, es), f32),
            pltpu.VMEM((total, es), f32),
            pltpu.VMEM((d, width), bf16),
            pltpu.SemaphoreType.DMA((wid,)),
            pltpu.SemaphoreType.DMA((1, CHUNKS)),
            pltpu.SemaphoreType.DMA((2, CHUNKS)),
        ],
        us=0.1,
    )
    px_total = add_narrow(px, act, cot_pieces[-1])
    res = scan_call(
        rank, xw, ns, meta, kinds, cot_pieces, gate_pieces, px_total, w_dt_l, table, mixed, act
    )
    branch_parts, (gated, dgs, cot, gmix, dpre, dpx, dlow, glog, gskip) = res[:nar], res[nar:]
    dpx_pieces = gather_narrow(dpx)
    branch_pieces = scatter_narrow(branch_parts)
    in_rows = d // wid
    dgate, gate_blocks, w_out_blocks, table_g = call(
        functools.partial(grads_kernel, wid, ep, rank),
        [
            ((total, es), bf16, "a"),
            ((wid, in_rows, width), bf16, "a"),
            ((wid, ep, out_cols), bf16, "a"),
            ((MODS * rank + table_rows, es), f32, "v"),
        ],
        [(meta, "s"), (kinds, "s")]
        + [(a, "a") for a in (gated, dgs, slope, cot, normed, dpre)]
        + [(a, "v") for a in (dlow, glog, gskip)],
        [
            pltpu.VMEM((total, es), bf16),
            pltpu.VMEM((total, es), f32),
            pltpu.VMEM((total, es), f32),
            pltpu.VMEM((total, d), bf16),
            pltpu.VMEM((total, d), bf16),
            pltpu.VMEM((total, es), bf16),
            pltpu.VMEM((total, es), bf16),
            pltpu.VMEM((wid, in_rows, width), bf16),
            pltpu.VMEM((wid, ep, out_cols), bf16),
            pltpu.VMEM((es, out_cols), f32),
            pltpu.VMEM((d, width), f32),
            pltpu.SemaphoreType.DMA((6, CHUNKS)),
            pltpu.SemaphoreType.DMA((1, CHUNKS)),
            pltpu.SemaphoreType.DMA((2, wid)),
        ],
        us=9.0,
    )

    def over_wide(same, peer, *earlier):
        peer = swap(peer, "wide", 1)
        same = after(same, *earlier) if earlier else same
        parts = call(
            functools.partial(pair_kernel, chips),
            [(same.shape[1:], bf16, "v")] * chips,
            [(meta, "s"), (same, "v"), (peer, "v")],
            us=3.0,
        )
        return [parts[0]] + [swap(parts[s], "wide", 2 * s) for s in range(1, chips)]

    gate_blocks = lax.all_to_all(gate_blocks, "wide", 0, 0)
    rows_b = in_rows + ep
    dfront, same_b, peer_b = call(
        functools.partial(conv_kernel, nar, wid, taps, ep),
        [((total, es), bf16, "a")] + [((chips, rows_b, width), bf16, "a")] * 2,
        [(meta, "s"), (kinds, "s")]
        + [(p, "v") for p in dpx_pieces]
        + [(a, "v") for a in (table, w_x_l, table_g)]
        + [(a, "a") for a in (gmix, csum, front, mixed, normed)],
        [
            pltpu.VMEM((total, es), f32),
            pltpu.VMEM((total, es), f32),
            pltpu.VMEM((total + 16, es), f32),
            pltpu.VMEM((total, es), bf16),
            pltpu.VMEM((total, d), bf16),
            pltpu.VMEM((total, es), bf16),
            pltpu.VMEM((chips, rows_b, width), bf16),
            pltpu.VMEM((chips, rows_b, width), bf16),
            pltpu.VMEM((d, width), f32),
            pltpu.VMEM((es, x_cols), f32),
            pltpu.VMEM((table_rows, es), f32),
            pltpu.VMEM((es, width), bf16),
            pltpu.SemaphoreType.DMA((5, CHUNKS)),
            pltpu.SemaphoreType.DMA((1, CHUNKS)),
            pltpu.SemaphoreType.DMA((2, chips)),
        ],
        us=12.0,
    )
    dn_parts = call(
        functools.partial(normed_kernel, nar, wid),
        [((own, d), bf16, "a")] * nar,
        [(meta, "s"), (kinds, "s")]
        + [(p, "a") for p in front_pieces]
        + [(p, "a") for p in gate_pieces]
        + [(dfront, "a"), (dgate, "a")],
        [
            pltpu.VMEM((total, es), bf16),
            pltpu.VMEM((total, es), bf16),
            pltpu.VMEM((d, width), bf16),
            pltpu.VMEM((d, width), bf16),
            pltpu.VMEM((total, d), bf16),
            pltpu.SemaphoreType.DMA((wid,)),
            pltpu.SemaphoreType.DMA((wid,)),
            pltpu.SemaphoreType.DMA((2, nar)),
            pltpu.SemaphoreType.DMA((nar,)),
        ],
        us=30.0,
    )
    pieces_b = over_wide(same_b, peer_b, dn_parts[0])
    dn_pieces, dn_kept = sum_narrow(dn_parts, pieces_b[0])

    mixed_out = call(
        mixed_kernel,
        [((own, d), bf16, "v")],
        [(tokens, "v")] + [(p, "v") for p in after(tuple(branch_pieces), pieces_b[0])],
        us=2.0,
    )[0]
    gate_sum = call(
        total_gate_kernel,
        [((in_rows, width), bf16, "v")],
        [(after(gate_blocks, mixed_out, dn_kept), "v")],
        us=2.0,
    )[0]
    res = call(
        functools.partial(total_b_kernel, nar, chips, er, rank, taps, ns),
        [((dr, 2 * width), bf16, "v")] * nar
        + [
            ((MODS, er, xw), f32, "v"),
            ((MODS, rank, er), f32, "v"),
            ((MODS, er), f32, "v"),
            ((taps, er), f32, "v"),
            ((1, er), f32, "v"),
            ((ns, er), f32, "v"),
            ((1, er), f32, "v"),
        ],
        [(meta, "s")] + [(p, "v") for p in pieces_b] + [(gate_sum, "v")],
        [pltpu.VMEM((nar, dr, 2 * width), bf16)],
        us=3.0,
    )
    back_parts = res[:nar]
    grad_w_x, grad_w_dt, grad_dt_bias, grad_conv_w, grad_conv_b, grad_log, grad_skip = res[nar:]
    back_pieces = scatter_narrow(back_parts)
    grad_tokens = call(
        tokens_kernel,
        [((own, d), bf16, "v")],
        [(tokens, "v"), (cotangent, "v"), (gain_full, "v")]
        + [(p, "v") for p in dn_pieces],
        us=0.1,
    )[0]
    w_out_blocks = lax.all_to_all(after(w_out_blocks, gate_sum), "wide", 0, 0)
    grad_w_in, grad_gain = call(
        functools.partial(w_in_kernel, nar, wid, er, ep),
        [((MODS, dr, 2 * inner), f32, "a"), ((1, dr), f32, "v")],
        [(meta, "s")] + [(p, "v") for p in back_pieces] + [(after(w_in_m, grad_tokens), "a"), (gain_row, "v")],
        [
            pltpu.VMEM((nar, dr, 2 * width), f32),
            pltpu.VMEM((MODS, dr, 2 * inner), bf16),
            pltpu.VMEM((MODS, dr, 2 * inner), f32),
            pltpu.SemaphoreType.DMA(()),
            pltpu.SemaphoreType.DMA((MODS,)),
        ],
        us=13.0,
    )
    grad_w_out = call(
        functools.partial(total_out_kernel, er),
        [((MODS, er, d), f32, "v")],
        [(after(w_out_blocks, grad_gain), "v")],
        us=3.0,
    )[0]
    grad_w_in, grad_w_out = grad_w_in.transpose(1, 0, 2), grad_w_out.transpose(1, 0, 2)
    grad_w_x, grad_w_dt = grad_w_x.transpose(1, 0, 2), grad_w_dt.transpose(1, 0, 2)
    grad_log = grad_log.T
    return (
        mixed_out,
        grad_tokens,
        grad_gain[0],
        grad_w_in,
        grad_conv_w,
        grad_conv_b[0],
        grad_w_x,
        grad_w_dt,
        grad_dt_bias,
        grad_log,
        grad_skip[0],
        grad_w_out,
    )


def solution(mesh):
    both = ("wide", "narrow")
    return jax.shard_map(
        body,
        mesh=mesh,
        in_specs=(
            P(both, None),
            P(both),
            P(both, None, None),
            P(None, both),
            P(both),
            P(both, None, None),
            P(None, None, both),
            P(None, both),
            P(both, None),
            P(both),
            P(both, None, None),
            P(both),
            P("wide"),
            P(both, None),
        ),
        out_specs=(
            P(both, None),
            P(both, None),
            P(both),
            P(both, None, None),
            P(None, both),
            P(both),
            P(both, None, None),
            P(None, None, both),
            P(None, both),
            P(both, None),
            P(both),
            P(both, None, None),
        ),
        check_vma=False,
    )
```

```python
import functools
import math

import jax
import jax.numpy as jnp
from jax import lax
from jax.experimental import pallas as pl
from jax.experimental.pallas import tpu as pltpu
from jax.sharding import PartitionSpec as P

MODS = 3
RUN = 128
CHUNKS = 4
LANES = 128
EPSILON = 1e-05
LOG2E = 1.4426950408889634
FAR = 1e30
VMEM_LIMIT = 60 * 1024 * 1024
VMEM_SPARE = 6 * 1024 * 1024

f32 = jnp.float32
bf16 = jnp.bfloat16


def swap(block, axis, flip):
    count = lax.axis_size(axis)
    return lax.ppermute(block, axis, [(i, i ^ flip) for i in range(count)])


def gather_narrow(block):
    return [block] + [swap(block, "narrow", s) for s in range(1, lax.axis_size("narrow"))]


def relay_narrow(block, *earlier):
    count = lax.axis_size("narrow")
    pieces = {0: block}
    for s in sorted(range(1, count), key=lambda s: (s.bit_count(), -s)):
        low_bit = s & -s
        if s == low_bit:
            pieces[s] = swap(block, "narrow", s)
        else:
            pieces[s] = swap(after(pieces[s ^ low_bit], *earlier), "narrow", low_bit)
    return [pieces[s] for s in range(count)]


def add_narrow(block, *beside):
    flip = lax.axis_size("narrow") // 2
    while flip:
        got = swap(block, "narrow", flip)
        block = (after(block, *beside).astype(f32) + got.astype(f32)).astype(bf16)
        flip //= 2
        beside = ()
    return block


def scatter_narrow(parts):
    return [parts[0]] + [swap(parts[s], "narrow", s) for s in range(1, len(parts))]


def sum_narrow(parts, *earlier):
    parts = list(parts)
    arrived = [parts[0]]
    for s in range(len(parts) - 1, 0, -1):
        low_bit = s & -s
        got = swap(parts[s], "narrow", low_bit)
        if s == low_bit:
            arrived.append(got)
        else:
            rest = s ^ low_bit
            parts[rest] = (after(parts[rest], *earlier).astype(f32) + got.astype(f32)).astype(bf16)
    return arrived, parts[-2]


def near_wide(block):
    return [block] + [swap(block, "wide", 2 * s) for s in range(1, lax.axis_size("wide") // 2)]


def far_wide(near):
    return [piece for block in near for piece in (block, swap(block, "wide", 1))]


def after(value, *earlier):
    return lax.optimization_barrier((value,) + earlier)[0] if earlier else value


def dot(a, b, ca, cb):
    return lax.dot_general(a, b, (((ca,), (cb,)), ((), ())), preferred_element_type=f32)


def call(kernel, outs, ins, scratch=(), us=1.0, small=False):
    spaces = {"v": pltpu.VMEM, "s": pltpu.SMEM, "a": pl.ANY}
    held = [(array.shape, array.dtype) for array, space in ins if space == "v"]
    held += [(shape, dtype) for shape, dtype, space in outs if space == "v"]
    held += [(part.shape, part.dtype) for part in scratch if part.memory_space == pltpu.VMEM]
    need = sum(math.prod(shape) * jnp.dtype(dtype).itemsize for shape, dtype in held)
    need = min(need + need // 4 + VMEM_SPARE, VMEM_LIMIT) if small else VMEM_LIMIT
    return pl.pallas_call(
        kernel,
        out_shape=[jax.ShapeDtypeStruct(shape, dtype) for shape, dtype, _ in outs],
        in_specs=[pl.BlockSpec(memory_space=spaces[space]) for _, space in ins],
        out_specs=[pl.BlockSpec(memory_space=spaces[space]) for _, _, space in outs],
        scratch_shapes=list(scratch),
        compiler_params=pltpu.CompilerParams(vmem_limit_bytes=need),
        cost_estimate=pl.CostEstimate(flops=int(us * 1.1e9), bytes_accessed=1, transcendentals=0),
    )(*[array for array, _ in ins])


def place_pieces(pieces, target, sem, me, rows):
    return [
        pltpu.make_async_copy(
            piece.at[pl.ds(0, rows), pl.ds(0, target.shape[1])],
            target.at[pl.ds(pl.multiple_of((me ^ s) * rows, 16), rows), :],
            sem.at[s],
        )
        for s, piece in enumerate(pieces)
    ]


def place_w_out(pieces, target, sem, me):
    wid, width = len(pieces), pieces[0].shape[1]
    ep, blocks = target.shape[0] // len(pieces), target.shape[1] // pieces[0].shape[1]
    first = pieces[0].shape[0] - blocks * ep
    return [
        pltpu.make_async_copy(
            pieces[s].at[pl.ds(first + k * ep, ep), :],
            target.at[pl.ds(pl.multiple_of((me ^ s) * ep, 16), ep), pl.ds(k * width, width)],
            sem.at[k, s],
        )
        for s in range(wid)
        for k in range(blocks)
    ]


def move_rows(pairs, sem, slot, first, rows):
    at = pl.multiple_of(first, 16)
    return [
        pltpu.make_async_copy(
            pair[0].at[pl.ds(at, rows), :],
            pair[1].at[pl.ds(pl.multiple_of(first + (pair[2] if len(pair) > 2 else 0), 16), rows), :],
            sem.at[k, slot],
        )
        for k, pair in enumerate(pairs)
    ]


def each(first, count, step, carry=0):
    for k in range(count):
        carry = step(first + k, carry)
    return carry


def begin(copies):
    for copy in copies:
        copy.start()


def finish(copies):
    for copy in copies:
        copy.wait()


def split_kernel(
    er, ep, wid, below, meta, w_r, gain_r, out_r, x_r, dt_r, bias_r, conv_r, conv_b_r, skip_r, log_r, *refs
):
    nar = len(refs) - 4
    outs, (small_o, out_o, rows_s, lanes) = refs[:nar], refs[nar:]
    inner = wid * nar * er
    es = wid * ep
    dr = w_r.shape[1]
    gain = gain_r[...].astype(f32)
    gain = jnp.concatenate([gain, jnp.zeros((1, LANES - dr), f32)], axis=1)
    gain = jnp.broadcast_to(gain, (LANES, LANES)).T[:dr].astype(bf16)
    for half in range(2):
        first = half * (MODS * es + LANES)
        for m in range(MODS):
            row = w_r[m, :, half * inner : (half + 1) * inner].astype(f32)
            for k in range(nar):
                parts = []
                for v in range(wid):
                    parts.append(row[:, (v * nar + k) * er : (v * nar + k + 1) * er])
                    if ep > er:
                        parts.append(jnp.zeros((dr, ep - er), f32))
                rows_s[k, :, first + m * es : first + (m + 1) * es] = jnp.concatenate(parts, axis=1).astype(bf16)
    for s in range(nar):
        rows_s[s, :, MODS * es : MODS * es + LANES] = gain
    for s in range(nar):
        outs[s][...] = rows_s[meta[0] ^ s]
    out_whole = jnp.concatenate([out_r[m].astype(f32) for m in range(MODS)], axis=1)
    if ep > er:
        out_whole = jnp.concatenate([out_whole, jnp.zeros((ep - er, out_whole.shape[1]), f32)], axis=0)
    out_w = out_o.shape[1]
    for k in range(out_whole.shape[1] // out_w):
        out_o[k * ep : (k + 1) * ep, :] = out_whole[:, k * out_w : (k + 1) * out_w].astype(bf16)
    rank = dt_r.shape[1]
    lanes[...] = jnp.zeros_like(lanes)
    for m in range(MODS):
        lanes[m * rank : (m + 1) * rank, :er] = dt_r[m].astype(f32)
    base = MODS * rank
    for at, ref in ((T_BIAS, bias_r), (T_CONV_B, conv_b_r), (T_CONV, conv_r), (T_SKIP, skip_r), (T_LOG, log_r)):
        lanes[base + at : base + at + ref.shape[0], :er] = ref[...].astype(f32)
    turned = lanes[...].T[:ep]
    xw = x_r.shape[2]
    columns = []
    for m in range(MODS):
        part = x_r[m].astype(f32)
        if ep > er:
            part = jnp.concatenate([part, jnp.zeros((ep - er, xw), f32)], axis=0)
        columns += [part, jnp.zeros((ep, LANES - xw), f32)]
    small = jnp.concatenate(columns + [turned], axis=1)
    cols = small.shape[1]
    small_o[...] = jnp.zeros_like(small_o)
    for c in range(-(-ep // below)):
        part = small[c * below : min(ep, (c + 1) * below)]
        small_o[: part.shape[0], c * cols : (c + 1) * cols] = part.astype(bf16)


def join_kernel(meta, *refs):
    pieces, (small, out_rows, front_o, gate_o) = refs[:-4], refs[-4:]
    nar, dr = len(pieces), pieces[0].shape[0]
    row = lax.broadcasted_iota(jnp.int32, (nar * dr, dr), 0)
    col = lax.broadcasted_iota(jnp.int32, (nar * dr, dr), 1)
    joined = sum(
        dot((row == (meta[0] ^ s) * dr + col).astype(bf16), piece[...], 1, 0)
        for s, piece in enumerate(pieces)
    ).astype(bf16)
    front_o[: nar * dr, :] = joined[:, : front_o.shape[1]]
    front_o[nar * dr :, :] = small[...]
    gate_o[: nar * dr, :] = joined[:, front_o.shape[1] :]
    gate_o[nar * dr :, :] = out_rows[...]


T_BIAS, T_CONV_B, T_CONV, T_SKIP, T_LOG = 0, 3, 4, 8, 16


def in_kernel(nar, wid, rpd, taps, ep, rank, meta, *refs):
    toks, w_pieces = refs[:nar], refs[nar : nar + wid]
    hbm_os = refs[nar + wid : nar + wid + 4]
    px_o, kinds_o, w_x, w_dt_o, table_o, gain_o = refs[nar + wid + 4 : nar + wid + 10]
    normed_o, front_o, csum_o, mixed_o, xs, wf, rest, tok_sem, w_sem, rest_sem, out_sem = refs[nar + wid + 10 :]
    outs = list(zip((normed_o, front_o, csum_o, mixed_o), hbm_os))
    n, w, split = meta[0], meta[1], meta[2]
    total, es = csum_o.shape
    width = MODS * es
    rows_w = wf.shape[0] // wid
    piece_rows = toks[0].shape[0]
    copies = []
    cols = rest.shape[1]
    below = w_pieces[0].shape[0] - rows_w
    x_cols = w_x.shape[1]
    for s, piece in enumerate(w_pieces):
        for c in range(-(-ep // below)):
            count = min(below, ep - c * below)
            at = pl.multiple_of((w ^ s) * ep + c * below, 16)
            copies.append(
                pltpu.make_async_copy(
                    piece.at[pl.ds(rows_w, count), pl.ds(c * cols, cols)],
                    rest.at[pl.ds(at, count), :],
                    rest_sem.at[c, s],
                )
            )
    tok_copies, w_copies = [], []
    for s, piece in enumerate(toks):
        at = pl.multiple_of((n ^ s) * piece_rows, 16)
        tok_copies.append(
            pltpu.make_async_copy(piece, xs.at[pl.ds(at, piece_rows), :], tok_sem.at[s])
        )
    for s, piece in enumerate(w_pieces):
        at = pl.multiple_of((w ^ s) * rows_w, 16)
        w_copies.append(
            pltpu.make_async_copy(
                piece.at[pl.ds(0, rows_w), pl.ds(0, wf.shape[1])], wf.at[pl.ds(at, rows_w), :], w_sem.at[s]
            )
        )
    for copy in copies + tok_copies + w_copies:
        copy.start()
    for copy in copies:
        copy.wait()
    w_x[...] = rest[:, :x_cols]
    turned = rest[:, x_cols:].astype(f32).T
    w_dt_o[...] = turned[: MODS * rank].astype(bf16)
    table_o[...] = turned[MODS * rank :]
    for copy in tok_copies:
        copy.wait()
    for p in range(nar):
        tail = xs[(p + 1) * piece_rows - 16 : (p + 1) * piece_rows, :LANES].astype(f32)
        row = lax.broadcasted_iota(jnp.int32, tail.shape, 0)
        for j in range(rpd):
            kinds_o[p * rpd + j] = jnp.max(jnp.where(row == j, tail, 0.0)).astype(jnp.int32)
    for copy in w_copies:
        copy.wait()
    gain = wf[:, width : width + LANES].astype(f32).T[0:1, :]
    gain_o[...] = gain

    def one_run(r, before):
        rows = pl.ds(pl.multiple_of(r * RUN, RUN), RUN)
        kind = kinds_o[r]
        x_at = pl.multiple_of((r // rpd) * piece_rows + (r % rpd) * RUN, 16)
        x = xs[pl.ds(x_at, RUN), :].astype(f32)
        scale = lax.rsqrt(jnp.mean(x * x, axis=1, keepdims=True) + EPSILON)
        normed = (x * scale * gain).astype(bf16)
        normed_o[rows, :] = normed
        front = dot(normed, wf[:, pl.ds(pl.multiple_of(kind * es, LANES), es)], 1, 0)
        front_o[rows, :] = front
        ext = jnp.concatenate([before, front], axis=0)
        place = r * RUN + lax.broadcasted_iota(jnp.int32, (RUN, 1), 0)
        offset = place - jnp.where(place >= split, split, 0)
        csum = jnp.broadcast_to(table_o[T_CONV_B : T_CONV_B + 1, :], (RUN, es))
        for lag in range(taps):
            tap = table_o[T_CONV + taps - 1 - lag : T_CONV + taps - lag, :]
            valid = (offset >= lag).astype(f32)
            csum = csum + tap * ext[8 - lag : 8 - lag + RUN, :] * valid
        csum_o[rows, :] = csum
        mixed = (csum * jax.nn.sigmoid(csum)).astype(bf16)
        mixed_o[rows, :] = mixed
        px = dot(mixed, w_x[:, pl.ds(pl.multiple_of(kind * LANES, LANES), LANES)], 1, 0)
        px_o[:, pl.ds(pl.multiple_of(r * RUN, LANES), RUN)] = px.T[: px_o.shape[0]].astype(bf16)
        return front[RUN - 8 :]

    before = jnp.zeros((8, es), f32)
    size = total // CHUNKS
    for c in range(CHUNKS):
        before = each(c * size // RUN, size // RUN, one_run, before)
        begin(move_rows(outs, out_sem, c, c * size, size))
    for c in range(CHUNKS):
        finish(move_rows(outs, out_sem, c, c * size, size))


def gate_kernel(wid, meta, kinds, *refs):
    pieces, (normed_h, act_h, slope_h, normed_r, act_o, slope_o, wg, w_sem, in_sem, out_sem) = refs[:wid], refs[wid:]
    total, es = act_o.shape
    size = total // CHUNKS
    weights = place_pieces(pieces, wg, w_sem, meta[1], wg.shape[0] // wid)
    arriving = [move_rows([(normed_h, normed_r)], in_sem, c, c * size, size) for c in range(CHUNKS)]
    leaving = [
        move_rows([(act_o, act_h), (slope_o, slope_h)], out_sem, c, c * size, size) for c in range(CHUNKS)
    ]
    begin(weights)
    for copies in arriving:
        begin(copies)
    finish(weights)

    def one_run(r, carry):
        rows = pl.ds(pl.multiple_of(r * RUN, RUN), RUN)
        gate = dot(normed_r[rows, :], wg[:, pl.ds(pl.multiple_of(kinds[r] * es, LANES), es)], 1, 0)
        sig = jax.nn.sigmoid(gate)
        act_o[rows, :] = gate * sig
        slope_o[rows, :] = sig * (1.0 + gate * (1.0 - sig))
        return carry

    for c in range(CHUNKS):
        finish(arriving[c])
        each(c * size // RUN, size // RUN, one_run)
        begin(leaving[c])
    for copies in leaving:
        finish(copies)


def softplus(v):
    return jnp.maximum(v, 0.0) + jnp.log1p(jnp.exp(-jnp.abs(v)))


def scan_kernel(nar, wid, rank, meta, kinds, *refs):
    cots, pieces, refs = refs[:nar], refs[nar : nar + wid], refs[nar + wid :]
    px_r, w_dt, table, mixed_h, act_h = refs[:5]
    parts_h, refs = refs[5 : 5 + nar], refs[5 + nar :]
    gated_h, dgs_h, cot_h, gmix_h, dpre_h, dpx_o, dlow_o, glog_o, gskip_o = refs[:9]
    mixed_r, act_r, cot_r, w_out, dssm_r, ssm_o, gated_o, dgs_o, branch, gmix_o, dpre_o = refs[9:20]
    in_sem, cot_sem, w_sem, mid_sem, part_sem, out_sem = refs[20:26]
    pxs, pre_s, step_s, states, bc, qs, gs, fs, dtk, dtu, r1s, r2s, cblk, bblk, adjs = refs[26:]
    split = meta[2]
    total, es = mixed_r.shape
    ns = states.shape[1]
    groups = es // LANES
    runs = total // RUN
    d, size = cot_r.shape[1], total // nar
    mixed_in = pltpu.make_async_copy(mixed_h, mixed_r, in_sem.at[0])
    arriving = place_w_out(pieces, w_out, w_sem, meta[1]) + place_pieces(cots, cot_r, cot_sem, meta[0], size)
    arriving.append(pltpu.make_async_copy(act_h, act_r, in_sem.at[1]))
    begin([mixed_in] + arriving)
    lane = [slice(g * LANES, (g + 1) * LANES) for g in range(groups)]
    rates = -jnp.exp(table[T_LOG : T_LOG + ns, :])
    r1s[...] = rates
    r2s[...] = rates * LOG2E
    half = ns // 2
    pxs[...] = px_r[...].astype(f32)
    skip = table[T_SKIP : T_SKIP + 1, :]

    def rows_of(r):
        return pl.ds(pl.multiple_of(r * RUN, RUN), RUN)

    k_row = lax.broadcasted_iota(jnp.int32, (ns, LANES), 1)
    own_row = (k_row % ns == lax.broadcasted_iota(jnp.int32, (ns, LANES), 0)) & (k_row < 2 * ns)
    own_row = own_row.astype(f32)
    k_col = lax.broadcasted_iota(jnp.int32, (LANES, 2 * LANES), 0)
    b_or_c = lax.broadcasted_iota(jnp.int32, (LANES, 2 * LANES), 1) // LANES
    ones = (k_col // ns == b_or_c).astype(bf16)

    tile_k = lax.broadcasted_iota(jnp.int32, (LANES, 16 * ns), 0)
    tile_l = lax.broadcasted_iota(jnp.int32, (LANES, 16 * ns), 1)
    tile_b = (tile_k == tile_l % ns).astype(bf16)
    tile_c = (tile_k == tile_l % ns + ns).astype(bf16)
    tile_t = lax.broadcasted_iota(jnp.int32, (RUN, 16 * ns), 0) % 16
    own_t = (tile_t == lax.broadcasted_iota(jnp.int32, (RUN, 16 * ns), 1) // ns).astype(f32)

    def spread(r):
        block = pxs[rank : rank + 2 * ns, pl.ds(pl.multiple_of(r * RUN, LANES), RUN)]
        parts = jnp.concatenate([block, jnp.zeros((LANES - 2 * ns, RUN), f32)], axis=0)
        picked = parts.T[:, None, :] * own_row[None]
        bc[bc_rows(r), :] = dot(picked.reshape(RUN * ns, LANES).astype(bf16), ones, 1, 0)
        cblk[rows_of(r), :] = (dot(parts.T.astype(bf16), tile_c, 1, 0) * own_t).astype(bf16)
        bblk[rows_of(r), :] = (dot(parts.T.astype(bf16), tile_b, 1, 0) * own_t).astype(bf16)

    def bc_rows(r):
        if bc.shape[0] == RUN * ns:
            return pl.ds(0, RUN * ns)
        return pl.ds(pl.multiple_of(r * (RUN * ns), RUN * ns), RUN * ns)

    mixed_in.wait()
    for r in range(runs):
        rows, lanes_at = slice(r * RUN, (r + 1) * RUN), slice(r * RUN, (r + 1) * RUN)
        low = px_r[:rank, lanes_at]
        dlow_o[:, lanes_at] = low
        weights = w_dt[pl.ds(pl.multiple_of(kinds[r] * rank, 16), rank), :]
        pre = dot(low, weights, 0, 0) + table[pl.ds(T_BIAS + kinds[r], 1), :]
        pre_s[rows, :] = pre
        steps = softplus(pre)
        step_s[rows, :] = steps
        place = r * RUN + lax.broadcasted_iota(jnp.int32, (RUN, 1), 0)
        dtk[rows, :] = jnp.where((place == 0) | (place == split), FAR, steps)
        dtu[rows, :] = steps * mixed_r[rows, :].astype(f32)
        if bc.shape[0] > RUN * ns:
            spread(r)

    def row(tile, j, g):
        return jnp.broadcast_to(tile[j : j + 1, lane[g]], (ns, LANES))

    def folded(ref):
        outs = []
        for g in range(groups):
            out = ref[g, pl.ds(0, RUN, stride=half), :]
            for s in range(1, half):
                out = out + ref[g, pl.ds(s, RUN, stride=half), :]
            outs.append(out)
        return jnp.concatenate(outs, axis=1)

    states[0] = jnp.zeros((ns, es), bf16)

    def forward(r, hs):
        rows = rows_of(r)
        if bc.shape[0] == RUN * ns:
            spread(r)

        def eight(i, hs):
            hs = list(hs)
            at = pl.ds(pl.multiple_of(r * RUN + i * 32, 32), 32)
            k8, u8 = dtk[at, :], dtu[at, :]
            bcv = bc.at[bc_rows(r), :].at[pl.ds(pl.multiple_of(i * (32 * ns), 32 * ns), 32 * ns), :]
            stv = states.at[pl.ds(r * RUN + i * 32 + 1, 32)]
            for j in range(32):
                bt = bcv[j * ns : (j + 1) * ns, :LANES]
                for g in range(groups):
                    decay = jnp.exp2(row(k8, j, g) * r2s[:, lane[g]])
                    hs[g] = decay * hs[g] + row(u8, j, g) * bt
                    stv[j, :, lane[g]] = hs[g].astype(bf16)
            return tuple(hs)

        hs = lax.fori_loop(0, RUN // 32, eight, hs)
        for q in range(RUN // 16):
            at = pl.ds(pl.multiple_of(r * RUN + q * 16, 16), 16)
            block = states[pl.ds(r * RUN + q * 16 + 1, 16)].reshape(16 * ns, es)
            ssm_o[at, :] = dot(cblk[at, :], block, 1, 0) + skip * mixed_r[at, :].astype(f32)
        return hs

    zero = jnp.zeros((ns, LANES), f32)
    lax.fori_loop(0, runs, forward, (zero,) * groups)
    gskip_o[...] = jnp.zeros_like(gskip_o)
    finish(arriving)
    leaving = []
    for r in range(runs):
        rows = slice(r * RUN, (r + 1) * RUN)
        wide_at = pl.ds(pl.multiple_of(kinds[r] * d, LANES), d)
        ssm, act = ssm_o[rows, :], act_r[rows, :]
        d_gated = dot(cot_r[rows, :], w_out[:, wide_at], 1, 1)
        dssm_r[rows, :] = d_gated * act
        dgs_o[rows, :] = d_gated * ssm
        gated = (ssm * act).astype(bf16)
        gated_o[rows, :] = gated
        branch[rows, :] = dot(gated, w_out[:, wide_at], 1, 0).astype(bf16)
    for k, (source, target) in enumerate(((gated_o, gated_h), (dgs_o, dgs_h), (cot_r, cot_h))):
        leaving.append(pltpu.make_async_copy(source, target, mid_sem.at[k]))
    for s, part in enumerate(parts_h):
        first = pl.multiple_of((meta[0] ^ s) * size, RUN)
        leaving.append(pltpu.make_async_copy(branch.at[pl.ds(first, size), :], part, part_sem.at[s]))
    begin(leaving)
    gather_k = lax.broadcasted_iota(jnp.int32, (2 * LANES, LANES), 0) // LANES
    gather_l = lax.broadcasted_iota(jnp.int32, (2 * LANES, LANES), 1) // ns
    gather = (gather_k == gather_l).astype(bf16)
    keep_n = lax.broadcasted_iota(jnp.int32, (ns, LANES), 0)
    keep = (lax.broadcasted_iota(jnp.int32, (ns, LANES), 1) % ns == keep_n).astype(f32)

    def backward(back, carry):
        r = runs - 1 - back
        rows = rows_of(r)
        kind = kinds[r]
        if bc.shape[0] == RUN * ns:
            spread(r)

        def eight(back_i, carry):
            ms, hs, gr = [list(part) for part in carry]
            i = RUN // 32 - 1 - back_i
            at = pl.ds(pl.multiple_of(r * RUN + i * 32, 32), 32)
            k8, u8 = dtk[at, :], dtu[at, :]
            y8 = dssm_r[pl.ds(pl.multiple_of(r * RUN + i * 32, 32), 32), :]
            bcv = bc.at[bc_rows(r), :].at[pl.ds(pl.multiple_of(i * (32 * ns), 32 * ns), 32 * ns), :]
            adv = adjs.at[pl.ds(i * 32, 32)]
            qsv = qs.at[:, pl.ds(pl.multiple_of(i * (32 * half), 32 * half), 32 * half), :]
            stv = states.at[pl.ds(r * RUN + i * 32, 32)]
            gsv = gs.at[pl.ds(pl.multiple_of(i * (32 * ns), 32 * ns), 32 * ns), :]
            for j in reversed(range(32)):
                ct = bcv[j * ns : (j + 1) * ns, LANES:]
                gb_sum, gc_sum = None, None
                for g in range(groups):
                    dt = row(k8, j, g)
                    dy = row(y8, j, g)
                    adjoint = dy * ct + ms[g]
                    before = stv[j, :, lane[g]].astype(f32)
                    c_part = dy * hs[g]
                    b_part = adjoint * row(u8, j, g)
                    gb_sum = b_part if gb_sum is None else gb_sum + b_part
                    gc_sum = c_part if gc_sum is None else gc_sum + c_part
                    fold_at = slice(j * half, (j + 1) * half)
                    adv[j, :, lane[g]] = adjoint.astype(bf16)
                    ms[g] = jnp.exp2(dt * r2s[:, lane[g]]) * adjoint
                    weighted = ms[g] * before
                    by_rate = weighted * r1s[:, lane[g]]
                    qsv[g, fold_at, :] = by_rate[:half] + by_rate[half:]
                    gr[g] = gr[g] + weighted * dt
                    hs[g] = before
                gsv[j * ns : (j + 1) * ns, :LANES] = gb_sum.astype(bf16)
                gsv[j * ns : (j + 1) * ns, LANES:] = gc_sum.astype(bf16)
            return tuple(ms), tuple(hs), tuple(gr)

        carry = lax.fori_loop(0, RUN // 32, eight, carry)
        mixed = mixed_r[rows, :].astype(f32)
        by_rate = folded(qs)
        lb = jnp.concatenate(
            [
                dot(
                    bblk[pl.ds(pl.multiple_of(r * RUN + q * 16, 16), 16), :],
                    adjs[q * 16 : (q + 1) * 16].reshape(16 * ns, es),
                    1,
                    0,
                )
                for q in range(RUN // 16)
            ],
            axis=0,
        )
        dssm = dssm_r[rows, :]
        grad_steps = by_rate + lb * mixed
        gmix_o[rows, :] = dssm * skip + lb * step_s[rows, :]
        gskip_o[...] += jnp.sum(dssm * mixed, axis=0, keepdims=True)
        dpre = (grad_steps * jax.nn.sigmoid(pre_s[rows, :])).astype(bf16)
        dpre_o[rows, :] = dpre
        weights = w_dt[pl.ds(pl.multiple_of(kind * rank, 16), rank), :]
        dlow = dot(weights, dpre, 1, 1)
        sums = dot(gs[...], gather, 1, 0).reshape(RUN, ns, LANES) * keep[None]
        fs[...] = (sums[:, :half] + sums[:, half:]).reshape(RUN * half, LANES)
        dbc = fs[pl.ds(0, RUN, stride=half), :]
        for s in range(1, half):
            dbc = dbc + fs[pl.ds(s, RUN, stride=half), :]
        dbc = dbc.T[: 2 * ns]
        at = pl.ds(pl.multiple_of(r * RUN, LANES), RUN)
        dpx_o[:rank, at] = dlow.astype(bf16)
        dpx_o[rank:, at] = dbc.astype(bf16)
        begin(move_rows([(gmix_o, gmix_h), (dpre_o, dpre_h)], out_sem, r, r * RUN, RUN))
        return carry

    last = tuple(states[total, :, lane[g]].astype(f32) for g in range(groups))
    done = lax.fori_loop(0, runs, backward, ((zero,) * groups, last, (zero,) * groups))
    for g in range(groups):
        glog_o[:, lane[g]] = done[2][g] * rates[:, lane[g]]

    def settle(r, carry):
        finish(move_rows([(gmix_o, gmix_h), (dpre_o, dpre_h)], out_sem, r, r * RUN, RUN))
        return carry

    lax.fori_loop(0, runs, settle, 0)
    finish(leaving)


def scan_call(rank, xw, ns, meta, kinds, cots, pieces, px, w_dt_l, table, mixed, act):
    (total, es), (own, d) = mixed.shape, cots[0].shape
    nar, wid = len(cots), len(pieces)
    out_cols = MODS * d
    bc_runs = total // RUN if total * ns * 2 * LANES * 4 <= 20 * 1024 * 1024 else 1
    return call(
        functools.partial(scan_kernel, nar, wid, rank),
        [((own, d), bf16, "a")] * nar
        + [
            ((total, es), bf16, "a"),
            ((total, es), f32, "a"),
            ((total, d), bf16, "a"),
            ((total, es), f32, "a"),
            ((total, es), bf16, "a"),
            ((xw, total), bf16, "v"),
            ((rank, total), bf16, "v"),
            ((ns, es), f32, "v"),
            ((1, es), f32, "v"),
        ],
        [(meta, "s"), (kinds, "s")]
        + [(p, "a") for p in cots]
        + [(p, "a") for p in pieces]
        + [(px, "v"), (w_dt_l, "v"), (table, "v"), (mixed, "a"), (act, "a")],
        [
            pltpu.VMEM((total, es), bf16),
            pltpu.VMEM((total, es), f32),
            pltpu.VMEM((total, d), bf16),
            pltpu.VMEM((es, out_cols), bf16),
            pltpu.VMEM((total, es), f32),
            pltpu.VMEM((total, es), f32),
            pltpu.VMEM((total, es), bf16),
            pltpu.VMEM((total, es), f32),
            pltpu.VMEM((total, d), bf16),
            pltpu.VMEM((total, es), f32),
            pltpu.VMEM((total, es), bf16),
            pltpu.SemaphoreType.DMA((2,)),
            pltpu.SemaphoreType.DMA((nar,)),
            pltpu.SemaphoreType.DMA((out_cols // pieces[0].shape[1], wid)),
            pltpu.SemaphoreType.DMA((3,)),
            pltpu.SemaphoreType.DMA((nar,)),
            pltpu.SemaphoreType.DMA((2, total // RUN)),
            pltpu.VMEM((xw, total), f32),
            pltpu.VMEM((total, es), f32),
            pltpu.VMEM((total, es), f32),
            pltpu.VMEM((total + 1, ns, es), bf16),
            pltpu.VMEM((bc_runs * RUN * ns, 2 * LANES), f32),
            pltpu.VMEM((es // LANES, RUN * ns // 2, LANES), f32),
            pltpu.VMEM((RUN * ns, 2 * LANES), bf16),
            pltpu.VMEM((RUN * ns // 2, LANES), f32),
            pltpu.VMEM((total, es), f32),
            pltpu.VMEM((total, es), f32),
            pltpu.VMEM((ns, es), f32),
            pltpu.VMEM((ns, es), f32),
            pltpu.VMEM((total, 16 * ns), bf16),
            pltpu.VMEM((total, 16 * ns), bf16),
            pltpu.VMEM((RUN, ns, es), bf16),
        ],
        us=40.0,
    )


def split_rows(acc, place, rows):
    return acc[pl.ds(pl.multiple_of(place * rows, 16), rows), :]


def grads_kernel(wid, ep, rank, meta, kinds, *refs):
    hbm, (dlow_r, glog_r, gskip_r) = refs[:6], refs[6:9]
    dgate_h, gate_h, w_out_h, table_o = refs[9:13]
    rows_in, (dgate_o, gate_o, w_out_o, acc_out, acc_in, in_sem, out_sem, block_sem) = refs[13:19], refs[19:]
    gated_r, dgs_r, slope_r, cot_r, normed_r, dpre_r = rows_in
    total, es = gated_r.shape
    d = cot_r.shape[1]
    size = total // CHUNKS
    arriving = [move_rows(list(zip(hbm, rows_in)), in_sem, c, c * size, size) for c in range(CHUNKS)]
    leaving = [move_rows([(dgate_o, dgate_h)], out_sem, c, c * size, size) for c in range(CHUNKS)]
    for copies in arriving:
        begin(copies)
    acc_out[...] = jnp.zeros_like(acc_out)
    acc_in[...] = jnp.zeros_like(acc_in)
    table_o[...] = jnp.zeros_like(table_o)
    base = MODS * rank

    def one_run(r, carry):
        rows = pl.ds(pl.multiple_of(r * RUN, RUN), RUN)
        kind = kinds[r]
        wide_at = pl.ds(pl.multiple_of(kind * d, LANES), d)
        es_at = pl.ds(pl.multiple_of(kind * es, LANES), es)
        acc_out[:, wide_at] += dot(gated_r[rows, :], cot_r[rows, :], 0, 0)
        dgate = (dgs_r[rows, :] * slope_r[rows, :]).astype(bf16)
        dgate_o[rows, :] = dgate
        acc_in[:, es_at] += dot(normed_r[rows, :], dgate, 0, 0)
        dpre = dpre_r[rows, :]
        low = dlow_r[:, pl.ds(pl.multiple_of(r * RUN, LANES), RUN)]
        table_o[pl.ds(pl.multiple_of(kind * rank, 8), rank), :] += dot(low, dpre, 1, 0)
        table_o[pl.ds(base + T_BIAS + kind, 1), :] += jnp.sum(dpre.astype(f32), axis=0, keepdims=True)
        return carry

    for c in range(CHUNKS):
        finish(arriving[c])
        each(c * size // RUN, size // RUN, one_run)
        begin(leaving[c])
    in_rows = acc_in.shape[0] // wid
    block_copies = []
    for k, (source, target) in enumerate(((gate_o, gate_h), (w_out_o, w_out_h))):
        for v in range(wid):
            if k == 0:
                gate_o[v] = acc_in[v * in_rows : (v + 1) * in_rows, :].astype(bf16)
            else:
                w_out_o[v] = acc_out[v * ep : (v + 1) * ep, :].astype(bf16)
            block_copies.append(pltpu.make_async_copy(source.at[v], target.at[v], block_sem.at[k, v]))
            block_copies[-1].start()
    table_o[base + T_SKIP : base + T_SKIP + 1, :] = gskip_r[...]
    table_o[base + T_LOG : base + T_LOG + glog_r.shape[0], :] = glog_r[...]
    for copies in leaving + [block_copies]:
        finish(copies)


def pair_kernel(chips, meta, same, peer, *outs):
    chip = meta[1] // 2
    for s in range(chips):
        outs[s][...] = (same[chip ^ s].astype(f32) + peer[chip ^ s].astype(f32)).astype(bf16)


def conv_kernel(nar, wid, taps, ep, meta, kinds, *refs):
    dpx_pieces = refs[:nar]
    table, w_x, table_r = refs[nar : nar + 3]
    hbm = refs[nar + 3 : nar + 8]
    dfront_h, same_h, peer_h = refs[nar + 8 : nar + 11]
    rows_in = refs[nar + 11 : nar + 16]
    dfront_o, same_o, peer_o, acc_in, acc_x, small, turned, in_sem, out_sem, block_sem = refs[nar + 16 :]
    gmix_r, csum_r, front_r, mixed_r, normed_r = rows_in
    split = meta[2]
    total, es = gmix_r.shape
    runs = total // RUN
    size = total // CHUNKS
    moves = [(a, b, 16) if b is front_r else (a, b) for a, b in zip(hbm, rows_in)]
    arriving = [move_rows(moves, in_sem, c, c * size, size) for c in range(CHUNKS)]
    leaving = [move_rows([(dfront_o, dfront_h)], out_sem, c, c * size, size) for c in range(CHUNKS)]
    for c in reversed(range(CHUNKS)):
        begin(arriving[c])
    front_r[0:16, :] = jnp.zeros((16, es), f32)
    acc_in[...] = jnp.zeros_like(acc_in)
    acc_x[...] = jnp.zeros_like(acc_x)
    small[...] = jnp.zeros_like(small)
    xw = dpx_pieces[0].shape[0]

    def one_run(back, later):
        r = runs - 1 - back
        rows = pl.ds(pl.multiple_of(r * RUN, RUN), RUN)
        kind = kinds[r]
        lanes_at = pl.ds(pl.multiple_of(r * RUN, LANES), RUN)
        dpx = sum(piece[:, lanes_at].astype(f32) for piece in dpx_pieces)
        dpx = jnp.concatenate([dpx, jnp.zeros((LANES - xw, RUN), f32)], axis=0).T.astype(bf16)
        x_at = pl.ds(pl.multiple_of(kind * LANES, LANES), LANES)
        acc_x[:, x_at] += dot(mixed_r[rows, :], dpx, 0, 0)
        gmix = gmix_r[rows, :] + dot(dpx, w_x[:, x_at], 1, 1)
        csum = csum_r[rows, :]
        sig = jax.nn.sigmoid(csum)
        dc = gmix * sig * (1.0 + csum * (1.0 - sig))
        place = r * RUN + lax.broadcasted_iota(jnp.int32, (RUN + 8, 1), 0)
        offset = place - jnp.where(place >= split, split, 0)
        ext = jnp.concatenate([dc, later], axis=0)
        lagged = front_r[pl.ds(pl.multiple_of(r * RUN + 8, 8), RUN + 8), :]
        d_front = jnp.zeros((RUN, es), f32)
        for lag in range(taps):
            tap = taps - 1 - lag
            masked = ext * (offset >= lag).astype(f32)
            d_front = d_front + table[T_CONV + tap : T_CONV + tap + 1, :] * masked[lag : lag + RUN, :]
            small[T_CONV + tap : T_CONV + tap + 1, :] += jnp.sum(
                masked[:RUN] * lagged[8 - lag : 8 - lag + RUN, :], axis=0, keepdims=True
            )
        small[T_CONV_B : T_CONV_B + 1, :] += jnp.sum(dc, axis=0, keepdims=True)
        d_front = d_front.astype(bf16)
        dfront_o[rows, :] = d_front
        acc_in[:, pl.ds(pl.multiple_of(kind * es, LANES), es)] += dot(normed_r[rows, :], d_front, 0, 0)
        return dc[:8]

    later = jnp.zeros((8, es), f32)
    for c in reversed(range(CHUNKS)):
        if c == CHUNKS - 1:
            finish(arriving[c])
        if c:
            finish(arriving[c - 1])
        back = (CHUNKS - 1 - c) * size // RUN
        later = each(back, size // RUN, one_run, later)
        begin(leaving[c])
    in_rows, width = acc_in.shape[0] // wid, acc_in.shape[1]
    base = table_r.shape[0] - small.shape[0]
    rest = jnp.concatenate([table_r[:base, :], table_r[base:, :] + small[...]], axis=0)
    rest = jnp.concatenate([rest, jnp.zeros((256 - rest.shape[0], es), f32)], axis=0).T
    x_cols = acc_x.shape[1]
    turned[:, :x_cols] = acc_x[...].astype(bf16)
    turned[:, x_cols : x_cols + 256] = rest.astype(bf16)
    turned[:, x_cols + 256 :] = jnp.zeros((es, width - x_cols - 256), bf16)
    core = meta[1] & 1
    block_copies = []
    for k, (ref, out, parity) in enumerate(((peer_o, peer_h, 1 - core), (same_o, same_h, core))):
        for c in range(wid // 2):
            place = 2 * c + parity
            ref[c, :in_rows, :] = split_rows(acc_in, place, in_rows).astype(bf16)
            ref[c, in_rows:, :] = split_rows(turned, place, ep)
            block_copies.append(pltpu.make_async_copy(ref.at[c], out.at[c], block_sem.at[k, c]))
            block_copies[-1].start()
    for copies in leaving + [block_copies]:
        finish(copies)


def normed_kernel(nar, wid, meta, kinds, *refs):
    fronts, gates = refs[:wid], refs[wid : 2 * wid]
    dfront_h, dgate_h = refs[2 * wid : 2 * wid + 2]
    outs = refs[2 * wid + 2 : 2 * wid + 2 + nar]
    dfront_r, dgate_r, wf, wg, dn, f_sem, g_sem, in_sem, part_sem = refs[2 * wid + 2 + nar :]
    total, es = dfront_r.shape
    size = total // nar
    weights = place_pieces(fronts, wf, f_sem, meta[1], wf.shape[0] // wid)
    weights += place_pieces(gates, wg, g_sem, meta[1], wg.shape[0] // wid)
    firsts = [(meta[0] ^ s) * size for s in range(nar)]
    arriving = [
        move_rows([(dfront_h, dfront_r), (dgate_h, dgate_r)], in_sem, s, firsts[s], size) for s in range(nar)
    ]
    part_copies = [
        pltpu.make_async_copy(dn.at[pl.ds(pl.multiple_of(firsts[s], RUN), size), :], outs[s], part_sem.at[s])
        for s in range(nar)
    ]
    begin(weights)
    for s in reversed(range(nar)):
        begin(arriving[s])
    finish(weights)

    def one_run(r, carry):
        rows = pl.ds(pl.multiple_of(r * RUN, RUN), RUN)
        at = pl.ds(pl.multiple_of(kinds[r] * es, LANES), es)
        dn[rows, :] = (dot(dfront_r[rows, :], wf[:, at], 1, 1) + dot(dgate_r[rows, :], wg[:, at], 1, 1)).astype(bf16)
        return carry

    for s in reversed(range(nar)):
        finish(arriving[s])
        first = (meta[0] ^ s) * (size // RUN)
        each(first, size // RUN, one_run)
        part_copies[s].start()
    finish(part_copies)


def total_gate_kernel(blocks, out):
    out[...] = sum(blocks[v].astype(f32) for v in range(blocks.shape[0])).astype(bf16)


def total_out_kernel(er, blocks, out):
    d = out.shape[2]
    summed = sum(blocks[v, :er, :].astype(f32) for v in range(blocks.shape[0]))
    for m in range(MODS):
        out[m] = summed[:, m * d : (m + 1) * d]


def total_b_kernel(nar, chips, er, rank, taps, ns, meta, *refs):
    pieces, gate_r, outs = refs[:chips], refs[chips], refs[chips + 1 : chips + 1 + nar]
    x_o, dt_o, bias_o, conv_o, conv_b_o, log_o, skip_o, rows_s = refs[chips + 1 + nar :]
    dr, width = outs[0].shape[0], gate_r.shape[1]
    in_rows = nar * dr
    summed = sum(piece[...].astype(f32) for piece in pieces)
    gate = gate_r[...].astype(f32)
    for k in range(nar):
        rows_s[k, :, :width] = summed[k * dr : (k + 1) * dr].astype(bf16)
        rows_s[k, :, width:] = gate[k * dr : (k + 1) * dr].astype(bf16)
    for s in range(nar):
        outs[s][...] = rows_s[meta[0] ^ s]
    rest = summed[in_rows:]
    x_cols = MODS * LANES
    for m in range(MODS):
        x_o[m] = rest[:er, m * LANES : m * LANES + x_o.shape[2]]
    lanes = rest[:, x_cols : x_cols + 256]
    pad = LANES - lanes.shape[0]
    turned = jnp.concatenate([lanes, jnp.zeros((pad, 256), f32)], axis=0).T[:, :er]
    base = MODS * rank
    for m in range(MODS):
        dt_o[m] = turned[m * rank : (m + 1) * rank]
    bias_o[...] = turned[base + T_BIAS : base + T_BIAS + MODS]
    conv_o[...] = turned[base + T_CONV : base + T_CONV + taps]
    conv_b_o[...] = turned[base + T_CONV_B : base + T_CONV_B + 1]
    skip_o[...] = turned[base + T_SKIP : base + T_SKIP + 1]
    log_o[...] = turned[base + T_LOG : base + T_LOG + ns]


def tokens_kernel(x_r, cot_r, gain_r, *refs):
    pieces, out = refs[:-1], refs[-1]
    x = x_r[...].astype(f32)
    scale = lax.rsqrt(jnp.mean(x * x, axis=1, keepdims=True) + EPSILON)
    q = sum(piece[...].astype(f32) for piece in pieces) * gain_r[...]
    dotted = jnp.mean(q * x, axis=1, keepdims=True)
    out[...] = (cot_r[...].astype(f32) + scale * q - x * (scale * scale * scale) * dotted).astype(bf16)


def mixed_kernel(x_r, *refs):
    pieces, out = refs[:-1], refs[-1]
    out[...] = (x_r[...].astype(f32) + sum(piece[...].astype(f32) for piece in pieces)).astype(bf16)


def in_order(parts, er, ep, wid):
    return jnp.concatenate([part[:, v * ep : v * ep + er] for v in range(wid) for part in parts], axis=1)


def w_in_kernel(nar, wid, er, ep, meta, *refs):
    pieces, (w_h, gain_r, grad_h, gain_o, rows_s, w_r, grad_s, w_sem, out_sem) = refs[:nar], refs[nar:]
    dr = pieces[0].shape[0]
    es, inner = wid * ep, wid * nar * er
    loading = pltpu.make_async_copy(w_h, w_r, w_sem)
    loading.start()
    for s in range(nar):
        rows_s[meta[0] ^ s] = pieces[s][...].astype(f32)
    sums, storing = 0.0, []
    for m in range(MODS):
        for half in range(2):
            first = (half * MODS + m) * es
            row = in_order([rows_s[k, :, first : first + es] for k in range(nar)], er, ep, wid)
            at = slice(half * inner, (half + 1) * inner)
            grad_s[m, :, at] = row
            if m + half == 0:
                loading.wait()
            sums = sums + jnp.sum(row * w_r[m, :, at].astype(f32), axis=1, keepdims=True)
        storing.append(pltpu.make_async_copy(grad_s.at[m], grad_h.at[m], out_sem.at[m]))
        storing[m].start()
    sums = jnp.broadcast_to(sums, (dr, LANES))
    sums = jnp.concatenate([sums, jnp.zeros((LANES - dr, LANES), f32)], axis=0).T[0:1, :dr]
    gain_o[...] = sums / gain_r[...].astype(f32)
    finish(storing)


def body(
    tokens,
    norm_gain,
    w_in,
    conv_w,
    conv_b,
    w_x,
    w_dt,
    dt_bias,
    a_log,
    d_skip,
    w_out,
    mod_ids,
    split_at,
    cotangent,
):
    nar, wid = lax.axis_size("narrow"), lax.axis_size("wide")
    chips = wid // 2
    n, w = lax.axis_index("narrow"), lax.axis_index("wide")
    own, d = tokens.shape
    total = nar * own
    rpd = own // RUN
    rank, xw, ns, taps = w_dt.shape[0], w_x.shape[2], a_log.shape[1], conv_w.shape[0]
    er = w_out.shape[0]
    inner = er * nar * wid
    ep = -(-er // 16) * 16
    es = ep * wid
    dr = w_in.shape[0]
    width = MODS * es
    meta = jnp.stack([n, w, split_at[0]]).astype(jnp.int32)

    front_w = width + LANES
    gain_row = norm_gain[None]
    w_in_m = w_in.transpose(1, 0, 2)
    out_cols, x_cols = MODS * d, MODS * LANES
    table_rows = T_LOG + ns
    small_cols = x_cols + 256
    blocks = front_w // small_cols
    below = -(-(-(-ep // blocks)) // 16) * 16
    res = call(
        functools.partial(split_kernel, er, ep, wid, below),
        [((dr, front_w + width), bf16, "v")] * nar
        + [((below, front_w), bf16, "v"), ((ep * (out_cols // width), width), bf16, "v")],
        [(meta, "s")]
        + [
            (a, "v")
            for a in (
                w_in_m,
                gain_row,
                w_out.transpose(1, 0, 2),
                w_x.transpose(1, 0, 2),
                w_dt.transpose(1, 0, 2),
                dt_bias,
                conv_w,
                conv_b[None],
                d_skip[None],
                a_log.T,
            )
        ],
        [
            pltpu.VMEM((nar, dr, front_w + width), bf16),
            pltpu.VMEM((256, LANES), f32),
        ],
        us=3.0,
    )
    parts, (small, out_rows) = res[:nar], res[nar:]

    parts = scatter_narrow(parts)
    front_rows, gate_rows = call(
        join_kernel,
        [
            ((nar * dr + below, front_w), bf16, "v"),
            ((nar * dr + out_rows.shape[0], width), bf16, "v"),
        ],
        [(meta, "s")] + [(p, "v") for p in parts] + [(small, "v"), (out_rows, "v")],
        us=2.0,
    )
    front_near = near_wide(front_rows)
    front_pieces = far_wide(front_near)
    run_kinds = mod_ids.reshape(rpd, RUN)[:, :1].astype(bf16)
    tail = jnp.pad(jnp.broadcast_to(run_kinds, (rpd, d)), ((0, 16 - rpd), (0, 0)))
    tok_pieces = relay_narrow(jnp.concatenate([tokens, tail], axis=0))
    gate_near = near_wide(after(gate_rows, *front_near[1:]))
    normed, front, csum, mixed, px, kinds, w_x_l, w_dt_l, table, gain_full = call(
        functools.partial(in_kernel, nar, wid, rpd, taps, ep, rank),
        [
            ((total, d), bf16, "a"),
            ((total, es), f32, "a"),
            ((total, es), f32, "a"),
            ((total, es), bf16, "a"),
            ((xw, total), bf16, "v"),
            ((nar * rpd,), jnp.int32, "s"),
            ((es, x_cols), bf16, "v"),
            ((MODS * rank, es), bf16, "v"),
            ((256 - MODS * rank, es), f32, "v"),
            ((1, d), f32, "v"),
        ],
        [(meta, "s")] + [(p, "a") for p in tok_pieces] + [(p, "a") for p in front_pieces],
        [
            pltpu.VMEM((total, d), bf16),
            pltpu.VMEM((total, es), f32),
            pltpu.VMEM((total, es), f32),
            pltpu.VMEM((total, es), bf16),
            pltpu.VMEM((nar * (own + 16), d), bf16),
            pltpu.VMEM((d, front_w), bf16),
            pltpu.VMEM((es, small_cols), bf16),
            pltpu.SemaphoreType.DMA((nar,)),
            pltpu.SemaphoreType.DMA((wid,)),
            pltpu.SemaphoreType.DMA((-(-ep // below), wid)),
            pltpu.SemaphoreType.DMA((4, CHUNKS)),
        ],
        us=9.0,
    )
    cot_pieces = relay_narrow(after(cotangent, *tok_pieces[1:]), px)
    gate_pieces = far_wide([after(piece, px) for piece in gate_near])
    act, slope = call(
        functools.partial(gate_kernel, wid),
        [((total, es), f32, "a")] * 2,
        [(meta, "s"), (kinds, "s")]
        + [(p, "a") for p in gate_pieces]
        + [(after(normed, *cot_pieces[1:3]), "a")],
        [
            pltpu.VMEM((total, d), bf16),
            pltpu.VMEM((total, es), f32),
            pltpu.VMEM((total, es), f32),
            pltpu.VMEM((d, width), bf16),
            pltpu.SemaphoreType.DMA((wid,)),
            pltpu.SemaphoreType.DMA((1, CHUNKS)),
            pltpu.SemaphoreType.DMA((2, CHUNKS)),
        ],
        us=0.1,
    )
    px_total = add_narrow(px, act, cot_pieces[-1])
    res = scan_call(
        rank, xw, ns, meta, kinds, cot_pieces, gate_pieces, px_total, w_dt_l, table, mixed, act
    )
    branch_parts, (gated, dgs, cot, gmix, dpre, dpx, dlow, glog, gskip) = res[:nar], res[nar:]
    dpx_pieces = gather_narrow(dpx)
    branch_pieces = scatter_narrow(branch_parts)
    in_rows = d // wid
    dgate, gate_blocks, w_out_blocks, table_g = call(
        functools.partial(grads_kernel, wid, ep, rank),
        [
            ((total, es), bf16, "a"),
            ((wid, in_rows, width), bf16, "a"),
            ((wid, ep, out_cols), bf16, "a"),
            ((MODS * rank + table_rows, es), f32, "v"),
        ],
        [(meta, "s"), (kinds, "s")]
        + [(a, "a") for a in (gated, dgs, slope, cot, normed, dpre)]
        + [(a, "v") for a in (dlow, glog, gskip)],
        [
            pltpu.VMEM((total, es), bf16),
            pltpu.VMEM((total, es), f32),
            pltpu.VMEM((total, es), f32),
            pltpu.VMEM((total, d), bf16),
            pltpu.VMEM((total, d), bf16),
            pltpu.VMEM((total, es), bf16),
            pltpu.VMEM((total, es), bf16),
            pltpu.VMEM((wid, in_rows, width), bf16),
            pltpu.VMEM((wid, ep, out_cols), bf16),
            pltpu.VMEM((es, out_cols), f32),
            pltpu.VMEM((d, width), f32),
            pltpu.SemaphoreType.DMA((6, CHUNKS)),
            pltpu.SemaphoreType.DMA((1, CHUNKS)),
            pltpu.SemaphoreType.DMA((2, wid)),
        ],
        us=9.0,
    )

    def over_wide(same, peer, *earlier):
        peer = swap(peer, "wide", 1)
        same = after(same, *earlier) if earlier else same
        parts = call(
            functools.partial(pair_kernel, chips),
            [(same.shape[1:], bf16, "v")] * chips,
            [(meta, "s"), (same, "v"), (peer, "v")],
            us=3.0,
        )
        return [parts[0]] + [swap(parts[s], "wide", 2 * s) for s in range(1, chips)]

    gate_blocks = lax.all_to_all(gate_blocks, "wide", 0, 0)
    rows_b = in_rows + ep
    dfront, same_b, peer_b = call(
        functools.partial(conv_kernel, nar, wid, taps, ep),
        [((total, es), bf16, "a")] + [((chips, rows_b, width), bf16, "a")] * 2,
        [(meta, "s"), (kinds, "s")]
        + [(p, "v") for p in dpx_pieces]
        + [(a, "v") for a in (table, w_x_l, table_g)]
        + [(a, "a") for a in (gmix, csum, front, mixed, normed)],
        [
            pltpu.VMEM((total, es), f32),
            pltpu.VMEM((total, es), f32),
            pltpu.VMEM((total + 16, es), f32),
            pltpu.VMEM((total, es), bf16),
            pltpu.VMEM((total, d), bf16),
            pltpu.VMEM((total, es), bf16),
            pltpu.VMEM((chips, rows_b, width), bf16),
            pltpu.VMEM((chips, rows_b, width), bf16),
            pltpu.VMEM((d, width), f32),
            pltpu.VMEM((es, x_cols), f32),
            pltpu.VMEM((table_rows, es), f32),
            pltpu.VMEM((es, width), bf16),
            pltpu.SemaphoreType.DMA((5, CHUNKS)),
            pltpu.SemaphoreType.DMA((1, CHUNKS)),
            pltpu.SemaphoreType.DMA((2, chips)),
        ],
        us=12.0,
    )
    dn_parts = call(
        functools.partial(normed_kernel, nar, wid),
        [((own, d), bf16, "a")] * nar,
        [(meta, "s"), (kinds, "s")]
        + [(p, "a") for p in front_pieces]
        + [(p, "a") for p in gate_pieces]
        + [(dfront, "a"), (dgate, "a")],
        [
            pltpu.VMEM((total, es), bf16),
            pltpu.VMEM((total, es), bf16),
            pltpu.VMEM((d, width), bf16),
            pltpu.VMEM((d, width), bf16),
            pltpu.VMEM((total, d), bf16),
            pltpu.SemaphoreType.DMA((wid,)),
            pltpu.SemaphoreType.DMA((wid,)),
            pltpu.SemaphoreType.DMA((2, nar)),
            pltpu.SemaphoreType.DMA((nar,)),
        ],
        us=30.0,
    )
    pieces_b = over_wide(same_b, peer_b, dn_parts[0])
    dn_pieces, dn_kept = sum_narrow(dn_parts, pieces_b[0])

    mixed_out = call(
        mixed_kernel,
        [((own, d), bf16, "v")],
        [(tokens, "v")] + [(p, "v") for p in after(tuple(branch_pieces), pieces_b[0])],
        us=2.0, small=True,
    )[0]
    gate_sum = call(
        total_gate_kernel,
        [((in_rows, width), bf16, "v")],
        [(after(gate_blocks, mixed_out, dn_kept), "v")],
        us=2.0, small=True,
    )[0]
    res = call(
        functools.partial(total_b_kernel, nar, chips, er, rank, taps, ns),
        [((dr, 2 * width), bf16, "v")] * nar
        + [
            ((MODS, er, xw), f32, "v"),
            ((MODS, rank, er), f32, "v"),
            ((MODS, er), f32, "v"),
            ((taps, er), f32, "v"),
            ((1, er), f32, "v"),
            ((ns, er), f32, "v"),
            ((1, er), f32, "v"),
        ],
        [(meta, "s")] + [(p, "v") for p in pieces_b] + [(gate_sum, "v")],
        [pltpu.VMEM((nar, dr, 2 * width), bf16)],
        us=3.0, small=True,
    )
    back_parts = res[:nar]
    grad_w_x, grad_w_dt, grad_dt_bias, grad_conv_w, grad_conv_b, grad_log, grad_skip = res[nar:]
    back_pieces = scatter_narrow(back_parts)
    grad_tokens = call(
        tokens_kernel,
        [((own, d), bf16, "v")],
        [(tokens, "v"), (cotangent, "v"), (gain_full, "v")]
        + [(p, "v") for p in dn_pieces],
        us=0.1, small=True,
    )[0]
    w_out_blocks = lax.all_to_all(after(w_out_blocks, gate_sum), "wide", 0, 0)
    grad_w_in, grad_gain = call(
        functools.partial(w_in_kernel, nar, wid, er, ep),
        [((MODS, dr, 2 * inner), f32, "a"), ((1, dr), f32, "v")],
        [(meta, "s")] + [(p, "v") for p in back_pieces] + [(after(w_in_m, grad_tokens), "a"), (gain_row, "v")],
        [
            pltpu.VMEM((nar, dr, 2 * width), f32),
            pltpu.VMEM((MODS, dr, 2 * inner), bf16),
            pltpu.VMEM((MODS, dr, 2 * inner), f32),
            pltpu.SemaphoreType.DMA(()),
            pltpu.SemaphoreType.DMA((MODS,)),
        ],
        us=13.0, small=True,
    )
    grad_w_out = call(
        functools.partial(total_out_kernel, er),
        [((MODS, er, d), f32, "v")],
        [(after(w_out_blocks, grad_gain), "v")],
        us=3.0, small=True,
    )[0]
    grad_w_in, grad_w_out = grad_w_in.transpose(1, 0, 2), grad_w_out.transpose(1, 0, 2)
    grad_w_x, grad_w_dt = grad_w_x.transpose(1, 0, 2), grad_w_dt.transpose(1, 0, 2)
    grad_log = grad_log.T
    return (
        mixed_out,
        grad_tokens,
        grad_gain[0],
        grad_w_in,
        grad_conv_w,
        grad_conv_b[0],
        grad_w_x,
        grad_w_dt,
        grad_dt_bias,
        grad_log,
        grad_skip[0],
        grad_w_out,
    )


def solution(mesh):
    both = ("wide", "narrow")
    return jax.shard_map(
        body,
        mesh=mesh,
        in_specs=(
            P(both, None),
            P(both),
            P(both, None, None),
            P(None, both),
            P(both),
            P(both, None, None),
            P(None, None, both),
            P(None, both),
            P(both, None),
            P(both),
            P(both, None, None),
            P(both),
            P("wide"),
            P(both, None),
        ),
        out_specs=(
            P(both, None),
            P(both, None),
            P(both),
            P(both, None, None),
            P(None, both),
            P(both),
            P(both, None, None),
            P(None, None, both),
            P(None, both),
            P(both, None),
            P(both),
            P(both, None, None),
        ),
        check_vma=False,
    )
```

```python
import functools
import math

import jax
import jax.numpy as jnp
from jax import lax
from jax.experimental import pallas as pl
from jax.experimental.pallas import tpu as pltpu
from jax.sharding import PartitionSpec as P

MODS = 3
RUN = 128
CHUNKS = 4
LANES = 128
EPSILON = 1e-05
LOG2E = 1.4426950408889634
FAR = 1e30
VMEM_LIMIT = 60 * 1024 * 1024
VMEM_SPARE = 6 * 1024 * 1024

f32 = jnp.float32
bf16 = jnp.bfloat16


def swap(block, axis, flip):
    count = lax.axis_size(axis)
    return lax.ppermute(block, axis, [(i, i ^ flip) for i in range(count)])


def gather_narrow(block):
    return [block] + [swap(block, "narrow", s) for s in range(1, lax.axis_size("narrow"))]


def relay_narrow(block, *earlier):
    count = lax.axis_size("narrow")
    pieces = {0: block}
    for s in sorted(range(1, count), key=lambda s: (s.bit_count(), -s)):
        low_bit = s & -s
        if s == low_bit:
            pieces[s] = swap(block, "narrow", s)
        else:
            pieces[s] = swap(after(pieces[s ^ low_bit], *earlier), "narrow", low_bit)
    return [pieces[s] for s in range(count)]


def add_narrow(block, *beside):
    flip = lax.axis_size("narrow") // 2
    while flip:
        got = swap(block, "narrow", flip)
        block = (after(block, *beside).astype(f32) + got.astype(f32)).astype(bf16)
        flip //= 2
        beside = ()
    return block


def scatter_narrow(parts):
    arrived = [swap(parts[s], "narrow", s) for s in range(len(parts) - 1, 0, -1)]
    return [parts[0]] + arrived[::-1]


def sum_narrow(parts, *earlier):
    parts = list(parts)
    arrived = [parts[0]]
    for s in range(len(parts) - 1, 0, -1):
        low_bit = s & -s
        got = swap(parts[s], "narrow", low_bit)
        if s == low_bit:
            arrived.append(got)
        else:
            rest = s ^ low_bit
            parts[rest] = (after(parts[rest], *earlier).astype(f32) + got.astype(f32)).astype(bf16)
    return arrived, parts[-2]


def near_wide(block):
    return [block] + [swap(block, "wide", 2 * s) for s in range(1, lax.axis_size("wide") // 2)]


def far_wide(near):
    return [piece for block in near for piece in (block, swap(block, "wide", 1))]


def after(value, *earlier):
    return lax.optimization_barrier((value,) + earlier)[0] if earlier else value


def dot(a, b, ca, cb):
    return lax.dot_general(a, b, (((ca,), (cb,)), ((), ())), preferred_element_type=f32)


def call(kernel, outs, ins, scratch=(), us=1.0, small=False):
    spaces = {"v": pltpu.VMEM, "s": pltpu.SMEM, "a": pl.ANY}
    held = [(array.shape, array.dtype) for array, space in ins if space == "v"]
    held += [(shape, dtype) for shape, dtype, space in outs if space == "v"]
    held += [(part.shape, part.dtype) for part in scratch if part.memory_space == pltpu.VMEM]
    need = sum(math.prod(shape) * jnp.dtype(dtype).itemsize for shape, dtype in held)
    need = min(need + need // 4 + VMEM_SPARE, VMEM_LIMIT) if small else VMEM_LIMIT
    return pl.pallas_call(
        kernel,
        out_shape=[jax.ShapeDtypeStruct(shape, dtype) for shape, dtype, _ in outs],
        in_specs=[pl.BlockSpec(memory_space=spaces[space]) for _, space in ins],
        out_specs=[pl.BlockSpec(memory_space=spaces[space]) for _, _, space in outs],
        scratch_shapes=list(scratch),
        compiler_params=pltpu.CompilerParams(vmem_limit_bytes=need),
        cost_estimate=pl.CostEstimate(flops=int(us * 1.1e9), bytes_accessed=1, transcendentals=0),
    )(*[array for array, _ in ins])


def place_pieces(pieces, target, sem, me, rows):
    return [
        pltpu.make_async_copy(
            piece.at[pl.ds(0, rows), pl.ds(0, target.shape[1])],
            target.at[pl.ds(pl.multiple_of((me ^ s) * rows, 16), rows), :],
            sem.at[s],
        )
        for s, piece in enumerate(pieces)
    ]


def place_w_out(pieces, target, sem, me):
    wid, width = len(pieces), pieces[0].shape[1]
    ep, blocks = target.shape[0] // len(pieces), target.shape[1] // pieces[0].shape[1]
    first = pieces[0].shape[0] - blocks * ep
    return [
        pltpu.make_async_copy(
            pieces[s].at[pl.ds(first + k * ep, ep), :],
            target.at[pl.ds(pl.multiple_of((me ^ s) * ep, 16), ep), pl.ds(k * width, width)],
            sem.at[k, s],
        )
        for s in range(wid)
        for k in range(blocks)
    ]


def move_rows(pairs, sem, slot, first, rows):
    at = pl.multiple_of(first, 16)
    return [
        pltpu.make_async_copy(
            pair[0].at[pl.ds(at, rows), :],
            pair[1].at[pl.ds(pl.multiple_of(first + (pair[2] if len(pair) > 2 else 0), 16), rows), :],
            sem.at[k, slot],
        )
        for k, pair in enumerate(pairs)
    ]


def each(first, count, step, carry=0):
    for k in range(count):
        carry = step(first + k, carry)
    return carry


def begin(copies):
    for copy in copies:
        copy.start()


def finish(copies):
    for copy in copies:
        copy.wait()


def split_kernel(
    er, ep, wid, below, w_r, gain_r, out_r, x_r, dt_r, bias_r, conv_r, conv_b_r, skip_r, log_r, *refs
):
    nar = len(refs) - 4
    outs, (small_o, out_o, rows_s, lanes) = refs[:nar], refs[nar:]
    inner = wid * nar * er
    es = wid * ep
    dr = w_r.shape[1]
    gain = gain_r[...].astype(f32)
    gain = jnp.concatenate([gain, jnp.zeros((1, LANES - dr), f32)], axis=1)
    gain = jnp.broadcast_to(gain, (LANES, LANES)).T[:dr].astype(bf16)
    for half in range(2):
        first = half * (MODS * es + LANES)
        for m in range(MODS):
            row = w_r[m, :, half * inner : (half + 1) * inner].astype(f32)
            for k in range(nar):
                parts = []
                for v in range(wid):
                    parts.append(row[:, (v * nar + k) * er : (v * nar + k + 1) * er])
                    if ep > er:
                        parts.append(jnp.zeros((dr, ep - er), f32))
                rows_s[k, :, first + m * es : first + (m + 1) * es] = jnp.concatenate(parts, axis=1).astype(bf16)
    for s in range(nar):
        rows_s[s, :, MODS * es : MODS * es + LANES] = gain
    for s in range(nar):
        outs[s][...] = rows_s[lax.axis_index("narrow") ^ s]
    out_whole = jnp.concatenate([out_r[m].astype(f32) for m in range(MODS)], axis=1)
    if ep > er:
        out_whole = jnp.concatenate([out_whole, jnp.zeros((ep - er, out_whole.shape[1]), f32)], axis=0)
    out_w = out_o.shape[1]
    for k in range(out_whole.shape[1] // out_w):
        out_o[k * ep : (k + 1) * ep, :] = out_whole[:, k * out_w : (k + 1) * out_w].astype(bf16)
    rank = dt_r.shape[1]
    lanes[...] = jnp.zeros_like(lanes)
    for m in range(MODS):
        lanes[m * rank : (m + 1) * rank, :er] = dt_r[m].astype(f32)
    base = MODS * rank
    for at, ref in ((T_BIAS, bias_r), (T_CONV_B, conv_b_r), (T_CONV, conv_r), (T_SKIP, skip_r), (T_LOG, log_r)):
        lanes[base + at : base + at + ref.shape[0], :er] = ref[...].astype(f32)
    turned = lanes[...].T[:ep]
    xw = x_r.shape[2]
    columns = []
    for m in range(MODS):
        part = x_r[m].astype(f32)
        if ep > er:
            part = jnp.concatenate([part, jnp.zeros((ep - er, xw), f32)], axis=0)
        columns += [part, jnp.zeros((ep, LANES - xw), f32)]
    small = jnp.concatenate(columns + [turned], axis=1)
    cols = small.shape[1]
    small_o[...] = jnp.zeros_like(small_o)
    for c in range(-(-ep // below)):
        part = small[c * below : min(ep, (c + 1) * below)]
        small_o[: part.shape[0], c * cols : (c + 1) * cols] = part.astype(bf16)


def join_kernel(meta, *refs):
    pieces, (small, out_rows, front_o, gate_o) = refs[:-4], refs[-4:]
    nar, dr = len(pieces), pieces[0].shape[0]
    row = lax.broadcasted_iota(jnp.int32, (nar * dr, dr), 0)
    col = lax.broadcasted_iota(jnp.int32, (nar * dr, dr), 1)
    joined = sum(
        dot((row == (meta[0] ^ s) * dr + col).astype(bf16), piece[...], 1, 0)
        for s, piece in enumerate(pieces)
    ).astype(bf16)
    front_o[: nar * dr, :] = joined[:, : front_o.shape[1]]
    front_o[nar * dr :, :] = small[...]
    gate_o[: nar * dr, :] = joined[:, front_o.shape[1] :]
    gate_o[nar * dr :, :] = out_rows[...]


T_BIAS, T_CONV_B, T_CONV, T_SKIP, T_LOG = 0, 3, 4, 8, 16


def in_kernel(nar, wid, rpd, taps, ep, rank, meta, *refs):
    toks, w_pieces = refs[:nar], refs[nar : nar + wid]
    hbm_os = refs[nar + wid : nar + wid + 4]
    px_o, kinds_o, w_x, w_dt_o, table_o, gain_o = refs[nar + wid + 4 : nar + wid + 10]
    normed_o, front_o, csum_o, mixed_o, xs, wf, rest, tok_sem, w_sem, rest_sem, out_sem = refs[nar + wid + 10 :]
    outs = list(zip((normed_o, front_o, csum_o, mixed_o), hbm_os))
    n, w, split = meta[0], meta[1], meta[2]
    total, es = csum_o.shape
    width = MODS * es
    rows_w = wf.shape[0] // wid
    piece_rows = toks[0].shape[0]
    copies = []
    cols = rest.shape[1]
    below = w_pieces[0].shape[0] - rows_w
    x_cols = w_x.shape[1]
    for s, piece in enumerate(w_pieces):
        for c in range(-(-ep // below)):
            count = min(below, ep - c * below)
            at = pl.multiple_of((w ^ s) * ep + c * below, 16)
            copies.append(
                pltpu.make_async_copy(
                    piece.at[pl.ds(rows_w, count), pl.ds(c * cols, cols)],
                    rest.at[pl.ds(at, count), :],
                    rest_sem.at[c, s],
                )
            )
    tok_copies, w_copies = [], []
    for s, piece in enumerate(toks):
        at = pl.multiple_of((n ^ s) * piece_rows, 16)
        tok_copies.append(
            pltpu.make_async_copy(piece, xs.at[pl.ds(at, piece_rows), :], tok_sem.at[s])
        )
    for s, piece in enumerate(w_pieces):
        at = pl.multiple_of((w ^ s) * rows_w, 16)
        w_copies.append(
            pltpu.make_async_copy(
                piece.at[pl.ds(0, rows_w), pl.ds(0, wf.shape[1])], wf.at[pl.ds(at, rows_w), :], w_sem.at[s]
            )
        )
    for copy in copies + tok_copies + w_copies:
        copy.start()
    for copy in copies:
        copy.wait()
    w_x[...] = rest[:, :x_cols]
    turned = rest[:, x_cols:].astype(f32).T
    w_dt_o[...] = turned[: MODS * rank].astype(bf16)
    table_o[...] = turned[MODS * rank :]
    for copy in tok_copies:
        copy.wait()
    for p in range(nar):
        tail = xs[(p + 1) * piece_rows - 16 : (p + 1) * piece_rows, :LANES].astype(f32)
        row = lax.broadcasted_iota(jnp.int32, tail.shape, 0)
        for j in range(rpd):
            kinds_o[p * rpd + j] = jnp.max(jnp.where(row == j, tail, 0.0)).astype(jnp.int32)
    for copy in w_copies:
        copy.wait()
    gain = wf[:, width : width + LANES].astype(f32).T[0:1, :]
    gain_o[...] = gain

    def one_run(r, before):
        rows = pl.ds(pl.multiple_of(r * RUN, RUN), RUN)
        kind = kinds_o[r]
        x_at = pl.multiple_of((r // rpd) * piece_rows + (r % rpd) * RUN, 16)
        x = xs[pl.ds(x_at, RUN), :].astype(f32)
        scale = lax.rsqrt(jnp.mean(x * x, axis=1, keepdims=True) + EPSILON)
        normed = (x * scale * gain).astype(bf16)
        normed_o[rows, :] = normed
        front = dot(normed, wf[:, pl.ds(pl.multiple_of(kind * es, LANES), es)], 1, 0)
        front_o[rows, :] = front
        ext = jnp.concatenate([before, front], axis=0)
        place = r * RUN + lax.broadcasted_iota(jnp.int32, (RUN, 1), 0)
        offset = place - jnp.where(place >= split, split, 0)
        csum = jnp.broadcast_to(table_o[T_CONV_B : T_CONV_B + 1, :], (RUN, es))
        for lag in range(taps):
            tap = table_o[T_CONV + taps - 1 - lag : T_CONV + taps - lag, :]
            valid = (offset >= lag).astype(f32)
            csum = csum + tap * ext[8 - lag : 8 - lag + RUN, :] * valid
        csum_o[rows, :] = csum
        mixed = (csum * jax.nn.sigmoid(csum)).astype(bf16)
        mixed_o[rows, :] = mixed
        px = dot(mixed, w_x[:, pl.ds(pl.multiple_of(kind * LANES, LANES), LANES)], 1, 0)
        px_o[:, pl.ds(pl.multiple_of(r * RUN, LANES), RUN)] = px.T[: px_o.shape[0]].astype(bf16)
        return front[RUN - 8 :]

    before = jnp.zeros((8, es), f32)
    size = total // CHUNKS
    for c in range(CHUNKS):
        before = each(c * size // RUN, size // RUN, one_run, before)
        begin(move_rows(outs, out_sem, c, c * size, size))
    for c in range(CHUNKS):
        finish(move_rows(outs, out_sem, c, c * size, size))


def gate_kernel(wid, meta, kinds, *refs):
    pieces, (normed_h, act_h, slope_h, normed_r, act_o, slope_o, wg, w_sem, in_sem, out_sem) = refs[:wid], refs[wid:]
    total, es = act_o.shape
    size = total // CHUNKS
    weights = place_pieces(pieces, wg, w_sem, meta[1], wg.shape[0] // wid)
    arriving = [move_rows([(normed_h, normed_r)], in_sem, c, c * size, size) for c in range(CHUNKS)]
    leaving = [
        move_rows([(act_o, act_h), (slope_o, slope_h)], out_sem, c, c * size, size) for c in range(CHUNKS)
    ]
    begin(weights)
    for copies in arriving:
        begin(copies)
    finish(weights)

    def one_run(r, carry):
        rows = pl.ds(pl.multiple_of(r * RUN, RUN), RUN)
        gate = dot(normed_r[rows, :], wg[:, pl.ds(pl.multiple_of(kinds[r] * es, LANES), es)], 1, 0)
        sig = jax.nn.sigmoid(gate)
        act_o[rows, :] = gate * sig
        slope_o[rows, :] = sig * (1.0 + gate * (1.0 - sig))
        return carry

    for c in range(CHUNKS):
        finish(arriving[c])
        each(c * size // RUN, size // RUN, one_run)
        begin(leaving[c])
    for copies in leaving:
        finish(copies)


def softplus(v):
    return jnp.maximum(v, 0.0) + jnp.log1p(jnp.exp(-jnp.abs(v)))


def scan_kernel(nar, wid, rank, meta, kinds, *refs):
    cots, pieces, refs = refs[:nar], refs[nar : nar + wid], refs[nar + wid :]
    px_r, w_dt, table, mixed_h, act_h = refs[:5]
    parts_h, refs = refs[5 : 5 + nar], refs[5 + nar :]
    gated_h, dgs_h, cot_h, gmix_h, dpre_h, dpx_o, dlow_o, glog_o, gskip_o = refs[:9]
    mixed_r, act_r, cot_r, w_out, dssm_r, ssm_o, gated_o, dgs_o, branch, gmix_o, dpre_o = refs[9:20]
    in_sem, cot_sem, w_sem, mid_sem, part_sem, out_sem = refs[20:26]
    pxs, pre_s, step_s, states, bc, qs, gs, fs, dtk, dtu, r1s, r2s, cblk, bblk, adjs = refs[26:]
    split = meta[2]
    total, es = mixed_r.shape
    ns = states.shape[1]
    groups = es // LANES
    runs = total // RUN
    d, size = cot_r.shape[1], total // nar
    mixed_in = pltpu.make_async_copy(mixed_h, mixed_r, in_sem.at[0])
    arriving = place_w_out(pieces, w_out, w_sem, meta[1]) + place_pieces(cots, cot_r, cot_sem, meta[0], size)
    arriving.append(pltpu.make_async_copy(act_h, act_r, in_sem.at[1]))
    begin([mixed_in] + arriving)
    lane = [slice(g * LANES, (g + 1) * LANES) for g in range(groups)]
    rates = -jnp.exp(table[T_LOG : T_LOG + ns, :])
    r1s[...] = rates
    r2s[...] = rates * LOG2E
    half = ns // 2
    pxs[...] = px_r[...].astype(f32)
    skip = table[T_SKIP : T_SKIP + 1, :]

    def rows_of(r):
        return pl.ds(pl.multiple_of(r * RUN, RUN), RUN)

    k_row = lax.broadcasted_iota(jnp.int32, (ns, LANES), 1)
    own_row = (k_row % ns == lax.broadcasted_iota(jnp.int32, (ns, LANES), 0)) & (k_row < 2 * ns)
    own_row = own_row.astype(f32)
    k_col = lax.broadcasted_iota(jnp.int32, (LANES, 2 * LANES), 0)
    b_or_c = lax.broadcasted_iota(jnp.int32, (LANES, 2 * LANES), 1) // LANES
    ones = (k_col // ns == b_or_c).astype(bf16)

    tile_k = lax.broadcasted_iota(jnp.int32, (LANES, 16 * ns), 0)
    tile_l = lax.broadcasted_iota(jnp.int32, (LANES, 16 * ns), 1)
    tile_b = (tile_k == tile_l % ns).astype(bf16)
    tile_c = (tile_k == tile_l % ns + ns).astype(bf16)
    tile_t = lax.broadcasted_iota(jnp.int32, (RUN, 16 * ns), 0) % 16
    own_t = (tile_t == lax.broadcasted_iota(jnp.int32, (RUN, 16 * ns), 1) // ns).astype(f32)

    def spread(r):
        block = pxs[rank : rank + 2 * ns, pl.ds(pl.multiple_of(r * RUN, LANES), RUN)]
        parts = jnp.concatenate([block, jnp.zeros((LANES - 2 * ns, RUN), f32)], axis=0)
        picked = parts.T[:, None, :] * own_row[None]
        bc[bc_rows(r), :] = dot(picked.reshape(RUN * ns, LANES).astype(bf16), ones, 1, 0)
        cblk[rows_of(r), :] = (dot(parts.T.astype(bf16), tile_c, 1, 0) * own_t).astype(bf16)
        bblk[rows_of(r), :] = (dot(parts.T.astype(bf16), tile_b, 1, 0) * own_t).astype(bf16)

    def bc_rows(r):
        if bc.shape[0] == RUN * ns:
            return pl.ds(0, RUN * ns)
        return pl.ds(pl.multiple_of(r * (RUN * ns), RUN * ns), RUN * ns)

    mixed_in.wait()
    for r in range(runs):
        rows, lanes_at = slice(r * RUN, (r + 1) * RUN), slice(r * RUN, (r + 1) * RUN)
        low = px_r[:rank, lanes_at]
        dlow_o[:, lanes_at] = low
        weights = w_dt[pl.ds(pl.multiple_of(kinds[r] * rank, 16), rank), :]
        pre = dot(low, weights, 0, 0) + table[pl.ds(T_BIAS + kinds[r], 1), :]
        pre_s[rows, :] = pre
        steps = softplus(pre)
        step_s[rows, :] = steps
        place = r * RUN + lax.broadcasted_iota(jnp.int32, (RUN, 1), 0)
        dtk[rows, :] = jnp.where((place == 0) | (place == split), FAR, steps)
        dtu[rows, :] = steps * mixed_r[rows, :].astype(f32)
        if bc.shape[0] > RUN * ns:
            spread(r)

    def row(tile, j, g):
        return jnp.broadcast_to(tile[j : j + 1, lane[g]], (ns, LANES))

    def folded(ref):
        outs = []
        for g in range(groups):
            out = ref[g, pl.ds(0, RUN, stride=half), :]
            for s in range(1, half):
                out = out + ref[g, pl.ds(s, RUN, stride=half), :]
            outs.append(out)
        return jnp.concatenate(outs, axis=1)

    states[0] = jnp.zeros((ns, es), bf16)

    def forward(r, hs):
        rows = rows_of(r)
        if bc.shape[0] == RUN * ns:
            spread(r)

        def eight(i, hs):
            hs = list(hs)
            at = pl.ds(pl.multiple_of(r * RUN + i * 32, 32), 32)
            k8, u8 = dtk[at, :], dtu[at, :]
            bcv = bc.at[bc_rows(r), :].at[pl.ds(pl.multiple_of(i * (32 * ns), 32 * ns), 32 * ns), :]
            stv = states.at[pl.ds(r * RUN + i * 32 + 1, 32)]
            for j in range(32):
                bt = bcv[j * ns : (j + 1) * ns, :LANES]
                for g in range(groups):
                    decay = jnp.exp2(row(k8, j, g) * r2s[:, lane[g]])
                    hs[g] = decay * hs[g] + row(u8, j, g) * bt
                    stv[j, :, lane[g]] = hs[g].astype(bf16)
            return tuple(hs)

        hs = lax.fori_loop(0, RUN // 32, eight, hs)
        for q in range(RUN // 16):
            at = pl.ds(pl.multiple_of(r * RUN + q * 16, 16), 16)
            block = states[pl.ds(r * RUN + q * 16 + 1, 16)].reshape(16 * ns, es)
            ssm_o[at, :] = dot(cblk[at, :], block, 1, 0) + skip * mixed_r[at, :].astype(f32)
        return hs

    zero = jnp.zeros((ns, LANES), f32)
    lax.fori_loop(0, runs, forward, (zero,) * groups)
    gskip_o[...] = jnp.zeros_like(gskip_o)
    finish(arriving)
    leaving = []
    for r in range(runs):
        rows = slice(r * RUN, (r + 1) * RUN)
        wide_at = pl.ds(pl.multiple_of(kinds[r] * d, LANES), d)
        ssm, act = ssm_o[rows, :], act_r[rows, :]
        d_gated = dot(cot_r[rows, :], w_out[:, wide_at], 1, 1)
        dssm_r[rows, :] = d_gated * act
        dgs_o[rows, :] = d_gated * ssm
        gated = (ssm * act).astype(bf16)
        gated_o[rows, :] = gated
        branch[rows, :] = dot(gated, w_out[:, wide_at], 1, 0).astype(bf16)
    for k, (source, target) in enumerate(((gated_o, gated_h), (dgs_o, dgs_h), (cot_r, cot_h))):
        leaving.append(pltpu.make_async_copy(source, target, mid_sem.at[k]))
    for s, part in enumerate(parts_h):
        first = pl.multiple_of((meta[0] ^ s) * size, RUN)
        leaving.append(pltpu.make_async_copy(branch.at[pl.ds(first, size), :], part, part_sem.at[s]))
    begin(leaving)
    gather_k = lax.broadcasted_iota(jnp.int32, (2 * LANES, LANES), 0) // LANES
    gather_l = lax.broadcasted_iota(jnp.int32, (2 * LANES, LANES), 1) // ns
    gather = (gather_k == gather_l).astype(bf16)
    keep_n = lax.broadcasted_iota(jnp.int32, (ns, LANES), 0)
    keep = (lax.broadcasted_iota(jnp.int32, (ns, LANES), 1) % ns == keep_n).astype(f32)

    def backward(back, carry):
        r = runs - 1 - back
        rows = rows_of(r)
        kind = kinds[r]
        if bc.shape[0] == RUN * ns:
            spread(r)

        def eight(back_i, carry):
            ms, hs, gr = [list(part) for part in carry]
            i = RUN // 32 - 1 - back_i
            at = pl.ds(pl.multiple_of(r * RUN + i * 32, 32), 32)
            k8, u8 = dtk[at, :], dtu[at, :]
            y8 = dssm_r[pl.ds(pl.multiple_of(r * RUN + i * 32, 32), 32), :]
            bcv = bc.at[bc_rows(r), :].at[pl.ds(pl.multiple_of(i * (32 * ns), 32 * ns), 32 * ns), :]
            adv = adjs.at[pl.ds(i * 32, 32)]
            qsv = qs.at[:, pl.ds(pl.multiple_of(i * (32 * half), 32 * half), 32 * half), :]
            stv = states.at[pl.ds(r * RUN + i * 32, 32)]
            gsv = gs.at[pl.ds(pl.multiple_of(i * (32 * ns), 32 * ns), 32 * ns), :]
            for j in reversed(range(32)):
                ct = bcv[j * ns : (j + 1) * ns, LANES:]
                gb_sum, gc_sum = None, None
                for g in range(groups):
                    dt = row(k8, j, g)
                    dy = row(y8, j, g)
                    adjoint = dy * ct + ms[g]
                    before = stv[j, :, lane[g]].astype(f32)
                    c_part = dy * hs[g]
                    b_part = adjoint * row(u8, j, g)
                    gb_sum = b_part if gb_sum is None else gb_sum + b_part
                    gc_sum = c_part if gc_sum is None else gc_sum + c_part
                    fold_at = slice(j * half, (j + 1) * half)
                    adv[j, :, lane[g]] = adjoint.astype(bf16)
                    ms[g] = jnp.exp2(dt * r2s[:, lane[g]]) * adjoint
                    weighted = ms[g] * before
                    by_rate = weighted * r1s[:, lane[g]]
                    qsv[g, fold_at, :] = by_rate[:half] + by_rate[half:]
                    gr[g] = gr[g] + weighted * dt
                    hs[g] = before
                gsv[j * ns : (j + 1) * ns, :LANES] = gb_sum.astype(bf16)
                gsv[j * ns : (j + 1) * ns, LANES:] = gc_sum.astype(bf16)
            return tuple(ms), tuple(hs), tuple(gr)

        carry = lax.fori_loop(0, RUN // 32, eight, carry)
        mixed = mixed_r[rows, :].astype(f32)
        by_rate = folded(qs)
        lb = jnp.concatenate(
            [
                dot(
                    bblk[pl.ds(pl.multiple_of(r * RUN + q * 16, 16), 16), :],
                    adjs[q * 16 : (q + 1) * 16].reshape(16 * ns, es),
                    1,
                    0,
                )
                for q in range(RUN // 16)
            ],
            axis=0,
        )
        dssm = dssm_r[rows, :]
        grad_steps = by_rate + lb * mixed
        gmix_o[rows, :] = dssm * skip + lb * step_s[rows, :]
        gskip_o[...] += jnp.sum(dssm * mixed, axis=0, keepdims=True)
        dpre = (grad_steps * jax.nn.sigmoid(pre_s[rows, :])).astype(bf16)
        dpre_o[rows, :] = dpre
        weights = w_dt[pl.ds(pl.multiple_of(kind * rank, 16), rank), :]
        dlow = dot(weights, dpre, 1, 1)
        sums = dot(gs[...], gather, 1, 0).reshape(RUN, ns, LANES) * keep[None]
        fs[...] = (sums[:, :half] + sums[:, half:]).reshape(RUN * half, LANES)
        dbc = fs[pl.ds(0, RUN, stride=half), :]
        for s in range(1, half):
            dbc = dbc + fs[pl.ds(s, RUN, stride=half), :]
        dbc = dbc.T[: 2 * ns]
        at = pl.ds(pl.multiple_of(r * RUN, LANES), RUN)
        dpx_o[:rank, at] = dlow.astype(bf16)
        dpx_o[rank:, at] = dbc.astype(bf16)
        begin(move_rows([(gmix_o, gmix_h), (dpre_o, dpre_h)], out_sem, r, r * RUN, RUN))
        return carry

    last = tuple(states[total, :, lane[g]].astype(f32) for g in range(groups))
    done = lax.fori_loop(0, runs, backward, ((zero,) * groups, last, (zero,) * groups))
    for g in range(groups):
        glog_o[:, lane[g]] = done[2][g] * rates[:, lane[g]]

    def settle(r, carry):
        finish(move_rows([(gmix_o, gmix_h), (dpre_o, dpre_h)], out_sem, r, r * RUN, RUN))
        return carry

    lax.fori_loop(0, runs, settle, 0)
    finish(leaving)


def scan_call(rank, xw, ns, meta, kinds, cots, pieces, px, w_dt_l, table, mixed, act):
    (total, es), (own, d) = mixed.shape, cots[0].shape
    nar, wid = len(cots), len(pieces)
    out_cols = MODS * d
    bc_runs = total // RUN if total * ns * 2 * LANES * 4 <= 20 * 1024 * 1024 else 1
    return call(
        functools.partial(scan_kernel, nar, wid, rank),
        [((own, d), bf16, "a")] * nar
        + [
            ((total, es), bf16, "a"),
            ((total, es), f32, "a"),
            ((total, d), bf16, "a"),
            ((total, es), f32, "a"),
            ((total, es), bf16, "a"),
            ((xw, total), bf16, "v"),
            ((rank, total), bf16, "v"),
            ((ns, es), f32, "v"),
            ((1, es), f32, "v"),
        ],
        [(meta, "s"), (kinds, "s")]
        + [(p, "a") for p in cots]
        + [(p, "a") for p in pieces]
        + [(px, "v"), (w_dt_l, "v"), (table, "v"), (mixed, "a"), (act, "a")],
        [
            pltpu.VMEM((total, es), bf16),
            pltpu.VMEM((total, es), f32),
            pltpu.VMEM((total, d), bf16),
            pltpu.VMEM((es, out_cols), bf16),
            pltpu.VMEM((total, es), f32),
            pltpu.VMEM((total, es), f32),
            pltpu.VMEM((total, es), bf16),
            pltpu.VMEM((total, es), f32),
            pltpu.VMEM((total, d), bf16),
            pltpu.VMEM((total, es), f32),
            pltpu.VMEM((total, es), bf16),
            pltpu.SemaphoreType.DMA((2,)),
            pltpu.SemaphoreType.DMA((nar,)),
            pltpu.SemaphoreType.DMA((out_cols // pieces[0].shape[1], wid)),
            pltpu.SemaphoreType.DMA((3,)),
            pltpu.SemaphoreType.DMA((nar,)),
            pltpu.SemaphoreType.DMA((2, total // RUN)),
            pltpu.VMEM((xw, total), f32),
            pltpu.VMEM((total, es), f32),
            pltpu.VMEM((total, es), f32),
            pltpu.VMEM((total + 1, ns, es), bf16),
            pltpu.VMEM((bc_runs * RUN * ns, 2 * LANES), f32),
            pltpu.VMEM((es // LANES, RUN * ns // 2, LANES), f32),
            pltpu.VMEM((RUN * ns, 2 * LANES), bf16),
            pltpu.VMEM((RUN * ns // 2, LANES), f32),
            pltpu.VMEM((total, es), f32),
            pltpu.VMEM((total, es), f32),
            pltpu.VMEM((ns, es), f32),
            pltpu.VMEM((ns, es), f32),
            pltpu.VMEM((total, 16 * ns), bf16),
            pltpu.VMEM((total, 16 * ns), bf16),
            pltpu.VMEM((RUN, ns, es), bf16),
        ],
        us=40.0,
    )


def split_rows(acc, place, rows):
    return acc[pl.ds(pl.multiple_of(place * rows, 16), rows), :]


def grads_kernel(wid, ep, rank, meta, kinds, *refs):
    hbm, (dlow_r, glog_r, gskip_r) = refs[:6], refs[6:9]
    dgate_h, gate_h, w_out_h, table_o = refs[9:13]
    rows_in, (dgate_o, gate_o, w_out_o, acc_out, acc_in, in_sem, out_sem, block_sem) = refs[13:19], refs[19:]
    gated_r, dgs_r, slope_r, cot_r, normed_r, dpre_r = rows_in
    total, es = gated_r.shape
    d = cot_r.shape[1]
    size = total // CHUNKS
    arriving = [move_rows(list(zip(hbm, rows_in)), in_sem, c, c * size, size) for c in range(CHUNKS)]
    leaving = [move_rows([(dgate_o, dgate_h)], out_sem, c, c * size, size) for c in range(CHUNKS)]
    for copies in arriving:
        begin(copies)
    acc_out[...] = jnp.zeros_like(acc_out)
    acc_in[...] = jnp.zeros_like(acc_in)
    table_o[...] = jnp.zeros_like(table_o)
    base = MODS * rank

    def one_run(r, carry):
        rows = pl.ds(pl.multiple_of(r * RUN, RUN), RUN)
        kind = kinds[r]
        wide_at = pl.ds(pl.multiple_of(kind * d, LANES), d)
        es_at = pl.ds(pl.multiple_of(kind * es, LANES), es)
        acc_out[:, wide_at] += dot(gated_r[rows, :], cot_r[rows, :], 0, 0)
        dgate = (dgs_r[rows, :] * slope_r[rows, :]).astype(bf16)
        dgate_o[rows, :] = dgate
        acc_in[:, es_at] += dot(normed_r[rows, :], dgate, 0, 0)
        dpre = dpre_r[rows, :]
        low = dlow_r[:, pl.ds(pl.multiple_of(r * RUN, LANES), RUN)]
        table_o[pl.ds(pl.multiple_of(kind * rank, 8), rank), :] += dot(low, dpre, 1, 0)
        table_o[pl.ds(base + T_BIAS + kind, 1), :] += jnp.sum(dpre.astype(f32), axis=0, keepdims=True)
        return carry

    for c in range(CHUNKS):
        finish(arriving[c])
        each(c * size // RUN, size // RUN, one_run)
        begin(leaving[c])
    in_rows = acc_in.shape[0] // wid
    block_copies = []
    for k, (source, target) in enumerate(((gate_o, gate_h), (w_out_o, w_out_h))):
        for v in range(wid):
            if k == 0:
                gate_o[v] = acc_in[v * in_rows : (v + 1) * in_rows, :].astype(bf16)
            else:
                w_out_o[v] = acc_out[v * ep : (v + 1) * ep, :].astype(bf16)
            block_copies.append(pltpu.make_async_copy(source.at[v], target.at[v], block_sem.at[k, v]))
            block_copies[-1].start()
    table_o[base + T_SKIP : base + T_SKIP + 1, :] = gskip_r[...]
    table_o[base + T_LOG : base + T_LOG + glog_r.shape[0], :] = glog_r[...]
    for copies in leaving + [block_copies]:
        finish(copies)


def pair_kernel(chips, meta, same, peer, *outs):
    chip = meta[1] // 2
    for s in range(chips):
        outs[s][...] = (same[chip ^ s].astype(f32) + peer[chip ^ s].astype(f32)).astype(bf16)


def conv_kernel(nar, wid, taps, ep, meta, kinds, *refs):
    dpx_pieces = refs[:nar]
    table, w_x, table_r = refs[nar : nar + 3]
    hbm = refs[nar + 3 : nar + 8]
    dfront_h, same_h, peer_h = refs[nar + 8 : nar + 11]
    rows_in = refs[nar + 11 : nar + 16]
    dfront_o, same_o, peer_o, acc_in, acc_x, small, turned, in_sem, out_sem, block_sem = refs[nar + 16 :]
    gmix_r, csum_r, front_r, mixed_r, normed_r = rows_in
    split = meta[2]
    total, es = gmix_r.shape
    runs = total // RUN
    size = total // CHUNKS
    moves = [(a, b, 16) if b is front_r else (a, b) for a, b in zip(hbm, rows_in)]
    arriving = [move_rows(moves, in_sem, c, c * size, size) for c in range(CHUNKS)]
    leaving = [move_rows([(dfront_o, dfront_h)], out_sem, c, c * size, size) for c in range(CHUNKS)]
    for c in reversed(range(CHUNKS)):
        begin(arriving[c])
    front_r[0:16, :] = jnp.zeros((16, es), f32)
    acc_in[...] = jnp.zeros_like(acc_in)
    acc_x[...] = jnp.zeros_like(acc_x)
    small[...] = jnp.zeros_like(small)
    xw = dpx_pieces[0].shape[0]

    def one_run(back, later):
        r = runs - 1 - back
        rows = pl.ds(pl.multiple_of(r * RUN, RUN), RUN)
        kind = kinds[r]
        lanes_at = pl.ds(pl.multiple_of(r * RUN, LANES), RUN)
        dpx = sum(piece[:, lanes_at].astype(f32) for piece in dpx_pieces)
        dpx = jnp.concatenate([dpx, jnp.zeros((LANES - xw, RUN), f32)], axis=0).T.astype(bf16)
        x_at = pl.ds(pl.multiple_of(kind * LANES, LANES), LANES)
        acc_x[:, x_at] += dot(mixed_r[rows, :], dpx, 0, 0)
        gmix = gmix_r[rows, :] + dot(dpx, w_x[:, x_at], 1, 1)
        csum = csum_r[rows, :]
        sig = jax.nn.sigmoid(csum)
        dc = gmix * sig * (1.0 + csum * (1.0 - sig))
        place = r * RUN + lax.broadcasted_iota(jnp.int32, (RUN + 8, 1), 0)
        offset = place - jnp.where(place >= split, split, 0)
        ext = jnp.concatenate([dc, later], axis=0)
        lagged = front_r[pl.ds(pl.multiple_of(r * RUN + 8, 8), RUN + 8), :]
        d_front = jnp.zeros((RUN, es), f32)
        for lag in range(taps):
            tap = taps - 1 - lag
            masked = ext * (offset >= lag).astype(f32)
            d_front = d_front + table[T_CONV + tap : T_CONV + tap + 1, :] * masked[lag : lag + RUN, :]
            small[T_CONV + tap : T_CONV + tap + 1, :] += jnp.sum(
                masked[:RUN] * lagged[8 - lag : 8 - lag + RUN, :], axis=0, keepdims=True
            )
        small[T_CONV_B : T_CONV_B + 1, :] += jnp.sum(dc, axis=0, keepdims=True)
        d_front = d_front.astype(bf16)
        dfront_o[rows, :] = d_front
        acc_in[:, pl.ds(pl.multiple_of(kind * es, LANES), es)] += dot(normed_r[rows, :], d_front, 0, 0)
        return dc[:8]

    later = jnp.zeros((8, es), f32)
    for c in reversed(range(CHUNKS)):
        if c == CHUNKS - 1:
            finish(arriving[c])
        if c:
            finish(arriving[c - 1])
        back = (CHUNKS - 1 - c) * size // RUN
        later = each(back, size // RUN, one_run, later)
        begin(leaving[c])
    in_rows, width = acc_in.shape[0] // wid, acc_in.shape[1]
    base = table_r.shape[0] - small.shape[0]
    rest = jnp.concatenate([table_r[:base, :], table_r[base:, :] + small[...]], axis=0)
    rest = jnp.concatenate([rest, jnp.zeros((256 - rest.shape[0], es), f32)], axis=0).T
    x_cols = acc_x.shape[1]
    turned[:, :x_cols] = acc_x[...].astype(bf16)
    turned[:, x_cols : x_cols + 256] = rest.astype(bf16)
    turned[:, x_cols + 256 :] = jnp.zeros((es, width - x_cols - 256), bf16)
    core = meta[1] & 1
    block_copies = []
    for k, (ref, out, parity) in enumerate(((peer_o, peer_h, 1 - core), (same_o, same_h, core))):
        for c in range(wid // 2):
            place = 2 * c + parity
            ref[c, :in_rows, :] = split_rows(acc_in, place, in_rows).astype(bf16)
            ref[c, in_rows:, :] = split_rows(turned, place, ep)
            block_copies.append(pltpu.make_async_copy(ref.at[c], out.at[c], block_sem.at[k, c]))
            block_copies[-1].start()
    for copies in leaving + [block_copies]:
        finish(copies)


def normed_kernel(nar, wid, meta, kinds, *refs):
    fronts, gates = refs[:wid], refs[wid : 2 * wid]
    dfront_h, dgate_h = refs[2 * wid : 2 * wid + 2]
    outs = refs[2 * wid + 2 : 2 * wid + 2 + nar]
    dfront_r, dgate_r, wf, wg, dn, f_sem, g_sem, in_sem, part_sem = refs[2 * wid + 2 + nar :]
    total, es = dfront_r.shape
    size = total // nar
    weights = place_pieces(fronts, wf, f_sem, meta[1], wf.shape[0] // wid)
    weights += place_pieces(gates, wg, g_sem, meta[1], wg.shape[0] // wid)
    firsts = [(meta[0] ^ s) * size for s in range(nar)]
    arriving = [
        move_rows([(dfront_h, dfront_r), (dgate_h, dgate_r)], in_sem, s, firsts[s], size) for s in range(nar)
    ]
    part_copies = [
        pltpu.make_async_copy(dn.at[pl.ds(pl.multiple_of(firsts[s], RUN), size), :], outs[s], part_sem.at[s])
        for s in range(nar)
    ]
    begin(weights)
    for s in reversed(range(nar)):
        begin(arriving[s])
    finish(weights)

    def one_run(r, carry):
        rows = pl.ds(pl.multiple_of(r * RUN, RUN), RUN)
        at = pl.ds(pl.multiple_of(kinds[r] * es, LANES), es)
        dn[rows, :] = (dot(dfront_r[rows, :], wf[:, at], 1, 1) + dot(dgate_r[rows, :], wg[:, at], 1, 1)).astype(bf16)
        return carry

    for s in reversed(range(nar)):
        finish(arriving[s])
        first = (meta[0] ^ s) * (size // RUN)
        each(first, size // RUN, one_run)
        part_copies[s].start()
    finish(part_copies)


def total_gate_kernel(blocks, out):
    out[...] = sum(blocks[v].astype(f32) for v in range(blocks.shape[0])).astype(bf16)


def total_out_kernel(er, blocks, out):
    d = out.shape[2]
    summed = sum(blocks[v, :er, :].astype(f32) for v in range(blocks.shape[0]))
    for m in range(MODS):
        out[m] = summed[:, m * d : (m + 1) * d]


def total_b_kernel(nar, chips, er, rank, taps, ns, meta, *refs):
    pieces, gate_r, outs = refs[:chips], refs[chips], refs[chips + 1 : chips + 1 + nar]
    x_o, dt_o, bias_o, conv_o, conv_b_o, log_o, skip_o, rows_s = refs[chips + 1 + nar :]
    dr, width = outs[0].shape[0], gate_r.shape[1]
    in_rows = nar * dr
    summed = sum(piece[...].astype(f32) for piece in pieces)
    gate = gate_r[...].astype(f32)
    for k in range(nar):
        rows_s[k, :, :width] = summed[k * dr : (k + 1) * dr].astype(bf16)
        rows_s[k, :, width:] = gate[k * dr : (k + 1) * dr].astype(bf16)
    for s in range(nar):
        outs[s][...] = rows_s[meta[0] ^ s]
    rest = summed[in_rows:]
    x_cols = MODS * LANES
    for m in range(MODS):
        x_o[m] = rest[:er, m * LANES : m * LANES + x_o.shape[2]]
    lanes = rest[:, x_cols : x_cols + 256]
    pad = LANES - lanes.shape[0]
    turned = jnp.concatenate([lanes, jnp.zeros((pad, 256), f32)], axis=0).T[:, :er]
    base = MODS * rank
    for m in range(MODS):
        dt_o[m] = turned[m * rank : (m + 1) * rank]
    bias_o[...] = turned[base + T_BIAS : base + T_BIAS + MODS]
    conv_o[...] = turned[base + T_CONV : base + T_CONV + taps]
    conv_b_o[...] = turned[base + T_CONV_B : base + T_CONV_B + 1]
    skip_o[...] = turned[base + T_SKIP : base + T_SKIP + 1]
    log_o[...] = turned[base + T_LOG : base + T_LOG + ns]


def tokens_kernel(x_r, cot_r, gain_r, *refs):
    pieces, out = refs[:-1], refs[-1]
    x = x_r[...].astype(f32)
    scale = lax.rsqrt(jnp.mean(x * x, axis=1, keepdims=True) + EPSILON)
    q = sum(piece[...].astype(f32) for piece in pieces) * gain_r[...]
    dotted = jnp.mean(q * x, axis=1, keepdims=True)
    out[...] = (cot_r[...].astype(f32) + scale * q - x * (scale * scale * scale) * dotted).astype(bf16)


def mixed_kernel(x_r, *refs):
    pieces, out = refs[:-1], refs[-1]
    out[...] = (x_r[...].astype(f32) + sum(piece[...].astype(f32) for piece in pieces)).astype(bf16)


def in_order(parts, er, ep, wid):
    return jnp.concatenate([part[:, v * ep : v * ep + er] for v in range(wid) for part in parts], axis=1)


def w_in_kernel(nar, wid, er, ep, meta, *refs):
    pieces, (w_h, gain_r, grad_h, gain_o, rows_s, w_r, grad_s, w_sem, out_sem) = refs[:nar], refs[nar:]
    dr = pieces[0].shape[0]
    es, inner = wid * ep, wid * nar * er
    loading = pltpu.make_async_copy(w_h, w_r, w_sem)
    loading.start()
    for s in range(nar):
        rows_s[meta[0] ^ s] = pieces[s][...].astype(f32)
    sums, storing = 0.0, []
    for m in range(MODS):
        for half in range(2):
            first = (half * MODS + m) * es
            row = in_order([rows_s[k, :, first : first + es] for k in range(nar)], er, ep, wid)
            at = slice(half * inner, (half + 1) * inner)
            grad_s[m, :, at] = row
            if m + half == 0:
                loading.wait()
            sums = sums + jnp.sum(row * w_r[m, :, at].astype(f32), axis=1, keepdims=True)
        storing.append(pltpu.make_async_copy(grad_s.at[m], grad_h.at[m], out_sem.at[m]))
        storing[m].start()
    sums = jnp.broadcast_to(sums, (dr, LANES))
    sums = jnp.concatenate([sums, jnp.zeros((LANES - dr, LANES), f32)], axis=0).T[0:1, :dr]
    gain_o[...] = sums / gain_r[...].astype(f32)
    finish(storing)


def body(
    tokens,
    norm_gain,
    w_in,
    conv_w,
    conv_b,
    w_x,
    w_dt,
    dt_bias,
    a_log,
    d_skip,
    w_out,
    mod_ids,
    split_at,
    cotangent,
):
    nar, wid = lax.axis_size("narrow"), lax.axis_size("wide")
    chips = wid // 2
    n, w = lax.axis_index("narrow"), lax.axis_index("wide")
    own, d = tokens.shape
    total = nar * own
    rpd = own // RUN
    rank, xw, ns, taps = w_dt.shape[0], w_x.shape[2], a_log.shape[1], conv_w.shape[0]
    er = w_out.shape[0]
    inner = er * nar * wid
    ep = -(-er // 16) * 16
    es = ep * wid
    dr = w_in.shape[0]
    width = MODS * es
    meta = jnp.stack([n, w, split_at[0]]).astype(jnp.int32)

    front_w = width + LANES
    gain_row = norm_gain[None]
    w_in_m = w_in.transpose(1, 0, 2)
    out_cols, x_cols = MODS * d, MODS * LANES
    table_rows = T_LOG + ns
    small_cols = x_cols + 256
    blocks = front_w // small_cols
    below = -(-(-(-ep // blocks)) // 16) * 16
    res = call(
        functools.partial(split_kernel, er, ep, wid, below),
        [((dr, front_w + width), bf16, "v")] * nar
        + [((below, front_w), bf16, "v"), ((ep * (out_cols // width), width), bf16, "v")],
        [
            (a, "v")
            for a in (
                w_in_m,
                gain_row,
                w_out.transpose(1, 0, 2),
                w_x.transpose(1, 0, 2),
                w_dt.transpose(1, 0, 2),
                dt_bias,
                conv_w,
                conv_b[None],
                d_skip[None],
                a_log.T,
            )
        ],
        [
            pltpu.VMEM((nar, dr, front_w + width), bf16),
            pltpu.VMEM((256, LANES), f32),
        ],
        us=3.0,
    )
    parts, (small, out_rows) = res[:nar], res[nar:]

    parts = scatter_narrow(parts)
    front_rows, gate_rows = call(
        join_kernel,
        [
            ((nar * dr + below, front_w), bf16, "v"),
            ((nar * dr + out_rows.shape[0], width), bf16, "v"),
        ],
        [(meta, "s")] + [(p, "v") for p in parts] + [(small, "v"), (out_rows, "v")],
        us=2.0,
    )
    front_near = near_wide(front_rows)
    front_pieces = far_wide(front_near)
    run_kinds = mod_ids.reshape(rpd, RUN)[:, :1].astype(bf16)
    tail = jnp.pad(jnp.broadcast_to(run_kinds, (rpd, d)), ((0, 16 - rpd), (0, 0)))
    tok_pieces = relay_narrow(jnp.concatenate([tokens, tail], axis=0))
    gate_near = near_wide(after(gate_rows, *front_near[1:]))
    normed, front, csum, mixed, px, kinds, w_x_l, w_dt_l, table, gain_full = call(
        functools.partial(in_kernel, nar, wid, rpd, taps, ep, rank),
        [
            ((total, d), bf16, "a"),
            ((total, es), f32, "a"),
            ((total, es), f32, "a"),
            ((total, es), bf16, "a"),
            ((xw, total), bf16, "v"),
            ((nar * rpd,), jnp.int32, "s"),
            ((es, x_cols), bf16, "v"),
            ((MODS * rank, es), bf16, "v"),
            ((256 - MODS * rank, es), f32, "v"),
            ((1, d), f32, "v"),
        ],
        [(meta, "s")] + [(p, "a") for p in tok_pieces] + [(p, "a") for p in front_pieces],
        [
            pltpu.VMEM((total, d), bf16),
            pltpu.VMEM((total, es), f32),
            pltpu.VMEM((total, es), f32),
            pltpu.VMEM((total, es), bf16),
            pltpu.VMEM((nar * (own + 16), d), bf16),
            pltpu.VMEM((d, front_w), bf16),
            pltpu.VMEM((es, small_cols), bf16),
            pltpu.SemaphoreType.DMA((nar,)),
            pltpu.SemaphoreType.DMA((wid,)),
            pltpu.SemaphoreType.DMA((-(-ep // below), wid)),
            pltpu.SemaphoreType.DMA((4, CHUNKS)),
        ],
        us=9.0,
    )
    cot_pieces = relay_narrow(after(cotangent, *tok_pieces[1:]), px)
    gate_pieces = far_wide([after(piece, px) for piece in gate_near])
    act, slope = call(
        functools.partial(gate_kernel, wid),
        [((total, es), f32, "a")] * 2,
        [(meta, "s"), (kinds, "s")]
        + [(p, "a") for p in gate_pieces]
        + [(after(normed, *cot_pieces[1:3]), "a")],
        [
            pltpu.VMEM((total, d), bf16),
            pltpu.VMEM((total, es), f32),
            pltpu.VMEM((total, es), f32),
            pltpu.VMEM((d, width), bf16),
            pltpu.SemaphoreType.DMA((wid,)),
            pltpu.SemaphoreType.DMA((1, CHUNKS)),
            pltpu.SemaphoreType.DMA((2, CHUNKS)),
        ],
        us=0.1,
    )
    px_total = add_narrow(px, act, cot_pieces[-1])
    res = scan_call(
        rank, xw, ns, meta, kinds, cot_pieces, gate_pieces, px_total, w_dt_l, table, mixed, act
    )
    branch_parts, (gated, dgs, cot, gmix, dpre, dpx, dlow, glog, gskip) = res[:nar], res[nar:]
    dpx_pieces = gather_narrow(dpx)
    branch_pieces = scatter_narrow(branch_parts)
    in_rows = d // wid
    dgate, gate_blocks, w_out_blocks, table_g = call(
        functools.partial(grads_kernel, wid, ep, rank),
        [
            ((total, es), bf16, "a"),
            ((wid, in_rows, width), bf16, "a"),
            ((wid, ep, out_cols), bf16, "a"),
            ((MODS * rank + table_rows, es), f32, "v"),
        ],
        [(meta, "s"), (kinds, "s")]
        + [(a, "a") for a in (gated, dgs, slope, cot, normed, dpre)]
        + [(a, "v") for a in (dlow, glog, gskip)],
        [
            pltpu.VMEM((total, es), bf16),
            pltpu.VMEM((total, es), f32),
            pltpu.VMEM((total, es), f32),
            pltpu.VMEM((total, d), bf16),
            pltpu.VMEM((total, d), bf16),
            pltpu.VMEM((total, es), bf16),
            pltpu.VMEM((total, es), bf16),
            pltpu.VMEM((wid, in_rows, width), bf16),
            pltpu.VMEM((wid, ep, out_cols), bf16),
            pltpu.VMEM((es, out_cols), f32),
            pltpu.VMEM((d, width), f32),
            pltpu.SemaphoreType.DMA((6, CHUNKS)),
            pltpu.SemaphoreType.DMA((1, CHUNKS)),
            pltpu.SemaphoreType.DMA((2, wid)),
        ],
        us=9.0,
    )

    def over_wide(same, peer, *earlier):
        peer = swap(peer, "wide", 1)
        same = after(same, *earlier) if earlier else same
        parts = call(
            functools.partial(pair_kernel, chips),
            [(same.shape[1:], bf16, "v")] * chips,
            [(meta, "s"), (same, "v"), (peer, "v")],
            us=3.0,
        )
        return [parts[0]] + [swap(parts[s], "wide", 2 * s) for s in range(1, chips)]

    gate_blocks = lax.all_to_all(gate_blocks, "wide", 0, 0)
    rows_b = in_rows + ep
    dfront, same_b, peer_b = call(
        functools.partial(conv_kernel, nar, wid, taps, ep),
        [((total, es), bf16, "a")] + [((chips, rows_b, width), bf16, "a")] * 2,
        [(meta, "s"), (kinds, "s")]
        + [(p, "v") for p in dpx_pieces]
        + [(a, "v") for a in (table, w_x_l, table_g)]
        + [(a, "a") for a in (gmix, csum, front, mixed, normed)],
        [
            pltpu.VMEM((total, es), f32),
            pltpu.VMEM((total, es), f32),
            pltpu.VMEM((total + 16, es), f32),
            pltpu.VMEM((total, es), bf16),
            pltpu.VMEM((total, d), bf16),
            pltpu.VMEM((total, es), bf16),
            pltpu.VMEM((chips, rows_b, width), bf16),
            pltpu.VMEM((chips, rows_b, width), bf16),
            pltpu.VMEM((d, width), f32),
            pltpu.VMEM((es, x_cols), f32),
            pltpu.VMEM((table_rows, es), f32),
            pltpu.VMEM((es, width), bf16),
            pltpu.SemaphoreType.DMA((5, CHUNKS)),
            pltpu.SemaphoreType.DMA((1, CHUNKS)),
            pltpu.SemaphoreType.DMA((2, chips)),
        ],
        us=12.0,
    )
    dn_parts = call(
        functools.partial(normed_kernel, nar, wid),
        [((own, d), bf16, "a")] * nar,
        [(meta, "s"), (kinds, "s")]
        + [(p, "a") for p in front_pieces]
        + [(p, "a") for p in gate_pieces]
        + [(dfront, "a"), (dgate, "a")],
        [
            pltpu.VMEM((total, es), bf16),
            pltpu.VMEM((total, es), bf16),
            pltpu.VMEM((d, width), bf16),
            pltpu.VMEM((d, width), bf16),
            pltpu.VMEM((total, d), bf16),
            pltpu.SemaphoreType.DMA((wid,)),
            pltpu.SemaphoreType.DMA((wid,)),
            pltpu.SemaphoreType.DMA((2, nar)),
            pltpu.SemaphoreType.DMA((nar,)),
        ],
        us=30.0,
    )
    pieces_b = over_wide(same_b, peer_b, dn_parts[0])
    dn_pieces, dn_kept = sum_narrow(dn_parts, pieces_b[0])

    mixed_out = call(
        mixed_kernel,
        [((own, d), bf16, "v")],
        [(tokens, "v")] + [(p, "v") for p in after(tuple(branch_pieces), pieces_b[0])],
        us=2.0, small=True,
    )[0]
    gate_sum = call(
        total_gate_kernel,
        [((in_rows, width), bf16, "v")],
        [(after(gate_blocks, mixed_out, dn_kept), "v")],
        us=2.0, small=True,
    )[0]
    res = call(
        functools.partial(total_b_kernel, nar, chips, er, rank, taps, ns),
        [((dr, 2 * width), bf16, "v")] * nar
        + [
            ((MODS, er, xw), f32, "v"),
            ((MODS, rank, er), f32, "v"),
            ((MODS, er), f32, "v"),
            ((taps, er), f32, "v"),
            ((1, er), f32, "v"),
            ((ns, er), f32, "v"),
            ((1, er), f32, "v"),
        ],
        [(meta, "s")] + [(p, "v") for p in pieces_b] + [(gate_sum, "v")],
        [pltpu.VMEM((nar, dr, 2 * width), bf16)],
        us=3.0, small=True,
    )
    back_parts = res[:nar]
    grad_w_x, grad_w_dt, grad_dt_bias, grad_conv_w, grad_conv_b, grad_log, grad_skip = res[nar:]
    back_pieces = scatter_narrow(back_parts)
    grad_tokens = call(
        tokens_kernel,
        [((own, d), bf16, "v")],
        [(tokens, "v"), (cotangent, "v"), (gain_full, "v")]
        + [(p, "v") for p in dn_pieces],
        us=0.1, small=True,
    )[0]
    w_out_blocks = lax.all_to_all(after(w_out_blocks, gate_sum), "wide", 0, 0)
    grad_w_in, grad_gain = call(
        functools.partial(w_in_kernel, nar, wid, er, ep),
        [((MODS, dr, 2 * inner), f32, "a"), ((1, dr), f32, "v")],
        [(meta, "s")] + [(p, "v") for p in back_pieces] + [(after(w_in_m, grad_tokens), "a"), (gain_row, "v")],
        [
            pltpu.VMEM((nar, dr, 2 * width), f32),
            pltpu.VMEM((MODS, dr, 2 * inner), bf16),
            pltpu.VMEM((MODS, dr, 2 * inner), f32),
            pltpu.SemaphoreType.DMA(()),
            pltpu.SemaphoreType.DMA((MODS,)),
        ],
        us=13.0, small=True,
    )
    grad_w_out = call(
        functools.partial(total_out_kernel, er),
        [((MODS, er, d), f32, "v")],
        [(after(w_out_blocks, grad_gain), "v")],
        us=3.0, small=True,
    )[0]
    grad_w_in, grad_w_out = grad_w_in.transpose(1, 0, 2), grad_w_out.transpose(1, 0, 2)
    grad_w_x, grad_w_dt = grad_w_x.transpose(1, 0, 2), grad_w_dt.transpose(1, 0, 2)
    grad_log = grad_log.T
    return (
        mixed_out,
        grad_tokens,
        grad_gain[0],
        grad_w_in,
        grad_conv_w,
        grad_conv_b[0],
        grad_w_x,
        grad_w_dt,
        grad_dt_bias,
        grad_log,
        grad_skip[0],
        grad_w_out,
    )


def solution(mesh):
    both = ("wide", "narrow")
    return jax.shard_map(
        body,
        mesh=mesh,
        in_specs=(
            P(both, None),
            P(both),
            P(both, None, None),
            P(None, both),
            P(both),
            P(both, None, None),
            P(None, None, both),
            P(None, both),
            P(both, None),
            P(both),
            P(both, None, None),
            P(both),
            P("wide"),
            P(both, None),
        ),
        out_specs=(
            P(both, None),
            P(both, None),
            P(both),
            P(both, None, None),
            P(None, both),
            P(both),
            P(both, None, None),
            P(None, None, both),
            P(None, both),
            P(both, None),
            P(both),
            P(both, None, None),
        ),
        check_vma=False,
    )
```

```python
import functools
import math

import jax
import jax.numpy as jnp
from jax import lax
from jax.experimental import pallas as pl
from jax.experimental.pallas import tpu as pltpu
from jax.sharding import PartitionSpec as P

MODS = 3
RUN = 128
CHUNKS = 4
LANES = 128
EPSILON = 1e-05
LOG2E = 1.4426950408889634
FAR = 1e30
VMEM_LIMIT = 60 * 1024 * 1024
VMEM_SPARE = 6 * 1024 * 1024

f32 = jnp.float32
bf16 = jnp.bfloat16


def swap(block, axis, flip):
    count = lax.axis_size(axis)
    return lax.ppermute(block, axis, [(i, i ^ flip) for i in range(count)])


def gather_narrow(block):
    return [block] + [swap(block, "narrow", s) for s in range(1, lax.axis_size("narrow"))]


def relay_narrow(block, *earlier):
    count = lax.axis_size("narrow")
    pieces = {0: block}
    for s in sorted(range(1, count), key=lambda s: (s.bit_count(), -s)):
        low_bit = s & -s
        if s == low_bit:
            pieces[s] = swap(block, "narrow", s)
        else:
            pieces[s] = swap(after(pieces[s ^ low_bit], *earlier), "narrow", low_bit)
    return [pieces[s] for s in range(count)]


def add_narrow(block, *beside):
    flip = lax.axis_size("narrow") // 2
    while flip:
        got = swap(block, "narrow", flip)
        block = (after(block, *beside).astype(f32) + got.astype(f32)).astype(bf16)
        flip //= 2
        beside = ()
    return block


def scatter_narrow(parts):
    arrived = [swap(parts[s], "narrow", s) for s in range(len(parts) - 1, 0, -1)]
    return [parts[0]] + arrived[::-1]


def sum_narrow(parts, *earlier):
    parts = list(parts)
    arrived = [parts[0]]
    for s in range(len(parts) - 1, 0, -1):
        low_bit = s & -s
        got = swap(parts[s], "narrow", low_bit)
        if s == low_bit:
            arrived.append(got)
        else:
            rest = s ^ low_bit
            parts[rest] = call(
                add_kernel,
                [(got.shape, bf16, "v")],
                [(after(parts[rest], *earlier), "v"), (got, "v")],
                us=0.1,
                small=True,
            )[0]
    return arrived, parts[-2]


def add_kernel(left, right, out):
    out[...] = (left[...].astype(f32) + right[...].astype(f32)).astype(bf16)


def near_wide(block):
    return [block] + [swap(block, "wide", 2 * s) for s in range(1, lax.axis_size("wide") // 2)]


def far_wide(near):
    return [piece for block in near for piece in (block, swap(block, "wide", 1))]


def after(value, *earlier):
    return lax.optimization_barrier((value,) + earlier)[0] if earlier else value


def dot(a, b, ca, cb):
    return lax.dot_general(a, b, (((ca,), (cb,)), ((), ())), preferred_element_type=f32)


def call(kernel, outs, ins, scratch=(), us=1.0, small=False):
    spaces = {"v": pltpu.VMEM, "s": pltpu.SMEM, "a": pl.ANY}
    held = [(array.shape, array.dtype) for array, space in ins if space == "v"]
    held += [(shape, dtype) for shape, dtype, space in outs if space == "v"]
    held += [(part.shape, part.dtype) for part in scratch if part.memory_space == pltpu.VMEM]
    need = sum(math.prod(shape) * jnp.dtype(dtype).itemsize for shape, dtype in held)
    need = min(need + need // 4 + VMEM_SPARE, VMEM_LIMIT) if small else VMEM_LIMIT
    return pl.pallas_call(
        kernel,
        out_shape=[jax.ShapeDtypeStruct(shape, dtype) for shape, dtype, _ in outs],
        in_specs=[pl.BlockSpec(memory_space=spaces[space]) for _, space in ins],
        out_specs=[pl.BlockSpec(memory_space=spaces[space]) for _, _, space in outs],
        scratch_shapes=list(scratch),
        compiler_params=pltpu.CompilerParams(vmem_limit_bytes=need),
        cost_estimate=pl.CostEstimate(flops=int(us * 1.1e9), bytes_accessed=1, transcendentals=0),
    )(*[array for array, _ in ins])


def place_pieces(pieces, target, sem, me, rows):
    return [
        pltpu.make_async_copy(
            piece.at[pl.ds(0, rows), pl.ds(0, target.shape[1])],
            target.at[pl.ds(pl.multiple_of((me ^ s) * rows, 16), rows), :],
            sem.at[s],
        )
        for s, piece in enumerate(pieces)
    ]


def place_w_out(pieces, target, sem, me):
    wid, width = len(pieces), pieces[0].shape[1]
    ep, blocks = target.shape[0] // len(pieces), target.shape[1] // pieces[0].shape[1]
    first = pieces[0].shape[0] - blocks * ep
    return [
        pltpu.make_async_copy(
            pieces[s].at[pl.ds(first + k * ep, ep), :],
            target.at[pl.ds(pl.multiple_of((me ^ s) * ep, 16), ep), pl.ds(k * width, width)],
            sem.at[k, s],
        )
        for s in range(wid)
        for k in range(blocks)
    ]


def move_rows(pairs, sem, slot, first, rows):
    at = pl.multiple_of(first, 16)
    return [
        pltpu.make_async_copy(
            pair[0].at[pl.ds(at, rows), :],
            pair[1].at[pl.ds(pl.multiple_of(first + (pair[2] if len(pair) > 2 else 0), 16), rows), :],
            sem.at[k, slot],
        )
        for k, pair in enumerate(pairs)
    ]


def each(first, count, step, carry=0):
    for k in range(count):
        carry = step(first + k, carry)
    return carry


def begin(copies):
    for copy in copies:
        copy.start()


def finish(copies):
    for copy in copies:
        copy.wait()


def split_kernel(
    er, ep, wid, below, w_r, gain_r, out_r, x_r, dt_r, bias_r, conv_r, conv_b_r, skip_r, log_r, *refs
):
    nar = len(refs) - 4
    outs, (small_o, out_o, rows_s, lanes) = refs[:nar], refs[nar:]
    inner = wid * nar * er
    es = wid * ep
    dr = w_r.shape[1]
    gain = gain_r[...].astype(f32)
    gain = jnp.concatenate([gain, jnp.zeros((1, LANES - dr), f32)], axis=1)
    gain = jnp.broadcast_to(gain, (LANES, LANES)).T[:dr].astype(bf16)
    for half in range(2):
        first = half * (MODS * es + LANES)
        for m in range(MODS):
            row = w_r[m, :, half * inner : (half + 1) * inner].astype(f32)
            for k in range(nar):
                parts = []
                for v in range(wid):
                    parts.append(row[:, (v * nar + k) * er : (v * nar + k + 1) * er])
                    if ep > er:
                        parts.append(jnp.zeros((dr, ep - er), f32))
                rows_s[k, :, first + m * es : first + (m + 1) * es] = jnp.concatenate(parts, axis=1).astype(bf16)
    for s in range(nar):
        rows_s[s, :, MODS * es : MODS * es + LANES] = gain
    for s in range(nar):
        outs[s][...] = rows_s[lax.axis_index("narrow") ^ s]
    out_whole = jnp.concatenate([out_r[m].astype(f32) for m in range(MODS)], axis=1)
    if ep > er:
        out_whole = jnp.concatenate([out_whole, jnp.zeros((ep - er, out_whole.shape[1]), f32)], axis=0)
    out_w = out_o.shape[1]
    for k in range(out_whole.shape[1] // out_w):
        out_o[k * ep : (k + 1) * ep, :] = out_whole[:, k * out_w : (k + 1) * out_w].astype(bf16)
    rank = dt_r.shape[1]
    lanes[...] = jnp.zeros_like(lanes)
    for m in range(MODS):
        lanes[m * rank : (m + 1) * rank, :er] = dt_r[m].astype(f32)
    base = MODS * rank
    for at, ref in ((T_BIAS, bias_r), (T_CONV_B, conv_b_r), (T_CONV, conv_r), (T_SKIP, skip_r), (T_LOG, log_r)):
        lanes[base + at : base + at + ref.shape[0], :er] = ref[...].astype(f32)
    turned = lanes[...].T[:ep]
    xw = x_r.shape[2]
    columns = []
    for m in range(MODS):
        part = x_r[m].astype(f32)
        if ep > er:
            part = jnp.concatenate([part, jnp.zeros((ep - er, xw), f32)], axis=0)
        columns += [part, jnp.zeros((ep, LANES - xw), f32)]
    small = jnp.concatenate(columns + [turned], axis=1)
    cols = small.shape[1]
    small_o[...] = jnp.zeros_like(small_o)
    for c in range(-(-ep // below)):
        part = small[c * below : min(ep, (c + 1) * below)]
        small_o[: part.shape[0], c * cols : (c + 1) * cols] = part.astype(bf16)


def join_kernel(meta, *refs):
    pieces, (small, out_rows, front_o, gate_o) = refs[:-4], refs[-4:]
    nar, dr = len(pieces), pieces[0].shape[0]
    row = lax.broadcasted_iota(jnp.int32, (nar * dr, dr), 0)
    col = lax.broadcasted_iota(jnp.int32, (nar * dr, dr), 1)
    joined = sum(
        dot((row == (meta[0] ^ s) * dr + col).astype(bf16), piece[...], 1, 0)
        for s, piece in enumerate(pieces)
    ).astype(bf16)
    front_o[: nar * dr, :] = joined[:, : front_o.shape[1]]
    front_o[nar * dr :, :] = small[...]
    gate_o[: nar * dr, :] = joined[:, front_o.shape[1] :]
    gate_o[nar * dr :, :] = out_rows[...]


T_BIAS, T_CONV_B, T_CONV, T_SKIP, T_LOG = 0, 3, 4, 8, 16


def in_kernel(nar, wid, rpd, taps, ep, rank, meta, *refs):
    toks, w_pieces = refs[:nar], refs[nar : nar + wid]
    hbm_os = refs[nar + wid : nar + wid + 4]
    px_o, kinds_o, w_x, w_dt_o, table_o, gain_o = refs[nar + wid + 4 : nar + wid + 10]
    normed_o, front_o, csum_o, mixed_o, xs, wf, rest, tok_sem, w_sem, rest_sem, out_sem = refs[nar + wid + 10 :]
    outs = list(zip((normed_o, front_o, csum_o, mixed_o), hbm_os))
    n, w, split = meta[0], meta[1], meta[2]
    total, es = csum_o.shape
    width = MODS * es
    rows_w = wf.shape[0] // wid
    piece_rows = toks[0].shape[0]
    copies = []
    cols = rest.shape[1]
    below = w_pieces[0].shape[0] - rows_w
    x_cols = w_x.shape[1]
    for s, piece in enumerate(w_pieces):
        for c in range(-(-ep // below)):
            count = min(below, ep - c * below)
            at = pl.multiple_of((w ^ s) * ep + c * below, 16)
            copies.append(
                pltpu.make_async_copy(
                    piece.at[pl.ds(rows_w, count), pl.ds(c * cols, cols)],
                    rest.at[pl.ds(at, count), :],
                    rest_sem.at[c, s],
                )
            )
    tok_copies, w_copies = [], []
    for s, piece in enumerate(toks):
        at = pl.multiple_of((n ^ s) * piece_rows, 16)
        tok_copies.append(
            pltpu.make_async_copy(piece, xs.at[pl.ds(at, piece_rows), :], tok_sem.at[s])
        )
    for s, piece in enumerate(w_pieces):
        at = pl.multiple_of((w ^ s) * rows_w, 16)
        w_copies.append(
            pltpu.make_async_copy(
                piece.at[pl.ds(0, rows_w), pl.ds(0, wf.shape[1])], wf.at[pl.ds(at, rows_w), :], w_sem.at[s]
            )
        )
    for copy in copies + tok_copies + w_copies:
        copy.start()
    for copy in copies:
        copy.wait()
    w_x[...] = rest[:, :x_cols]
    turned = rest[:, x_cols:].astype(f32).T
    w_dt_o[...] = turned[: MODS * rank].astype(bf16)
    table_o[...] = turned[MODS * rank :]
    for copy in tok_copies:
        copy.wait()
    for p in range(nar):
        tail = xs[(p + 1) * piece_rows - 16 : (p + 1) * piece_rows, :LANES].astype(f32)
        row = lax.broadcasted_iota(jnp.int32, tail.shape, 0)
        for j in range(rpd):
            kinds_o[p * rpd + j] = jnp.max(jnp.where(row == j, tail, 0.0)).astype(jnp.int32)
    for copy in w_copies:
        copy.wait()
    gain = wf[:, width : width + LANES].astype(f32).T[0:1, :]
    gain_o[...] = gain

    def one_run(r, before):
        rows = pl.ds(pl.multiple_of(r * RUN, RUN), RUN)
        kind = kinds_o[r]
        x_at = pl.multiple_of((r // rpd) * piece_rows + (r % rpd) * RUN, 16)
        x = xs[pl.ds(x_at, RUN), :].astype(f32)
        scale = lax.rsqrt(jnp.mean(x * x, axis=1, keepdims=True) + EPSILON)
        normed = (x * scale * gain).astype(bf16)
        normed_o[rows, :] = normed
        front = dot(normed, wf[:, pl.ds(pl.multiple_of(kind * es, LANES), es)], 1, 0)
        front_o[rows, :] = front
        ext = jnp.concatenate([before, front], axis=0)
        place = r * RUN + lax.broadcasted_iota(jnp.int32, (RUN, 1), 0)
        offset = place - jnp.where(place >= split, split, 0)
        csum = jnp.broadcast_to(table_o[T_CONV_B : T_CONV_B + 1, :], (RUN, es))
        for lag in range(taps):
            tap = table_o[T_CONV + taps - 1 - lag : T_CONV + taps - lag, :]
            valid = (offset >= lag).astype(f32)
            csum = csum + tap * ext[8 - lag : 8 - lag + RUN, :] * valid
        csum_o[rows, :] = csum
        mixed = (csum * jax.nn.sigmoid(csum)).astype(bf16)
        mixed_o[rows, :] = mixed
        px = dot(mixed, w_x[:, pl.ds(pl.multiple_of(kind * LANES, LANES), LANES)], 1, 0)
        px_o[:, pl.ds(pl.multiple_of(r * RUN, LANES), RUN)] = px.T[: px_o.shape[0]].astype(bf16)
        return front[RUN - 8 :]

    before = jnp.zeros((8, es), f32)
    size = total // CHUNKS
    for c in range(CHUNKS):
        before = each(c * size // RUN, size // RUN, one_run, before)
        begin(move_rows(outs, out_sem, c, c * size, size))
    for c in range(CHUNKS):
        finish(move_rows(outs, out_sem, c, c * size, size))


def gate_kernel(wid, meta, kinds, *refs):
    pieces, (normed_h, act_h, slope_h, normed_r, act_o, slope_o, wg, w_sem, in_sem, out_sem) = refs[:wid], refs[wid:]
    total, es = act_o.shape
    size = total // CHUNKS
    weights = place_pieces(pieces, wg, w_sem, meta[1], wg.shape[0] // wid)
    arriving = [move_rows([(normed_h, normed_r)], in_sem, c, c * size, size) for c in range(CHUNKS)]
    leaving = [
        move_rows([(act_o, act_h), (slope_o, slope_h)], out_sem, c, c * size, size) for c in range(CHUNKS)
    ]
    begin(weights)
    for copies in arriving:
        begin(copies)
    finish(weights)

    def one_run(r, carry):
        rows = pl.ds(pl.multiple_of(r * RUN, RUN), RUN)
        gate = dot(normed_r[rows, :], wg[:, pl.ds(pl.multiple_of(kinds[r] * es, LANES), es)], 1, 0)
        sig = jax.nn.sigmoid(gate)
        act_o[rows, :] = gate * sig
        slope_o[rows, :] = sig * (1.0 + gate * (1.0 - sig))
        return carry

    for c in range(CHUNKS):
        finish(arriving[c])
        each(c * size // RUN, size // RUN, one_run)
        begin(leaving[c])
    for copies in leaving:
        finish(copies)


def softplus(v):
    return jnp.maximum(v, 0.0) + jnp.log1p(jnp.exp(-jnp.abs(v)))


def scan_kernel(nar, wid, rank, meta, kinds, *refs):
    cots, pieces, refs = refs[:nar], refs[nar : nar + wid], refs[nar + wid :]
    px_r, w_dt, table, mixed_h, act_h = refs[:5]
    parts_h, refs = refs[5 : 5 + nar], refs[5 + nar :]
    gated_h, dgs_h, cot_h, gmix_h, dpre_h, dpx_o, dlow_o, glog_o, gskip_o = refs[:9]
    mixed_r, act_r, cot_r, w_out, dssm_r, ssm_o, gated_o, dgs_o, branch, gmix_o, dpre_o = refs[9:20]
    in_sem, cot_sem, w_sem, mid_sem, part_sem, out_sem = refs[20:26]
    pxs, pre_s, step_s, states, bc, qs, gs, fs, dtk, dtu, r1s, r2s, cblk, bblk, adjs = refs[26:]
    split = meta[2]
    total, es = mixed_r.shape
    ns = states.shape[1]
    groups = es // LANES
    runs = total // RUN
    d, size = cot_r.shape[1], total // nar
    mixed_in = pltpu.make_async_copy(mixed_h, mixed_r, in_sem.at[0])
    arriving = place_w_out(pieces, w_out, w_sem, meta[1]) + place_pieces(cots, cot_r, cot_sem, meta[0], size)
    arriving.append(pltpu.make_async_copy(act_h, act_r, in_sem.at[1]))
    begin([mixed_in] + arriving)
    lane = [slice(g * LANES, (g + 1) * LANES) for g in range(groups)]
    rates = -jnp.exp(table[T_LOG : T_LOG + ns, :])
    r1s[...] = rates
    r2s[...] = rates * LOG2E
    half = ns // 2
    pxs[...] = px_r[...].astype(f32)
    skip = table[T_SKIP : T_SKIP + 1, :]

    def rows_of(r):
        return pl.ds(pl.multiple_of(r * RUN, RUN), RUN)

    k_row = lax.broadcasted_iota(jnp.int32, (ns, LANES), 1)
    own_row = (k_row % ns == lax.broadcasted_iota(jnp.int32, (ns, LANES), 0)) & (k_row < 2 * ns)
    own_row = own_row.astype(f32)
    k_col = lax.broadcasted_iota(jnp.int32, (LANES, 2 * LANES), 0)
    b_or_c = lax.broadcasted_iota(jnp.int32, (LANES, 2 * LANES), 1) // LANES
    ones = (k_col // ns == b_or_c).astype(bf16)

    tile_k = lax.broadcasted_iota(jnp.int32, (LANES, 16 * ns), 0)
    tile_l = lax.broadcasted_iota(jnp.int32, (LANES, 16 * ns), 1)
    tile_b = (tile_k == tile_l % ns).astype(bf16)
    tile_c = (tile_k == tile_l % ns + ns).astype(bf16)
    tile_t = lax.broadcasted_iota(jnp.int32, (RUN, 16 * ns), 0) % 16
    own_t = (tile_t == lax.broadcasted_iota(jnp.int32, (RUN, 16 * ns), 1) // ns).astype(f32)

    def spread(r):
        block = pxs[rank : rank + 2 * ns, pl.ds(pl.multiple_of(r * RUN, LANES), RUN)]
        parts = jnp.concatenate([block, jnp.zeros((LANES - 2 * ns, RUN), f32)], axis=0)
        picked = parts.T[:, None, :] * own_row[None]
        bc[bc_rows(r), :] = dot(picked.reshape(RUN * ns, LANES).astype(bf16), ones, 1, 0)
        cblk[rows_of(r), :] = (dot(parts.T.astype(bf16), tile_c, 1, 0) * own_t).astype(bf16)
        bblk[rows_of(r), :] = (dot(parts.T.astype(bf16), tile_b, 1, 0) * own_t).astype(bf16)

    def bc_rows(r):
        if bc.shape[0] == RUN * ns:
            return pl.ds(0, RUN * ns)
        return pl.ds(pl.multiple_of(r * (RUN * ns), RUN * ns), RUN * ns)

    mixed_in.wait()
    for r in range(runs):
        rows, lanes_at = slice(r * RUN, (r + 1) * RUN), slice(r * RUN, (r + 1) * RUN)
        low = px_r[:rank, lanes_at]
        dlow_o[:, lanes_at] = low
        weights = w_dt[pl.ds(pl.multiple_of(kinds[r] * rank, 16), rank), :]
        pre = dot(low, weights, 0, 0) + table[pl.ds(T_BIAS + kinds[r], 1), :]
        pre_s[rows, :] = pre
        steps = softplus(pre)
        step_s[rows, :] = steps
        place = r * RUN + lax.broadcasted_iota(jnp.int32, (RUN, 1), 0)
        dtk[rows, :] = jnp.where((place == 0) | (place == split), FAR, steps)
        dtu[rows, :] = steps * mixed_r[rows, :].astype(f32)
        if bc.shape[0] > RUN * ns:
            spread(r)

    def row(tile, j, g):
        return jnp.broadcast_to(tile[j : j + 1, lane[g]], (ns, LANES))

    def folded(ref):
        outs = []
        for g in range(groups):
            out = ref[g, pl.ds(0, RUN, stride=half), :]
            for s in range(1, half):
                out = out + ref[g, pl.ds(s, RUN, stride=half), :]
            outs.append(out)
        return jnp.concatenate(outs, axis=1)

    states[0] = jnp.zeros((ns, es), bf16)

    def forward(r, hs):
        rows = rows_of(r)
        if bc.shape[0] == RUN * ns:
            spread(r)

        def eight(i, hs):
            hs = list(hs)
            at = pl.ds(pl.multiple_of(r * RUN + i * 32, 32), 32)
            k8, u8 = dtk[at, :], dtu[at, :]
            bcv = bc.at[bc_rows(r), :].at[pl.ds(pl.multiple_of(i * (32 * ns), 32 * ns), 32 * ns), :]
            stv = states.at[pl.ds(r * RUN + i * 32 + 1, 32)]
            for j in range(32):
                bt = bcv[j * ns : (j + 1) * ns, :LANES]
                for g in range(groups):
                    decay = jnp.exp2(row(k8, j, g) * r2s[:, lane[g]])
                    hs[g] = decay * hs[g] + row(u8, j, g) * bt
                    stv[j, :, lane[g]] = hs[g].astype(bf16)
            return tuple(hs)

        hs = lax.fori_loop(0, RUN // 32, eight, hs)
        for q in range(RUN // 16):
            at = pl.ds(pl.multiple_of(r * RUN + q * 16, 16), 16)
            block = states[pl.ds(r * RUN + q * 16 + 1, 16)].reshape(16 * ns, es)
            ssm_o[at, :] = dot(cblk[at, :], block, 1, 0) + skip * mixed_r[at, :].astype(f32)
        return hs

    zero = jnp.zeros((ns, LANES), f32)
    lax.fori_loop(0, runs, forward, (zero,) * groups)
    gskip_o[...] = jnp.zeros_like(gskip_o)
    finish(arriving)
    leaving = []
    for r in range(runs):
        rows = slice(r * RUN, (r + 1) * RUN)
        wide_at = pl.ds(pl.multiple_of(kinds[r] * d, LANES), d)
        ssm, act = ssm_o[rows, :], act_r[rows, :]
        d_gated = dot(cot_r[rows, :], w_out[:, wide_at], 1, 1)
        dssm_r[rows, :] = d_gated * act
        dgs_o[rows, :] = d_gated * ssm
        gated = (ssm * act).astype(bf16)
        gated_o[rows, :] = gated
        branch[rows, :] = dot(gated, w_out[:, wide_at], 1, 0).astype(bf16)
    for k, (source, target) in enumerate(((gated_o, gated_h), (dgs_o, dgs_h), (cot_r, cot_h))):
        leaving.append(pltpu.make_async_copy(source, target, mid_sem.at[k]))
    for s, part in enumerate(parts_h):
        first = pl.multiple_of((meta[0] ^ s) * size, RUN)
        leaving.append(pltpu.make_async_copy(branch.at[pl.ds(first, size), :], part, part_sem.at[s]))
    begin(leaving)
    gather_k = lax.broadcasted_iota(jnp.int32, (2 * LANES, LANES), 0) // LANES
    gather_l = lax.broadcasted_iota(jnp.int32, (2 * LANES, LANES), 1) // ns
    gather = (gather_k == gather_l).astype(bf16)
    keep_n = lax.broadcasted_iota(jnp.int32, (ns, LANES), 0)
    keep = (lax.broadcasted_iota(jnp.int32, (ns, LANES), 1) % ns == keep_n).astype(f32)

    def backward(back, carry):
        r = runs - 1 - back
        rows = rows_of(r)
        kind = kinds[r]
        if bc.shape[0] == RUN * ns:
            spread(r)

        def eight(back_i, carry):
            ms, hs, gr = [list(part) for part in carry]
            i = RUN // 32 - 1 - back_i
            at = pl.ds(pl.multiple_of(r * RUN + i * 32, 32), 32)
            k8, u8 = dtk[at, :], dtu[at, :]
            y8 = dssm_r[pl.ds(pl.multiple_of(r * RUN + i * 32, 32), 32), :]
            bcv = bc.at[bc_rows(r), :].at[pl.ds(pl.multiple_of(i * (32 * ns), 32 * ns), 32 * ns), :]
            adv = adjs.at[pl.ds(i * 32, 32)]
            qsv = qs.at[:, pl.ds(pl.multiple_of(i * (32 * half), 32 * half), 32 * half), :]
            stv = states.at[pl.ds(r * RUN + i * 32, 32)]
            gsv = gs.at[pl.ds(pl.multiple_of(i * (32 * ns), 32 * ns), 32 * ns), :]
            for j in reversed(range(32)):
                ct = bcv[j * ns : (j + 1) * ns, LANES:]
                gb_sum, gc_sum = None, None
                for g in range(groups):
                    dt = row(k8, j, g)
                    dy = row(y8, j, g)
                    adjoint = dy * ct + ms[g]
                    before = stv[j, :, lane[g]].astype(f32)
                    c_part = dy * hs[g]
                    b_part = adjoint * row(u8, j, g)
                    gb_sum = b_part if gb_sum is None else gb_sum + b_part
                    gc_sum = c_part if gc_sum is None else gc_sum + c_part
                    fold_at = slice(j * half, (j + 1) * half)
                    adv[j, :, lane[g]] = adjoint.astype(bf16)
                    ms[g] = jnp.exp2(dt * r2s[:, lane[g]]) * adjoint
                    weighted = ms[g] * before
                    by_rate = weighted * r1s[:, lane[g]]
                    qsv[g, fold_at, :] = by_rate[:half] + by_rate[half:]
                    gr[g] = gr[g] + weighted * dt
                    hs[g] = before
                gsv[j * ns : (j + 1) * ns, :LANES] = gb_sum.astype(bf16)
                gsv[j * ns : (j + 1) * ns, LANES:] = gc_sum.astype(bf16)
            return tuple(ms), tuple(hs), tuple(gr)

        carry = lax.fori_loop(0, RUN // 32, eight, carry)
        mixed = mixed_r[rows, :].astype(f32)
        by_rate = folded(qs)
        lb = jnp.concatenate(
            [
                dot(
                    bblk[pl.ds(pl.multiple_of(r * RUN + q * 16, 16), 16), :],
                    adjs[q * 16 : (q + 1) * 16].reshape(16 * ns, es),
                    1,
                    0,
                )
                for q in range(RUN // 16)
            ],
            axis=0,
        )
        dssm = dssm_r[rows, :]
        grad_steps = by_rate + lb * mixed
        gmix_o[rows, :] = dssm * skip + lb * step_s[rows, :]
        gskip_o[...] += jnp.sum(dssm * mixed, axis=0, keepdims=True)
        dpre = (grad_steps * jax.nn.sigmoid(pre_s[rows, :])).astype(bf16)
        dpre_o[rows, :] = dpre
        weights = w_dt[pl.ds(pl.multiple_of(kind * rank, 16), rank), :]
        dlow = dot(weights, dpre, 1, 1)
        sums = dot(gs[...], gather, 1, 0).reshape(RUN, ns, LANES) * keep[None]
        fs[...] = (sums[:, :half] + sums[:, half:]).reshape(RUN * half, LANES)
        dbc = fs[pl.ds(0, RUN, stride=half), :]
        for s in range(1, half):
            dbc = dbc + fs[pl.ds(s, RUN, stride=half), :]
        dbc = dbc.T[: 2 * ns]
        at = pl.ds(pl.multiple_of(r * RUN, LANES), RUN)
        dpx_o[:rank, at] = dlow.astype(bf16)
        dpx_o[rank:, at] = dbc.astype(bf16)
        begin(move_rows([(gmix_o, gmix_h), (dpre_o, dpre_h)], out_sem, r, r * RUN, RUN))
        return carry

    last = tuple(states[total, :, lane[g]].astype(f32) for g in range(groups))
    done = lax.fori_loop(0, runs, backward, ((zero,) * groups, last, (zero,) * groups))
    for g in range(groups):
        glog_o[:, lane[g]] = done[2][g] * rates[:, lane[g]]

    def settle(r, carry):
        finish(move_rows([(gmix_o, gmix_h), (dpre_o, dpre_h)], out_sem, r, r * RUN, RUN))
        return carry

    lax.fori_loop(0, runs, settle, 0)
    finish(leaving)


def scan_call(rank, xw, ns, meta, kinds, cots, pieces, px, w_dt_l, table, mixed, act):
    (total, es), (own, d) = mixed.shape, cots[0].shape
    nar, wid = len(cots), len(pieces)
    out_cols = MODS * d
    bc_runs = total // RUN if total * ns * 2 * LANES * 4 <= 20 * 1024 * 1024 else 1
    return call(
        functools.partial(scan_kernel, nar, wid, rank),
        [((own, d), bf16, "a")] * nar
        + [
            ((total, es), bf16, "a"),
            ((total, es), f32, "a"),
            ((total, d), bf16, "a"),
            ((total, es), f32, "a"),
            ((total, es), bf16, "a"),
            ((xw, total), bf16, "v"),
            ((rank, total), bf16, "v"),
            ((ns, es), f32, "v"),
            ((1, es), f32, "v"),
        ],
        [(meta, "s"), (kinds, "s")]
        + [(p, "a") for p in cots]
        + [(p, "a") for p in pieces]
        + [(px, "v"), (w_dt_l, "v"), (table, "v"), (mixed, "a"), (act, "a")],
        [
            pltpu.VMEM((total, es), bf16),
            pltpu.VMEM((total, es), f32),
            pltpu.VMEM((total, d), bf16),
            pltpu.VMEM((es, out_cols), bf16),
            pltpu.VMEM((total, es), f32),
            pltpu.VMEM((total, es), f32),
            pltpu.VMEM((total, es), bf16),
            pltpu.VMEM((total, es), f32),
            pltpu.VMEM((total, d), bf16),
            pltpu.VMEM((total, es), f32),
            pltpu.VMEM((total, es), bf16),
            pltpu.SemaphoreType.DMA((2,)),
            pltpu.SemaphoreType.DMA((nar,)),
            pltpu.SemaphoreType.DMA((out_cols // pieces[0].shape[1], wid)),
            pltpu.SemaphoreType.DMA((3,)),
            pltpu.SemaphoreType.DMA((nar,)),
            pltpu.SemaphoreType.DMA((2, total // RUN)),
            pltpu.VMEM((xw, total), f32),
            pltpu.VMEM((total, es), f32),
            pltpu.VMEM((total, es), f32),
            pltpu.VMEM((total + 1, ns, es), bf16),
            pltpu.VMEM((bc_runs * RUN * ns, 2 * LANES), f32),
            pltpu.VMEM((es // LANES, RUN * ns // 2, LANES), f32),
            pltpu.VMEM((RUN * ns, 2 * LANES), bf16),
            pltpu.VMEM((RUN * ns // 2, LANES), f32),
            pltpu.VMEM((total, es), f32),
            pltpu.VMEM((total, es), f32),
            pltpu.VMEM((ns, es), f32),
            pltpu.VMEM((ns, es), f32),
            pltpu.VMEM((total, 16 * ns), bf16),
            pltpu.VMEM((total, 16 * ns), bf16),
            pltpu.VMEM((RUN, ns, es), bf16),
        ],
        us=40.0,
    )


def split_rows(acc, place, rows):
    return acc[pl.ds(pl.multiple_of(place * rows, 16), rows), :]


def grads_kernel(wid, ep, rank, meta, kinds, *refs):
    hbm, (dlow_r, glog_r, gskip_r) = refs[:6], refs[6:9]
    dgate_h, gate_h, w_out_h, table_o = refs[9:13]
    rows_in, (dgate_o, gate_o, w_out_o, acc_out, acc_in, in_sem, out_sem, block_sem) = refs[13:19], refs[19:]
    gated_r, dgs_r, slope_r, cot_r, normed_r, dpre_r = rows_in
    total, es = gated_r.shape
    d = cot_r.shape[1]
    size = total // CHUNKS
    arriving = [move_rows(list(zip(hbm, rows_in)), in_sem, c, c * size, size) for c in range(CHUNKS)]
    leaving = [move_rows([(dgate_o, dgate_h)], out_sem, c, c * size, size) for c in range(CHUNKS)]
    for copies in arriving:
        begin(copies)
    acc_out[...] = jnp.zeros_like(acc_out)
    acc_in[...] = jnp.zeros_like(acc_in)
    table_o[...] = jnp.zeros_like(table_o)
    base = MODS * rank

    def one_run(r, carry):
        rows = pl.ds(pl.multiple_of(r * RUN, RUN), RUN)
        kind = kinds[r]
        wide_at = pl.ds(pl.multiple_of(kind * d, LANES), d)
        es_at = pl.ds(pl.multiple_of(kind * es, LANES), es)
        acc_out[:, wide_at] += dot(gated_r[rows, :], cot_r[rows, :], 0, 0)
        dgate = (dgs_r[rows, :] * slope_r[rows, :]).astype(bf16)
        dgate_o[rows, :] = dgate
        acc_in[:, es_at] += dot(normed_r[rows, :], dgate, 0, 0)
        dpre = dpre_r[rows, :]
        low = dlow_r[:, pl.ds(pl.multiple_of(r * RUN, LANES), RUN)]
        table_o[pl.ds(pl.multiple_of(kind * rank, 8), rank), :] += dot(low, dpre, 1, 0)
        table_o[pl.ds(base + T_BIAS + kind, 1), :] += jnp.sum(dpre.astype(f32), axis=0, keepdims=True)
        return carry

    for c in range(CHUNKS):
        finish(arriving[c])
        each(c * size // RUN, size // RUN, one_run)
        begin(leaving[c])
    in_rows = acc_in.shape[0] // wid
    block_copies = []
    for k, (source, target) in enumerate(((gate_o, gate_h), (w_out_o, w_out_h))):
        for v in range(wid):
            if k == 0:
                gate_o[v] = acc_in[v * in_rows : (v + 1) * in_rows, :].astype(bf16)
            else:
                w_out_o[v] = acc_out[v * ep : (v + 1) * ep, :].astype(bf16)
            block_copies.append(pltpu.make_async_copy(source.at[v], target.at[v], block_sem.at[k, v]))
            block_copies[-1].start()
    table_o[base + T_SKIP : base + T_SKIP + 1, :] = gskip_r[...]
    table_o[base + T_LOG : base + T_LOG + glog_r.shape[0], :] = glog_r[...]
    for copies in leaving + [block_copies]:
        finish(copies)


def pair_kernel(chips, meta, same, peer, *outs):
    chip = meta[1] // 2
    for s in range(chips):
        outs[s][...] = (same[chip ^ s].astype(f32) + peer[chip ^ s].astype(f32)).astype(bf16)


def conv_kernel(nar, wid, taps, ep, meta, kinds, *refs):
    dpx_pieces = refs[:nar]
    table, w_x, table_r = refs[nar : nar + 3]
    hbm = refs[nar + 3 : nar + 8]
    dfront_h, same_h, peer_h = refs[nar + 8 : nar + 11]
    rows_in = refs[nar + 11 : nar + 16]
    dfront_o, same_o, peer_o, acc_in, acc_x, small, turned, in_sem, out_sem, block_sem = refs[nar + 16 :]
    gmix_r, csum_r, front_r, mixed_r, normed_r = rows_in
    split = meta[2]
    total, es = gmix_r.shape
    runs = total // RUN
    size = total // CHUNKS
    moves = [(a, b, 16) if b is front_r else (a, b) for a, b in zip(hbm, rows_in)]
    arriving = [move_rows(moves, in_sem, c, c * size, size) for c in range(CHUNKS)]
    leaving = [move_rows([(dfront_o, dfront_h)], out_sem, c, c * size, size) for c in range(CHUNKS)]
    for c in reversed(range(CHUNKS)):
        begin(arriving[c])
    front_r[0:16, :] = jnp.zeros((16, es), f32)
    acc_in[...] = jnp.zeros_like(acc_in)
    acc_x[...] = jnp.zeros_like(acc_x)
    small[...] = jnp.zeros_like(small)
    xw = dpx_pieces[0].shape[0]

    def one_run(back, later):
        r = runs - 1 - back
        rows = pl.ds(pl.multiple_of(r * RUN, RUN), RUN)
        kind = kinds[r]
        lanes_at = pl.ds(pl.multiple_of(r * RUN, LANES), RUN)
        dpx = sum(piece[:, lanes_at].astype(f32) for piece in dpx_pieces)
        dpx = jnp.concatenate([dpx, jnp.zeros((LANES - xw, RUN), f32)], axis=0).T.astype(bf16)
        x_at = pl.ds(pl.multiple_of(kind * LANES, LANES), LANES)
        acc_x[:, x_at] += dot(mixed_r[rows, :], dpx, 0, 0)
        gmix = gmix_r[rows, :] + dot(dpx, w_x[:, x_at], 1, 1)
        csum = csum_r[rows, :]
        sig = jax.nn.sigmoid(csum)
        dc = gmix * sig * (1.0 + csum * (1.0 - sig))
        place = r * RUN + lax.broadcasted_iota(jnp.int32, (RUN + 8, 1), 0)
        offset = place - jnp.where(place >= split, split, 0)
        ext = jnp.concatenate([dc, later], axis=0)
        lagged = front_r[pl.ds(pl.multiple_of(r * RUN + 8, 8), RUN + 8), :]
        d_front = jnp.zeros((RUN, es), f32)
        for lag in range(taps):
            tap = taps - 1 - lag
            masked = ext * (offset >= lag).astype(f32)
            d_front = d_front + table[T_CONV + tap : T_CONV + tap + 1, :] * masked[lag : lag + RUN, :]
            small[T_CONV + tap : T_CONV + tap + 1, :] += jnp.sum(
                masked[:RUN] * lagged[8 - lag : 8 - lag + RUN, :], axis=0, keepdims=True
            )
        small[T_CONV_B : T_CONV_B + 1, :] += jnp.sum(dc, axis=0, keepdims=True)
        d_front = d_front.astype(bf16)
        dfront_o[rows, :] = d_front
        acc_in[:, pl.ds(pl.multiple_of(kind * es, LANES), es)] += dot(normed_r[rows, :], d_front, 0, 0)
        return dc[:8]

    later = jnp.zeros((8, es), f32)
    for c in reversed(range(CHUNKS)):
        if c == CHUNKS - 1:
            finish(arriving[c])
        if c:
            finish(arriving[c - 1])
        back = (CHUNKS - 1 - c) * size // RUN
        later = each(back, size // RUN, one_run, later)
        begin(leaving[c])
    in_rows, width = acc_in.shape[0] // wid, acc_in.shape[1]
    base = table_r.shape[0] - small.shape[0]
    rest = jnp.concatenate([table_r[:base, :], table_r[base:, :] + small[...]], axis=0)
    rest = jnp.concatenate([rest, jnp.zeros((256 - rest.shape[0], es), f32)], axis=0).T
    x_cols = acc_x.shape[1]
    turned[:, :x_cols] = acc_x[...].astype(bf16)
    turned[:, x_cols : x_cols + 256] = rest.astype(bf16)
    turned[:, x_cols + 256 :] = jnp.zeros((es, width - x_cols - 256), bf16)
    core = meta[1] & 1
    block_copies = []
    for k, (ref, out, parity) in enumerate(((peer_o, peer_h, 1 - core), (same_o, same_h, core))):
        for c in range(wid // 2):
            place = 2 * c + parity
            ref[c, :in_rows, :] = split_rows(acc_in, place, in_rows).astype(bf16)
            ref[c, in_rows:, :] = split_rows(turned, place, ep)
            block_copies.append(pltpu.make_async_copy(ref.at[c], out.at[c], block_sem.at[k, c]))
            block_copies[-1].start()
    for copies in leaving + [block_copies]:
        finish(copies)


def normed_kernel(nar, wid, meta, kinds, *refs):
    fronts, gates = refs[:wid], refs[wid : 2 * wid]
    dfront_h, dgate_h = refs[2 * wid : 2 * wid + 2]
    outs = refs[2 * wid + 2 : 2 * wid + 2 + nar]
    dfront_r, dgate_r, wf, wg, dn, f_sem, g_sem, in_sem, part_sem = refs[2 * wid + 2 + nar :]
    total, es = dfront_r.shape
    size = total // nar
    weights = place_pieces(fronts, wf, f_sem, meta[1], wf.shape[0] // wid)
    weights += place_pieces(gates, wg, g_sem, meta[1], wg.shape[0] // wid)
    firsts = [(meta[0] ^ s) * size for s in range(nar)]
    arriving = [
        move_rows([(dfront_h, dfront_r), (dgate_h, dgate_r)], in_sem, s, firsts[s], size) for s in range(nar)
    ]
    part_copies = [
        pltpu.make_async_copy(dn.at[pl.ds(pl.multiple_of(firsts[s], RUN), size), :], outs[s], part_sem.at[s])
        for s in range(nar)
    ]
    begin(weights)
    for s in reversed(range(nar)):
        begin(arriving[s])
    finish(weights)

    def one_run(r, carry):
        rows = pl.ds(pl.multiple_of(r * RUN, RUN), RUN)
        at = pl.ds(pl.multiple_of(kinds[r] * es, LANES), es)
        dn[rows, :] = (dot(dfront_r[rows, :], wf[:, at], 1, 1) + dot(dgate_r[rows, :], wg[:, at], 1, 1)).astype(bf16)
        return carry

    for s in reversed(range(nar)):
        finish(arriving[s])
        first = (meta[0] ^ s) * (size // RUN)
        each(first, size // RUN, one_run)
        part_copies[s].start()
    finish(part_copies)


def total_gate_kernel(blocks, out):
    out[...] = sum(blocks[v].astype(f32) for v in range(blocks.shape[0])).astype(bf16)


def total_out_kernel(er, blocks, out):
    d = out.shape[2]
    summed = sum(blocks[v, :er, :].astype(f32) for v in range(blocks.shape[0]))
    for m in range(MODS):
        out[m] = summed[:, m * d : (m + 1) * d]


def total_b_kernel(nar, chips, er, rank, taps, ns, meta, *refs):
    pieces, gate_r, outs = refs[:chips], refs[chips], refs[chips + 1 : chips + 1 + nar]
    x_o, dt_o, bias_o, conv_o, conv_b_o, log_o, skip_o, rows_s = refs[chips + 1 + nar :]
    dr, width = outs[0].shape[0], gate_r.shape[1]
    in_rows = nar * dr
    summed = sum(piece[...].astype(f32) for piece in pieces)
    gate = gate_r[...].astype(f32)
    for k in range(nar):
        rows_s[k, :, :width] = summed[k * dr : (k + 1) * dr].astype(bf16)
        rows_s[k, :, width:] = gate[k * dr : (k + 1) * dr].astype(bf16)
    for s in range(nar):
        outs[s][...] = rows_s[meta[0] ^ s]
    rest = summed[in_rows:]
    x_cols = MODS * LANES
    for m in range(MODS):
        x_o[m] = rest[:er, m * LANES : m * LANES + x_o.shape[2]]
    lanes = rest[:, x_cols : x_cols + 256]
    pad = LANES - lanes.shape[0]
    turned = jnp.concatenate([lanes, jnp.zeros((pad, 256), f32)], axis=0).T[:, :er]
    base = MODS * rank
    for m in range(MODS):
        dt_o[m] = turned[m * rank : (m + 1) * rank]
    bias_o[...] = turned[base + T_BIAS : base + T_BIAS + MODS]
    conv_o[...] = turned[base + T_CONV : base + T_CONV + taps]
    conv_b_o[...] = turned[base + T_CONV_B : base + T_CONV_B + 1]
    skip_o[...] = turned[base + T_SKIP : base + T_SKIP + 1]
    log_o[...] = turned[base + T_LOG : base + T_LOG + ns]


def tokens_kernel(x_r, cot_r, gain_r, *refs):
    pieces, out = refs[:-1], refs[-1]
    x = x_r[...].astype(f32)
    scale = lax.rsqrt(jnp.mean(x * x, axis=1, keepdims=True) + EPSILON)
    q = sum(piece[...].astype(f32) for piece in pieces) * gain_r[...]
    dotted = jnp.mean(q * x, axis=1, keepdims=True)
    out[...] = (cot_r[...].astype(f32) + scale * q - x * (scale * scale * scale) * dotted).astype(bf16)


def mixed_kernel(x_r, *refs):
    pieces, out = refs[:-1], refs[-1]
    out[...] = (x_r[...].astype(f32) + sum(piece[...].astype(f32) for piece in pieces)).astype(bf16)


def in_order(parts, er, ep, wid):
    return jnp.concatenate([part[:, v * ep : v * ep + er] for v in range(wid) for part in parts], axis=1)


def w_in_kernel(nar, wid, er, ep, meta, *refs):
    pieces, (w_h, gain_r, grad_h, gain_o, rows_s, w_r, grad_s, w_sem, out_sem) = refs[:nar], refs[nar:]
    dr = pieces[0].shape[0]
    es, inner = wid * ep, wid * nar * er
    loading = pltpu.make_async_copy(w_h, w_r, w_sem)
    loading.start()
    for s in range(nar):
        rows_s[meta[0] ^ s] = pieces[s][...].astype(f32)
    sums, storing = 0.0, []
    for m in range(MODS):
        for half in range(2):
            first = (half * MODS + m) * es
            row = in_order([rows_s[k, :, first : first + es] for k in range(nar)], er, ep, wid)
            at = slice(half * inner, (half + 1) * inner)
            grad_s[m, :, at] = row
            if m + half == 0:
                loading.wait()
            sums = sums + jnp.sum(row * w_r[m, :, at].astype(f32), axis=1, keepdims=True)
        storing.append(pltpu.make_async_copy(grad_s.at[m], grad_h.at[m], out_sem.at[m]))
        storing[m].start()
    sums = jnp.broadcast_to(sums, (dr, LANES))
    sums = jnp.concatenate([sums, jnp.zeros((LANES - dr, LANES), f32)], axis=0).T[0:1, :dr]
    gain_o[...] = sums / gain_r[...].astype(f32)
    finish(storing)


def body(
    tokens,
    norm_gain,
    w_in,
    conv_w,
    conv_b,
    w_x,
    w_dt,
    dt_bias,
    a_log,
    d_skip,
    w_out,
    mod_ids,
    split_at,
    cotangent,
):
    nar, wid = lax.axis_size("narrow"), lax.axis_size("wide")
    chips = wid // 2
    n, w = lax.axis_index("narrow"), lax.axis_index("wide")
    own, d = tokens.shape
    total = nar * own
    rpd = own // RUN
    rank, xw, ns, taps = w_dt.shape[0], w_x.shape[2], a_log.shape[1], conv_w.shape[0]
    er = w_out.shape[0]
    inner = er * nar * wid
    ep = -(-er // 16) * 16
    es = ep * wid
    dr = w_in.shape[0]
    width = MODS * es
    meta = jnp.stack([n, w, split_at[0]]).astype(jnp.int32)

    front_w = width + LANES
    gain_row = norm_gain[None]
    w_in_m = w_in.transpose(1, 0, 2)
    out_cols, x_cols = MODS * d, MODS * LANES
    table_rows = T_LOG + ns
    small_cols = x_cols + 256
    blocks = front_w // small_cols
    below = -(-(-(-ep // blocks)) // 16) * 16
    res = call(
        functools.partial(split_kernel, er, ep, wid, below),
        [((dr, front_w + width), bf16, "v")] * nar
        + [((below, front_w), bf16, "v"), ((ep * (out_cols // width), width), bf16, "v")],
        [
            (a, "v")
            for a in (
                w_in_m,
                gain_row,
                w_out.transpose(1, 0, 2),
                w_x.transpose(1, 0, 2),
                w_dt.transpose(1, 0, 2),
                dt_bias,
                conv_w,
                conv_b[None],
                d_skip[None],
                a_log.T,
            )
        ],
        [
            pltpu.VMEM((nar, dr, front_w + width), bf16),
            pltpu.VMEM((256, LANES), f32),
        ],
        us=3.0,
    )
    parts, (small, out_rows) = res[:nar], res[nar:]

    parts = scatter_narrow(parts)
    front_rows, gate_rows = call(
        join_kernel,
        [
            ((nar * dr + below, front_w), bf16, "v"),
            ((nar * dr + out_rows.shape[0], width), bf16, "v"),
        ],
        [(meta, "s")] + [(p, "v") for p in parts] + [(small, "v"), (out_rows, "v")],
        us=2.0,
    )
    front_near = near_wide(front_rows)
    front_pieces = far_wide(front_near)
    run_kinds = mod_ids.reshape(rpd, RUN)[:, :1].astype(bf16)
    tail = jnp.pad(jnp.broadcast_to(run_kinds, (rpd, d)), ((0, 16 - rpd), (0, 0)))
    tok_pieces = relay_narrow(jnp.concatenate([tokens, tail], axis=0))
    gate_near = near_wide(after(gate_rows, *front_near[1:]))
    normed, front, csum, mixed, px, kinds, w_x_l, w_dt_l, table, gain_full = call(
        functools.partial(in_kernel, nar, wid, rpd, taps, ep, rank),
        [
            ((total, d), bf16, "a"),
            ((total, es), f32, "a"),
            ((total, es), f32, "a"),
            ((total, es), bf16, "a"),
            ((xw, total), bf16, "v"),
            ((nar * rpd,), jnp.int32, "s"),
            ((es, x_cols), bf16, "v"),
            ((MODS * rank, es), bf16, "v"),
            ((256 - MODS * rank, es), f32, "v"),
            ((1, d), f32, "v"),
        ],
        [(meta, "s")] + [(p, "a") for p in tok_pieces] + [(p, "a") for p in front_pieces],
        [
            pltpu.VMEM((total, d), bf16),
            pltpu.VMEM((total, es), f32),
            pltpu.VMEM((total, es), f32),
            pltpu.VMEM((total, es), bf16),
            pltpu.VMEM((nar * (own + 16), d), bf16),
            pltpu.VMEM((d, front_w), bf16),
            pltpu.VMEM((es, small_cols), bf16),
            pltpu.SemaphoreType.DMA((nar,)),
            pltpu.SemaphoreType.DMA((wid,)),
            pltpu.SemaphoreType.DMA((-(-ep // below), wid)),
            pltpu.SemaphoreType.DMA((4, CHUNKS)),
        ],
        us=9.0,
    )
    cot_pieces = relay_narrow(after(cotangent, *tok_pieces[1:]), px)
    gate_pieces = far_wide([after(piece, px) for piece in gate_near])
    act, slope = call(
        functools.partial(gate_kernel, wid),
        [((total, es), f32, "a")] * 2,
        [(meta, "s"), (kinds, "s")]
        + [(p, "a") for p in gate_pieces]
        + [(after(normed, *cot_pieces[1:3]), "a")],
        [
            pltpu.VMEM((total, d), bf16),
            pltpu.VMEM((total, es), f32),
            pltpu.VMEM((total, es), f32),
            pltpu.VMEM((d, width), bf16),
            pltpu.SemaphoreType.DMA((wid,)),
            pltpu.SemaphoreType.DMA((1, CHUNKS)),
            pltpu.SemaphoreType.DMA((2, CHUNKS)),
        ],
        us=0.1,
    )
    px_total = add_narrow(px, act, cot_pieces[-1])
    res = scan_call(
        rank, xw, ns, meta, kinds, cot_pieces, gate_pieces, px_total, w_dt_l, table, mixed, act
    )
    branch_parts, (gated, dgs, cot, gmix, dpre, dpx, dlow, glog, gskip) = res[:nar], res[nar:]
    dpx_pieces = gather_narrow(dpx)
    branch_pieces = scatter_narrow(branch_parts)
    in_rows = d // wid
    dgate, gate_blocks, w_out_blocks, table_g = call(
        functools.partial(grads_kernel, wid, ep, rank),
        [
            ((total, es), bf16, "a"),
            ((wid, in_rows, width), bf16, "a"),
            ((wid, ep, out_cols), bf16, "a"),
            ((MODS * rank + table_rows, es), f32, "v"),
        ],
        [(meta, "s"), (kinds, "s")]
        + [(a, "a") for a in (gated, dgs, slope, cot, normed, dpre)]
        + [(a, "v") for a in (dlow, glog, gskip)],
        [
            pltpu.VMEM((total, es), bf16),
            pltpu.VMEM((total, es), f32),
            pltpu.VMEM((total, es), f32),
            pltpu.VMEM((total, d), bf16),
            pltpu.VMEM((total, d), bf16),
            pltpu.VMEM((total, es), bf16),
            pltpu.VMEM((total, es), bf16),
            pltpu.VMEM((wid, in_rows, width), bf16),
            pltpu.VMEM((wid, ep, out_cols), bf16),
            pltpu.VMEM((es, out_cols), f32),
            pltpu.VMEM((d, width), f32),
            pltpu.SemaphoreType.DMA((6, CHUNKS)),
            pltpu.SemaphoreType.DMA((1, CHUNKS)),
            pltpu.SemaphoreType.DMA((2, wid)),
        ],
        us=9.0,
    )

    def over_wide(same, peer, *earlier):
        peer = swap(peer, "wide", 1)
        same = after(same, *earlier) if earlier else same
        parts = call(
            functools.partial(pair_kernel, chips),
            [(same.shape[1:], bf16, "v")] * chips,
            [(meta, "s"), (same, "v"), (peer, "v")],
            us=3.0,
        )
        return [parts[0]] + [swap(parts[s], "wide", 2 * s) for s in range(1, chips)]

    gate_blocks = lax.all_to_all(gate_blocks, "wide", 0, 0)
    rows_b = in_rows + ep
    dfront, same_b, peer_b = call(
        functools.partial(conv_kernel, nar, wid, taps, ep),
        [((total, es), bf16, "a")] + [((chips, rows_b, width), bf16, "a")] * 2,
        [(meta, "s"), (kinds, "s")]
        + [(p, "v") for p in dpx_pieces]
        + [(a, "v") for a in (table, w_x_l, table_g)]
        + [(a, "a") for a in (gmix, csum, front, mixed, normed)],
        [
            pltpu.VMEM((total, es), f32),
            pltpu.VMEM((total, es), f32),
            pltpu.VMEM((total + 16, es), f32),
            pltpu.VMEM((total, es), bf16),
            pltpu.VMEM((total, d), bf16),
            pltpu.VMEM((total, es), bf16),
            pltpu.VMEM((chips, rows_b, width), bf16),
            pltpu.VMEM((chips, rows_b, width), bf16),
            pltpu.VMEM((d, width), f32),
            pltpu.VMEM((es, x_cols), f32),
            pltpu.VMEM((table_rows, es), f32),
            pltpu.VMEM((es, width), bf16),
            pltpu.SemaphoreType.DMA((5, CHUNKS)),
            pltpu.SemaphoreType.DMA((1, CHUNKS)),
            pltpu.SemaphoreType.DMA((2, chips)),
        ],
        us=12.0,
    )
    dn_parts = call(
        functools.partial(normed_kernel, nar, wid),
        [((own, d), bf16, "a")] * nar,
        [(meta, "s"), (kinds, "s")]
        + [(p, "a") for p in front_pieces]
        + [(p, "a") for p in gate_pieces]
        + [(dfront, "a"), (dgate, "a")],
        [
            pltpu.VMEM((total, es), bf16),
            pltpu.VMEM((total, es), bf16),
            pltpu.VMEM((d, width), bf16),
            pltpu.VMEM((d, width), bf16),
            pltpu.VMEM((total, d), bf16),
            pltpu.SemaphoreType.DMA((wid,)),
            pltpu.SemaphoreType.DMA((wid,)),
            pltpu.SemaphoreType.DMA((2, nar)),
            pltpu.SemaphoreType.DMA((nar,)),
        ],
        us=30.0,
    )
    pieces_b = over_wide(same_b, peer_b, dn_parts[0])
    dn_pieces, dn_kept = sum_narrow(dn_parts, pieces_b[0])

    mixed_out = call(
        mixed_kernel,
        [((own, d), bf16, "v")],
        [(tokens, "v")] + [(p, "v") for p in after(tuple(branch_pieces), pieces_b[0])],
        us=2.0, small=True,
    )[0]
    gate_sum = call(
        total_gate_kernel,
        [((in_rows, width), bf16, "v")],
        [(after(gate_blocks, mixed_out, dn_kept), "v")],
        us=2.0, small=True,
    )[0]
    res = call(
        functools.partial(total_b_kernel, nar, chips, er, rank, taps, ns),
        [((dr, 2 * width), bf16, "v")] * nar
        + [
            ((MODS, er, xw), f32, "v"),
            ((MODS, rank, er), f32, "v"),
            ((MODS, er), f32, "v"),
            ((taps, er), f32, "v"),
            ((1, er), f32, "v"),
            ((ns, er), f32, "v"),
            ((1, er), f32, "v"),
        ],
        [(meta, "s")] + [(p, "v") for p in pieces_b] + [(gate_sum, "v")],
        [pltpu.VMEM((nar, dr, 2 * width), bf16)],
        us=3.0, small=True,
    )
    back_parts = res[:nar]
    grad_w_x, grad_w_dt, grad_dt_bias, grad_conv_w, grad_conv_b, grad_log, grad_skip = res[nar:]
    back_pieces = scatter_narrow(back_parts)
    grad_tokens = call(
        tokens_kernel,
        [((own, d), bf16, "v")],
        [(tokens, "v"), (cotangent, "v"), (gain_full, "v")]
        + [(p, "v") for p in dn_pieces],
        us=0.1, small=True,
    )[0]
    w_out_blocks = lax.all_to_all(after(w_out_blocks, gate_sum), "wide", 0, 0)
    grad_w_in, grad_gain = call(
        functools.partial(w_in_kernel, nar, wid, er, ep),
        [((MODS, dr, 2 * inner), f32, "a"), ((1, dr), f32, "v")],
        [(meta, "s")] + [(p, "v") for p in back_pieces] + [(after(w_in_m, grad_tokens), "a"), (gain_row, "v")],
        [
            pltpu.VMEM((nar, dr, 2 * width), f32),
            pltpu.VMEM((MODS, dr, 2 * inner), bf16),
            pltpu.VMEM((MODS, dr, 2 * inner), f32),
            pltpu.SemaphoreType.DMA(()),
            pltpu.SemaphoreType.DMA((MODS,)),
        ],
        us=13.0, small=True,
    )
    grad_w_out = call(
        functools.partial(total_out_kernel, er),
        [((MODS, er, d), f32, "v")],
        [(after(w_out_blocks, grad_gain), "v")],
        us=3.0, small=True,
    )[0]
    grad_w_in, grad_w_out = grad_w_in.transpose(1, 0, 2), grad_w_out.transpose(1, 0, 2)
    grad_w_x, grad_w_dt = grad_w_x.transpose(1, 0, 2), grad_w_dt.transpose(1, 0, 2)
    grad_log = grad_log.T
    return (
        mixed_out,
        grad_tokens,
        grad_gain[0],
        grad_w_in,
        grad_conv_w,
        grad_conv_b[0],
        grad_w_x,
        grad_w_dt,
        grad_dt_bias,
        grad_log,
        grad_skip[0],
        grad_w_out,
    )


def solution(mesh):
    both = ("wide", "narrow")
    return jax.shard_map(
        body,
        mesh=mesh,
        in_specs=(
            P(both, None),
            P(both),
            P(both, None, None),
            P(None, both),
            P(both),
            P(both, None, None),
            P(None, None, both),
            P(None, both),
            P(both, None),
            P(both),
            P(both, None, None),
            P(both),
            P("wide"),
            P(both, None),
        ),
        out_specs=(
            P(both, None),
            P(both, None),
            P(both),
            P(both, None, None),
            P(None, both),
            P(both),
            P(both, None, None),
            P(None, None, both),
            P(None, both),
            P(both, None),
            P(both),
            P(both, None, None),
        ),
        check_vma=False,
    )
```
